32 devices in a mesh: band: 8 (over y, x, core), samp: 4 (over z).
Axes of the slice: x: 2, y: 2, z: 4, core: 2. Of those that a mesh axis runs over, the one named last changes fastest.
Arguments:
- tokens: bfloat16 [4, 1024, 1024], P('samp', 'band'), may hold values from -6 to 6
- cotangent: bfloat16 [4, 1024, 1024], P('samp', 'band'), may hold values from -6 to 6
- w_qkv: bfloat16 [1024, 3072], P(('band', 'samp')), may hold values from -0.25 to 0.25
- w_out: bfloat16 [1024, 1024], P(('band', 'samp')), may hold values from -0.375 to 0.375
- w_up: bfloat16 [1024, 4096], P(('band', 'samp')), may hold values from -0.1875 to 0.1875
- w_down: bfloat16 [4096, 1024], P(('band', 'samp')), may hold values from -0.1875 to 0.1875
- up_bias: bfloat16 [4096], P(('band', 'samp')), may hold values from -3 to 3
- norm_gains: bfloat16 [2, 1024], P(None, ('band', 'samp')), may hold values from 0.099609375 to 1.8984375
- shift_rows: bfloat16 [6, 1024], P(None, ('band', 'samp')), may hold values from -3 to 3
- lead_weight: bfloat16 [2, 1024], P(None, ('band', 'samp')), may hold values from -3 to 3
- lead_steps: int32 [4], P('samp'), may hold values from 0 to 28
- valid_cells: int32 [4, 1024], P('samp', 'band'), may hold values from 0 to 4, as said below
Outputs:
- output: bfloat16 [4, 1024, 1024], P('samp', 'band')
- input_grad: bfloat16 [4, 1024, 1024], P('samp', 'band')
- grad_qkv: float32 [1024, 3072], P(('band', 'samp'))
- grad_out: float32 [1024, 1024], P(('band', 'samp'))
- grad_up: float32 [1024, 4096], P(('band', 'samp'))
- grad_down: float32 [4096, 1024], P(('band', 'samp'))
- grad_up_bias: float32 [4096], P(('band', 'samp'))
- grad_gains: float32 [2, 1024], P(None, ('band', 'samp'))
- grad_shifts: float32 [6, 1024], P(None, ('band', 'samp'))
- grad_lead: float32 [2, 1024], P(None, ('band', 'samp'))
The draws below stay inside these ranges and needn't reach their ends.
Inputs may be any that keep to these rules, and one draw needn't show every extreme that they name: `valid_cells`: each entry counts the valid cells among a patch's 4 cells; a patch with none is masked as a key. Each sample's first and last patches are valid.
All inputs are finite; a program needn't handle non-finite values.
Results may differ from the reference program's by a relative error of at most 0.015.
Values may be sent and summed in bfloat16 or wider, within the bound.
A program may use at most 320 MiB of HBM per device.

```python
import jax
import jax.numpy as jnp
from jax import lax

D = 1024
HEADS = 16
FF = 4096
SEQ = 1024
SAMPLES = 4
KEY_BLOCK = 512


def draw_valid_cells(key, part):
    key = jax.random.fold_in(key, 7)
    key_rate, key_roll, key_count = jax.random.split(key, 3)
    position = jnp.arange(SEQ, dtype=jnp.int32)
    polar = jnp.abs(2 * position - (SEQ - 1)) * 1000 // SEQ
    rate = jax.random.randint(key_rate, (SAMPLES, 1), 200, 900)
    cutoff = rate * polar[None, :] * polar[None, :] // 1000000
    roll = jax.random.randint(key_roll, (SAMPLES, SEQ), 0, 1000)
    counts = jax.random.randint(key_count, (SAMPLES, SEQ), 1, 5)
    cells = jnp.where(roll < cutoff, 0, counts)
    cells = cells.at[:, 0].set(4).at[:, SEQ - 1].set(4).at[:, 1].set(0)
    return cells.astype(jnp.int32)


def place_ends(drawn, own_key, smallest, top_value):
    dims = drawn.shape
    spot = [jax.random.randint(jax.random.fold_in(own_key, axis), (), 0, dims[axis]) for axis in range(len(dims))]
    drawn = drawn.at[tuple(spot)].set(smallest)
    longest = dims.index(max(dims))
    spot[longest] = (spot[longest] + 1) % dims[longest]
    return drawn.at[tuple(spot)].set(top_value)


def level_of(stream_key, dims, cuts, smallest, high):
    gain = 1.0
    for axis_at, parts in cuts:
        draws = jax.random.uniform(jax.random.fold_in(jax.random.fold_in(stream_key, 6), axis_at), (parts,), jnp.float32, smallest / len(cuts), high / len(cuts))
        gain = gain * jnp.repeat(jnp.exp(draws), dims[axis_at] // parts).reshape((-1,) + (1,) * (len(dims) - 1 - axis_at))
    return gain


def bell_draw(own_key, shape, deviation, most, cuts=(), kind=jnp.bfloat16):
    entries = deviation * jax.random.normal(own_key, shape, jnp.float32)
    if cuts:
        entries = entries * level_of(own_key, shape, cuts, -0.22, 0.18)
    return jnp.clip(entries, -most, most).astype(kind)


def setup_inputs(seed: int = 0) -> dict:
    key_of = jax.random.split(jax.random.key(seed), 13)
    return {
        "tokens": bell_draw(key_of[0], (SAMPLES, SEQ, D), 1.0, 6.0, ((0, 4), (1, 8))),
        "cotangent": bell_draw(key_of[1], (SAMPLES, SEQ, D), 1.0, 6.0, ((0, 4), (1, 8))),
        "w_qkv": bell_draw(key_of[2], (D, 3 * D), (D // 2) ** -0.5, 0.25, ((0, 32),)),
        "w_out": bell_draw(key_of[3], (D, D), (D // 4) ** -0.5, 0.375, ((0, 32),)),
        "w_up": bell_draw(key_of[4], (D, FF), D ** -0.5, 0.1875, ((0, 32),)),
        "w_down": bell_draw(key_of[5], (FF, D), (FF // 4) ** -0.5, 0.1875, ((0, 32),)),
        "up_bias": bell_draw(key_of[6], (FF,), 0.5, 3.0, ((0, 32),)),
        "norm_gains": jnp.clip(1.0 + 0.18 * jax.random.normal(key_of[7], (2, D), jnp.float32), 0.099609375, 1.8984375).astype(jnp.bfloat16),
        "shift_rows": bell_draw(key_of[8], (6, D), 0.5, 3.0, ((1, 32),)),
        "lead_weight": bell_draw(key_of[9], (2, D), 0.5, 3.0, ((1, 32),)),
        "lead_steps": place_ends(jax.random.randint(key_of[10], (SAMPLES,), 0, 29), jax.random.fold_in(key_of[10], 1), 0, 28).astype(jnp.int32),
        "valid_cells": draw_valid_cells(jax.random.fold_in(key_of[12], 71), 0),
    }


eps = 1e-05
masked = 10000.0
highest = lax.Precision.HIGHEST

@jax.custom_vjp
def low(v):
    return lax.optimization_barrier(v.astype(jnp.bfloat16)).astype(jnp.float32)

@jax.custom_vjp
def low_back(v):
    return v

def low_keep(v):
    return (low(v), None)

def low_pass(kept, grad):
    return (grad,)

def back_keep(v):
    return (v, None)

def back_low(kept, grad):
    return (low(grad),)
low.defvjp(low_keep, low_pass)
low_back.defvjp(back_keep, back_low)

def layer_norm(values, gain_row, shift_row):
    centered = values - lax.optimization_barrier(jnp.mean(values, axis=-1, keepdims=True))
    variance = lax.optimization_barrier(jnp.mean(centered * centered, axis=-1, keepdims=True))
    return centered * lax.rsqrt(variance + eps) * gain_row + shift_row

def one_sample(params, sample_rows, lead_days, open_keys):
    w_qkv, w_out, w_up, w_down, up_bias, norm_gains, shift_rows, lead_weight = params
    head_size = D // HEADS
    score_scale = head_size ** (-0.5)
    entering = sample_rows + lead_days * lead_weight[0] + lead_weight[1]
    normed = low(layer_norm(entering, norm_gains[0], shift_rows[0]))
    project = jnp.dot(normed, w_qkv, precision=highest)
    queries = low(low_back(project[:, :D] + shift_rows[1]))
    keys_all = low(low_back(project[:, D:2 * D]))
    values_all = low(low_back(project[:, 2 * D:] + shift_rows[2]))
    query_heads = queries.reshape(SEQ // KEY_BLOCK, KEY_BLOCK, HEADS, head_size)
    key_heads = keys_all.reshape(SEQ, HEADS, head_size)
    value_heads = values_all.reshape(SEQ, HEADS, head_size)
    key_bias = (open_keys - 1.0) * masked

    def attend(query_block):
        scores = jnp.einsum('qhe,khe->hqk', query_block, key_heads, precision=highest) * score_scale + key_bias
        scores = low_back(scores)
        weights = jax.nn.softmax(scores, axis=-1)
        return jnp.einsum('hqk,khe->qhe', low(weights), value_heads, precision=highest)
    attended = lax.map(jax.checkpoint(attend), query_heads).reshape(SEQ, D)
    attended = low(low_back(attended))
    branch = low_back(jnp.dot(attended, w_out, precision=highest) + shift_rows[3])
    middle = entering + branch
    second = low(layer_norm(middle, norm_gains[1], shift_rows[4]))
    hidden_pre = low_back(jnp.dot(second, w_up, precision=highest) + up_bias)
    hidden = low(jax.nn.gelu(hidden_pre, approximate=False))
    return middle + jnp.dot(hidden, w_down, precision=highest) + shift_rows[5]

def reference(tokens, cotangent, w_qkv, w_out, w_up, w_down, up_bias, norm_gains, shift_rows, lead_weight, lead_steps, valid_cells):
    params = tuple((tensor.astype(jnp.float32) for tensor in (w_qkv, w_out, w_up, w_down, up_bias, norm_gains, shift_rows, lead_weight)))
    lead_days = lead_steps.astype(jnp.float32) * 0.25
    open_keys = (valid_cells > 0).astype(jnp.float32)

    def forward(inputs, weights):

        def per_sample(pieces):
            return one_sample(weights, pieces[0], pieces[1], pieces[2])
        return lax.map(per_sample, (inputs, lead_days, open_keys))
    result, pullback = jax.vjp(forward, tokens.astype(jnp.float32), params)
    input_grad, gradients = pullback(cotangent.astype(jnp.float32))
    return (result.astype(jnp.bfloat16), input_grad.astype(jnp.bfloat16), gradients[0], gradients[1], gradients[2], gradients[3], gradients[4], gradients[5], gradients[6], gradients[7])
```

```python
import jax
import jax.numpy as jnp
from jax import lax
from jax.experimental import pallas as pl
from jax.experimental.pallas import tpu as pltpu
from jax.sharding import PartitionSpec as P

HEADS = 16


eps = 1e-05
masked = 10000.0


def layer_norm(values, gain_row, shift_row):
    centered = values - jnp.mean(values, axis=-1, keepdims=True)
    variance = jnp.mean(centered * centered, axis=-1, keepdims=True)
    return centered * lax.rsqrt(variance + eps) * gain_row + shift_row


def gelu_exact(values):
    return jax.nn.gelu(values, approximate=False)


def body(
    tokens,
    cotangent,
    w_qkv,
    w_out,
    w_up,
    w_down,
    up_bias,
    norm_gains,
    shift_rows,
    lead_weight,
    lead_steps,
    valid_cells,
):
    whole = (
        lax.all_gather(w_qkv, ("band", "samp"), axis=0, tiled=True),
        lax.all_gather(w_out, ("band", "samp"), axis=0, tiled=True),
        lax.all_gather(w_up, ("band", "samp"), axis=0, tiled=True),
        lax.all_gather(w_down, ("band", "samp"), axis=0, tiled=True),
        lax.all_gather(up_bias, ("band", "samp"), axis=0, tiled=True),
        lax.all_gather(norm_gains, ("band", "samp"), axis=1, tiled=True),
        lax.all_gather(shift_rows, ("band", "samp"), axis=1, tiled=True),
        lax.all_gather(lead_weight, ("band", "samp"), axis=1, tiled=True),
    )
    qkv_full = whole[0]
    out_full = whole[1]
    up_full = whole[2]
    down_full = whole[3]
    up_shift = whole[4].astype(jnp.float32)
    gain_all = whole[5].astype(jnp.float32)
    shift_all = whole[6].astype(jnp.float32)
    lead_all = whole[7].astype(jnp.float32)
    row_count = tokens.shape[1]
    width = tokens.shape[2]
    head_count = HEADS
    head_size = width // head_count
    score_scale = head_size ** (-0.5)
    lead_days = lead_steps[0].astype(jnp.float32) * 0.25
    entering = tokens[0].astype(jnp.float32) + lead_days * lead_all[0] + lead_all[1]
    normed, norm_first_back = jax.vjp(layer_norm, entering, gain_all[0], shift_all[0])
    normed_low = normed.astype(jnp.bfloat16)
    project = jnp.dot(normed_low, qkv_full, preferred_element_type=jnp.float32)
    queries = (project[:, :width] + shift_all[1]).astype(jnp.bfloat16)
    key_rows = project[:, width : 2 * width].astype(jnp.bfloat16)
    value_rows = (project[:, 2 * width :] + shift_all[2]).astype(jnp.bfloat16)
    key_open = (valid_cells[0] > 0).astype(jnp.bfloat16)
    keys_all, values_all, open_all = (
        lax.all_gather(key_rows, "band", axis=0, tiled=True),
        lax.all_gather(value_rows, "band", axis=0, tiled=True),
        lax.all_gather(key_open, "band", axis=0, tiled=True),
    )
    seq_total = keys_all.shape[0]
    block_rows = min(512, seq_total)
    block_count = seq_total // block_rows
    block_ids = jnp.arange(block_count)
    bias_all = (open_all.astype(jnp.float32) - 1.0) * masked
    query_heads = queries.reshape(row_count, head_count, head_size)

    def block_keys(step_index):
        first_row = step_index * block_rows
        key_block = lax.dynamic_slice_in_dim(keys_all, first_row, block_rows, 0).reshape(
            block_rows, head_count, head_size
        )
        value_block = lax.dynamic_slice_in_dim(values_all, first_row, block_rows, 0).reshape(
            block_rows, head_count, head_size
        )
        bias_block = lax.dynamic_slice_in_dim(bias_all, first_row, block_rows, 0)
        scores = (
            jnp.einsum("qhe,khe->hqk", query_heads, key_block, preferred_element_type=jnp.float32)
            * score_scale
            + bias_block
        )
        return (scores, key_block, value_block)

    def max_step(running, step_index):
        row_max, exp_total = running
        scores = block_keys(step_index)[0]
        new_max = jnp.maximum(row_max, jnp.max(scores, axis=-1))
        exp_total = exp_total * jnp.exp(row_max - new_max) + jnp.sum(
            jnp.exp(scores - new_max[..., None]), axis=-1
        )
        return ((new_max, exp_total), None)

    start_max = jnp.full((head_count, row_count), -jnp.inf, jnp.float32)
    start_total = jnp.zeros((head_count, row_count), jnp.float32)
    row_max, exp_total = lax.scan(max_step, (start_max, start_total), block_ids)[0]
    log_total = row_max + jnp.log(exp_total)

    def out_step(running, step_index):
        scores, key_block, value_block = block_keys(step_index)
        weights_low = jnp.exp(scores - log_total[..., None]).astype(jnp.bfloat16)
        return (
            running
            + jnp.einsum(
                "hqk,khe->qhe", weights_low, value_block, preferred_element_type=jnp.float32
            ),
            None,
        )

    attended_heads = lax.scan(
        out_step, jnp.zeros((row_count, head_count, head_size), jnp.float32), block_ids
    )[0]
    attended_low = attended_heads.reshape(row_count, width).astype(jnp.bfloat16)
    middle = (
        entering
        + jnp.dot(attended_low, out_full, preferred_element_type=jnp.float32)
        + shift_all[3]
    )
    second, norm_second_back = jax.vjp(layer_norm, middle, gain_all[1], shift_all[4])
    second_low = second.astype(jnp.bfloat16)
    hidden_pre = jnp.dot(second_low, up_full, preferred_element_type=jnp.float32) + up_shift
    hidden, gelu_back = jax.vjp(gelu_exact, hidden_pre)
    hidden_low = hidden.astype(jnp.bfloat16)
    result = (
        middle + jnp.dot(hidden_low, down_full, preferred_element_type=jnp.float32) + shift_all[5]
    )
    output = result.astype(jnp.bfloat16)
    grad_result = cotangent[0]
    grad_result_f = grad_result.astype(jnp.float32)
    grad_down_w = jnp.einsum(
        "tf,td->fd", hidden_low, grad_result, preferred_element_type=jnp.float32
    )
    grad_shift_down = jnp.sum(grad_result_f, axis=0)
    grad_hidden = jnp.einsum(
        "td,fd->tf", grad_result, down_full, preferred_element_type=jnp.float32
    )
    grad_pre_low = gelu_back(grad_hidden)[0].astype(jnp.bfloat16)
    grad_up_w = jnp.einsum(
        "td,tf->df", second_low, grad_pre_low, preferred_element_type=jnp.float32
    )
    grad_up_shift = jnp.sum(grad_pre_low.astype(jnp.float32), axis=0)
    grad_second = jnp.einsum("tf,df->td", grad_pre_low, up_full, preferred_element_type=jnp.float32)
    grad_middle_norm, grad_gain_second, grad_shift_second = norm_second_back(grad_second)
    grad_middle = grad_result_f + grad_middle_norm
    ffn_sums = (
        lax.psum_scatter(grad_up_w, ("band", "samp"), scatter_dimension=0, tiled=True),
        lax.psum_scatter(grad_down_w, ("band", "samp"), scatter_dimension=0, tiled=True),
        lax.psum_scatter(grad_up_shift, ("band", "samp"), scatter_dimension=0, tiled=True),
    )
    grad_branch = grad_middle.astype(jnp.bfloat16)
    grad_shift_out = jnp.sum(grad_branch.astype(jnp.float32), axis=0)
    grad_out_w = jnp.einsum(
        "td,te->de", attended_low, grad_branch, preferred_element_type=jnp.float32
    )
    grad_attended = jnp.einsum(
        "te,de->td", grad_branch, out_full, preferred_element_type=jnp.float32
    ).astype(jnp.bfloat16)
    grad_heads = grad_attended.reshape(row_count, head_count, head_size)
    delta = jnp.einsum("qhe,qhe->hq", grad_heads.astype(jnp.float32), attended_heads)
    zero_heads = jnp.zeros((row_count, head_count, head_size), jnp.float32)

    def key_grad_step(g_queries, step_index):
        scores, key_block, value_block = block_keys(step_index)
        weights_full = jnp.exp(scores - log_total[..., None])
        g_weights = jnp.einsum(
            "qhe,khe->hqk", grad_heads, value_block, preferred_element_type=jnp.float32
        )
        g_scores = (weights_full * (g_weights - delta[..., None])).astype(jnp.bfloat16)
        g_queries = (
            g_queries
            + jnp.einsum("hqk,khe->qhe", g_scores, key_block, preferred_element_type=jnp.float32)
            * score_scale
        )
        key_term = (
            jnp.einsum("hqk,qhe->khe", g_scores, query_heads, preferred_element_type=jnp.float32)
            * score_scale
        )
        value_term = jnp.einsum(
            "hqk,qhe->khe",
            weights_full.astype(jnp.bfloat16),
            grad_heads,
            preferred_element_type=jnp.float32,
        )
        return (
            g_queries,
            (key_term.reshape(block_rows, width), value_term.reshape(block_rows, width)),
        )

    grad_query_heads, block_terms = lax.scan(key_grad_step, zero_heads, block_ids)
    grad_query_f = grad_query_heads.reshape(row_count, width)
    key_sum, value_sum = (
        lax.psum_scatter(
            block_terms[0].reshape(seq_total, width), "band", scatter_dimension=0, tiled=True
        ),
        lax.psum_scatter(
            block_terms[1].reshape(seq_total, width), "band", scatter_dimension=0, tiled=True
        ),
    )
    grad_query_low = grad_query_f.astype(jnp.bfloat16)
    grad_key_low = key_sum.astype(jnp.bfloat16)
    grad_value_low = value_sum.astype(jnp.bfloat16)
    grad_project = jnp.concatenate([grad_query_low, grad_key_low, grad_value_low], axis=-1)
    grad_qkv_w = jnp.einsum(
        "td,te->de", normed_low, grad_project, preferred_element_type=jnp.float32
    )
    grad_shift_query = jnp.sum(grad_query_low.astype(jnp.float32), axis=0)
    grad_shift_value = jnp.sum(grad_value_low.astype(jnp.float32), axis=0)
    grad_normed = jnp.einsum(
        "te,de->td", grad_project, qkv_full, preferred_element_type=jnp.float32
    )
    grad_entering_norm, grad_gain_first, grad_shift_first = norm_first_back(grad_normed)
    grad_entering = grad_middle + grad_entering_norm
    input_grad = grad_entering.astype(jnp.bfloat16)
    entering_sum = jnp.sum(grad_entering, axis=0)
    grad_lead_rows = jnp.stack([lead_days * entering_sum, entering_sum])
    grad_gain_rows = jnp.stack([grad_gain_first, grad_gain_second])
    grad_shift_stack = jnp.stack(
        [
            grad_shift_first,
            grad_shift_query,
            grad_shift_value,
            grad_shift_out,
            grad_shift_second,
            grad_shift_down,
        ]
    )
    attention_sums = (
        lax.psum_scatter(grad_qkv_w, ("band", "samp"), scatter_dimension=0, tiled=True),
        lax.psum_scatter(grad_out_w, ("band", "samp"), scatter_dimension=0, tiled=True),
        lax.psum_scatter(grad_gain_rows, ("band", "samp"), scatter_dimension=1, tiled=True),
        lax.psum_scatter(grad_shift_stack, ("band", "samp"), scatter_dimension=1, tiled=True),
        lax.psum_scatter(grad_lead_rows, ("band", "samp"), scatter_dimension=1, tiled=True),
    )
    return (
        output[None],
        input_grad[None],
        attention_sums[0],
        attention_sums[1],
        ffn_sums[0],
        ffn_sums[1],
        ffn_sums[2],
        attention_sums[2],
        attention_sums[3],
        attention_sums[4],
    )


MESH = pl.DeviceIdType.MESH
F32 = jnp.float32
BF16 = jnp.bfloat16
PLANE = 8
DEPTH = 4
ROWS = 128
BLOCK = 256
CHIPS = 4
NN = (((1,), (0,)), ((), ()))
NT = (((1,), (1,)), ((), ()))
TN = (((0,), (0,)), ((), ()))
INNER = 32


def mm(left, right, dims=NN):
    return lax.dot_general(left, right, dims, preferred_element_type=F32)


def plane_kernel(
    lead_ref, tok, cot, wqkv, wout, wup, wdown, vec_in,
    out_o, ig_o, gqkv_o, gout_o, gup_o, gdown_o, vec_o,
    agf, wq, wo, wu, wd, sq, su, ztr, vt, vecf, vrow,
    normed, qaug, kaug, kt, vv, vt2, pst, ot, invl, att, gproj, dk, dv,
    hid, gder, gpre, mid, gmid,
    part, pr, cs, rr,
    gds, gus, gqs, gos, gdr, gur, gqr, gor_, gu2, gq2, gua, gqa, goa,
    acc, gub, vs, vsr, vz, vzr,
    ag_s, ag_r, fw_s, fw_r, aq_s, aq_r, v_s, v_r, z_s, z_r, p_s, p_r, c_s, c_r,
):
    b = lax.axis_index("band")
    s = lax.axis_index("samp")
    c = b % 2
    x = (b // 2) % 2
    y = b // 4
    mate = b + 1 - 2 * c
    own = b // 2

    def chip(r):
        dx = r % 2
        dy = r // 2
        xx = x + dx * (1 - 2 * x)
        yy = y + dy * (1 - 2 * y)
        return yy * 2 + xx

    def peer(k):
        return (b + k) % PLANE

    def level(k):
        return (s + k) % DEPTH

    barrier = pltpu.get_barrier_semaphore()
    for k in range(1, PLANE):
        pl.semaphore_signal(barrier, inc=1, device_id=(peer(k), s), device_id_type=MESH)
    for k in range(1, DEPTH):
        pl.semaphore_signal(barrier, inc=1, device_id=(b, level(k)), device_id_type=MESH)
    pl.semaphore_wait(barrier, PLANE - 1 + DEPTH - 1)

    def rc(src, dst, ss, rs, band, samp):
        return pltpu.make_async_remote_copy(
            src_ref=src, dst_ref=dst, send_sem=ss, recv_sem=rs,
            device_id=(band, samp), device_id_type=MESH,
        )

    def zc(kind, k, src, dst):
        return rc(src, dst, z_s.at[kind, k - 1], z_r.at[kind, k - 1], b, level(k))

    def gather(op, r):
        dst = mate if r == 0 else chip(r) * 2 + c
        src = tok if op == 0 else (cot if op == 1 else agf.at[op, b])
        return rc(src, agf.at[op, b], ag_s.at[op, r], ag_r.at[op, r], dst, s)

    def forward(op, r):
        blk = chip(r) * 2 + c
        return rc(agf.at[op, blk], agf.at[op, blk], fw_s.at[op, r], fw_r.at[op, r], mate, s)

    def start_gather(op):
        for r in (1, 2, 3, 0):
            gather(op, r).start()

    def pass_on(op, rs):
        for r in rs:
            gather(op, r).wait_recv()
            forward(op, r).start()

    def block(op, q):
        return agf[op, pl.ds(2 * q, 2)].reshape(BLOCK, -1)

    def swap(kind, k, src, dst):
        return rc(src, dst, aq_s.at[kind, k - 1], aq_r.at[kind, k - 1], peer(k), s)

    start_gather(0)
    for k in range(1, DEPTH):
        zc(0, k, vec_in.at[0], ztr.at[k - 1]).start()
    agf[0, b] = tok[...]
    agf[1, b] = cot[...]
    width = tok.shape[1]
    for d in range(PLANE):
        for j in range(3):
            sq[d, :, j * 128:(j + 1) * 128] = wqkv[:, j * width + d * 128:j * width + (d + 1) * 128]
    for k in range(1, PLANE):
        swap(0, k, sq.at[peer(k)], wq.at[b, s]).start()
    wq[b, s] = sq[b]
    wo[s] = wout[...]
    for k in range(1, DEPTH):
        zc(1, k, wo.at[s], wo.at[s]).start()
    for d in range(PLANE):
        su[d] = wup[:, d * 512:(d + 1) * 512]
    wu[b, s] = su[b]
    wd[s] = wdown[...]

    for k in range(1, DEPTH):
        zc(0, k, vec_in.at[0], ztr.at[k - 1]).wait_recv()
    vt[...] = (
        vec_in[0].astype(F32) + vec_in[1].astype(F32)
        + ztr[0].astype(F32) + ztr[1].astype(F32) + ztr[2].astype(F32)
    ).astype(BF16)

    def spread(k):
        return rc(vt, vecf.at[b], v_s.at[0, k - 1], v_r.at[0, k - 1], peer(k), s)

    for k in range(1, PLANE):
        spread(k).start()
    vecf[b] = vt[...]
    for k in range(1, PLANE):
        swap(0, k, sq.at[peer(k)], wq.at[b, s]).wait_recv()
    for k in range(1, DEPTH):
        zc(2, k, wq.at[:, s], wq.at[:, s]).start()
    for k in range(1, PLANE):
        swap(1, k, su.at[peer(k)], wu.at[b, s]).start()
    for k in range(1, PLANE):
        spread(k).wait_recv()
    for d in range(PLANE):
        vrow[:, d * 128:(d + 1) * 128] = vecf[d].astype(F32)
    lead_days = lead_ref[0].astype(F32) * 0.25
    lane = lax.broadcasted_iota(jnp.int32, (1, 128), 1)
    head_lane = [(lane < 64).astype(F32), (lane >= 64).astype(F32)]
    ones_lane = jnp.where(lane < 2, 1.0, 0.0).astype(F32)
    ends_lane = jnp.where(lane == 0, 9984.0, jnp.where(lane == 1, 16.0, 0.0)).astype(F32)
    gain1, gain2 = vrow[0:1, :], vrow[1:2, :]
    shift1, shift_out, shift2, shift_down = vrow[2:3, :], vrow[5:6, :], vrow[6:7, :], vrow[7:8, :]
    lead_row = lead_days * vrow[8:9, :] + vrow[9:10, :]
    mine = vecf[b].astype(F32)

    def stats(v):
        mean = jnp.mean(v, axis=-1, keepdims=True)
        centered = v - mean
        variance = jnp.mean(centered * centered, axis=-1, keepdims=True)
        rstd = lax.rsqrt(variance + eps)
        return centered * rstd, rstd

    for d in range(PLANE):
        row = jnp.broadcast_to(vecf[d].astype(F32)[10:11, :], (128, 128))
        column = row.T - 1.0
        kaug[d * 128:(d + 1) * 128, 128:256] = (column * ends_lane).astype(BF16)
    for h in range(2):
        for q in range(CHIPS):
            qaug[h, q, :, 128:256] = jnp.broadcast_to(ones_lane, (BLOCK, 128)).astype(BF16)

    def norm_block(d):
        def chunk(j, _):
            rows = pl.ds(pl.multiple_of(j * INNER, INNER), INNER)
            ent = agf[0, d, rows, :].astype(F32) + lead_row
            xhat = stats(ent)[0]
            normed[d, rows, :] = (xhat * gain1 + shift1).astype(BF16)
            return 0

        lax.fori_loop(0, ROWS // INNER, chunk, 0)

    norm_block(b)
    gather(0, 0).wait_recv()
    norm_block(mate)
    pass_on(0, (1, 2))
    for r in (1, 2):
        norm_block(chip(r) * 2 + c)
        forward(0, r).wait_recv()
        norm_block(chip(r) * 2 + 1 - c)
    pass_on(0, (3,))
    start_gather(1)
    norm_block(chip(3) * 2 + c)
    forward(0, 3).wait_recv()
    norm_block(chip(3) * 2 + 1 - c)

    for k in range(1, DEPTH):
        zc(2, k, wq.at[:, s], wq.at[:, s]).wait_recv()
    for k in range(1, PLANE):
        swap(1, k, su.at[peer(k)], wu.at[b, s]).wait_recv()
    for k in range(1, DEPTH):
        zc(3, k, wu.at[:, s], wu.at[:, s]).start()
    for k in range(1, DEPTH):
        zc(4, k, wd.at[s], wd.at[s]).start()

    def project_block(q, _):
        rows = pl.ds(pl.multiple_of(q * BLOCK, BLOCK), BLOCK)
        pj = mm(normed[pl.ds(2 * q, 2)].reshape(BLOCK, width), wq[...].reshape(width, 384))
        qv = (pj[:, 0:128] + mine[3:4, :]).astype(BF16).astype(F32) * 0.125
        for h in range(2):
            qaug[h, q, :, 0:128] = (qv * head_lane[h]).astype(BF16)
        kv = pj[:, 128:256].astype(BF16)
        kaug[rows, 0:128] = kv
        kt[:, rows] = kv.T
        vb = (pj[:, 256:384] + mine[4:5, :]).astype(BF16)
        vv[rows, :] = vb
        vt2[:, rows] = vb.T
        return 0

    lax.fori_loop(0, CHIPS, project_block, 0)
    for k in range(1, DEPTH):
        zc(1, k, wo.at[s], wo.at[s]).wait_recv()

    def mate_copy(op, slot, r):
        return rc(part.at[slot, r, 1 - c], pr.at[op, r], p_s.at[op, r], p_r.at[op, r], mate, s)

    def chip_copy(op, slot, r):
        return rc(cs.at[slot, r], rr.at[op, r], c_s.at[op, r], c_r.at[op, r], chip(r) * 2 + c, s)

    def put_part(op, slot, r, blk):
        part[slot, r] = blk.astype(BF16).reshape(2, ROWS, width)
        mate_copy(op, slot, r).start()

    def fold(op, slot, r, send=True):
        mate_copy(op, slot, r).wait_recv()

        def chunk(j, _):
            rows = pl.ds(pl.multiple_of(j * INNER, INNER), INNER)
            cs[slot, r, rows, :] = (
                part[slot, r, c, rows, :].astype(F32) + pr[op, r, rows, :].astype(F32)
            ).astype(BF16)
            return 0

        lax.fori_loop(0, ROWS // INNER, chunk, 0)

        if send:
            @pl.when(r > 0)
            def _():
                chip_copy(op, slot, r).start()

    def plane_total(op, slot, rows):
        total = cs[slot, 0, rows, :].astype(F32)
        for r in (1, 2, 3):
            total = total + rr[op, r, rows, :].astype(F32)
        return total

    def end_sums(op, slot):
        for r in range(CHIPS):
            mate_copy(op, slot, r).wait_send()
        for r in (1, 2, 3):
            chip_copy(op, slot, r).wait_send()

    def attend_block(i, _):
        r = 3 - i
        q = chip(r)

        def head(h, _):
            top = pl.ds(pl.multiple_of(h * 64, 64), 64)
            st = mm(kaug[...], qaug[h, q], NT)
            p = jnp.exp(st - jnp.max(st, axis=0, keepdims=True))
            inverse = 1.0 / jnp.sum(p, axis=0, keepdims=True)
            pb = p.astype(BF16)
            pst[h, q] = pb
            ot[q, top, :] = mm(vt2[top, :], pb) * inverse
            invl[q, h] = jnp.broadcast_to(inverse, (8, BLOCK))
            return 0

        lax.fori_loop(0, 2, head, 0)
        low = ot[q].T.astype(BF16)
        att[q] = low
        put_part(0, 0, r, mm(low, wo[...].reshape(128, width)))

        @pl.when(i > 0)
        def _():
            fold(0, 0, r + 1)

        return 0

    lax.fori_loop(0, CHIPS, attend_block, 0)
    fold(0, 0, 0)
    pass_on(1, (1, 2, 3))
    for r in (1, 2, 3):
        chip_copy(0, 0, r).wait_recv()

    def middle_chunk(j, _):
        rows = pl.ds(pl.multiple_of(j * INNER, INNER), INNER)
        ent = tok[rows, :].astype(F32) + lead_row
        m = ent + plane_total(0, 0, rows) + shift_out
        mid[rows, :] = m
        agf[2, b, rows, :] = (stats(m)[0] * gain2 + shift2).astype(BF16)
        return 0

    lax.fori_loop(0, ROWS // INNER, middle_chunk, 0)
    start_gather(2)
    end_sums(0, 0)

    for k in range(1, DEPTH):
        zc(3, k, wu.at[:, s], wu.at[:, s]).wait_recv()
    bias = jnp.concatenate([mine[11 + j:12 + j, :] for j in range(4)], axis=1)

    def arrivals(op, i):
        @pl.when(i == 0)
        def _():
            gather(op, 0).wait_recv()

        @pl.when(i == 1)
        def _():
            pass_on(op, (1, 2))
            forward(op, 1).wait_recv()

        @pl.when(i == 2)
        def _():
            forward(op, 2).wait_recv()

        @pl.when(i == 3)
        def _():
            pass_on(op, (3,))
            forward(op, 3).wait_recv()

    def up_block(i, _):
        arrivals(2, i)
        q = chip(i)
        hp = mm(block(2, q), wu[...].reshape(width, 512)) + bias
        phi = 0.5 + 0.5 * lax.erf(hp * 0.7071067811865476)
        hid[pl.ds(pl.multiple_of(q * BLOCK, BLOCK), BLOCK), :] = (hp * phi).astype(BF16)
        gder[q] = phi + hp * jnp.exp(hp * hp * -0.5) * 0.3989422804014327
        return 0

    lax.fori_loop(0, CHIPS, up_block, 0)
    gather(1, 0).wait_recv()
    for r in (1, 2, 3):
        forward(1, r).wait_recv()

    def down_grad(f, _):
        cols = pl.ds(pl.multiple_of(f * BLOCK, BLOCK), BLOCK)
        g = mm(hid[:, cols], agf[1].reshape(PLANE * ROWS, width), TN)
        gds[pl.ds(2 * f, 2)] = g.astype(BF16).reshape(2, 128, width)
        return 0

    lax.fori_loop(0, 2, down_grad, 0)
    for k in range(1, DEPTH):
        zc(4, k, wd.at[s], wd.at[s]).wait_recv()
    for k in range(1, DEPTH):
        zc(5, k, gds.at[level(k)], gdr.at[k - 1]).start()
    gub[...] = jnp.zeros_like(gub)

    def back_block(i, _):
        r = 3 - i
        q = chip(r)
        rows = pl.ds(pl.multiple_of(q * BLOCK, BLOCK), BLOCK)
        gh = mm(block(1, q), wd[...].reshape(512, width), NT)
        gp = (gder[q] * gh).astype(BF16)
        gpre[rows, :] = gp
        gub[...] += jnp.sum(gp.astype(F32).reshape(BLOCK // 8, 8, 512), axis=0)
        put_part(1, 1, r, mm(gp, wu[...].reshape(width, 512), NT))

        @pl.when(i > 0)
        def _():
            fold(1, 1, r + 1)

        return 0

    lax.fori_loop(0, CHIPS, back_block, 0)
    fold(1, 1, 0)

    def up_grad(f, _):
        cols = pl.ds(pl.multiple_of(f * BLOCK, BLOCK), BLOCK)
        g = mm(agf[2, :, :, cols].reshape(PLANE * ROWS, BLOCK), gpre[...], TN)
        gus[pl.ds(2 * f, 2)] = g.astype(BF16).reshape(2, 4, 32, 512)
        return 0

    lax.fori_loop(0, CHIPS, up_grad, 0)
    for k in range(1, DEPTH):
        zc(6, k, gus.at[:, level(k)], gur.at[k - 1]).start()

    def out_block(i, _):
        r = 3 - i
        q = chip(r)
        rows = pl.ds(pl.multiple_of(q * BLOCK, BLOCK), BLOCK)
        put_part(2, 2, r, mm(hid[rows, :], wd[...].reshape(512, width)))

        @pl.when(i > 0)
        def _():
            fold(2, 2, r + 1, send=False)

        return 0

    lax.fori_loop(0, CHIPS, out_block, 0)
    fold(2, 2, 0, send=False)

    for r in (1, 2, 3):
        chip_copy(1, 1, r).wait_recv()
    acc[...] = jnp.zeros_like(acc)

    def add_row(n, v):
        acc[n] += jnp.sum(v.reshape(INNER // 8, 8, width), axis=0)

    def norm_back(v, grad, gain):
        xhat, rstd = stats(v)
        d = grad * gain
        mean_d = jnp.mean(d, axis=-1, keepdims=True)
        mean_dx = jnp.mean(d * xhat, axis=-1, keepdims=True)
        return rstd * (d - mean_d - xhat * mean_dx), xhat

    def second_chunk(j, _):
        rows = pl.ds(pl.multiple_of(j * INNER, INNER), INNER)
        gs = plane_total(1, 1, rows)
        g, xhat = norm_back(mid[rows, :], gs, gain2)
        ct = cot[rows, :].astype(F32)
        gm = ct + g
        gmid[rows, :] = gm
        gb = gm.astype(BF16)
        agf[3, b, rows, :] = gb
        add_row(1, gs * xhat)
        add_row(6, gs)
        add_row(5, gb.astype(F32))
        add_row(7, ct)
        return 0

    lax.fori_loop(0, ROWS // INNER, second_chunk, 0)
    start_gather(3)

    dk[...] = jnp.zeros_like(dk)
    dv[...] = jnp.zeros_like(dv)
    goa[...] = jnp.zeros_like(goa)

    def attend_back(i, _):
        arrivals(3, i)
        q = chip(i)
        gbk = block(3, q)
        wo_all = wo[...].reshape(128, width)
        dot_t = mm(wo_all, gbk, NT)
        inv = jnp.concatenate(
            [jnp.broadcast_to(invl[q, h, 0:1, :], (64, BLOCK)) for h in range(2)], axis=0
        )
        dos = dot_t * inv
        prod = dos * ot[q]
        deltas = [jnp.sum(prod[h * 64:(h + 1) * 64], axis=0, keepdims=True) for h in range(2)]
        do_rows = dos.T
        zero = jnp.zeros((64, BLOCK), F32)
        dq_parts = []
        for h in range(2):
            halves = [dos[0:64], zero] if h == 0 else [zero, dos[64:128]]
            dp = mm(vv[...], jnp.concatenate(halves, axis=0).astype(BF16))
            pb = pst[h, q]
            ds = (pb.astype(F32) * (dp - deltas[h])).astype(BF16)
            dv[...] += mm(pb, (do_rows * head_lane[h]).astype(BF16))
            dk[...] += mm(ds, qaug[h, q, :, 0:128])
            dq_parts.append(mm(kt[h * 64:(h + 1) * 64, :], ds))
        dq = jnp.concatenate(dq_parts, axis=0).T * 0.125
        gproj[pl.ds(pl.multiple_of(q * BLOCK, BLOCK), BLOCK), 0:128] = dq.astype(BF16)
        goa[...] += mm(att[q], gbk, TN)
        return 0

    lax.fori_loop(0, CHIPS, attend_back, 0)
    for r in (1, 2, 3):
        chip_copy(2, 2, r).start()
    gproj[:, 128:256] = dk[...].astype(BF16)
    gproj[:, 256:384] = dv[...].astype(BF16)

    def project_back(i, _):
        r = 3 - i
        q = chip(r)
        rows = pl.ds(pl.multiple_of(q * BLOCK, BLOCK), BLOCK)
        put_part(3, 0, r, mm(gproj[rows, :], wq[...].reshape(width, 384), NT))

        @pl.when(i > 0)
        def _():
            fold(3, 0, r + 1)

        return 0

    lax.fori_loop(0, CHIPS, project_back, 0)
    fold(3, 0, 0)

    def qkv_grad(f, _):
        cols = pl.ds(pl.multiple_of(f * BLOCK, BLOCK), BLOCK)
        g = mm(normed[:, :, cols].reshape(PLANE * ROWS, BLOCK), gproj[...], TN)
        gqs[pl.ds(2 * f, 2)] = g.astype(BF16).reshape(2, 4, 32, 384)
        return 0

    lax.fori_loop(0, CHIPS, qkv_grad, 0)
    gos[...] = goa[...].astype(BF16).reshape(4, 32, width)
    for k in range(1, DEPTH):
        zc(7, k, gqs.at[:, level(k)], gqr.at[k - 1]).start()
    for k in range(1, DEPTH):
        zc(8, k, gos.at[level(k)], gor_.at[k - 1]).start()

    for k in range(1, DEPTH):
        zc(5, k, gds.at[level(k)], gdr.at[k - 1]).wait_recv()
    gdown_o[...] = (
        gds[s].astype(F32) + gdr[0].astype(F32) + gdr[1].astype(F32) + gdr[2].astype(F32)
    )
    for k in range(1, DEPTH):
        zc(6, k, gus.at[:, level(k)], gur.at[k - 1]).wait_recv()
    for d in range(PLANE):
        gu2[d] = (
            gus[d, s].astype(F32) + gur[0, d].astype(F32)
            + gur[1, d].astype(F32) + gur[2, d].astype(F32)
        ).astype(BF16)
    for k in range(1, PLANE):
        swap(2, k, gu2.at[peer(k)], gua.at[b]).start()
    gua[b] = gu2[b]

    for r in (1, 2, 3):
        chip_copy(2, 2, r).wait_recv()

    def output_chunk(j, _):
        rows = pl.ds(pl.multiple_of(j * INNER, INNER), INNER)
        out_o[rows, :] = (mid[rows, :] + plane_total(2, 2, rows) + shift_down).astype(BF16)
        return 0

    lax.fori_loop(0, ROWS // INNER, output_chunk, 0)

    for r in (1, 2, 3):
        chip_copy(3, 0, r).wait_recv()

    def first_chunk(j, _):
        rows = pl.ds(pl.multiple_of(j * INNER, INNER), INNER)
        gn = plane_total(3, 0, rows)
        g, xhat = norm_back(tok[rows, :].astype(F32) + lead_row, gn, gain1)
        ge = gmid[rows, :] + g
        ig_o[rows, :] = ge.astype(BF16)
        add_row(0, gn * xhat)
        add_row(2, gn)
        add_row(9, ge)
        return 0

    lax.fori_loop(0, ROWS // INNER, first_chunk, 0)
    acc[8] = acc[9] * lead_days

    sums = [jnp.sum(acc[n], axis=0, keepdims=True) for n in range(10)]
    packed = jnp.concatenate(sums + [jnp.zeros((6, width), F32)], axis=0)
    for d in range(PLANE):
        vs[d] = packed[:, d * 128:(d + 1) * 128]

    def vec_swap(k):
        return rc(vs.at[peer(k)], vsr.at[k - 1], v_s.at[1, k - 1], v_r.at[1, k - 1], peer(k), s)

    for k in range(1, PLANE):
        vec_swap(k).start()
    gq_cols = jnp.sum(gproj[:, 0:128].astype(F32), axis=0, keepdims=True)
    gv_cols = jnp.sum(gproj[:, 256:384].astype(F32), axis=0, keepdims=True)
    gub_row = jnp.sum(gub[...], axis=0, keepdims=True)
    extra = jnp.concatenate(
        [jnp.zeros((3, 128), F32), gq_cols, gv_cols, jnp.zeros((6, 128), F32)]
        + [gub_row[:, j * 128:(j + 1) * 128] for j in range(4)]
        + [jnp.zeros((1, 128), F32)],
        axis=0,
    )
    for k in range(1, PLANE):
        vec_swap(k).wait_recv()
    total = vs[b] + extra
    for k in range(PLANE - 1):
        total = total + vsr[k]
    vz[...] = total
    for k in range(1, DEPTH):
        zc(9, k, vz, vzr.at[k - 1]).start()

    for k in range(1, DEPTH):
        zc(8, k, gos.at[level(k)], gor_.at[k - 1]).wait_recv()
    gout_o[...] = (
        gos[s].astype(F32) + gor_[0].astype(F32) + gor_[1].astype(F32) + gor_[2].astype(F32)
    )
    for k in range(1, DEPTH):
        zc(7, k, gqs.at[:, level(k)], gqr.at[k - 1]).wait_recv()
    for d in range(PLANE):
        gq2[d] = (
            gqs[d, s].astype(F32) + gqr[0, d].astype(F32)
            + gqr[1, d].astype(F32) + gqr[2, d].astype(F32)
        ).astype(BF16)
    for k in range(1, PLANE):
        swap(3, k, gq2.at[peer(k)], gqa.at[b]).start()
    gqa[b] = gq2[b]
    for k in range(1, PLANE):
        swap(2, k, gu2.at[peer(k)], gua.at[b]).wait_recv()
    for d in range(PLANE):
        gup_o[:, d * 512:(d + 1) * 512] = gua[d].astype(F32)
    for k in range(1, DEPTH):
        zc(9, k, vz, vzr.at[k - 1]).wait_recv()
    vec_o[...] = vz[...] + vzr[0] + vzr[1] + vzr[2]
    for k in range(1, PLANE):
        swap(3, k, gq2.at[peer(k)], gqa.at[b]).wait_recv()
    for d in range(PLANE):
        for j in range(3):
            gqkv_o[:, j * width + d * 128:j * width + (d + 1) * 128] = (
                gqa[d, :, j * 128:(j + 1) * 128].astype(F32)
            )

    for op in range(4):
        for r in range(CHIPS):
            gather(op, r).wait_send()
        for r in (1, 2, 3):
            forward(op, r).wait_send()
    for op, slot in ((1, 1), (2, 2), (3, 0)):
        end_sums(op, slot)
    for k in range(1, PLANE):
        swap(0, k, sq.at[peer(k)], wq.at[b, s]).wait_send()
        swap(1, k, su.at[peer(k)], wu.at[b, s]).wait_send()
        swap(2, k, gu2.at[peer(k)], gua.at[b]).wait_send()
        swap(3, k, gq2.at[peer(k)], gqa.at[b]).wait_send()
        spread(k).wait_send()
        vec_swap(k).wait_send()
    for k in range(1, DEPTH):
        zc(0, k, vec_in.at[0], ztr.at[k - 1]).wait_send()
        zc(1, k, wo.at[s], wo.at[s]).wait_send()
        zc(2, k, wq.at[:, s], wq.at[:, s]).wait_send()
        zc(3, k, wu.at[:, s], wu.at[:, s]).wait_send()
        zc(4, k, wd.at[s], wd.at[s]).wait_send()
        zc(5, k, gds.at[level(k)], gdr.at[k - 1]).wait_send()
        zc(6, k, gus.at[:, level(k)], gur.at[k - 1]).wait_send()
        zc(7, k, gqs.at[:, level(k)], gqr.at[k - 1]).wait_send()
        zc(8, k, gos.at[level(k)], gor_.at[k - 1]).wait_send()
        zc(9, k, vz, vzr.at[k - 1]).wait_send()


def plane_body(
    tokens, cotangent, w_qkv, w_out, w_up, w_down,
    up_bias, norm_gains, shift_rows, lead_weight, lead_steps, valid_cells,
):
    s = lax.axis_index("samp")
    width = tokens.shape[2]
    columns = jnp.concatenate([norm_gains, shift_rows, lead_weight], axis=0)
    tile = jnp.zeros((16, 128), BF16)
    tile = lax.dynamic_update_slice(tile, columns, (0, s * 32))
    tile = lax.dynamic_update_slice(tile, up_bias[None], (11 + s, 0))
    flags = jnp.zeros((16, 128), BF16)
    flags = lax.dynamic_update_slice(flags, (valid_cells > 0).astype(BF16), (10, 0))
    vectors = jnp.stack([tile, flags])
    vmem = pl.BlockSpec(memory_space=pltpu.VMEM)
    dma = pltpu.SemaphoreType.DMA
    V = pltpu.VMEM
    out_shape = (
        jax.ShapeDtypeStruct((ROWS, width), BF16),
        jax.ShapeDtypeStruct((ROWS, width), BF16),
        jax.ShapeDtypeStruct((32, 3 * width), F32),
        jax.ShapeDtypeStruct((32, width), F32),
        jax.ShapeDtypeStruct((32, 4 * width), F32),
        jax.ShapeDtypeStruct((128, width), F32),
        jax.ShapeDtypeStruct((16, 128), F32),
    )
    scratch = [
        V((4, PLANE, ROWS, width), BF16),
        V((PLANE, DEPTH, 32, 384), BF16),
        V((DEPTH, 32, width), BF16),
        V((PLANE, DEPTH, 32, 512), BF16),
        V((DEPTH, 128, width), BF16),
        V((PLANE, 32, 384), BF16),
        V((PLANE, 32, 512), BF16),
        V((3, 16, 128), BF16),
        V((16, 128), BF16),
        V((PLANE, 16, 128), BF16),
        V((16, width), F32),
        V((PLANE, ROWS, width), BF16),
        V((2, CHIPS, BLOCK, 256), BF16),
        V((1024, 256), BF16),
        V((128, 1024), BF16),
        V((1024, 128), BF16),
        V((128, 1024), BF16),
        V((2, CHIPS, 1024, BLOCK), BF16),
        V((CHIPS, 128, BLOCK), F32),
        V((CHIPS, 2, 8, BLOCK), F32),
        V((CHIPS, BLOCK, 128), BF16),
        V((1024, 384), BF16),
        V((1024, 128), F32),
        V((1024, 128), F32),
        V((1024, 512), BF16),
        V((CHIPS, BLOCK, 512), F32),
        V((1024, 512), BF16),
        V((ROWS, width), F32),
        V((ROWS, width), F32),
        V((3, CHIPS, 2, ROWS, width), BF16),
        V((4, CHIPS, ROWS, width), BF16),
        V((3, CHIPS, ROWS, width), BF16),
        V((4, CHIPS, ROWS, width), BF16),
        V((DEPTH, 128, width), BF16),
        V((PLANE, DEPTH, 32, 512), BF16),
        V((PLANE, DEPTH, 32, 384), BF16),
        V((DEPTH, 32, width), BF16),
        V((3, 128, width), BF16),
        V((3, PLANE, 32, 512), BF16),
        V((3, PLANE, 32, 384), BF16),
        V((3, 32, width), BF16),
        V((PLANE, 32, 512), BF16),
        V((PLANE, 32, 384), BF16),
        V((PLANE, 32, 512), BF16),
        V((PLANE, 32, 384), BF16),
        V((128, width), F32),
        V((10, 8, width), F32),
        V((8, 512), F32),
        V((PLANE, 16, 128), F32),
        V((PLANE - 1, 16, 128), F32),
        V((16, 128), F32),
        V((3, 16, 128), F32),
        dma((4, 4)), dma((4, 4)), dma((4, 4)), dma((4, 4)),
        dma((4, 7)), dma((4, 7)), dma((2, 7)), dma((2, 7)),
        dma((10, 3)), dma((10, 3)),
        dma((4, 4)), dma((4, 4)), dma((4, 4)), dma((4, 4)),
    ]
    results = pl.pallas_call(
        plane_kernel,
        out_shape=out_shape,
        in_specs=[pl.BlockSpec(memory_space=pltpu.SMEM)] + [vmem] * 7,
        out_specs=tuple([vmem] * 7),
        scratch_shapes=scratch,
        compiler_params=pltpu.CompilerParams(
            collective_id=0, has_side_effects=True, vmem_limit_bytes=63 * 2**20
        ),
    )(lead_steps, tokens[0], cotangent[0], w_qkv, w_out, w_up, w_down, vectors)
    output, input_grad, g_qkv, g_out, g_up, g_down, vec = results
    rows = lax.dynamic_slice(vec, (0, s * 32), (10, 32))
    g_bias = lax.dynamic_slice(vec, (11 + s, 0), (1, 128))[0]
    return (
        output[None], input_grad[None], g_qkv, g_out, g_up, g_down, g_bias,
        rows[0:2], rows[2:8], rows[8:10],
    )


def plane_fits(mesh):
    return mesh.shape["band"] == PLANE and mesh.shape["samp"] == DEPTH


def solution(mesh):
    return jax.shard_map(
        plane_body if plane_fits(mesh) else body,
        mesh=mesh,
        in_specs=(
            P("samp", "band", None),
            P("samp", "band", None),
            P(("band", "samp"), None),
            P(("band", "samp"), None),
            P(("band", "samp"), None),
            P(("band", "samp"), None),
            P(("band", "samp")),
            P(None, ("band", "samp")),
            P(None, ("band", "samp")),
            P(None, ("band", "samp")),
            P("samp"),
            P("samp", "band"),
        ),
        out_specs=(
            P("samp", "band", None),
            P("samp", "band", None),
            P(("band", "samp"), None),
            P(("band", "samp"), None),
            P(("band", "samp"), None),
            P(("band", "samp"), None),
            P(("band", "samp")),
            P(None, ("band", "samp")),
            P(None, ("band", "samp")),
            P(None, ("band", "samp")),
        ),
        check_vma=False,
    )
```

```python
import jax
import jax.numpy as jnp
from jax import lax
from jax.experimental import pallas as pl
from jax.experimental.pallas import tpu as pltpu
from jax.sharding import PartitionSpec as P

HEADS = 16


eps = 1e-05
masked = 10000.0


def layer_norm(values, gain_row, shift_row):
    centered = values - jnp.mean(values, axis=-1, keepdims=True)
    variance = jnp.mean(centered * centered, axis=-1, keepdims=True)
    return centered * lax.rsqrt(variance + eps) * gain_row + shift_row


def gelu_exact(values):
    return jax.nn.gelu(values, approximate=False)


def body(
    tokens,
    cotangent,
    w_qkv,
    w_out,
    w_up,
    w_down,
    up_bias,
    norm_gains,
    shift_rows,
    lead_weight,
    lead_steps,
    valid_cells,
):
    whole = (
        lax.all_gather(w_qkv, ("band", "samp"), axis=0, tiled=True),
        lax.all_gather(w_out, ("band", "samp"), axis=0, tiled=True),
        lax.all_gather(w_up, ("band", "samp"), axis=0, tiled=True),
        lax.all_gather(w_down, ("band", "samp"), axis=0, tiled=True),
        lax.all_gather(up_bias, ("band", "samp"), axis=0, tiled=True),
        lax.all_gather(norm_gains, ("band", "samp"), axis=1, tiled=True),
        lax.all_gather(shift_rows, ("band", "samp"), axis=1, tiled=True),
        lax.all_gather(lead_weight, ("band", "samp"), axis=1, tiled=True),
    )
    qkv_full = whole[0]
    out_full = whole[1]
    up_full = whole[2]
    down_full = whole[3]
    up_shift = whole[4].astype(jnp.float32)
    gain_all = whole[5].astype(jnp.float32)
    shift_all = whole[6].astype(jnp.float32)
    lead_all = whole[7].astype(jnp.float32)
    row_count = tokens.shape[1]
    width = tokens.shape[2]
    head_count = HEADS
    head_size = width // head_count
    score_scale = head_size ** (-0.5)
    lead_days = lead_steps[0].astype(jnp.float32) * 0.25
    entering = tokens[0].astype(jnp.float32) + lead_days * lead_all[0] + lead_all[1]
    normed, norm_first_back = jax.vjp(layer_norm, entering, gain_all[0], shift_all[0])
    normed_low = normed.astype(jnp.bfloat16)
    project = jnp.dot(normed_low, qkv_full, preferred_element_type=jnp.float32)
    queries = (project[:, :width] + shift_all[1]).astype(jnp.bfloat16)
    key_rows = project[:, width : 2 * width].astype(jnp.bfloat16)
    value_rows = (project[:, 2 * width :] + shift_all[2]).astype(jnp.bfloat16)
    key_open = (valid_cells[0] > 0).astype(jnp.bfloat16)
    keys_all, values_all, open_all = (
        lax.all_gather(key_rows, "band", axis=0, tiled=True),
        lax.all_gather(value_rows, "band", axis=0, tiled=True),
        lax.all_gather(key_open, "band", axis=0, tiled=True),
    )
    seq_total = keys_all.shape[0]
    block_rows = min(512, seq_total)
    block_count = seq_total // block_rows
    block_ids = jnp.arange(block_count)
    bias_all = (open_all.astype(jnp.float32) - 1.0) * masked
    query_heads = queries.reshape(row_count, head_count, head_size)

    def block_keys(step_index):
        first_row = step_index * block_rows
        key_block = lax.dynamic_slice_in_dim(keys_all, first_row, block_rows, 0).reshape(
            block_rows, head_count, head_size
        )
        value_block = lax.dynamic_slice_in_dim(values_all, first_row, block_rows, 0).reshape(
            block_rows, head_count, head_size
        )
        bias_block = lax.dynamic_slice_in_dim(bias_all, first_row, block_rows, 0)
        scores = (
            jnp.einsum("qhe,khe->hqk", query_heads, key_block, preferred_element_type=jnp.float32)
            * score_scale
            + bias_block
        )
        return (scores, key_block, value_block)

    def max_step(running, step_index):
        row_max, exp_total = running
        scores = block_keys(step_index)[0]
        new_max = jnp.maximum(row_max, jnp.max(scores, axis=-1))
        exp_total = exp_total * jnp.exp(row_max - new_max) + jnp.sum(
            jnp.exp(scores - new_max[..., None]), axis=-1
        )
        return ((new_max, exp_total), None)

    start_max = jnp.full((head_count, row_count), -jnp.inf, jnp.float32)
    start_total = jnp.zeros((head_count, row_count), jnp.float32)
    row_max, exp_total = lax.scan(max_step, (start_max, start_total), block_ids)[0]
    log_total = row_max + jnp.log(exp_total)

    def out_step(running, step_index):
        scores, key_block, value_block = block_keys(step_index)
        weights_low = jnp.exp(scores - log_total[..., None]).astype(jnp.bfloat16)
        return (
            running
            + jnp.einsum(
                "hqk,khe->qhe", weights_low, value_block, preferred_element_type=jnp.float32
            ),
            None,
        )

    attended_heads = lax.scan(
        out_step, jnp.zeros((row_count, head_count, head_size), jnp.float32), block_ids
    )[0]
    attended_low = attended_heads.reshape(row_count, width).astype(jnp.bfloat16)
    middle = (
        entering
        + jnp.dot(attended_low, out_full, preferred_element_type=jnp.float32)
        + shift_all[3]
    )
    second, norm_second_back = jax.vjp(layer_norm, middle, gain_all[1], shift_all[4])
    second_low = second.astype(jnp.bfloat16)
    hidden_pre = jnp.dot(second_low, up_full, preferred_element_type=jnp.float32) + up_shift
    hidden, gelu_back = jax.vjp(gelu_exact, hidden_pre)
    hidden_low = hidden.astype(jnp.bfloat16)
    result = (
        middle + jnp.dot(hidden_low, down_full, preferred_element_type=jnp.float32) + shift_all[5]
    )
    output = result.astype(jnp.bfloat16)
    grad_result = cotangent[0]
    grad_result_f = grad_result.astype(jnp.float32)
    grad_down_w = jnp.einsum(
        "tf,td->fd", hidden_low, grad_result, preferred_element_type=jnp.float32
    )
    grad_shift_down = jnp.sum(grad_result_f, axis=0)
    grad_hidden = jnp.einsum(
        "td,fd->tf", grad_result, down_full, preferred_element_type=jnp.float32
    )
    grad_pre_low = gelu_back(grad_hidden)[0].astype(jnp.bfloat16)
    grad_up_w = jnp.einsum(
        "td,tf->df", second_low, grad_pre_low, preferred_element_type=jnp.float32
    )
    grad_up_shift = jnp.sum(grad_pre_low.astype(jnp.float32), axis=0)
    grad_second = jnp.einsum("tf,df->td", grad_pre_low, up_full, preferred_element_type=jnp.float32)
    grad_middle_norm, grad_gain_second, grad_shift_second = norm_second_back(grad_second)
    grad_middle = grad_result_f + grad_middle_norm
    ffn_sums = (
        lax.psum_scatter(grad_up_w, ("band", "samp"), scatter_dimension=0, tiled=True),
        lax.psum_scatter(grad_down_w, ("band", "samp"), scatter_dimension=0, tiled=True),
        lax.psum_scatter(grad_up_shift, ("band", "samp"), scatter_dimension=0, tiled=True),
    )
    grad_branch = grad_middle.astype(jnp.bfloat16)
    grad_shift_out = jnp.sum(grad_branch.astype(jnp.float32), axis=0)
    grad_out_w = jnp.einsum(
        "td,te->de", attended_low, grad_branch, preferred_element_type=jnp.float32
    )
    grad_attended = jnp.einsum(
        "te,de->td", grad_branch, out_full, preferred_element_type=jnp.float32
    ).astype(jnp.bfloat16)
    grad_heads = grad_attended.reshape(row_count, head_count, head_size)
    delta = jnp.einsum("qhe,qhe->hq", grad_heads.astype(jnp.float32), attended_heads)
    zero_heads = jnp.zeros((row_count, head_count, head_size), jnp.float32)

    def key_grad_step(g_queries, step_index):
        scores, key_block, value_block = block_keys(step_index)
        weights_full = jnp.exp(scores - log_total[..., None])
        g_weights = jnp.einsum(
            "qhe,khe->hqk", grad_heads, value_block, preferred_element_type=jnp.float32
        )
        g_scores = (weights_full * (g_weights - delta[..., None])).astype(jnp.bfloat16)
        g_queries = (
            g_queries
            + jnp.einsum("hqk,khe->qhe", g_scores, key_block, preferred_element_type=jnp.float32)
            * score_scale
        )
        key_term = (
            jnp.einsum("hqk,qhe->khe", g_scores, query_heads, preferred_element_type=jnp.float32)
            * score_scale
        )
        value_term = jnp.einsum(
            "hqk,qhe->khe",
            weights_full.astype(jnp.bfloat16),
            grad_heads,
            preferred_element_type=jnp.float32,
        )
        return (
            g_queries,
            (key_term.reshape(block_rows, width), value_term.reshape(block_rows, width)),
        )

    grad_query_heads, block_terms = lax.scan(key_grad_step, zero_heads, block_ids)
    grad_query_f = grad_query_heads.reshape(row_count, width)
    key_sum, value_sum = (
        lax.psum_scatter(
            block_terms[0].reshape(seq_total, width), "band", scatter_dimension=0, tiled=True
        ),
        lax.psum_scatter(
            block_terms[1].reshape(seq_total, width), "band", scatter_dimension=0, tiled=True
        ),
    )
    grad_query_low = grad_query_f.astype(jnp.bfloat16)
    grad_key_low = key_sum.astype(jnp.bfloat16)
    grad_value_low = value_sum.astype(jnp.bfloat16)
    grad_project = jnp.concatenate([grad_query_low, grad_key_low, grad_value_low], axis=-1)
    grad_qkv_w = jnp.einsum(
        "td,te->de", normed_low, grad_project, preferred_element_type=jnp.float32
    )
    grad_shift_query = jnp.sum(grad_query_low.astype(jnp.float32), axis=0)
    grad_shift_value = jnp.sum(grad_value_low.astype(jnp.float32), axis=0)
    grad_normed = jnp.einsum(
        "te,de->td", grad_project, qkv_full, preferred_element_type=jnp.float32
    )
    grad_entering_norm, grad_gain_first, grad_shift_first = norm_first_back(grad_normed)
    grad_entering = grad_middle + grad_entering_norm
    input_grad = grad_entering.astype(jnp.bfloat16)
    entering_sum = jnp.sum(grad_entering, axis=0)
    grad_lead_rows = jnp.stack([lead_days * entering_sum, entering_sum])
    grad_gain_rows = jnp.stack([grad_gain_first, grad_gain_second])
    grad_shift_stack = jnp.stack(
        [
            grad_shift_first,
            grad_shift_query,
            grad_shift_value,
            grad_shift_out,
            grad_shift_second,
            grad_shift_down,
        ]
    )
    attention_sums = (
        lax.psum_scatter(grad_qkv_w, ("band", "samp"), scatter_dimension=0, tiled=True),
        lax.psum_scatter(grad_out_w, ("band", "samp"), scatter_dimension=0, tiled=True),
        lax.psum_scatter(grad_gain_rows, ("band", "samp"), scatter_dimension=1, tiled=True),
        lax.psum_scatter(grad_shift_stack, ("band", "samp"), scatter_dimension=1, tiled=True),
        lax.psum_scatter(grad_lead_rows, ("band", "samp"), scatter_dimension=1, tiled=True),
    )
    return (
        output[None],
        input_grad[None],
        attention_sums[0],
        attention_sums[1],
        ffn_sums[0],
        ffn_sums[1],
        ffn_sums[2],
        attention_sums[2],
        attention_sums[3],
        attention_sums[4],
    )


MESH = pl.DeviceIdType.MESH
F32 = jnp.float32
BF16 = jnp.bfloat16
PLANE = 8
DEPTH = 4
ROWS = 128
HALF = 64
BLOCK = 256
CHIPS = 4
NN = (((1,), (0,)), ((), ()))
NT = (((1,), (1,)), ((), ()))
TN = (((0,), (0,)), ((), ()))
INNER = 32


def mm(left, right, dims=NN):
    return lax.dot_general(left, right, dims, preferred_element_type=F32)


def plane_kernel(
    lead_ref, gain_in, shift_in, leadw_in, bias_in, valid_in,
    tok_in, cot_in, wqkv_in, wout_in, wup_in, wdown_in,
    out_h, ig_h, gqkv_h, gout_h, gup_h, gdown_h, gain_o, shift_o, lead_o, bias_o,
    out_o, ig_o, gqkv_o, gout_o, gup_o, gdown_o,
    wqkv, wup, vcol, vec_in,
    agf, wq, wo, wu, wd, sq, su, ztr, vt, vecf, vrow,
    normed, qaug, kaug, kt, vv, vt2, pst, ot, invl, att, gproj, dk, dv,
    hid, gder, gpre, mid, gmid,
    part, pr, cs, rr,
    gds, gus, gqs, gos, gdr, gur, gqr, gor_, gda, guc, gqc, goc, gu2, gq2, gua, gqa, goa,
    acc, gub, vs, vsr, vz, vzr,
    in_s, out_s, ag_s, ag_r, ac_s, ac_r, fw_s, fw_r, aq_s, aq_r, v_s, v_r, y_s, y_r, z_s, z_r, za_r,
    p_s, p_r, c_s, c_r,
):
    b = lax.axis_index("band")
    s = lax.axis_index("samp")
    c = b % 2
    x = (b // 2) % 2
    y = b // 4
    mate = b + 1 - 2 * c
    own = b // 2

    def chip(r):
        dx = r % 2
        dy = r // 2
        xx = x + dx * (1 - 2 * x)
        yy = y + dy * (1 - 2 * y)
        return yy * 2 + xx

    def peer(k):
        return (b + k) % PLANE

    def level(k):
        return (s + k) % DEPTH

    barrier = pltpu.get_barrier_semaphore()
    for k in range(1, PLANE):
        pl.semaphore_signal(barrier, inc=1, device_id=(peer(k), s), device_id_type=MESH)
    for k in range(1, DEPTH):
        pl.semaphore_signal(barrier, inc=1, device_id=(b, level(k)), device_id_type=MESH)

    width = tok_in.shape[1]
    fetches = [
        pltpu.make_async_copy(src, dst, in_s.at[n])
        for n, (src, dst) in enumerate((
            (wqkv_in, wqkv), (wout_in, wo.at[s]), (tok_in, agf.at[0, b]),
            (wup_in, wup), (wdown_in, wd.at[s]), (cot_in, agf.at[1, b]),
        ))
    ]
    for fetch in fetches:
        fetch.start()
    vcol[...] = jnp.zeros_like(vcol)
    vcol[0:2, 0:32] = gain_in[...].astype(F32)
    vcol[2:8, 0:32] = shift_in[...].astype(F32)
    vcol[8:10, 0:32] = leadw_in[...].astype(F32)
    line = lax.broadcasted_iota(jnp.int32, (16, 128), 0)
    tile = pltpu.roll(vcol[...], s * 32, 1)
    tile = jnp.where(line == 11 + s, bias_in[...].astype(F32), tile)
    vec_in[0] = tile.astype(BF16)
    opened = jnp.where(valid_in[...] > 0, 1.0, 0.0)
    vec_in[1] = jnp.where(line == 10, opened, 0.0).astype(BF16)
    far = (s + 2) % DEPTH
    ends = (s == 0) | (s == DEPTH - 1)
    inner = (s > 0) & (s < DEPTH - 1)

    @pl.when(ends)
    def _():
        for kept in (gdr, gur, gqr, gor_):
            kept[DEPTH - 1 - s] = jnp.zeros(kept.shape[1:], BF16)

    fetches[0].wait()
    for d in range(PLANE):
        for j in range(3):
            sq[d, :, j * 128:(j + 1) * 128] = wqkv[:, j * width + d * 128:j * width + (d + 1) * 128]
    fetches[1].wait()
    pl.semaphore_wait(barrier, PLANE - 1 + DEPTH - 1)

    def rc(src, dst, ss, rs, band, samp):
        return pltpu.make_async_remote_copy(
            src_ref=src, dst_ref=dst, send_sem=ss, recv_sem=rs,
            device_id=(band, samp), device_id_type=MESH,
        )

    def yc(kind, k, src, dst):
        return rc(src, dst, y_s.at[kind, k - 1], y_r.at[kind, k - 1], b, level(k))

    def weight_copy(kind, region, role, to):
        return rc(region(s), region(s), z_s.at[kind, role], z_r.at[kind, s], b, to)

    def weight_hand(kind, region):
        return rc(region(far), region(far), z_s.at[kind, 3], z_r.at[kind, far], b, 3 * (s - 1))

    def weight_from(kind, region, t):
        rc(region(t), region(t), z_s.at[kind, 3], z_r.at[kind, t], b, t).wait_recv()

    def weight_start(kind, region):
        @pl.when(s == 1)
        def _():
            weight_copy(kind, region, 2, s - 1).start()

        weight_copy(kind, region, 0, far).start()

        @pl.when(s < DEPTH - 1)
        def _():
            weight_copy(kind, region, 1, s + 1).start()

        @pl.when(s > 1)
        def _():
            weight_copy(kind, region, 2, s - 1).start()

    def weight_pass(kind, region):
        @pl.when(inner)
        def _():
            weight_from(kind, region, far)
            weight_hand(kind, region).start()

    def weight_finish(kind, region):
        @pl.when(s < DEPTH - 1)
        def _():
            weight_from(kind, region, s + 1)

        @pl.when(s > 0)
        def _():
            weight_from(kind, region, s - 1)

        @pl.when(ends)
        def _():
            weight_from(kind, region, far)
            weight_from(kind, region, DEPTH - 1 - s)

    def weight_sent(kind, region):
        weight_copy(kind, region, 0, far).wait_send()

        @pl.when(s < DEPTH - 1)
        def _():
            weight_copy(kind, region, 1, s + 1).wait_send()

        @pl.when(s > 0)
        def _():
            weight_copy(kind, region, 2, s - 1).wait_send()

        @pl.when(inner)
        def _():
            weight_hand(kind, region).wait_send()

    def grad_copy(kind, stage, got, role, to):
        return rc(stage(to), got(s), z_s.at[kind, role], z_r.at[kind, s], b, to)

    def grad_via(kind, stage, via):
        return rc(stage(DEPTH - 1 - s), via, z_s.at[kind, 3], za_r.at[kind - 5], b, 1 + s // 3)

    def grad_start(kind, stage, got, via):
        @pl.when(ends)
        def _():
            grad_via(kind, stage, via).start()
            grad_copy(kind, stage, got, 0, far).start()

        @pl.when(s < DEPTH - 1)
        def _():
            grad_copy(kind, stage, got, 1, s + 1).start()

        @pl.when(s > 0)
        def _():
            grad_copy(kind, stage, got, 2, s - 1).start()

    def grad_pass(kind, stage, got, via):
        @pl.when(inner)
        def _():
            rc(via, via, z_s.at[kind, 3], za_r.at[kind - 5], b, far).wait_recv()
            term = stage(far)
            count = via.shape[0]

            def add(j, _):
                term[j] = (term[j].astype(F32) + via[j].astype(F32)).astype(BF16)
                return 0

            if len(via.shape) == 3:
                lax.fori_loop(0, count, add, 0)
            else:
                def add_rows(j, _):
                    rows = pl.ds(pl.multiple_of(j * INNER, INNER), INNER)
                    term[rows, :] = (term[rows, :].astype(F32) + via[rows, :].astype(F32)).astype(BF16)
                    return 0

                lax.fori_loop(0, count // INNER, add_rows, 0)
            grad_copy(kind, stage, got, 0, far).start()

    def grad_finish(kind, stage, got, via):
        rc(got(far), got(far), z_s.at[kind, 0], z_r.at[kind, far], b, far).wait_recv()

        @pl.when(s < DEPTH - 1)
        def _():
            rc(got(s + 1), got(s + 1), z_s.at[kind, 1], z_r.at[kind, s + 1], b, s + 1).wait_recv()

        @pl.when(s > 0)
        def _():
            rc(got(s - 1), got(s - 1), z_s.at[kind, 2], z_r.at[kind, s - 1], b, s - 1).wait_recv()

    def grad_sent(kind, stage, got, via):
        grad_copy(kind, stage, got, 0, far).wait_send()

        @pl.when(s < DEPTH - 1)
        def _():
            grad_copy(kind, stage, got, 1, s + 1).wait_send()

        @pl.when(s > 0)
        def _():
            grad_copy(kind, stage, got, 2, s - 1).wait_send()

        @pl.when(ends)
        def _():
            grad_via(kind, stage, via).wait_send()

    results = ((out_o, out_h), (ig_o, ig_h), (gqkv_o, gqkv_h), (gout_o, gout_h), (gup_o, gup_h), (gdown_o, gdown_h))

    def deliver(n):
        return pltpu.make_async_copy(results[n][0], results[n][1], out_s.at[n])

    w_out_z = (1, lambda t: wo.at[t])
    w_qkv_z = (2, lambda t: wq.at[:, t])
    w_up_z = (3, lambda t: wu.at[:, t])
    w_down_z = (4, lambda t: wd.at[t])
    g_down_z = (5, lambda t: gds.at[t], lambda t: gdr.at[t], gda)
    g_up_z = (6, lambda t: gus.at[:, t], lambda t: gur.at[t], guc)
    g_qkv_z = (7, lambda t: gqs.at[:, t], lambda t: gqr.at[t], gqc)
    g_out_z = (8, lambda t: gos.at[t], lambda t: gor_.at[t], goc)

    def gather(op, r, half):
        dst = chip(r) * 2 + c
        rows = pl.ds(HALF * ((half + r) % 2), HALF)
        return rc(
            agf.at[op, b, rows], agf.at[op, b, rows],
            ag_s.at[op, r - 1, half], ag_r.at[op, r - 1, half], dst, s,
        )

    def across(op, r):
        blk = chip(r) * 2 + c
        rows = pl.ds(HALF * (r % 2), HALF)
        return rc(
            agf.at[op, blk, rows], agf.at[op, blk, rows],
            ac_s.at[op, r - 1], ac_r.at[op, r - 1], chip(3 - r) * 2 + c, s,
        )

    def share(op, r):
        blk = chip(r) * 2 + c
        return rc(agf.at[op, blk], agf.at[op, blk], fw_s.at[op, r], fw_r.at[op, r], mate, s)

    def start_gather(op):
        for half in (0, 1):
            for r in (1, 2):
                gather(op, r, half).start()
        share(op, 0).start()

    def pass_first(op):
        for r in (1, 2):
            gather(op, r, 0).wait_recv()
            across(op, r).start()

    def pass_second(op):
        for r in (1, 2):
            gather(op, r, 1).wait_recv()
            share(op, r).start()

    def pass_far(op):
        across(op, 1).wait_recv()
        across(op, 2).wait_recv()
        share(op, 3).start()

    def block(op, q):
        return agf[op, pl.ds(2 * q, 2)].reshape(BLOCK, -1)

    def swap(kind, k, src, dst):
        return rc(src, dst, aq_s.at[kind, k - 1], aq_r.at[kind, k - 1], peer(k), s)

    for k in range(1, DEPTH):
        yc(0, k, vec_in.at[0], ztr.at[k - 1]).start()
    for k in range(1, PLANE):
        swap(0, k, sq.at[peer(k)], wq.at[b, s]).start()
    weight_start(*w_out_z)
    fetches[2].wait()
    for r in (1, 2):
        gather(0, r, 0).start()
    wq[b, s] = sq[b]
    fetches[3].wait()
    for d in range(PLANE):
        su[d] = wup[:, d * 512:(d + 1) * 512]
    wu[b, s] = su[b]

    for k in range(1, DEPTH):
        yc(0, k, vec_in.at[0], ztr.at[k - 1]).wait_recv()
    vt[...] = (
        vec_in[0].astype(F32) + vec_in[1].astype(F32)
        + ztr[0].astype(F32) + ztr[1].astype(F32) + ztr[2].astype(F32)
    ).astype(BF16)

    def spread(k):
        return rc(vt, vecf.at[b], v_s.at[0, k - 1], v_r.at[0, k - 1], peer(k), s)

    for k in range(1, PLANE):
        spread(k).start()
    for r in (1, 2):
        gather(0, r, 1).start()
    share(0, 0).start()
    vecf[b] = vt[...]
    for k in range(1, PLANE):
        swap(0, k, sq.at[peer(k)], wq.at[b, s]).wait_recv()
    weight_start(*w_qkv_z)
    for k in range(1, PLANE):
        swap(1, k, su.at[peer(k)], wu.at[b, s]).start()
    pass_first(0)
    for k in range(1, PLANE):
        spread(k).wait_recv()
    for d in range(PLANE):
        vrow[:, d * 128:(d + 1) * 128] = vecf[d].astype(F32)
    lead_days = lead_ref[0].astype(F32) * 0.25
    lane = lax.broadcasted_iota(jnp.int32, (1, 128), 1)
    head_lane = [(lane < 64).astype(F32), (lane >= 64).astype(F32)]
    ones_lane = jnp.where(lane < 2, 1.0, 0.0).astype(F32)
    ends_lane = jnp.where(lane == 0, 9984.0, jnp.where(lane == 1, 16.0, 0.0)).astype(F32)
    gain1, gain2 = vrow[0:1, :], vrow[1:2, :]
    shift1, shift_out, shift2, shift_down = vrow[2:3, :], vrow[5:6, :], vrow[6:7, :], vrow[7:8, :]
    lead_row = lead_days * vrow[8:9, :] + vrow[9:10, :]
    mine = vecf[b].astype(F32)

    def stats(v):
        mean = jnp.mean(v, axis=-1, keepdims=True)
        centered = v - mean
        variance = jnp.mean(centered * centered, axis=-1, keepdims=True)
        rstd = lax.rsqrt(variance + eps)
        return centered * rstd, rstd

    for d in range(PLANE):
        row = jnp.broadcast_to(vecf[d].astype(F32)[10:11, :], (128, 128))
        column = row.T - 1.0
        kaug[d * 128:(d + 1) * 128, 128:256] = (column * ends_lane).astype(BF16)
    for h in range(2):
        for q in range(CHIPS):
            qaug[h, q, :, 128:256] = jnp.broadcast_to(ones_lane, (BLOCK, 128)).astype(BF16)

    def norm_block(d):
        def chunk(j, _):
            rows = pl.ds(pl.multiple_of(j * INNER, INNER), INNER)
            ent = agf[0, d, rows, :].astype(F32) + lead_row
            xhat = stats(ent)[0]
            normed[d, rows, :] = (xhat * gain1 + shift1).astype(BF16)
            return 0

        lax.fori_loop(0, ROWS // INNER, chunk, 0)

    norm_block(b)
    share(0, 0).wait_recv()
    norm_block(mate)
    pass_second(0)
    for r in (1, 2):
        norm_block(chip(r) * 2 + c)
        share(0, r).wait_recv()
        norm_block(chip(r) * 2 + 1 - c)
    weight_pass(*w_qkv_z)
    pass_far(0)
    fetches[5].wait()
    start_gather(1)
    norm_block(chip(3) * 2 + c)
    share(0, 3).wait_recv()
    norm_block(chip(3) * 2 + 1 - c)

    for k in range(1, PLANE):
        swap(1, k, su.at[peer(k)], wu.at[b, s]).wait_recv()
    weight_pass(*w_out_z)
    weight_finish(*w_qkv_z)
    weight_start(*w_up_z)

    def project_block(q, _):
        rows = pl.ds(pl.multiple_of(q * BLOCK, BLOCK), BLOCK)
        pj = mm(normed[pl.ds(2 * q, 2)].reshape(BLOCK, width), wq[...].reshape(width, 384))
        qv = (pj[:, 0:128] + mine[3:4, :]).astype(BF16).astype(F32) * 0.125
        for h in range(2):
            qaug[h, q, :, 0:128] = (qv * head_lane[h]).astype(BF16)
        kv = pj[:, 128:256].astype(BF16)
        kaug[rows, 0:128] = kv
        kt[:, rows] = kv.T
        vb = (pj[:, 256:384] + mine[4:5, :]).astype(BF16)
        vv[rows, :] = vb
        vt2[:, rows] = vb.T
        return 0

    lax.fori_loop(0, CHIPS, project_block, 0)
    weight_finish(*w_out_z)

    def mate_copy(op, slot, r):
        return rc(part.at[slot, r, 1 - c], pr.at[op, r], p_s.at[op, r], p_r.at[op, r], mate, s)

    def chip_copy(op, slot, r):
        return rc(cs.at[slot, r], rr.at[op, r], c_s.at[op, r], c_r.at[op, r], chip(r) * 2 + c, s)

    def put_part(op, slot, r, blk):
        part[slot, r] = blk.astype(BF16).reshape(2, ROWS, width)
        mate_copy(op, slot, r).start()

    def fold(op, slot, r, send=True):
        mate_copy(op, slot, r).wait_recv()

        def chunk(j, _):
            rows = pl.ds(pl.multiple_of(j * INNER, INNER), INNER)
            cs[slot, r, rows, :] = (
                part[slot, r, c, rows, :].astype(F32) + pr[op, r, rows, :].astype(F32)
            ).astype(BF16)
            return 0

        lax.fori_loop(0, ROWS // INNER, chunk, 0)

        if send:
            @pl.when(r > 0)
            def _():
                chip_copy(op, slot, r).start()

    def plane_total(op, slot, rows):
        total = cs[slot, 0, rows, :].astype(F32)
        for r in (1, 2, 3):
            total = total + rr[op, r, rows, :].astype(F32)
        return total

    def end_sums(op, slot):
        for r in range(CHIPS):
            mate_copy(op, slot, r).wait_send()
        for r in (1, 2, 3):
            chip_copy(op, slot, r).wait_send()

    def attend_block(i, _):
        r = 3 - i
        q = chip(r)

        @pl.when(i == 1)
        def _():
            pass_first(1)
            pass_second(1)

        def head(h, _):
            top = pl.ds(pl.multiple_of(h * 64, 64), 64)
            st = mm(kaug[...], qaug[h, q], NT)
            p = jnp.exp(st - jnp.max(st, axis=0, keepdims=True))
            inverse = 1.0 / jnp.sum(p, axis=0, keepdims=True)
            pb = p.astype(BF16)
            pst[h, q] = pb
            ot[q, top, :] = mm(vt2[top, :], pb) * inverse
            invl[q, h] = jnp.broadcast_to(inverse, (8, BLOCK))
            return 0

        lax.fori_loop(0, 2, head, 0)
        low = ot[q].T.astype(BF16)
        att[q] = low
        put_part(0, 0, r, mm(low, wo[...].reshape(128, width)))

        @pl.when(i > 0)
        def _():
            fold(0, 0, r + 1)

        return 0

    lax.fori_loop(0, CHIPS, attend_block, 0)
    fold(0, 0, 0)
    weight_pass(*w_up_z)
    fetches[4].wait()
    weight_start(*w_down_z)
    for r in (1, 2, 3):
        chip_copy(0, 0, r).wait_recv()

    def middle_chunk(j, _):
        rows = pl.ds(pl.multiple_of(j * INNER, INNER), INNER)
        ent = agf[0, b, rows, :].astype(F32) + lead_row
        m = ent + plane_total(0, 0, rows) + shift_out
        mid[rows, :] = m
        agf[2, b, rows, :] = (stats(m)[0] * gain2 + shift2).astype(BF16)
        return 0

    lax.fori_loop(0, ROWS // INNER, middle_chunk, 0)
    start_gather(2)
    pass_far(1)
    end_sums(0, 0)

    weight_finish(*w_up_z)
    bias = jnp.concatenate([mine[11 + j:12 + j, :] for j in range(4)], axis=1)

    def arrivals(op, i):
        @pl.when(i == 0)
        def _():
            share(op, 0).wait_recv()

        @pl.when(i == 1)
        def _():
            pass_first(op)
            pass_second(op)
            share(op, 1).wait_recv()

        @pl.when(i == 2)
        def _():
            share(op, 2).wait_recv()

        @pl.when(i == 3)
        def _():
            pass_far(op)
            share(op, 3).wait_recv()

    def up_block(i, _):
        arrivals(2, i)
        q = chip(i)

        @pl.when(i == 2)
        def _():
            weight_pass(*w_down_z)

        hp = mm(block(2, q), wu[...].reshape(width, 512)) + bias
        phi = 0.5 + 0.5 * lax.erf(hp * 0.7071067811865476)
        hid[pl.ds(pl.multiple_of(q * BLOCK, BLOCK), BLOCK), :] = (hp * phi).astype(BF16)
        gder[q] = phi + hp * jnp.exp(hp * hp * -0.5) * 0.3989422804014327
        return 0

    lax.fori_loop(0, CHIPS, up_block, 0)
    for r in range(CHIPS):
        share(1, r).wait_recv()

    def down_grad(f, _):
        cols = pl.ds(pl.multiple_of(f * BLOCK, BLOCK), BLOCK)
        g = mm(hid[:, cols], agf[1].reshape(PLANE * ROWS, width), TN)
        gds[pl.ds(2 * f, 2)] = g.astype(BF16).reshape(2, 128, width)
        return 0

    lax.fori_loop(0, 2, down_grad, 0)
    grad_start(*g_down_z)
    weight_finish(*w_down_z)
    gub[...] = jnp.zeros_like(gub)

    def back_block(i, _):
        r = 3 - i
        q = chip(r)
        rows = pl.ds(pl.multiple_of(q * BLOCK, BLOCK), BLOCK)
        gh = mm(block(1, q), wd[...].reshape(512, width), NT)
        gp = (gder[q] * gh).astype(BF16)
        gpre[rows, :] = gp
        gub[...] += jnp.sum(gp.astype(F32).reshape(BLOCK // 8, 8, 512), axis=0)
        put_part(1, 1, r, mm(gp, wu[...].reshape(width, 512), NT))

        @pl.when(i > 0)
        def _():
            fold(1, 1, r + 1)

        return 0

    lax.fori_loop(0, CHIPS, back_block, 0)
    fold(1, 1, 0)

    def up_grad(f, _):
        cols = pl.ds(pl.multiple_of(f * BLOCK, BLOCK), BLOCK)
        g = mm(agf[2, :, :, cols].reshape(PLANE * ROWS, BLOCK), gpre[...], TN)
        gus[pl.ds(2 * f, 2)] = g.astype(BF16).reshape(2, 4, 32, 512)
        return 0

    lax.fori_loop(0, CHIPS, up_grad, 0)
    grad_start(*g_up_z)

    def out_block(i, _):
        r = 3 - i
        q = chip(r)
        rows = pl.ds(pl.multiple_of(q * BLOCK, BLOCK), BLOCK)
        put_part(2, 2, r, mm(hid[rows, :], wd[...].reshape(512, width)))

        @pl.when(i > 0)
        def _():
            fold(2, 2, r + 1, send=False)

        return 0

    lax.fori_loop(0, CHIPS, out_block, 0)
    fold(2, 2, 0, send=False)

    grad_pass(*g_down_z)
    for r in (1, 2, 3):
        chip_copy(1, 1, r).wait_recv()
    acc[...] = jnp.zeros_like(acc)

    def add_row(n, v):
        acc[n] += jnp.sum(v.reshape(INNER // 8, 8, width), axis=0)

    def norm_back(v, grad, gain):
        xhat, rstd = stats(v)
        d = grad * gain
        mean_d = jnp.mean(d, axis=-1, keepdims=True)
        mean_dx = jnp.mean(d * xhat, axis=-1, keepdims=True)
        return rstd * (d - mean_d - xhat * mean_dx), xhat

    def second_chunk(j, _):
        rows = pl.ds(pl.multiple_of(j * INNER, INNER), INNER)
        gs = plane_total(1, 1, rows)
        g, xhat = norm_back(mid[rows, :], gs, gain2)
        ct = agf[1, b, rows, :].astype(F32)
        gm = ct + g
        gmid[rows, :] = gm
        gb = gm.astype(BF16)
        agf[3, b, rows, :] = gb
        add_row(1, gs * xhat)
        add_row(6, gs)
        add_row(5, gb.astype(F32))
        add_row(7, ct)
        return 0

    lax.fori_loop(0, ROWS // INNER, second_chunk, 0)
    start_gather(3)

    dk[...] = jnp.zeros_like(dk)
    dv[...] = jnp.zeros_like(dv)
    goa[...] = jnp.zeros_like(goa)

    def attend_back(i, _):
        arrivals(3, i)

        @pl.when(i == 2)
        def _():
            for r in (3, 2, 1):
                chip_copy(2, 2, r).start()

        @pl.when(i == 3)
        def _():
            grad_pass(*g_up_z)

        q = chip(i)
        gbk = block(3, q)
        wo_all = wo[...].reshape(128, width)
        dot_t = mm(wo_all, gbk, NT)
        inv = jnp.concatenate(
            [jnp.broadcast_to(invl[q, h, 0:1, :], (64, BLOCK)) for h in range(2)], axis=0
        )
        dos = dot_t * inv
        prod = dos * ot[q]
        deltas = [jnp.sum(prod[h * 64:(h + 1) * 64], axis=0, keepdims=True) for h in range(2)]
        do_rows = dos.T
        zero = jnp.zeros((64, BLOCK), F32)
        dq_parts = []
        for h in range(2):
            halves = [dos[0:64], zero] if h == 0 else [zero, dos[64:128]]
            dp = mm(vv[...], jnp.concatenate(halves, axis=0).astype(BF16))
            pb = pst[h, q]
            ds = (pb.astype(F32) * (dp - deltas[h])).astype(BF16)
            dv[...] += mm(pb, (do_rows * head_lane[h]).astype(BF16))
            dk[...] += mm(ds, qaug[h, q, :, 0:128])
            dq_parts.append(mm(kt[h * 64:(h + 1) * 64, :], ds))
        dq = jnp.concatenate(dq_parts, axis=0).T * 0.125
        gproj[pl.ds(pl.multiple_of(q * BLOCK, BLOCK), BLOCK), 0:128] = dq.astype(BF16)
        goa[...] += mm(att[q], gbk, TN)
        return 0

    lax.fori_loop(0, CHIPS, attend_back, 0)
    gproj[:, 128:256] = dk[...].astype(BF16)
    gproj[:, 256:384] = dv[...].astype(BF16)

    def qkv_grad(f, _):
        cols = pl.ds(pl.multiple_of(f * BLOCK, BLOCK), BLOCK)
        g = mm(normed[:, :, cols].reshape(PLANE * ROWS, BLOCK), gproj[...], TN)
        gqs[pl.ds(2 * f, 2)] = g.astype(BF16).reshape(2, 4, 32, 384)
        return 0

    lax.fori_loop(0, CHIPS, qkv_grad, 0)
    gos[...] = goa[...].astype(BF16).reshape(4, 32, width)
    grad_start(*g_out_z)
    grad_start(*g_qkv_z)

    def project_back(i, _):
        r = 3 - i
        q = chip(r)
        rows = pl.ds(pl.multiple_of(q * BLOCK, BLOCK), BLOCK)
        put_part(3, 0, r, mm(gproj[rows, :], wq[...].reshape(width, 384), NT))

        @pl.when(i > 0)
        def _():
            fold(3, 0, r + 1)

        return 0

    lax.fori_loop(0, CHIPS, project_back, 0)
    fold(3, 0, 0)

    def others(got):
        return [got(level(k)) for k in range(1, DEPTH)]

    grad_finish(*g_down_z)
    gdown_o[...] = sum([t[...].astype(F32) for t in others(g_down_z[2])], gds[s].astype(F32))
    deliver(5).start()
    for r in (1, 2, 3):
        chip_copy(2, 2, r).wait_recv()

    def output_chunk(j, _):
        rows = pl.ds(pl.multiple_of(j * INNER, INNER), INNER)
        out_o[rows, :] = (mid[rows, :] + plane_total(2, 2, rows) + shift_down).astype(BF16)
        return 0

    lax.fori_loop(0, ROWS // INNER, output_chunk, 0)
    deliver(0).start()

    grad_pass(*g_out_z)
    grad_pass(*g_qkv_z)
    grad_finish(*g_up_z)
    for d in range(PLANE):
        gu2[d] = sum(
            [t[d].astype(F32) for t in others(g_up_z[2])], gus[d, s].astype(F32)
        ).astype(BF16)
    for k in range(1, PLANE):
        swap(2, k, gu2.at[peer(k)], gua.at[b]).start()
    gua[b] = gu2[b]
    for r in (1, 2, 3):
        chip_copy(3, 0, r).wait_recv()

    def first_chunk(j, _):
        rows = pl.ds(pl.multiple_of(j * INNER, INNER), INNER)
        gn = plane_total(3, 0, rows)
        g, xhat = norm_back(agf[0, b, rows, :].astype(F32) + lead_row, gn, gain1)
        ge = gmid[rows, :] + g
        ig_o[rows, :] = ge.astype(BF16)
        add_row(0, gn * xhat)
        add_row(2, gn)
        add_row(9, ge)
        return 0

    lax.fori_loop(0, ROWS // INNER, first_chunk, 0)
    deliver(1).start()
    acc[8] = acc[9] * lead_days

    sums = [jnp.sum(acc[n], axis=0, keepdims=True) for n in range(10)]
    packed = jnp.concatenate(sums + [jnp.zeros((6, width), F32)], axis=0)
    for d in range(PLANE):
        vs[d] = packed[:, d * 128:(d + 1) * 128]

    def vec_swap(k):
        return rc(vs.at[peer(k)], vsr.at[k - 1], v_s.at[1, k - 1], v_r.at[1, k - 1], peer(k), s)

    for k in range(1, PLANE):
        vec_swap(k).start()
    gq_cols = jnp.sum(gproj[:, 0:128].astype(F32), axis=0, keepdims=True)
    gv_cols = jnp.sum(gproj[:, 256:384].astype(F32), axis=0, keepdims=True)
    gub_row = jnp.sum(gub[...], axis=0, keepdims=True)
    extra = jnp.concatenate(
        [jnp.zeros((3, 128), F32), gq_cols, gv_cols, jnp.zeros((6, 128), F32)]
        + [gub_row[:, j * 128:(j + 1) * 128] for j in range(4)]
        + [jnp.zeros((1, 128), F32)],
        axis=0,
    )
    for k in range(1, PLANE):
        vec_swap(k).wait_recv()
    total = vs[b] + extra
    for k in range(PLANE - 1):
        total = total + vsr[k]
    vz[...] = total
    for k in range(1, DEPTH):
        yc(1, k, vz, vzr.at[k - 1]).start()

    grad_finish(*g_out_z)
    gout_o[...] = sum([t[...].astype(F32) for t in others(g_out_z[2])], gos[s].astype(F32))
    deliver(3).start()
    grad_finish(*g_qkv_z)
    for d in range(PLANE):
        gq2[d] = sum(
            [t[d].astype(F32) for t in others(g_qkv_z[2])], gqs[d, s].astype(F32)
        ).astype(BF16)
    for k in range(1, PLANE):
        swap(3, k, gq2.at[peer(k)], gqa.at[b]).start()
    gqa[b] = gq2[b]
    for k in range(1, PLANE):
        swap(2, k, gu2.at[peer(k)], gua.at[b]).wait_recv()
    for d in range(PLANE):
        gup_o[:, d * 512:(d + 1) * 512] = gua[d].astype(F32)
    deliver(4).start()
    for k in range(1, DEPTH):
        yc(1, k, vz, vzr.at[k - 1]).wait_recv()
    vz_sum = vz[...] + vzr[0] + vzr[1] + vzr[2]
    columns = pltpu.roll(vz_sum, (128 - 32 * s) % 128, 1)
    gain_o[...] = columns[0:2, 0:32]
    shift_o[...] = columns[2:8, 0:32]
    lead_o[...] = columns[8:10, 0:32]
    bias_o[...] = jnp.sum(jnp.where(line == 11 + s, vz_sum, 0.0), axis=0, keepdims=True)
    for k in range(1, PLANE):
        swap(3, k, gq2.at[peer(k)], gqa.at[b]).wait_recv()
    for d in range(PLANE):
        for j in range(3):
            gqkv_o[:, j * width + d * 128:j * width + (d + 1) * 128] = (
                gqa[d, :, j * 128:(j + 1) * 128].astype(F32)
            )

    deliver(2).start()
    for op in range(4):
        for r in (1, 2):
            gather(op, r, 0).wait_send()
            gather(op, r, 1).wait_send()
            across(op, r).wait_send()
        for r in range(CHIPS):
            share(op, r).wait_send()
    for op, slot in ((1, 1), (2, 2), (3, 0)):
        end_sums(op, slot)
    for k in range(1, PLANE):
        swap(0, k, sq.at[peer(k)], wq.at[b, s]).wait_send()
        swap(1, k, su.at[peer(k)], wu.at[b, s]).wait_send()
        swap(2, k, gu2.at[peer(k)], gua.at[b]).wait_send()
        swap(3, k, gq2.at[peer(k)], gqa.at[b]).wait_send()
        spread(k).wait_send()
        vec_swap(k).wait_send()
    for k in range(1, DEPTH):
        yc(0, k, vec_in.at[0], ztr.at[k - 1]).wait_send()
        yc(1, k, vz, vzr.at[k - 1]).wait_send()
    for moved in (w_out_z, w_qkv_z, w_up_z, w_down_z):
        weight_sent(*moved)
    for moved in (g_down_z, g_up_z, g_qkv_z, g_out_z):
        grad_sent(*moved)
    for n in range(6):
        deliver(n).wait()


def hand_over(*refs):
    count = len(refs) // 2
    sems = refs[-1]
    copies = [pltpu.make_async_copy(refs[n], refs[count + n], sems.at[n]) for n in range(count)]
    for copy in copies:
        copy.start()
    for copy in copies:
        copy.wait()


def plane_body(
    tokens, cotangent, w_qkv, w_out, w_up, w_down,
    up_bias, norm_gains, shift_rows, lead_weight, lead_steps, valid_cells,
):
    width = tokens.shape[2]
    vmem = pl.BlockSpec(memory_space=pltpu.VMEM)
    anywhere = pl.BlockSpec(memory_space=pl.ANY)
    dma = pltpu.SemaphoreType.DMA
    V = pltpu.VMEM
    out_shape = (
        jax.ShapeDtypeStruct((ROWS, width), BF16),
        jax.ShapeDtypeStruct((ROWS, width), BF16),
        jax.ShapeDtypeStruct((32, 3 * width), F32),
        jax.ShapeDtypeStruct((32, width), F32),
        jax.ShapeDtypeStruct((32, 4 * width), F32),
        jax.ShapeDtypeStruct((128, width), F32),
        jax.ShapeDtypeStruct((2, 32), F32),
        jax.ShapeDtypeStruct((6, 32), F32),
        jax.ShapeDtypeStruct((2, 32), F32),
        jax.ShapeDtypeStruct((1, 128), F32),
    )
    scratch = [
        V((ROWS, width), BF16), V((ROWS, width), BF16),
        V((32, 3 * width), F32), V((32, width), F32),
        V((32, 4 * width), F32), V((128, width), F32),
        V((32, 3 * width), BF16), V((32, 4 * width), BF16),
        V((16, 128), F32), V((2, 16, 128), BF16),
        V((4, PLANE, ROWS, width), BF16),
        V((PLANE, DEPTH, 32, 384), BF16),
        V((DEPTH, 32, width), BF16),
        V((PLANE, DEPTH, 32, 512), BF16),
        V((DEPTH, 128, width), BF16),
        V((PLANE, 32, 384), BF16),
        V((PLANE, 32, 512), BF16),
        V((3, 16, 128), BF16),
        V((16, 128), BF16),
        V((PLANE, 16, 128), BF16),
        V((16, width), F32),
        V((PLANE, ROWS, width), BF16),
        V((2, CHIPS, BLOCK, 256), BF16),
        V((1024, 256), BF16),
        V((128, 1024), BF16),
        V((1024, 128), BF16),
        V((128, 1024), BF16),
        V((2, CHIPS, 1024, BLOCK), BF16),
        V((CHIPS, 128, BLOCK), F32),
        V((CHIPS, 2, 8, BLOCK), F32),
        V((CHIPS, BLOCK, 128), BF16),
        V((1024, 384), BF16),
        V((1024, 128), F32),
        V((1024, 128), F32),
        V((1024, 512), BF16),
        V((CHIPS, BLOCK, 512), F32),
        V((1024, 512), BF16),
        V((ROWS, width), F32),
        V((ROWS, width), F32),
        V((3, CHIPS, 2, ROWS, width), BF16),
        V((4, CHIPS, ROWS, width), BF16),
        V((3, CHIPS, ROWS, width), BF16),
        V((4, CHIPS, ROWS, width), BF16),
        V((DEPTH, 128, width), BF16),
        V((PLANE, DEPTH, 32, 512), BF16),
        V((PLANE, DEPTH, 32, 384), BF16),
        V((DEPTH, 32, width), BF16),
        V((DEPTH, 128, width), BF16),
        V((DEPTH, PLANE, 32, 512), BF16),
        V((DEPTH, PLANE, 32, 384), BF16),
        V((DEPTH, 32, width), BF16),
        V((128, width), BF16),
        V((PLANE, 32, 512), BF16),
        V((PLANE, 32, 384), BF16),
        V((32, width), BF16),
        V((PLANE, 32, 512), BF16),
        V((PLANE, 32, 384), BF16),
        V((PLANE, 32, 512), BF16),
        V((PLANE, 32, 384), BF16),
        V((128, width), F32),
        V((10, 8, width), F32),
        V((8, 512), F32),
        V((PLANE, 16, 128), F32),
        V((PLANE - 1, 16, 128), F32),
        V((16, 128), F32),
        V((3, 16, 128), F32),
        dma((6,)), dma((6,)),
        dma((4, 2, 2)), dma((4, 2, 2)), dma((4, 2)), dma((4, 2)), dma((4, 4)), dma((4, 4)),
        dma((4, 7)), dma((4, 7)), dma((2, 7)), dma((2, 7)),
        dma((2, 3)), dma((2, 3)), dma((9, 4)), dma((9, 4)), dma((4,)),
        dma((4, 4)), dma((4, 4)), dma((4, 4)), dma((4, 4)),
    ]
    results = pl.pallas_call(
        plane_kernel,
        out_shape=out_shape,
        in_specs=[pl.BlockSpec(memory_space=pltpu.SMEM)] + [vmem] * 5 + [anywhere] * 6,
        out_specs=tuple([anywhere] * 6 + [vmem] * 4),
        scratch_shapes=scratch,
        compiler_params=pltpu.CompilerParams(
            collective_id=0, has_side_effects=True, vmem_limit_bytes=63 * 2**20
        ),
    )(
        lead_steps, norm_gains, shift_rows, lead_weight, up_bias[None], valid_cells,
        tokens[0], cotangent[0], w_qkv, w_out, w_up, w_down,
    )
    results = pl.pallas_call(
        hand_over,
        out_shape=out_shape,
        in_specs=[vmem] * len(out_shape),
        out_specs=tuple([anywhere] * len(out_shape)),
        scratch_shapes=[dma((len(out_shape),))],
    )(*results)
    output, input_grad, g_qkv, g_out, g_up, g_down, g_gains, g_shifts, g_lead, g_bias = results
    return (
        output[None], input_grad[None], g_qkv, g_out, g_up, g_down, g_bias[0],
        g_gains, g_shifts, g_lead,
    )


def plane_fits(mesh):
    return mesh.shape["band"] == PLANE and mesh.shape["samp"] == DEPTH


def solution(mesh):
    return jax.shard_map(
        plane_body if plane_fits(mesh) else body,
        mesh=mesh,
        in_specs=(
            P("samp", "band", None),
            P("samp", "band", None),
            P(("band", "samp"), None),
            P(("band", "samp"), None),
            P(("band", "samp"), None),
            P(("band", "samp"), None),
            P(("band", "samp")),
            P(None, ("band", "samp")),
            P(None, ("band", "samp")),
            P(None, ("band", "samp")),
            P("samp"),
            P("samp", "band"),
        ),
        out_specs=(
            P("samp", "band", None),
            P("samp", "band", None),
            P(("band", "samp"), None),
            P(("band", "samp"), None),
            P(("band", "samp"), None),
            P(("band", "samp"), None),
            P(("band", "samp")),
            P(None, ("band", "samp")),
            P(None, ("band", "samp")),
            P(None, ("band", "samp")),
        ),
        check_vma=False,
    )
```

```python
import jax
import jax.numpy as jnp
from jax import lax
from jax.experimental import pallas as pl
from jax.experimental.pallas import tpu as pltpu
from jax.sharding import PartitionSpec as P

HEADS = 16


eps = 1e-05
masked = 10000.0


def layer_norm(values, gain_row, shift_row):
    centered = values - jnp.mean(values, axis=-1, keepdims=True)
    variance = jnp.mean(centered * centered, axis=-1, keepdims=True)
    return centered * lax.rsqrt(variance + eps) * gain_row + shift_row


def gelu_exact(values):
    return jax.nn.gelu(values, approximate=False)


def body(
    tokens,
    cotangent,
    w_qkv,
    w_out,
    w_up,
    w_down,
    up_bias,
    norm_gains,
    shift_rows,
    lead_weight,
    lead_steps,
    valid_cells,
):
    whole = (
        lax.all_gather(w_qkv, ("band", "samp"), axis=0, tiled=True),
        lax.all_gather(w_out, ("band", "samp"), axis=0, tiled=True),
        lax.all_gather(w_up, ("band", "samp"), axis=0, tiled=True),
        lax.all_gather(w_down, ("band", "samp"), axis=0, tiled=True),
        lax.all_gather(up_bias, ("band", "samp"), axis=0, tiled=True),
        lax.all_gather(norm_gains, ("band", "samp"), axis=1, tiled=True),
        lax.all_gather(shift_rows, ("band", "samp"), axis=1, tiled=True),
        lax.all_gather(lead_weight, ("band", "samp"), axis=1, tiled=True),
    )
    qkv_full = whole[0]
    out_full = whole[1]
    up_full = whole[2]
    down_full = whole[3]
    up_shift = whole[4].astype(jnp.float32)
    gain_all = whole[5].astype(jnp.float32)
    shift_all = whole[6].astype(jnp.float32)
    lead_all = whole[7].astype(jnp.float32)
    row_count = tokens.shape[1]
    width = tokens.shape[2]
    head_count = HEADS
    head_size = width // head_count
    score_scale = head_size ** (-0.5)
    lead_days = lead_steps[0].astype(jnp.float32) * 0.25
    entering = tokens[0].astype(jnp.float32) + lead_days * lead_all[0] + lead_all[1]
    normed, norm_first_back = jax.vjp(layer_norm, entering, gain_all[0], shift_all[0])
    normed_low = normed.astype(jnp.bfloat16)
    project = jnp.dot(normed_low, qkv_full, preferred_element_type=jnp.float32)
    queries = (project[:, :width] + shift_all[1]).astype(jnp.bfloat16)
    key_rows = project[:, width : 2 * width].astype(jnp.bfloat16)
    value_rows = (project[:, 2 * width :] + shift_all[2]).astype(jnp.bfloat16)
    key_open = (valid_cells[0] > 0).astype(jnp.bfloat16)
    keys_all, values_all, open_all = (
        lax.all_gather(key_rows, "band", axis=0, tiled=True),
        lax.all_gather(value_rows, "band", axis=0, tiled=True),
        lax.all_gather(key_open, "band", axis=0, tiled=True),
    )
    seq_total = keys_all.shape[0]
    block_rows = min(512, seq_total)
    block_count = seq_total // block_rows
    block_ids = jnp.arange(block_count)
    bias_all = (open_all.astype(jnp.float32) - 1.0) * masked
    query_heads = queries.reshape(row_count, head_count, head_size)

    def block_keys(step_index):
        first_row = step_index * block_rows
        key_block = lax.dynamic_slice_in_dim(keys_all, first_row, block_rows, 0).reshape(
            block_rows, head_count, head_size
        )
        value_block = lax.dynamic_slice_in_dim(values_all, first_row, block_rows, 0).reshape(
            block_rows, head_count, head_size
        )
        bias_block = lax.dynamic_slice_in_dim(bias_all, first_row, block_rows, 0)
        scores = (
            jnp.einsum("qhe,khe->hqk", query_heads, key_block, preferred_element_type=jnp.float32)
            * score_scale
            + bias_block
        )
        return (scores, key_block, value_block)

    def max_step(running, step_index):
        row_max, exp_total = running
        scores = block_keys(step_index)[0]
        new_max = jnp.maximum(row_max, jnp.max(scores, axis=-1))
        exp_total = exp_total * jnp.exp(row_max - new_max) + jnp.sum(
            jnp.exp(scores - new_max[..., None]), axis=-1
        )
        return ((new_max, exp_total), None)

    start_max = jnp.full((head_count, row_count), -jnp.inf, jnp.float32)
    start_total = jnp.zeros((head_count, row_count), jnp.float32)
    row_max, exp_total = lax.scan(max_step, (start_max, start_total), block_ids)[0]
    log_total = row_max + jnp.log(exp_total)

    def out_step(running, step_index):
        scores, key_block, value_block = block_keys(step_index)
        weights_low = jnp.exp(scores - log_total[..., None]).astype(jnp.bfloat16)
        return (
            running
            + jnp.einsum(
                "hqk,khe->qhe", weights_low, value_block, preferred_element_type=jnp.float32
            ),
            None,
        )

    attended_heads = lax.scan(
        out_step, jnp.zeros((row_count, head_count, head_size), jnp.float32), block_ids
    )[0]
    attended_low = attended_heads.reshape(row_count, width).astype(jnp.bfloat16)
    middle = (
        entering
        + jnp.dot(attended_low, out_full, preferred_element_type=jnp.float32)
        + shift_all[3]
    )
    second, norm_second_back = jax.vjp(layer_norm, middle, gain_all[1], shift_all[4])
    second_low = second.astype(jnp.bfloat16)
    hidden_pre = jnp.dot(second_low, up_full, preferred_element_type=jnp.float32) + up_shift
    hidden, gelu_back = jax.vjp(gelu_exact, hidden_pre)
    hidden_low = hidden.astype(jnp.bfloat16)
    result = (
        middle + jnp.dot(hidden_low, down_full, preferred_element_type=jnp.float32) + shift_all[5]
    )
    output = result.astype(jnp.bfloat16)
    grad_result = cotangent[0]
    grad_result_f = grad_result.astype(jnp.float32)
    grad_down_w = jnp.einsum(
        "tf,td->fd", hidden_low, grad_result, preferred_element_type=jnp.float32
    )
    grad_shift_down = jnp.sum(grad_result_f, axis=0)
    grad_hidden = jnp.einsum(
        "td,fd->tf", grad_result, down_full, preferred_element_type=jnp.float32
    )
    grad_pre_low = gelu_back(grad_hidden)[0].astype(jnp.bfloat16)
    grad_up_w = jnp.einsum(
        "td,tf->df", second_low, grad_pre_low, preferred_element_type=jnp.float32
    )
    grad_up_shift = jnp.sum(grad_pre_low.astype(jnp.float32), axis=0)
    grad_second = jnp.einsum("tf,df->td", grad_pre_low, up_full, preferred_element_type=jnp.float32)
    grad_middle_norm, grad_gain_second, grad_shift_second = norm_second_back(grad_second)
    grad_middle = grad_result_f + grad_middle_norm
    ffn_sums = (
        lax.psum_scatter(grad_up_w, ("band", "samp"), scatter_dimension=0, tiled=True),
        lax.psum_scatter(grad_down_w, ("band", "samp"), scatter_dimension=0, tiled=True),
        lax.psum_scatter(grad_up_shift, ("band", "samp"), scatter_dimension=0, tiled=True),
    )
    grad_branch = grad_middle.astype(jnp.bfloat16)
    grad_shift_out = jnp.sum(grad_branch.astype(jnp.float32), axis=0)
    grad_out_w = jnp.einsum(
        "td,te->de", attended_low, grad_branch, preferred_element_type=jnp.float32
    )
    grad_attended = jnp.einsum(
        "te,de->td", grad_branch, out_full, preferred_element_type=jnp.float32
    ).astype(jnp.bfloat16)
    grad_heads = grad_attended.reshape(row_count, head_count, head_size)
    delta = jnp.einsum("qhe,qhe->hq", grad_heads.astype(jnp.float32), attended_heads)
    zero_heads = jnp.zeros((row_count, head_count, head_size), jnp.float32)

    def key_grad_step(g_queries, step_index):
        scores, key_block, value_block = block_keys(step_index)
        weights_full = jnp.exp(scores - log_total[..., None])
        g_weights = jnp.einsum(
            "qhe,khe->hqk", grad_heads, value_block, preferred_element_type=jnp.float32
        )
        g_scores = (weights_full * (g_weights - delta[..., None])).astype(jnp.bfloat16)
        g_queries = (
            g_queries
            + jnp.einsum("hqk,khe->qhe", g_scores, key_block, preferred_element_type=jnp.float32)
            * score_scale
        )
        key_term = (
            jnp.einsum("hqk,qhe->khe", g_scores, query_heads, preferred_element_type=jnp.float32)
            * score_scale
        )
        value_term = jnp.einsum(
            "hqk,qhe->khe",
            weights_full.astype(jnp.bfloat16),
            grad_heads,
            preferred_element_type=jnp.float32,
        )
        return (
            g_queries,
            (key_term.reshape(block_rows, width), value_term.reshape(block_rows, width)),
        )

    grad_query_heads, block_terms = lax.scan(key_grad_step, zero_heads, block_ids)
    grad_query_f = grad_query_heads.reshape(row_count, width)
    key_sum, value_sum = (
        lax.psum_scatter(
            block_terms[0].reshape(seq_total, width), "band", scatter_dimension=0, tiled=True
        ),
        lax.psum_scatter(
            block_terms[1].reshape(seq_total, width), "band", scatter_dimension=0, tiled=True
        ),
    )
    grad_query_low = grad_query_f.astype(jnp.bfloat16)
    grad_key_low = key_sum.astype(jnp.bfloat16)
    grad_value_low = value_sum.astype(jnp.bfloat16)
    grad_project = jnp.concatenate([grad_query_low, grad_key_low, grad_value_low], axis=-1)
    grad_qkv_w = jnp.einsum(
        "td,te->de", normed_low, grad_project, preferred_element_type=jnp.float32
    )
    grad_shift_query = jnp.sum(grad_query_low.astype(jnp.float32), axis=0)
    grad_shift_value = jnp.sum(grad_value_low.astype(jnp.float32), axis=0)
    grad_normed = jnp.einsum(
        "te,de->td", grad_project, qkv_full, preferred_element_type=jnp.float32
    )
    grad_entering_norm, grad_gain_first, grad_shift_first = norm_first_back(grad_normed)
    grad_entering = grad_middle + grad_entering_norm
    input_grad = grad_entering.astype(jnp.bfloat16)
    entering_sum = jnp.sum(grad_entering, axis=0)
    grad_lead_rows = jnp.stack([lead_days * entering_sum, entering_sum])
    grad_gain_rows = jnp.stack([grad_gain_first, grad_gain_second])
    grad_shift_stack = jnp.stack(
        [
            grad_shift_first,
            grad_shift_query,
            grad_shift_value,
            grad_shift_out,
            grad_shift_second,
            grad_shift_down,
        ]
    )
    attention_sums = (
        lax.psum_scatter(grad_qkv_w, ("band", "samp"), scatter_dimension=0, tiled=True),
        lax.psum_scatter(grad_out_w, ("band", "samp"), scatter_dimension=0, tiled=True),
        lax.psum_scatter(grad_gain_rows, ("band", "samp"), scatter_dimension=1, tiled=True),
        lax.psum_scatter(grad_shift_stack, ("band", "samp"), scatter_dimension=1, tiled=True),
        lax.psum_scatter(grad_lead_rows, ("band", "samp"), scatter_dimension=1, tiled=True),
    )
    return (
        output[None],
        input_grad[None],
        attention_sums[0],
        attention_sums[1],
        ffn_sums[0],
        ffn_sums[1],
        ffn_sums[2],
        attention_sums[2],
        attention_sums[3],
        attention_sums[4],
    )


MESH = pl.DeviceIdType.MESH
F32 = jnp.float32
BF16 = jnp.bfloat16
PLANE = 8
DEPTH = 4
ROWS = 128
HALF = 64
BLOCK = 256
NN = (((1,), (0,)), ((), ()))
NT = (((1,), (1,)), ((), ()))
TN = (((0,), (0,)), ((), ()))
INNER = 32


def mm(left, right, dims=NN):
    return lax.dot_general(left, right, dims, preferred_element_type=F32)


def plane_kernel(
    lead_ref, gain_in, shift_in, leadw_in, bias_in, valid_in,
    tok_in, cot_in, wqkv_in, wout_in, wup_in, wdown_in,
    out_h, ig_h, gqkv_h, gout_h, gup_h, gdown_h, gain_h, shift_h, lead_h, bias_h,
    out_o, ig_o, gqkv_o, gout_o, gup_o, gdown_o, gain_o, shift_o, lead_o, bias_o,
    wqkv, wup, vcol, vec_in,
    agf, wq, wo, wu, wd, sq, su, ztr, vt, vecf, vrow,
    normed, qaug, kaug, kt, vv, vt2, pst, ot, invl, att, aown, dsend, dob, gproj, dk, dv,
    hid, gder, gpre, mid, gmid,
    part, pr, cs, au, rr,
    gds, gus, gqs, gos, gdr, gur, gqr, gor_, gda, guc, gqc, gu2, gq2, gua, gqa, goa,
    acc, gub, vs, vsr, vz, vzr,
    in_s, out_s, ag_s, ag_r, ac_s, ac_r, fw_s, fw_r, aq_s, aq_r, v_s, v_r, y_s, y_r, z_s, z_r, za_r,
    p_s, p_r, f_s, f_r, n_s, n_r, wg_s, wg_r, h_s, h_r, g_s, g_r,
):
    b = lax.axis_index("band")
    s = lax.axis_index("samp")
    c = b % 2
    x = (b // 2) % 2
    y = b // 4
    mate = b + 1 - 2 * c

    def chip(r):
        xx = x + (r % 2) * (1 - 2 * x)
        yy = y + (r // 2) * (1 - 2 * y)
        return yy * 2 + xx

    def near(r):
        return chip(r) * 2 + c

    def peer(k):
        return (b + k) % PLANE

    def level(k):
        return (s + k) % DEPTH

    barrier = pltpu.get_barrier_semaphore()
    for k in range(1, PLANE):
        pl.semaphore_signal(barrier, inc=1, device_id=(peer(k), s), device_id_type=MESH)
    for k in range(1, DEPTH):
        pl.semaphore_signal(barrier, inc=1, device_id=(b, level(k)), device_id_type=MESH)

    width = tok_in.shape[1]
    fetches = [
        pltpu.make_async_copy(src, dst, in_s.at[n])
        for n, (src, dst) in enumerate((
            (wqkv_in, wqkv), (wout_in, wo.at[b, pl.ds(pl.multiple_of(s * 32, 32), 32)]),
            (tok_in.at[pl.ds(0, HALF)], agf.at[0, 0, 0, c]),
            (tok_in.at[pl.ds(HALF, HALF)], agf.at[0, 0, 1, c]),
            (wup_in, wup), (wdown_in, wd.at[s]),
            (cot_in.at[pl.ds(0, HALF)], agf.at[1, 0, 0, c]),
            (cot_in.at[pl.ds(HALF, HALF)], agf.at[1, 0, 1, c]),
        ))
    ]
    for fetch in fetches:
        fetch.start()
    vcol[...] = jnp.zeros_like(vcol)
    vcol[0:2, 0:32] = gain_in[...].astype(F32)
    vcol[2:8, 0:32] = shift_in[...].astype(F32)
    vcol[8:10, 0:32] = leadw_in[...].astype(F32)
    line = lax.broadcasted_iota(jnp.int32, (16, 128), 0)
    tile = pltpu.roll(vcol[...], s * 32, 1)
    tile = jnp.where(line == 11 + s, bias_in[...].astype(F32), tile)
    vec_in[0] = tile.astype(BF16)
    opened = jnp.where(valid_in[...] > 0, 1.0, 0.0)
    vec_in[1] = jnp.where(line == 10, opened, 0.0).astype(BF16)
    far = (s + 2) % DEPTH
    ends = (s == 0) | (s == DEPTH - 1)
    inner = (s > 0) & (s < DEPTH - 1)

    @pl.when(s == 0)
    def _():
        for kept in (gdr, gur, gqr):
            kept[0] = jnp.zeros(kept.shape[1:], BF16)

    @pl.when(s == DEPTH - 1)
    def _():
        for kept in (gda, guc, gqc):
            kept[...] = jnp.zeros(kept.shape, BF16)

    fetches[0].wait()
    for d in range(PLANE):
        for j in range(3):
            sq[d, :, j * 128:(j + 1) * 128] = wqkv[:, j * width + d * 128:j * width + (d + 1) * 128]
    fetches[1].wait()
    pl.semaphore_wait(barrier, PLANE - 1 + DEPTH - 1)

    def rc(src, dst, ss, rs, band, samp):
        return pltpu.make_async_remote_copy(
            src_ref=src, dst_ref=dst, send_sem=ss, recv_sem=rs,
            device_id=(band, samp), device_id_type=MESH,
        )

    def yc(kind, k, src, dst):
        return rc(src, dst, y_s.at[kind, k - 1], y_r.at[kind, k - 1], b, level(k))

    def weight_copy(kind, region, role, to):
        return rc(region(s), region(s), z_s.at[kind, role], z_r.at[kind, s], b, to)

    def weight_hand(kind, region):
        return rc(region(far), region(far), z_s.at[kind, 3], z_r.at[kind, far], b, 3 * (s - 1))

    def weight_from(kind, region, t):
        rc(region(t), region(t), z_s.at[kind, 3], z_r.at[kind, t], b, t).wait_recv()

    def weight_start(kind, region):
        @pl.when(s == 1)
        def _():
            weight_copy(kind, region, 2, s - 1).start()

        weight_copy(kind, region, 0, far).start()

        @pl.when(s < DEPTH - 1)
        def _():
            weight_copy(kind, region, 1, s + 1).start()

        @pl.when(s > 1)
        def _():
            weight_copy(kind, region, 2, s - 1).start()

    def weight_pass(kind, region):
        @pl.when(inner)
        def _():
            weight_from(kind, region, far)
            weight_hand(kind, region).start()

    def weight_finish(kind, region):
        @pl.when(s < DEPTH - 1)
        def _():
            weight_from(kind, region, s + 1)

        @pl.when(s > 0)
        def _():
            weight_from(kind, region, s - 1)

        @pl.when(ends)
        def _():
            weight_from(kind, region, far)
            weight_from(kind, region, DEPTH - 1 - s)

    def weight_sent(kind, region):
        weight_copy(kind, region, 0, far).wait_send()

        @pl.when(s < DEPTH - 1)
        def _():
            weight_copy(kind, region, 1, s + 1).wait_send()

        @pl.when(s > 0)
        def _():
            weight_copy(kind, region, 2, s - 1).wait_send()

        @pl.when(inner)
        def _():
            weight_hand(kind, region).wait_send()

    def grad_up(kind, stage, got, via, t):
        return rc(stage(t), got(t), z_s.at[kind, t], z_r.at[kind, t], b, s + 1)

    def grad_down_to(kind, stage, got, via, t):
        return rc(stage(t), got(t), z_s.at[kind, t], z_r.at[kind, t], b, s - 1)

    def grad_down_last(kind, stage, got, via):
        return rc(stage(s - 1), via, z_s.at[kind, s - 1], za_r.at[kind - 5], b, s - 1)

    def grad_start(kind, stage, got, via):
        @pl.when(s == 0)
        def _():
            for t in (3, 2, 1):
                grad_up(kind, stage, got, via, t).start()

        @pl.when(s == DEPTH - 1)
        def _():
            for t in (0, 1):
                grad_down_to(kind, stage, got, via, t).start()
            grad_down_last(kind, stage, got, via).start()

    def add_in(kind, stage, got, via, t):
        rc(got(t), got(t), z_s.at[kind, t], z_r.at[kind, t], b, s).wait_recv()
        term, more = stage(t), got(t)
        if len(via.shape) == 3:
            def add(j, _):
                term[j] = (term[j].astype(F32) + more[j].astype(F32)).astype(BF16)
                return 0

            lax.fori_loop(0, via.shape[0], add, 0)
        else:
            def add_rows(j, _):
                rows = pl.ds(pl.multiple_of(j * INNER, INNER), INNER)
                term[rows, :] = (term[rows, :].astype(F32) + more[rows, :].astype(F32)).astype(BF16)
                return 0

            lax.fori_loop(0, via.shape[0] // INNER, add_rows, 0)

    def grad_pass(*moved):
        @pl.when(s == 1)
        def _():
            add_in(*moved, 3)
            grad_up(*moved, 3).start()

        @pl.when(s == 2)
        def _():
            add_in(*moved, 0)
            grad_down_to(*moved, 0).start()

    def grad_pass_on(*moved):
        @pl.when(s == 1)
        def _():
            add_in(*moved, 2)
            grad_up(*moved, 2).start()
            add_in(*moved, 0)
            grad_down_last(*moved).start()

        @pl.when(s == 2)
        def _():
            add_in(*moved, 1)
            grad_down_last(*moved).start()
            add_in(*moved, 3)
            grad_up(*moved, 3).start()

    def grad_finish(kind, stage, got, via):
        @pl.when(s > 0)
        def _():
            rc(got(s), got(s), z_s.at[kind, 0], z_r.at[kind, s], b, s).wait_recv()

        @pl.when(s < DEPTH - 1)
        def _():
            rc(via, via, z_s.at[kind, 0], za_r.at[kind - 5], b, s).wait_recv()

    def grad_sent(kind, stage, got, via):
        for k in range(1, DEPTH):
            t = level(k)
            rc(stage(t), got(t), z_s.at[kind, t], z_r.at[kind, t], b, s).wait_send()

    def direct_copy(kind, stage, got, t):
        return rc(stage(t), got(s), z_s.at[kind, t], z_r.at[kind, s], b, t)

    def direct_start(kind, stage, got):
        for t in (3, 2, 1, 0):
            @pl.when((s != t) & (s < 2))
            def _():
                direct_copy(kind, stage, got, t).start()

        for t in (0, 1, 2, 3):
            @pl.when((s != t) & (s >= 2))
            def _():
                direct_copy(kind, stage, got, t).start()

    def direct_finish(kind, stage, got):
        for k in range(1, DEPTH):
            t = level(k)
            rc(got(t), got(t), z_s.at[kind, t], z_r.at[kind, t], b, t).wait_recv()

    def direct_sent(kind, stage, got):
        for k in range(1, DEPTH):
            direct_copy(kind, stage, got, level(k)).wait_send()

    results = ((out_o, out_h), (ig_o, ig_h), (gqkv_o, gqkv_h), (gout_o, gout_h), (gup_o, gup_h), (gdown_o, gdown_h),
               (gain_o, gain_h), (shift_o, shift_h), (lead_o, lead_h), (bias_o, bias_h))

    def deliver(n):
        return pltpu.make_async_copy(results[n][0], results[n][1], out_s.at[n])

    w_out_z = (1, lambda t: wo.at[b, pl.ds(pl.multiple_of(t * 32, 32), 32)])
    w_qkv_z = (2, lambda t: wq.at[:, t])
    w_up_z = (3, lambda t: wu.at[:, t])
    w_down_z = (4, lambda t: wd.at[t])
    g_down_z = (5, lambda t: gds.at[t], lambda t: gdr.at[t], gda)
    g_up_z = (6, lambda t: gus.at[:, t], lambda t: gur.at[t], guc)
    g_qkv_z = (7, lambda t: gqs.at[:, t], lambda t: gqr.at[t], gqc)
    g_out_z = (8, lambda t: gos.at[t], lambda t: gor_.at[t])

    def gather(op, r, turn):
        return rc(
            agf.at[op, 0, (turn + r) % 2, c], agf.at[op, 1 + turn, r - 1, c],
            ag_s.at[op, r - 1, turn], ag_r.at[op, r - 1, turn], near(r), s,
        )

    def across(op, r):
        return rc(
            agf.at[op, 1, r - 1, c], agf.at[op, 3, r % 2, c],
            ac_s.at[op, r - 1], ac_r.at[op, r - 1], near(3 - r), s,
        )

    def share(op, blk):
        return rc(
            agf.at[op, blk, :, c], agf.at[op, blk, :, c],
            fw_s.at[op, blk], fw_r.at[op, blk], mate, s,
        )

    def start_gather(op):
        for turn in (0, 1):
            for r in (1, 2):
                gather(op, r, turn).start()
        share(op, 0).start()

    def arrive(op, blk):
        if blk in (1, 2):
            for r in (1, 2):
                gather(op, r, blk - 1).wait_recv()
                if blk == 1:
                    across(op, r).start()
        if blk == 3:
            across(op, 1).wait_recv()
            across(op, 2).wait_recv()
        if blk:
            share(op, blk).start()

    def block(op, i):
        return agf[op, i].reshape(BLOCK, -1)

    def rows_half(dev, h):
        return wo.at[dev, pl.ds(h * HALF, HALF)]

    def rows_copy(r, turn):
        part_ = rows_half(b, (turn + r) % 2)
        return rc(part_, part_, wg_s.at[r - 1, turn], wg_r.at[r - 1, turn], near(r), s)

    def rows_across(r):
        part_ = rows_half(near(r), r % 2)
        return rc(part_, part_, wg_s.at[2, r - 1], wg_r.at[2, r - 1], near(3 - r), s)

    def rows_share(r):
        dev = near(r) if r else b
        return rc(wo.at[dev], wo.at[dev], wg_s.at[3, r], wg_r.at[3, r], mate, s)

    def rows_start():
        for turn in (0, 1):
            for r in (1, 2):
                rows_copy(r, turn).start()
        rows_share(0).start()

    def granule(i, a):
        return (i, a) if i in (0, 3) else (a + 1, 1 - a if i == 1 else a)

    GRANULES = [(i, a) for i in (3, 2, 1, 0) for a in (0, 1)]

    def heads_copy(i, a, k):
        r, h = granule(i, a)
        rows = pl.ds(pl.multiple_of((a * 2 + k) * HALF, HALF), HALF)
        return rc(
            att.at[i, rows], aown.at[b, pl.ds(h * HALF, HALF)],
            h_s.at[i, a, k], h_r.at[r, h, c], chip(r) * 2 + k, s,
        )

    def heads_from(r, h, k):
        dst = aown.at[chip(r) * 2 + k, pl.ds(h * HALF, HALF)]
        return rc(dst, dst, h_s.at[0, 0, 0], h_r.at[r, h, k], mate, s)

    def cores(i):
        return (1 - c,) if i == 0 else (0, 1)

    def back_copy(i, a, k):
        r, h = granule(i, a)
        dev = chip(r) * 2 + k
        return rc(
            dsend.at[dev, pl.ds(h * HALF, HALF)], dob.at[i, a, c],
            g_s.at[i, a, k], g_r.at[i, a, c], dev, s,
        )

    def back_from(i, a, k):
        return rc(dob.at[i, a, k], dob.at[i, a, k], g_s.at[0, 0, 0], g_r.at[i, a, k], mate, s)

    def swap(kind, k, src, dst):
        return rc(src, dst, aq_s.at[kind, k - 1], aq_r.at[kind, k - 1], peer(k), s)

    for k in range(1, DEPTH):
        yc(0, k, vec_in.at[0], ztr.at[k - 1]).start()
    for k in range(1, PLANE):
        swap(0, k, sq.at[peer(k)], wq.at[b, s]).start()
    weight_start(*w_out_z)
    fetches[2].wait()
    fetches[3].wait()
    for r in (1, 2):
        gather(0, r, 0).start()
    wq[b, s] = sq[b]
    fetches[4].wait()
    for d in range(PLANE):
        su[d] = wup[:, d * 512:(d + 1) * 512]
    wu[b, s] = su[b]

    for k in range(1, DEPTH):
        yc(0, k, vec_in.at[0], ztr.at[k - 1]).wait_recv()
    vt[...] = (
        vec_in[0].astype(F32) + vec_in[1].astype(F32)
        + ztr[0].astype(F32) + ztr[1].astype(F32) + ztr[2].astype(F32)
    ).astype(BF16)

    def spread(k):
        return rc(vt, vecf.at[b], v_s.at[0, k - 1], v_r.at[0, k - 1], peer(k), s)

    for k in range(1, PLANE):
        spread(k).start()
    for r in (1, 2):
        gather(0, r, 1).start()
    share(0, 0).start()
    vecf[b] = vt[...]
    for k in range(1, PLANE):
        swap(0, k, sq.at[peer(k)], wq.at[b, s]).wait_recv()
    weight_start(*w_qkv_z)
    for k in range(1, PLANE):
        swap(1, k, su.at[peer(k)], wu.at[b, s]).start()
    arrive(0, 1)
    fetches[6].wait()
    fetches[7].wait()
    for r in (1, 2):
        gather(1, r, 0).start()
    share(1, 0).start()
    for k in range(1, PLANE):
        spread(k).wait_recv()
    for d in range(PLANE):
        vrow[:, d * 128:(d + 1) * 128] = vecf[d].astype(F32)
    lead_days = lead_ref[0].astype(F32) * 0.25
    lane = lax.broadcasted_iota(jnp.int32, (1, 128), 1)
    head_lane = [(lane < 64).astype(F32), (lane >= 64).astype(F32)]
    ones_lane = jnp.where(lane < 2, 1.0, 0.0).astype(F32)
    ends_lane = jnp.where(lane == 0, 9984.0, jnp.where(lane == 1, 16.0, 0.0)).astype(F32)
    gain1, gain2 = vrow[0:1, :], vrow[1:2, :]
    shift1, shift_out, shift2, shift_down = vrow[2:3, :], vrow[5:6, :], vrow[6:7, :], vrow[7:8, :]
    lead_row = lead_days * vrow[8:9, :] + vrow[9:10, :]
    mine = vecf[b].astype(F32)

    def stats(v):
        mean = jnp.mean(v, axis=-1, keepdims=True)
        centered = v - mean
        variance = jnp.mean(centered * centered, axis=-1, keepdims=True)
        rstd = lax.rsqrt(variance + eps)
        return centered * rstd, rstd

    for r in range(4):
        for k in range(2):
            row = jnp.broadcast_to(vecf[chip(r) * 2 + k].astype(F32)[10:11, :], (128, 128))
            column = ((row.T - 1.0) * ends_lane).astype(BF16)
            for h in range(2):
                if r in (0, 3):
                    blk, a = r, h
                else:
                    blk, a = (1 if h == r % 2 else 2), r - 1
                top = blk * BLOCK + (a * 2 + k) * HALF
                kaug[top:top + HALF, 128:256] = column[h * HALF:(h + 1) * HALF]
    for h in range(2):
        for i in range(4):
            qaug[h, i, :, 128:256] = jnp.broadcast_to(ones_lane, (BLOCK, 128)).astype(BF16)

    def norm_block(i):
        def chunk(j, _):
            rows = pl.ds(pl.multiple_of((j % 2) * INNER, INNER), INNER)
            ent = agf[0, i, j // 4, (j // 2) % 2, rows, :].astype(F32) + lead_row
            xhat = stats(ent)[0]
            put = pl.ds(pl.multiple_of(j * INNER, INNER), INNER)
            normed[i, put, :] = (xhat * gain1 + shift1).astype(BF16)
            return 0

        lax.fori_loop(0, BLOCK // INNER, chunk, 0)

    share(0, 0).wait_recv()
    norm_block(0)
    share(0, 1).wait_recv()
    arrive(0, 2)
    norm_block(1)
    weight_pass(*w_out_z)
    weight_pass(*w_qkv_z)
    share(0, 2).wait_recv()
    norm_block(2)
    weight_finish(*w_out_z)
    rows_start()
    arrive(0, 3)
    share(0, 3).wait_recv()
    norm_block(3)

    for k in range(1, PLANE):
        swap(1, k, su.at[peer(k)], wu.at[b, s]).wait_recv()
    weight_finish(*w_qkv_z)
    weight_start(*w_up_z)

    def project_block(q, _):
        rows = pl.ds(pl.multiple_of(q * BLOCK, BLOCK), BLOCK)
        pj = mm(normed[q], wq[...].reshape(width, 384))
        qv = (pj[:, 0:128] + mine[3:4, :]).astype(BF16).astype(F32) * 0.125
        for h in range(2):
            qaug[h, q, :, 0:128] = (qv * head_lane[h]).astype(BF16)
        kv = pj[:, 128:256].astype(BF16)
        kaug[rows, 0:128] = kv
        kt[:, rows] = kv.T
        vb = (pj[:, 256:384] + mine[4:5, :]).astype(BF16)
        vv[rows, :] = vb
        vt2[:, rows] = vb.T
        return 0

    lax.fori_loop(0, 4, project_block, 0)

    def mate_copy(op, i):
        return rc(part.at[op, i, :, 1 - c], pr.at[op, i], p_s.at[op, i], p_r.at[op, i], mate, s)

    def far_copy(op, h):
        return rc(cs.at[op, 3, h], au.at[op, 1 - h], f_s.at[op, h], f_r.at[op, 1 - h], near(h + 1), s)

    def near_copy(op, i, a):
        h = a if i == 2 else 1 - a
        return rc(cs.at[op, i, a], rr.at[op, a, h], n_s.at[op, a, h], n_r.at[op, a, h], near(a + 1), s)

    def put_part(op, i, blk):
        part[op, i] = blk.astype(BF16).reshape(2, 2, HALF, width)
        mate_copy(op, i).start()

    def fold(op, i):
        mate_copy(op, i).wait_recv()

        def chunk(j, _):
            a = j // 2
            rows = pl.ds(pl.multiple_of((j % 2) * INNER, INNER), INNER)
            cs[op, i, a, rows, :] = (
                part[op, i, a, c, rows, :].astype(F32) + pr[op, i, a, rows, :].astype(F32)
            ).astype(BF16)
            return 0

        lax.fori_loop(0, ROWS // INNER, chunk, 0)

    def fold_before(op, i, near_too=True):
        @pl.when(i < 3)
        def _():
            fold(op, i + 1)

        @pl.when(i == 2)
        def _():
            send_far(op)

        if near_too:
            @pl.when(i == 1)
            def _():
                send_near(op, 2)

    def send_far(op):
        for h in (0, 1):
            far_copy(op, h).start()

    def send_near(op, i):
        for a in (0, 1):
            near_copy(op, i, a).start()

    def send_last(op):
        for a in (0, 1):
            far_copy(op, 1 - a).wait_recv()

            def chunk(j, _):
                rows = pl.ds(pl.multiple_of(j * INNER, INNER), INNER)
                cs[op, 1, a, rows, :] = (
                    cs[op, 1, a, rows, :].astype(F32) + au[op, a, rows, :].astype(F32)
                ).astype(BF16)
                return 0

            lax.fori_loop(0, HALF // INNER, chunk, 0)
            near_copy(op, 1, a).start()

    def wait_sums(op):
        for i in (2, 1):
            for a in (0, 1):
                near_copy(op, i, a).wait_recv()

    def place(j):
        return j // 2, pl.ds(pl.multiple_of((j % 2) * INNER, INNER), INNER)

    def plane_total(op, j):
        h, rows = place(j)
        total = cs[op, 0, h, rows, :].astype(F32)
        return total + rr[op, 0, h, rows, :].astype(F32) + rr[op, 1, h, rows, :].astype(F32)

    def own_rows(op, j):
        h, rows = place(j)
        return agf[op, 0, h, c, rows, :].astype(F32)

    def set_rows(op, j, v):
        h, rows = place(j)
        agf[op, 0, h, c, rows, :] = v

    def end_sums(op):
        for i in range(4):
            mate_copy(op, i).wait_send()
        for h in (0, 1):
            far_copy(op, h).wait_send()
        for i in (2, 1):
            for a in (0, 1):
                near_copy(op, i, a).wait_send()

    def attend_block(n, _):
        i = 3 - n

        @pl.when(n == 3)
        def _():
            for r in (1, 2):
                rows_copy(r, 1).wait_recv()
                rows_share(r).start()

        for h in range(2):
            st = mm(kaug[...], qaug[h, i], NT)
            p = jnp.exp(st - jnp.max(st, axis=0, keepdims=True))
            inverse = 1.0 / jnp.sum(p, axis=0, keepdims=True)
            pb = p.astype(BF16)
            pst[h, i] = pb
            ot[i, h * 64:(h + 1) * 64, :] = mm(vt2[h * 64:(h + 1) * 64, :], pb) * inverse
            invl[i, h] = jnp.broadcast_to(inverse, (8, BLOCK))
        att[i] = ot[i].T.astype(BF16)
        for blk in range(4):
            @pl.when(i == blk)
            def _():
                for a in (0, 1):
                    for k in cores(blk):
                        heads_copy(blk, a, k).start()

        return 0

    arrive(1, 1)
    for r in (1, 2):
        rows_copy(r, 0).wait_recv()
        rows_across(r).start()
    lax.fori_loop(0, 4, attend_block, 0)
    for r in (1, 2):
        gather(1, r, 1).start()
    for h in (0, 1):
        top = pl.multiple_of((h * 2 + c) * HALF, HALF)
        aown[b, h * HALF:(h + 1) * HALF] = att[0, pl.ds(top, HALF), :]
    weight_pass(*w_up_z)
    fetches[5].wait()

    @pl.when(inner)
    def _():
        weight_start(*w_down_z)

    arrive(1, 3)
    for r in (1, 2):
        rows_across(r).wait_recv()
    rows_share(3).start()
    for r in range(4):
        rows_share(r).wait_recv()
    for r in (3, 2, 1, 0):
        for h in (0, 1):
            for k in cores(r):
                heads_from(r, h, k).wait_recv()
    heads = jnp.concatenate([aown[d] for d in range(PLANE)], axis=1)
    mid[...] = mm(heads, wo[...].reshape(1024, width))

    def middle_chunk(j, _):
        rows = pl.ds(pl.multiple_of(j * INNER, INNER), INNER)
        m = own_rows(0, j) + lead_row + mid[rows, :] + shift_out
        mid[rows, :] = m
        set_rows(2, j, (stats(m)[0] * gain2 + shift2).astype(BF16))
        return 0

    lax.fori_loop(0, ROWS // INNER, middle_chunk, 0)
    start_gather(2)

    weight_finish(*w_up_z)

    @pl.when(ends)
    def _():
        weight_start(*w_down_z)

    bias = jnp.concatenate([mine[11 + j:12 + j, :] for j in range(4)], axis=1)

    def arrivals(op, i):
        for blk in range(4):
            @pl.when(i == blk)
            def _():
                arrive(op, blk)
                share(op, blk).wait_recv()

    def up_block(i, _):
        arrivals(2, i)


        hp = mm(block(2, i), wu[...].reshape(width, 512)) + bias
        phi = 0.5 + 0.5 * lax.erf(hp * 0.7071067811865476)
        hid[pl.ds(pl.multiple_of(i * BLOCK, BLOCK), BLOCK), :] = (hp * phi).astype(BF16)
        gder[i] = phi + hp * jnp.exp(hp * hp * -0.5) * 0.3989422804014327
        return 0

    lax.fori_loop(0, 4, up_block, 0)
    weight_pass(*w_down_z)
    arrive(1, 2)
    for i in range(4):
        share(1, i).wait_recv()

    def down_grad(f, _):
        cols = pl.ds(pl.multiple_of(f * BLOCK, BLOCK), BLOCK)
        g = mm(hid[:, cols], agf[1].reshape(1024, width), TN)
        gds[pl.ds(2 * f, 2)] = g.astype(BF16).reshape(2, 128, width)
        return 0

    lax.fori_loop(0, 2, down_grad, 0)
    grad_start(*g_down_z)
    weight_finish(*w_down_z)
    gub[...] = jnp.zeros_like(gub)

    def back_block(n, _):
        i = 3 - n
        rows = pl.ds(pl.multiple_of(i * BLOCK, BLOCK), BLOCK)
        gh = mm(block(1, i), wd[...].reshape(512, width), NT)
        gp = (gder[i] * gh).astype(BF16)
        gpre[rows, :] = gp
        gub[...] += jnp.sum(gp.astype(F32).reshape(BLOCK // 8, 8, 512), axis=0)
        put_part(0, i, mm(gp, wu[...].reshape(width, 512), NT))
        fold_before(0, i)
        return 0

    lax.fori_loop(0, 4, back_block, 0)
    fold(0, 0)

    def up_grad(f, _):
        cols = pl.ds(pl.multiple_of(f * BLOCK, BLOCK), BLOCK)
        g = mm(agf[2, :, :, :, :, cols].reshape(1024, BLOCK), gpre[...], TN)
        gus[pl.ds(2 * f, 2)] = g.astype(BF16).reshape(2, 4, 32, 512)
        return 0

    grad_pass(*g_down_z)
    lax.fori_loop(0, 4, up_grad, 0)
    grad_start(*g_up_z)

    def out_block(n, _):
        i = 3 - n
        rows = pl.ds(pl.multiple_of(i * BLOCK, BLOCK), BLOCK)
        put_part(1, i, mm(hid[rows, :], wd[...].reshape(512, width)))
        fold_before(1, i, near_too=False)
        return 0

    send_last(0)
    lax.fori_loop(0, 4, out_block, 0)
    fold(1, 0)

    wait_sums(0)
    acc[...] = jnp.zeros_like(acc)

    def add_row(n, v):
        acc[n] += jnp.sum(v.reshape(INNER // 8, 8, width), axis=0)

    def norm_back(v, grad, gain):
        xhat, rstd = stats(v)
        d = grad * gain
        mean_d = jnp.mean(d, axis=-1, keepdims=True)
        mean_dx = jnp.mean(d * xhat, axis=-1, keepdims=True)
        return rstd * (d - mean_d - xhat * mean_dx), xhat

    def second_chunk(j, _):
        rows = pl.ds(pl.multiple_of(j * INNER, INNER), INNER)
        gs = plane_total(0, j)
        g, xhat = norm_back(mid[rows, :], gs, gain2)
        ct = own_rows(1, j)
        gm = ct + g
        gmid[rows, :] = gm
        gb = gm.astype(BF16)
        set_rows(3, j, gb)
        add_row(1, gs * xhat)
        add_row(6, gs)
        add_row(5, gb.astype(F32))
        add_row(7, ct)
        return 0

    grad_pass_on(*g_down_z)
    lax.fori_loop(0, ROWS // INNER, second_chunk, 0)
    gbo = agf[3, 0, :, c].reshape(ROWS, width)
    gha = mm(gbo, wo[...].reshape(1024, width), NT).astype(BF16)
    for d in range(PLANE):
        dsend[d] = gha[:, d * 128:(d + 1) * 128]
    for i, a in GRANULES:
        for k in cores(i):
            back_copy(i, a, k).start()
    for h in (0, 1):
        dob[0, h, c] = dsend[b, h * HALF:(h + 1) * HALF, :]
    start_gather(3)

    dk[...] = jnp.zeros_like(dk)
    dv[...] = jnp.zeros_like(dv)
    goa[...] = jnp.zeros_like(goa)

    def attend_back(i, _):
        for blk in range(4):
            @pl.when(i == blk)
            def _():
                for a in (0, 1):
                    for k in cores(blk):
                        back_from(blk, a, k).wait_recv()

        @pl.when(i == 2)
        def _():
            send_near(1, 2)
            send_last(1)

        @pl.when(i == 3)
        def _():
            arrive(3, 1)
            grad_pass(*g_up_z)

        dot_t = dob[i].reshape(BLOCK, 128).astype(F32).T
        inv = jnp.concatenate(
            [jnp.broadcast_to(invl[i, h, 0:1, :], (64, BLOCK)) for h in range(2)], axis=0
        )
        dos = dot_t * inv
        prod = dos * ot[i]
        deltas = [jnp.sum(prod[h * 64:(h + 1) * 64], axis=0, keepdims=True) for h in range(2)]
        do_rows = dos.T
        zero = jnp.zeros((64, BLOCK), F32)
        dq_parts = []
        for h in range(2):
            halves = [dos[0:64], zero] if h == 0 else [zero, dos[64:128]]
            dp = mm(vv[...], jnp.concatenate(halves, axis=0).astype(BF16))
            pb = pst[h, i]
            ds = (pb.astype(F32) * (dp - deltas[h])).astype(BF16)
            dv[...] += mm(pb, (do_rows * head_lane[h]).astype(BF16))
            dk[...] += mm(ds, qaug[h, i, :, 0:128])
            dq_parts.append(mm(kt[h * 64:(h + 1) * 64, :], ds))
        dq = jnp.concatenate(dq_parts, axis=0).T * 0.125
        gproj[pl.ds(pl.multiple_of(i * BLOCK, BLOCK), BLOCK), 0:128] = dq.astype(BF16)
        return 0

    lax.fori_loop(0, 4, attend_back, 0)
    gproj[:, 128:256] = dk[...].astype(BF16)
    gproj[:, 256:384] = dv[...].astype(BF16)

    def qkv_grad(f, _):
        cols = pl.ds(pl.multiple_of(f * BLOCK, BLOCK), BLOCK)
        g = mm(normed[:, :, cols].reshape(1024, BLOCK), gproj[...], TN)
        gqs[pl.ds(2 * f, 2)] = g.astype(BF16).reshape(2, 4, 32, 384)
        return 0

    lax.fori_loop(0, 4, qkv_grad, 0)
    grad_start(*g_qkv_z)

    def project_back(n, _):
        i = 3 - n
        rows = pl.ds(pl.multiple_of(i * BLOCK, BLOCK), BLOCK)
        put_part(2, i, mm(gproj[rows, :], wq[...].reshape(width, 384), NT))
        fold_before(2, i)
        return 0

    arrive(3, 2)
    lax.fori_loop(0, 4, project_back, 0)
    fold(2, 0)

    grad_pass_on(*g_up_z)
    share(3, 0).wait_recv()
    arrive(3, 3)

    def out_grad(i, _):
        for blk in (1, 2, 3):
            @pl.when(i == blk)
            def _():
                share(3, blk).wait_recv()

        goa[...] += mm(att[i], block(3, i), TN)
        return 0

    lax.fori_loop(0, 4, out_grad, 0)
    gos[...] = goa[...].astype(BF16).reshape(4, 32, width)

    @pl.when(ends)
    def _():
        direct_start(*g_out_z)

    send_last(2)
    def others(kind, stage, got, via):
        return [got(s), via]

    def from_planes(got):
        return [got(level(k)) for k in range(1, DEPTH)]

    grad_finish(*g_down_z)
    gdown_o[...] = sum([t[...].astype(F32) for t in others(*g_down_z)], gds[s].astype(F32))
    deliver(5).start()
    grad_pass(*g_qkv_z)
    wait_sums(2)

    def first_chunk(j, _):
        rows = pl.ds(pl.multiple_of(j * INNER, INNER), INNER)
        gn = plane_total(2, j)
        g, xhat = norm_back(own_rows(0, j) + lead_row, gn, gain1)
        ge = gmid[rows, :] + g
        ig_o[rows, :] = ge.astype(BF16)
        add_row(0, gn * xhat)
        add_row(2, gn)
        add_row(9, ge)
        return 0

    lax.fori_loop(0, ROWS // INNER, first_chunk, 0)
    deliver(1).start()
    acc[8] = acc[9] * lead_days

    sums = [jnp.sum(acc[n], axis=0, keepdims=True) for n in range(10)]
    packed = jnp.concatenate(sums + [jnp.zeros((6, width), F32)], axis=0)
    for d in range(PLANE):
        vs[d] = packed[:, d * 128:(d + 1) * 128]

    def vec_swap(k):
        return rc(vs.at[peer(k)], vsr.at[k - 1], v_s.at[1, k - 1], v_r.at[1, k - 1], peer(k), s)

    for k in range(1, PLANE):
        vec_swap(k).start()
    gq_cols = jnp.sum(gproj[:, 0:128].astype(F32), axis=0, keepdims=True)
    gv_cols = jnp.sum(gproj[:, 256:384].astype(F32), axis=0, keepdims=True)
    gub_row = jnp.sum(gub[...], axis=0, keepdims=True)
    extra = jnp.concatenate(
        [jnp.zeros((3, 128), F32), gq_cols, gv_cols, jnp.zeros((6, 128), F32)]
        + [gub_row[:, j * 128:(j + 1) * 128] for j in range(4)]
        + [jnp.zeros((1, 128), F32)],
        axis=0,
    )
    wait_sums(1)

    def output_chunk(j, _):
        rows = pl.ds(pl.multiple_of(j * INNER, INNER), INNER)
        out_o[rows, :] = (mid[rows, :] + plane_total(1, j) + shift_down).astype(BF16)
        return 0

    lax.fori_loop(0, ROWS // INNER, output_chunk, 0)
    deliver(0).start()

    grad_finish(*g_up_z)
    for d in range(PLANE):
        gu2[d] = sum(
            [t[d].astype(F32) for t in others(*g_up_z)], gus[d, s].astype(F32)
        ).astype(BF16)
    for k in range(1, PLANE):
        swap(2, k, gu2.at[peer(k)], gua.at[b]).start()
    gua[b] = gu2[b]
    grad_pass_on(*g_qkv_z)

    @pl.when(inner)
    def _():
        direct_start(*g_out_z)

    for k in range(1, PLANE):
        vec_swap(k).wait_recv()
    total = vs[b] + extra
    for k in range(PLANE - 1):
        total = total + vsr[k]
    vz[...] = total
    for k in range(1, DEPTH):
        yc(1, k, vz, vzr.at[k - 1]).start()

    grad_finish(*g_qkv_z)
    for d in range(PLANE):
        gq2[d] = sum(
            [t[d].astype(F32) for t in others(*g_qkv_z)], gqs[d, s].astype(F32)
        ).astype(BF16)
    for k in range(1, PLANE):
        swap(3, k, gq2.at[peer(k)], gqa.at[b]).start()
    gqa[b] = gq2[b]
    direct_finish(*g_out_z)
    gout_o[...] = sum([t[...].astype(F32) for t in from_planes(g_out_z[2])], gos[s].astype(F32))
    deliver(3).start()
    for k in range(1, PLANE):
        swap(2, k, gu2.at[peer(k)], gua.at[b]).wait_recv()
    for d in range(PLANE):
        gup_o[:, d * 512:(d + 1) * 512] = gua[d].astype(F32)
    deliver(4).start()
    for k in range(1, DEPTH):
        yc(1, k, vz, vzr.at[k - 1]).wait_recv()
    vz_sum = vz[...] + vzr[0] + vzr[1] + vzr[2]
    columns = pltpu.roll(vz_sum, (128 - 32 * s) % 128, 1)
    gain_o[...] = columns[0:2, 0:32]
    shift_o[...] = columns[2:8, 0:32]
    lead_o[...] = columns[8:10, 0:32]
    bias_o[...] = jnp.sum(jnp.where(line == 11 + s, vz_sum, 0.0), axis=0, keepdims=True)
    for n in range(6, 10):
        deliver(n).start()
    for k in range(1, PLANE):
        swap(3, k, gq2.at[peer(k)], gqa.at[b]).wait_recv()
    for d in range(PLANE):
        for j in range(3):
            gqkv_o[:, j * width + d * 128:j * width + (d + 1) * 128] = (
                gqa[d, :, j * 128:(j + 1) * 128].astype(F32)
            )

    deliver(2).start()
    for op in range(4):
        for r in (1, 2):
            gather(op, r, 0).wait_send()
            gather(op, r, 1).wait_send()
            across(op, r).wait_send()
        for i in range(4):
            share(op, i).wait_send()
    for op in range(3):
        end_sums(op)
    for r in (1, 2):
        rows_copy(r, 0).wait_send()
        rows_copy(r, 1).wait_send()
        rows_across(r).wait_send()
    for r in range(4):
        rows_share(r).wait_send()
    for i, a in GRANULES:
        for k in cores(i):
            heads_copy(i, a, k).wait_send()
            back_copy(i, a, k).wait_send()
    for k in range(1, PLANE):
        swap(0, k, sq.at[peer(k)], wq.at[b, s]).wait_send()
        swap(1, k, su.at[peer(k)], wu.at[b, s]).wait_send()
        swap(2, k, gu2.at[peer(k)], gua.at[b]).wait_send()
        swap(3, k, gq2.at[peer(k)], gqa.at[b]).wait_send()
        spread(k).wait_send()
        vec_swap(k).wait_send()
    for k in range(1, DEPTH):
        yc(0, k, vec_in.at[0], ztr.at[k - 1]).wait_send()
        yc(1, k, vz, vzr.at[k - 1]).wait_send()
    for moved in (w_out_z, w_qkv_z, w_up_z, w_down_z):
        weight_sent(*moved)
    for moved in (g_down_z, g_up_z, g_qkv_z):
        grad_sent(*moved)
    direct_sent(*g_out_z)
    for n in range(10):
        deliver(n).wait()


def hand_over(*refs):
    count = len(refs) // 3
    given, taken, held, sems = refs[:count], refs[count:2 * count], refs[2 * count:3 * count], refs[-1]
    into = [pltpu.make_async_copy(given[n], held[n], sems.at[0, n]) for n in range(count)]
    out = [pltpu.make_async_copy(held[n], taken[n], sems.at[1, n]) for n in range(count)]
    for copy in into:
        copy.start()
    for n in range(count):
        into[n].wait()
        out[n].start()
    for copy in out:
        copy.wait()


def plane_body(
    tokens, cotangent, w_qkv, w_out, w_up, w_down,
    up_bias, norm_gains, shift_rows, lead_weight, lead_steps, valid_cells,
):
    width = tokens.shape[2]
    vmem = pl.BlockSpec(memory_space=pltpu.VMEM)
    anywhere = pl.BlockSpec(memory_space=pl.ANY)
    dma = pltpu.SemaphoreType.DMA
    V = pltpu.VMEM
    out_shape = (
        jax.ShapeDtypeStruct((ROWS, width), BF16),
        jax.ShapeDtypeStruct((ROWS, width), BF16),
        jax.ShapeDtypeStruct((32, 3 * width), F32),
        jax.ShapeDtypeStruct((32, width), F32),
        jax.ShapeDtypeStruct((32, 4 * width), F32),
        jax.ShapeDtypeStruct((128, width), F32),
        jax.ShapeDtypeStruct((2, 32), F32),
        jax.ShapeDtypeStruct((6, 32), F32),
        jax.ShapeDtypeStruct((2, 32), F32),
        jax.ShapeDtypeStruct((1, 128), F32),
    )
    scratch = [
        V((ROWS, width), BF16), V((ROWS, width), BF16),
        V((32, 3 * width), F32), V((32, width), F32),
        V((32, 4 * width), F32), V((128, width), F32),
        V((2, 32), F32), V((6, 32), F32), V((2, 32), F32), V((1, 128), F32),
        V((32, 3 * width), BF16), V((32, 4 * width), BF16),
        V((16, 128), F32), V((2, 16, 128), BF16),
        V((4, 4, 2, 2, HALF, width), BF16),
        V((PLANE, DEPTH, 32, 384), BF16),
        V((PLANE, 128, width), BF16),
        V((PLANE, DEPTH, 32, 512), BF16),
        V((DEPTH, 128, width), BF16),
        V((PLANE, 32, 384), BF16),
        V((PLANE, 32, 512), BF16),
        V((3, 16, 128), BF16),
        V((16, 128), BF16),
        V((PLANE, 16, 128), BF16),
        V((16, width), F32),
        V((4, BLOCK, width), BF16),
        V((2, 4, BLOCK, 256), BF16),
        V((1024, 256), BF16),
        V((128, 1024), BF16),
        V((1024, 128), BF16),
        V((128, 1024), BF16),
        V((2, 4, 1024, BLOCK), BF16),
        V((4, 128, BLOCK), F32),
        V((4, 2, 8, BLOCK), F32),
        V((4, BLOCK, 128), BF16),
        V((PLANE, ROWS, 128), BF16),
        V((PLANE, ROWS, 128), BF16),
        V((4, 2, 2, HALF, 128), BF16),
        V((1024, 384), BF16),
        V((1024, 128), F32),
        V((1024, 128), F32),
        V((1024, 512), BF16),
        V((4, BLOCK, 512), F32),
        V((1024, 512), BF16),
        V((ROWS, width), F32),
        V((ROWS, width), F32),
        V((3, 4, 2, 2, HALF, width), BF16),
        V((3, 4, 2, HALF, width), BF16),
        V((3, 4, 2, HALF, width), BF16),
        V((3, 2, HALF, width), BF16),
        V((3, 2, 2, HALF, width), BF16),
        V((DEPTH, 128, width), BF16),
        V((PLANE, DEPTH, 32, 512), BF16),
        V((PLANE, DEPTH, 32, 384), BF16),
        V((DEPTH, 32, width), BF16),
        V((DEPTH, 128, width), BF16),
        V((DEPTH, PLANE, 32, 512), BF16),
        V((DEPTH, PLANE, 32, 384), BF16),
        V((DEPTH, 32, width), BF16),
        V((128, width), BF16),
        V((PLANE, 32, 512), BF16),
        V((PLANE, 32, 384), BF16),
        V((PLANE, 32, 512), BF16),
        V((PLANE, 32, 384), BF16),
        V((PLANE, 32, 512), BF16),
        V((PLANE, 32, 384), BF16),
        V((128, width), F32),
        V((10, 8, width), F32),
        V((8, 512), F32),
        V((PLANE, 16, 128), F32),
        V((PLANE - 1, 16, 128), F32),
        V((16, 128), F32),
        V((3, 16, 128), F32),
        dma((8,)), dma((10,)),
        dma((4, 2, 2)), dma((4, 2, 2)), dma((4, 2)), dma((4, 2)), dma((4, 4)), dma((4, 4)),
        dma((4, 7)), dma((4, 7)), dma((2, 7)), dma((2, 7)),
        dma((2, 3)), dma((2, 3)), dma((9, 4)), dma((9, 4)), dma((3,)),
        dma((3, 4)), dma((3, 4)), dma((3, 2)), dma((3, 2)), dma((3, 2, 2)), dma((3, 2, 2)),
        dma((4, 4)), dma((4, 4)), dma((4, 2, 2)), dma((4, 2, 2)), dma((4, 2, 2)), dma((4, 2, 2)),
    ]
    results = pl.pallas_call(
        plane_kernel,
        out_shape=out_shape,
        in_specs=[pl.BlockSpec(memory_space=pltpu.SMEM)] + [vmem] * 5 + [anywhere] * 6,
        out_specs=tuple([anywhere] * 10),
        scratch_shapes=scratch,
        compiler_params=pltpu.CompilerParams(
            collective_id=0, has_side_effects=True, vmem_limit_bytes=63 * 2**20
        ),
    )(
        lead_steps, norm_gains, shift_rows, lead_weight, up_bias[None], valid_cells,
        tokens[0], cotangent[0], w_qkv, w_out, w_up, w_down,
    )
    results = pl.pallas_call(
        hand_over,
        out_shape=out_shape,
        in_specs=[anywhere] * len(out_shape),
        out_specs=tuple([anywhere] * len(out_shape)),
        scratch_shapes=[V(o.shape, o.dtype) for o in out_shape] + [dma((2, len(out_shape)))],
    )(*results)
    output, input_grad, g_qkv, g_out, g_up, g_down, g_gains, g_shifts, g_lead, g_bias = results
    return (
        output[None], input_grad[None], g_qkv, g_out, g_up, g_down, g_bias[0],
        g_gains, g_shifts, g_lead,
    )


def plane_fits(mesh):
    return mesh.shape["band"] == PLANE and mesh.shape["samp"] == DEPTH


def solution(mesh):
    return jax.shard_map(
        plane_body if plane_fits(mesh) else body,
        mesh=mesh,
        in_specs=(
            P("samp", "band", None),
            P("samp", "band", None),
            P(("band", "samp"), None),
            P(("band", "samp"), None),
            P(("band", "samp"), None),
            P(("band", "samp"), None),
            P(("band", "samp")),
            P(None, ("band", "samp")),
            P(None, ("band", "samp")),
            P(None, ("band", "samp")),
            P("samp"),
            P("samp", "band"),
        ),
        out_specs=(
            P("samp", "band", None),
            P("samp", "band", None),
            P(("band", "samp"), None),
            P(("band", "samp"), None),
            P(("band", "samp"), None),
            P(("band", "samp"), None),
            P(("band", "samp")),
            P(None, ("band", "samp")),
            P(None, ("band", "samp")),
            P(None, ("band", "samp")),
        ),
        check_vma=False,
    )
```

```python
import jax
import jax.numpy as jnp
from jax import lax
from jax.experimental import pallas as pl
from jax.experimental.pallas import tpu as pltpu
from jax.sharding import PartitionSpec as P

HEADS = 16


eps = 1e-05
masked = 10000.0


def layer_norm(values, gain_row, shift_row):
    centered = values - jnp.mean(values, axis=-1, keepdims=True)
    variance = jnp.mean(centered * centered, axis=-1, keepdims=True)
    return centered * lax.rsqrt(variance + eps) * gain_row + shift_row


def gelu_exact(values):
    return jax.nn.gelu(values, approximate=False)


def body(
    tokens,
    cotangent,
    w_qkv,
    w_out,
    w_up,
    w_down,
    up_bias,
    norm_gains,
    shift_rows,
    lead_weight,
    lead_steps,
    valid_cells,
):
    whole = (
        lax.all_gather(w_qkv, ("band", "samp"), axis=0, tiled=True),
        lax.all_gather(w_out, ("band", "samp"), axis=0, tiled=True),
        lax.all_gather(w_up, ("band", "samp"), axis=0, tiled=True),
        lax.all_gather(w_down, ("band", "samp"), axis=0, tiled=True),
        lax.all_gather(up_bias, ("band", "samp"), axis=0, tiled=True),
        lax.all_gather(norm_gains, ("band", "samp"), axis=1, tiled=True),
        lax.all_gather(shift_rows, ("band", "samp"), axis=1, tiled=True),
        lax.all_gather(lead_weight, ("band", "samp"), axis=1, tiled=True),
    )
    qkv_full = whole[0]
    out_full = whole[1]
    up_full = whole[2]
    down_full = whole[3]
    up_shift = whole[4].astype(jnp.float32)
    gain_all = whole[5].astype(jnp.float32)
    shift_all = whole[6].astype(jnp.float32)
    lead_all = whole[7].astype(jnp.float32)
    row_count = tokens.shape[1]
    width = tokens.shape[2]
    head_count = HEADS
    head_size = width // head_count
    score_scale = head_size ** (-0.5)
    lead_days = lead_steps[0].astype(jnp.float32) * 0.25
    entering = tokens[0].astype(jnp.float32) + lead_days * lead_all[0] + lead_all[1]
    normed, norm_first_back = jax.vjp(layer_norm, entering, gain_all[0], shift_all[0])
    normed_low = normed.astype(jnp.bfloat16)
    project = jnp.dot(normed_low, qkv_full, preferred_element_type=jnp.float32)
    queries = (project[:, :width] + shift_all[1]).astype(jnp.bfloat16)
    key_rows = project[:, width : 2 * width].astype(jnp.bfloat16)
    value_rows = (project[:, 2 * width :] + shift_all[2]).astype(jnp.bfloat16)
    key_open = (valid_cells[0] > 0).astype(jnp.bfloat16)
    keys_all, values_all, open_all = (
        lax.all_gather(key_rows, "band", axis=0, tiled=True),
        lax.all_gather(value_rows, "band", axis=0, tiled=True),
        lax.all_gather(key_open, "band", axis=0, tiled=True),
    )
    seq_total = keys_all.shape[0]
    block_rows = min(512, seq_total)
    block_count = seq_total // block_rows
    block_ids = jnp.arange(block_count)
    bias_all = (open_all.astype(jnp.float32) - 1.0) * masked
    query_heads = queries.reshape(row_count, head_count, head_size)

    def block_keys(step_index):
        first_row = step_index * block_rows
        key_block = lax.dynamic_slice_in_dim(keys_all, first_row, block_rows, 0).reshape(
            block_rows, head_count, head_size
        )
        value_block = lax.dynamic_slice_in_dim(values_all, first_row, block_rows, 0).reshape(
            block_rows, head_count, head_size
        )
        bias_block = lax.dynamic_slice_in_dim(bias_all, first_row, block_rows, 0)
        scores = (
            jnp.einsum("qhe,khe->hqk", query_heads, key_block, preferred_element_type=jnp.float32)
            * score_scale
            + bias_block
        )
        return (scores, key_block, value_block)

    def max_step(running, step_index):
        row_max, exp_total = running
        scores = block_keys(step_index)[0]
        new_max = jnp.maximum(row_max, jnp.max(scores, axis=-1))
        exp_total = exp_total * jnp.exp(row_max - new_max) + jnp.sum(
            jnp.exp(scores - new_max[..., None]), axis=-1
        )
        return ((new_max, exp_total), None)

    start_max = jnp.full((head_count, row_count), -jnp.inf, jnp.float32)
    start_total = jnp.zeros((head_count, row_count), jnp.float32)
    row_max, exp_total = lax.scan(max_step, (start_max, start_total), block_ids)[0]
    log_total = row_max + jnp.log(exp_total)

    def out_step(running, step_index):
        scores, key_block, value_block = block_keys(step_index)
        weights_low = jnp.exp(scores - log_total[..., None]).astype(jnp.bfloat16)
        return (
            running
            + jnp.einsum(
                "hqk,khe->qhe", weights_low, value_block, preferred_element_type=jnp.float32
            ),
            None,
        )

    attended_heads = lax.scan(
        out_step, jnp.zeros((row_count, head_count, head_size), jnp.float32), block_ids
    )[0]
    attended_low = attended_heads.reshape(row_count, width).astype(jnp.bfloat16)
    middle = (
        entering
        + jnp.dot(attended_low, out_full, preferred_element_type=jnp.float32)
        + shift_all[3]
    )
    second, norm_second_back = jax.vjp(layer_norm, middle, gain_all[1], shift_all[4])
    second_low = second.astype(jnp.bfloat16)
    hidden_pre = jnp.dot(second_low, up_full, preferred_element_type=jnp.float32) + up_shift
    hidden, gelu_back = jax.vjp(gelu_exact, hidden_pre)
    hidden_low = hidden.astype(jnp.bfloat16)
    result = (
        middle + jnp.dot(hidden_low, down_full, preferred_element_type=jnp.float32) + shift_all[5]
    )
    output = result.astype(jnp.bfloat16)
    grad_result = cotangent[0]
    grad_result_f = grad_result.astype(jnp.float32)
    grad_down_w = jnp.einsum(
        "tf,td->fd", hidden_low, grad_result, preferred_element_type=jnp.float32
    )
    grad_shift_down = jnp.sum(grad_result_f, axis=0)
    grad_hidden = jnp.einsum(
        "td,fd->tf", grad_result, down_full, preferred_element_type=jnp.float32
    )
    grad_pre_low = gelu_back(grad_hidden)[0].astype(jnp.bfloat16)
    grad_up_w = jnp.einsum(
        "td,tf->df", second_low, grad_pre_low, preferred_element_type=jnp.float32
    )
    grad_up_shift = jnp.sum(grad_pre_low.astype(jnp.float32), axis=0)
    grad_second = jnp.einsum("tf,df->td", grad_pre_low, up_full, preferred_element_type=jnp.float32)
    grad_middle_norm, grad_gain_second, grad_shift_second = norm_second_back(grad_second)
    grad_middle = grad_result_f + grad_middle_norm
    ffn_sums = (
        lax.psum_scatter(grad_up_w, ("band", "samp"), scatter_dimension=0, tiled=True),
        lax.psum_scatter(grad_down_w, ("band", "samp"), scatter_dimension=0, tiled=True),
        lax.psum_scatter(grad_up_shift, ("band", "samp"), scatter_dimension=0, tiled=True),
    )
    grad_branch = grad_middle.astype(jnp.bfloat16)
    grad_shift_out = jnp.sum(grad_branch.astype(jnp.float32), axis=0)
    grad_out_w = jnp.einsum(
        "td,te->de", attended_low, grad_branch, preferred_element_type=jnp.float32
    )
    grad_attended = jnp.einsum(
        "te,de->td", grad_branch, out_full, preferred_element_type=jnp.float32
    ).astype(jnp.bfloat16)
    grad_heads = grad_attended.reshape(row_count, head_count, head_size)
    delta = jnp.einsum("qhe,qhe->hq", grad_heads.astype(jnp.float32), attended_heads)
    zero_heads = jnp.zeros((row_count, head_count, head_size), jnp.float32)

    def key_grad_step(g_queries, step_index):
        scores, key_block, value_block = block_keys(step_index)
        weights_full = jnp.exp(scores - log_total[..., None])
        g_weights = jnp.einsum(
            "qhe,khe->hqk", grad_heads, value_block, preferred_element_type=jnp.float32
        )
        g_scores = (weights_full * (g_weights - delta[..., None])).astype(jnp.bfloat16)
        g_queries = (
            g_queries
            + jnp.einsum("hqk,khe->qhe", g_scores, key_block, preferred_element_type=jnp.float32)
            * score_scale
        )
        key_term = (
            jnp.einsum("hqk,qhe->khe", g_scores, query_heads, preferred_element_type=jnp.float32)
            * score_scale
        )
        value_term = jnp.einsum(
            "hqk,qhe->khe",
            weights_full.astype(jnp.bfloat16),
            grad_heads,
            preferred_element_type=jnp.float32,
        )
        return (
            g_queries,
            (key_term.reshape(block_rows, width), value_term.reshape(block_rows, width)),
        )

    grad_query_heads, block_terms = lax.scan(key_grad_step, zero_heads, block_ids)
    grad_query_f = grad_query_heads.reshape(row_count, width)
    key_sum, value_sum = (
        lax.psum_scatter(
            block_terms[0].reshape(seq_total, width), "band", scatter_dimension=0, tiled=True
        ),
        lax.psum_scatter(
            block_terms[1].reshape(seq_total, width), "band", scatter_dimension=0, tiled=True
        ),
    )
    grad_query_low = grad_query_f.astype(jnp.bfloat16)
    grad_key_low = key_sum.astype(jnp.bfloat16)
    grad_value_low = value_sum.astype(jnp.bfloat16)
    grad_project = jnp.concatenate([grad_query_low, grad_key_low, grad_value_low], axis=-1)
    grad_qkv_w = jnp.einsum(
        "td,te->de", normed_low, grad_project, preferred_element_type=jnp.float32
    )
    grad_shift_query = jnp.sum(grad_query_low.astype(jnp.float32), axis=0)
    grad_shift_value = jnp.sum(grad_value_low.astype(jnp.float32), axis=0)
    grad_normed = jnp.einsum(
        "te,de->td", grad_project, qkv_full, preferred_element_type=jnp.float32
    )
    grad_entering_norm, grad_gain_first, grad_shift_first = norm_first_back(grad_normed)
    grad_entering = grad_middle + grad_entering_norm
    input_grad = grad_entering.astype(jnp.bfloat16)
    entering_sum = jnp.sum(grad_entering, axis=0)
    grad_lead_rows = jnp.stack([lead_days * entering_sum, entering_sum])
    grad_gain_rows = jnp.stack([grad_gain_first, grad_gain_second])
    grad_shift_stack = jnp.stack(
        [
            grad_shift_first,
            grad_shift_query,
            grad_shift_value,
            grad_shift_out,
            grad_shift_second,
            grad_shift_down,
        ]
    )
    attention_sums = (
        lax.psum_scatter(grad_qkv_w, ("band", "samp"), scatter_dimension=0, tiled=True),
        lax.psum_scatter(grad_out_w, ("band", "samp"), scatter_dimension=0, tiled=True),
        lax.psum_scatter(grad_gain_rows, ("band", "samp"), scatter_dimension=1, tiled=True),
        lax.psum_scatter(grad_shift_stack, ("band", "samp"), scatter_dimension=1, tiled=True),
        lax.psum_scatter(grad_lead_rows, ("band", "samp"), scatter_dimension=1, tiled=True),
    )
    return (
        output[None],
        input_grad[None],
        attention_sums[0],
        attention_sums[1],
        ffn_sums[0],
        ffn_sums[1],
        ffn_sums[2],
        attention_sums[2],
        attention_sums[3],
        attention_sums[4],
    )


MESH = pl.DeviceIdType.MESH
F32 = jnp.float32
BF16 = jnp.bfloat16
PLANE = 8
DEPTH = 4
ROWS = 128
HALF = 64
BLOCK = 256
NN = (((1,), (0,)), ((), ()))
NT = (((1,), (1,)), ((), ()))
TN = (((0,), (0,)), ((), ()))
INNER = 32


def mm(left, right, dims=NN):
    return lax.dot_general(left, right, dims, preferred_element_type=F32)


def plane_kernel(
    lead_ref, gain_in, shift_in, leadw_in, bias_in, valid_in,
    tok_in, cot_in, wqkv_in, wout_in, wup_in, wdown_in,
    out_h, ig_h, gqkv_h, gout_h, gup_h, gdown_h, gain_h, shift_h, lead_h, bias_h,
    out_o, ig_o, gqkv_o, gout_o, gup_o, gdown_o, gain_o, shift_o, lead_o, bias_o,
    wqkv, wup, vcol, vec_in,
    agf, wq, wo, wu, wd, sq, su, ztr, vt, vecf, vrow,
    normed, qaug, kaug, kt, vv, vt2, pst, ot, invl, att, aown, dsend, dob, gproj, dk, dv,
    hid, gder, gpre, mid, gmid, gdf,
    part, pr, cs, au, rr,
    gds, gus, gqs, gos, gdr, gur, gqr, gor_, gda, guc, gqc, goc, gu2, gq2, gua, gqa, goa,
    acc, gub, vs, vsr, vz, vzr,
    in_s, out_s, ag_s, ag_r, ac_r, fw_s, fw_r, aq_s, aq_r, v_s, v_r, y_s, y_r, w_s, w_r, z_s, z_r,
    p_s, p_r, f_r, n_s, n_r, wg_s, wg_r, h_s, h_r, g_s, g_r,
):
    b = lax.axis_index("band")
    s = lax.axis_index("samp")
    c = b % 2
    x = (b // 2) % 2
    y = b // 4
    mate = b + 1 - 2 * c

    def chip(r):
        xx = x + (r % 2) * (1 - 2 * x)
        yy = y + (r // 2) * (1 - 2 * y)
        return yy * 2 + xx

    def near(r):
        return chip(r) * 2 + c

    def peer(k):
        return (b + k) % PLANE

    def level(k):
        return (s + k) % DEPTH

    barrier = pltpu.get_barrier_semaphore()
    for k in range(1, PLANE):
        pl.semaphore_signal(barrier, inc=1, device_id=(peer(k), s), device_id_type=MESH)
    for k in range(1, DEPTH):
        pl.semaphore_signal(barrier, inc=1, device_id=(b, level(k)), device_id_type=MESH)

    width = tok_in.shape[1]
    fetches = [
        pltpu.make_async_copy(src, dst, in_s.at[n])
        for n, (src, dst) in enumerate((
            (wqkv_in, wqkv), (wout_in, wo.at[b, pl.ds(pl.multiple_of(s * 32, 32), 32)]),
            (tok_in.at[pl.ds(0, HALF)], agf.at[0, 0, 0, c]),
            (tok_in.at[pl.ds(HALF, HALF)], agf.at[0, 0, 1, c]),
            (wup_in, wup), (wdown_in, wd.at[s]),
            (cot_in.at[pl.ds(0, HALF)], agf.at[1, 0, 0, c]),
            (cot_in.at[pl.ds(HALF, HALF)], agf.at[1, 0, 1, c]),
        ))
    ]
    for fetch in fetches:
        fetch.start()
    vcol[...] = jnp.zeros_like(vcol)
    vcol[0:2, 0:32] = gain_in[...].astype(F32)
    vcol[2:8, 0:32] = shift_in[...].astype(F32)
    vcol[8:10, 0:32] = leadw_in[...].astype(F32)
    line = lax.broadcasted_iota(jnp.int32, (16, 128), 0)
    tile = pltpu.roll(vcol[...], s * 32, 1)
    tile = jnp.where(line == 11 + s, bias_in[...].astype(F32), tile)
    vec_in[0] = tile.astype(BF16)
    opened = jnp.where(valid_in[...] > 0, 1.0, 0.0)
    vec_in[1] = jnp.where(line == 10, opened, 0.0).astype(BF16)
    far = (s + 2) % DEPTH
    ends = (s == 0) | (s == DEPTH - 1)
    inner = (s > 0) & (s < DEPTH - 1)

    @pl.when(s == 0)
    def _():
        for kept in (gdr, gur, gqr, gor_):
            kept[0] = jnp.zeros(kept.shape[1:], BF16)

    @pl.when(s == DEPTH - 1)
    def _():
        for kept in (gda, guc, gqc, goc):
            kept[...] = jnp.zeros(kept.shape, BF16)

    fetches[0].wait()
    for d in range(PLANE):
        for j in range(3):
            sq[d, :, j * 128:(j + 1) * 128] = wqkv[:, j * width + d * 128:j * width + (d + 1) * 128]
    fetches[1].wait()
    pl.semaphore_wait(barrier, PLANE - 1 + DEPTH - 1)

    def rc(src, dst, ss, rs, band, samp):
        return pltpu.make_async_remote_copy(
            src_ref=src, dst_ref=dst, send_sem=ss, recv_sem=rs,
            device_id=(band, samp), device_id_type=MESH,
        )

    def landed(ref, sem):
        rc(ref, ref, aq_s.at[0], sem, mate, s).wait_recv()

    def left(ref, sem):
        rc(ref, ref, sem, aq_r.at[0], mate, s).wait_send()

    def yc(kind, k, src, dst):
        return rc(src, dst, y_s.at[kind], y_r.at[kind], b, level(k))

    def weight_copy(kind, region, pieces, role, to):
        return rc(region(s), region(s), w_s.at[kind], w_r.at[kind, role], b, to)

    def weight_hand(kind, region, pieces):
        return rc(region(far), region(far), w_s.at[kind], w_r.at[kind, 1], b, 3 * (s - 1))

    def weight_start(*moved):
        @pl.when(s == 1)
        def _():
            weight_copy(*moved, 1, s - 1).start()

        weight_copy(*moved, 0, far).start()

        @pl.when(s < DEPTH - 1)
        def _():
            weight_copy(*moved, 1, s + 1).start()

        @pl.when(s > 1)
        def _():
            weight_copy(*moved, 1, s - 1).start()

    def weight_pass(kind, region, pieces):
        @pl.when(inner)
        def _():
            landed(region(far), w_r.at[kind, 0])
            weight_hand(kind, region, pieces).start()

    def weight_finish(kind, region, pieces):
        landed(pieces(2), w_r.at[kind, 1])

        @pl.when(ends)
        def _():
            landed(region(far), w_r.at[kind, 0])

    def weight_sent(kind, region, pieces):
        @pl.when(ends)
        def _():
            left(pieces(2), w_s.at[kind])

        @pl.when(inner)
        def _():
            left(pieces(4), w_s.at[kind])

    def grad_up(kind, stage, got, via, pieces, t):
        return rc(stage(t), got(t), z_s.at[kind], z_r.at[kind, t], b, s + 1)

    def grad_down_to(kind, stage, got, via, pieces, t):
        return rc(stage(t), got(t), z_s.at[kind], z_r.at[kind, t], b, s - 1)

    def grad_down_last(kind, stage, got, via, pieces):
        return rc(stage(s - 1), via, z_s.at[kind], z_r.at[kind, DEPTH], b, s - 1)

    def grad_start(*moved):
        for hops in (3, 2, 1):
            grad_start_some(*moved, hops)

    def grad_start_some(kind, stage, got, via, pieces, hops):
        @pl.when(s == 0)
        def _():
            grad_up(kind, stage, got, via, pieces, hops).start()

        @pl.when(s == DEPTH - 1)
        def _():
            if hops == 1:
                grad_down_last(kind, stage, got, via, pieces).start()
            else:
                grad_down_to(kind, stage, got, via, pieces, DEPTH - 1 - hops).start()

    def down_half(half):
        rows = pl.ds(half * HALF, HALF)

        @pl.when(s == 0)
        def _():
            rc(gds.at[1, rows], gdr.at[1, rows], z_s.at[0], z_r.at[0, 1], b, 1).start()

        @pl.when(s == DEPTH - 1)
        def _():
            rc(gds.at[2, rows], gda.at[rows], z_s.at[0], z_r.at[0, DEPTH], b, DEPTH - 2).start()

    def add_in(kind, stage, got, via, pieces, t):
        landed(got(t), z_r.at[kind, t])
        term, more = stage(t), got(t)
        if len(via.shape) == 3:
            def add(j, _):
                term[j] = (term[j].astype(F32) + more[j].astype(F32)).astype(BF16)
                return 0

            lax.fori_loop(0, via.shape[0], add, 0)
        else:
            def add_rows(j, _):
                rows = pl.ds(pl.multiple_of(j * INNER, INNER), INNER)
                term[rows, :] = (term[rows, :].astype(F32) + more[rows, :].astype(F32)).astype(BF16)
                return 0

            lax.fori_loop(0, via.shape[0] // INNER, add_rows, 0)

    def grad_pass(*moved):
        @pl.when(s == 1)
        def _():
            add_in(*moved, 3)
            grad_up(*moved, 3).start()

        @pl.when(s == 2)
        def _():
            add_in(*moved, 0)
            grad_down_to(*moved, 0).start()

    def grad_pass_on(*moved):
        @pl.when(s == 1)
        def _():
            add_in(*moved, 2)
            grad_up(*moved, 2).start()
            add_in(*moved, 0)
            grad_down_last(*moved).start()

        @pl.when(s == 2)
        def _():
            add_in(*moved, 1)
            grad_down_last(*moved).start()
            add_in(*moved, 3)
            grad_up(*moved, 3).start()

    def grad_finish(kind, stage, got, via, pieces):
        @pl.when(s > 0)
        def _():
            landed(got(s), z_r.at[kind, s])

        @pl.when(s < DEPTH - 1)
        def _():
            landed(via, z_r.at[kind, DEPTH])

    def grad_sent(kind, stage, got, via, pieces):
        left(pieces(3), z_s.at[kind])

    results = ((out_o, out_h), (ig_o, ig_h), (gqkv_o, gqkv_h), (gout_o, gout_h), (gup_o, gup_h), (gdown_o, gdown_h),
               (gain_o, gain_h), (shift_o, shift_h), (lead_o, lead_h), (bias_o, bias_h))

    def deliver(n):
        return pltpu.make_async_copy(results[n][0], results[n][1], out_s.at[n])

    w_out_z = (
        0, lambda t: wo.at[b, pl.ds(pl.multiple_of(t * 32, 32), 32)],
        lambda n: wo.at[b, pl.ds(0, n * 32)],
    )
    w_qkv_z = (1, lambda t: wq.at[:, t], lambda n: wq.at[:, pl.ds(0, n)])
    w_up_z = (2, lambda t: wu.at[:, t], lambda n: wu.at[:, pl.ds(0, n)])
    w_down_z = (3, lambda t: wd.at[t], lambda n: wd.at[pl.ds(0, n)])
    g_down_z = (0, lambda t: gds.at[t], lambda t: gdr.at[t], gda, lambda n: gds.at[pl.ds(0, n)])
    g_up_z = (1, lambda t: gus.at[:, t], lambda t: gur.at[t], guc, lambda n: gus.at[:, pl.ds(0, n)])
    g_qkv_z = (2, lambda t: gqs.at[:, t], lambda t: gqr.at[t], gqc, lambda n: gqs.at[:, pl.ds(0, n)])
    g_out_z = (3, lambda t: gos.at[t], lambda t: gor_.at[t], goc, lambda n: gos.at[pl.ds(0, n)])

    def gather(op, r, turn):
        return rc(
            agf.at[op, 0, (turn + r) % 2, c], agf.at[op, 1 + turn, r - 1, c],
            ag_s.at[op], ag_r.at[op, turn], near(r), s,
        )

    def across(op, r):
        return rc(
            agf.at[op, 1, r - 1, c], agf.at[op, 3, r % 2, c],
            ag_s.at[op], ac_r.at[op], near(3 - r), s,
        )

    def share(op, blk):
        return rc(
            agf.at[op, blk, :, c], agf.at[op, blk, :, c],
            fw_s.at[op], fw_r.at[op, blk], mate, s,
        )

    def start_gather(op):
        for turn in (0, 1):
            for r in (1, 2):
                gather(op, r, turn).start()
        share(op, 0).start()

    def arrive(op, blk):
        if blk in (1, 2):
            landed(agf.at[op, blk, :, c], ag_r.at[op, blk - 1])
        if blk == 1:
            for r in (1, 2):
                across(op, r).start()
        if blk == 3:
            landed(agf.at[op, 3, :, c], ac_r.at[op])
        if blk:
            share(op, blk).start()

    def block(op, i):
        return agf[op, i].reshape(BLOCK, -1)

    def rows_half(dev, h):
        return wo.at[dev, pl.ds(h * HALF, HALF)]

    def rows_copy(r, turn):
        part_ = rows_half(b, (turn + r) % 2)
        return rc(part_, part_, wg_s.at[0], wg_r.at[turn], near(r), s)

    def rows_across(r):
        part_ = rows_half(near(r), r % 2)
        return rc(part_, part_, wg_s.at[0], wg_r.at[2], near(3 - r), s)

    def rows_share(r):
        dev = near(r) if r else b
        return rc(wo.at[dev], wo.at[dev], wg_s.at[1], wg_r.at[3], mate, s)

    def rows_start():
        for turn in (0, 1):
            for r in (1, 2):
                rows_copy(r, turn).start()
        rows_share(0).start()

    def granule(i, a):
        return (i, a) if i in (0, 3) else (a + 1, 1 - a if i == 1 else a)

    GRANULES = [(i, a) for i in (1, 0, 2, 3) for a in (0, 1)]

    def heads_copy(i, a, k):
        r, h = granule(i, a)
        rows = pl.ds(pl.multiple_of((a * 2 + k) * HALF, HALF), HALF)
        return rc(
            att.at[i, rows], aown.at[b, pl.ds(h * HALF, HALF)],
            h_s.at[0], h_r.at[0], chip(r) * 2 + k, s,
        )

    def cores(i):
        return (1 - c,) if i == 0 else (0, 1)

    def back_copy(i, a, k):
        r, h = granule(i, a)
        dev = chip(r) * 2 + k
        return rc(
            dsend.at[dev, pl.ds(h * HALF, HALF)], dob.at[i, a, c],
            g_s.at[0], g_r.at[i], dev, s,
        )

    def swap(kind, k, src, dst):
        return rc(src, dst, aq_s.at[kind], aq_r.at[kind], peer(k), s)

    for k in range(1, DEPTH):
        yc(0, k, vec_in.at[0], ztr.at[k - 1]).start()
    for k in range(1, PLANE):
        swap(0, k, sq.at[peer(k)], wq.at[b, s]).start()
    weight_start(*w_out_z)
    fetches[2].wait()
    fetches[3].wait()
    for r in (1, 2):
        gather(0, r, 0).start()
    wq[b, s] = sq[b]
    fetches[4].wait()
    for d in range(PLANE):
        su[d] = wup[:, d * 512:(d + 1) * 512]
    wu[b, s] = su[b]

    landed(ztr, y_r.at[0])
    vt[...] = (
        vec_in[0].astype(F32) + vec_in[1].astype(F32)
        + ztr[0].astype(F32) + ztr[1].astype(F32) + ztr[2].astype(F32)
    ).astype(BF16)

    def spread(k):
        return rc(vt, vecf.at[b], v_s.at[0], v_r.at[0], peer(k), s)

    for k in range(1, PLANE):
        spread(k).start()
    for r in (1, 2):
        gather(0, r, 1).start()
    share(0, 0).start()
    vecf[b] = vt[...]
    landed(sq.at[pl.ds(0, 7)], aq_r.at[0])
    weight_start(*w_qkv_z)
    for k in range(1, PLANE):
        swap(1, k, su.at[peer(k)], wu.at[b, s]).start()
    arrive(0, 1)
    fetches[6].wait()
    fetches[7].wait()
    for r in (1, 2):
        gather(1, r, 0).start()
    share(1, 0).start()
    landed(vecf.at[pl.ds(0, 7)], v_r.at[0])
    for d in range(PLANE):
        vrow[:, d * 128:(d + 1) * 128] = vecf[d].astype(F32)
    lead_days = lead_ref[0].astype(F32) * 0.25
    lane = lax.broadcasted_iota(jnp.int32, (1, 128), 1)
    head_lane = [(lane < 64).astype(F32), (lane >= 64).astype(F32)]
    ones_lane = jnp.where(lane < 2, 1.0, 0.0).astype(F32)
    ends_lane = jnp.where(lane == 0, 9984.0, jnp.where(lane == 1, 16.0, 0.0)).astype(F32)
    gain1, gain2 = vrow[0:1, :], vrow[1:2, :]
    shift1, shift_out, shift2, shift_down = vrow[2:3, :], vrow[5:6, :], vrow[6:7, :], vrow[7:8, :]
    lead_row = lead_days * vrow[8:9, :] + vrow[9:10, :]
    mine = vecf[b].astype(F32)

    def stats(v):
        mean = jnp.mean(v, axis=-1, keepdims=True)
        centered = v - mean
        variance = jnp.mean(centered * centered, axis=-1, keepdims=True)
        rstd = lax.rsqrt(variance + eps)
        return centered * rstd, rstd

    for r in range(4):
        for k in range(2):
            row = jnp.broadcast_to(vecf[chip(r) * 2 + k].astype(F32)[10:11, :], (128, 128))
            column = ((row.T - 1.0) * ends_lane).astype(BF16)
            for h in range(2):
                if r in (0, 3):
                    blk, a = r, h
                else:
                    blk, a = (1 if h == r % 2 else 2), r - 1
                top = blk * BLOCK + (a * 2 + k) * HALF
                kaug[top:top + HALF, 128:256] = column[h * HALF:(h + 1) * HALF]
    for h in range(2):
        for i in range(4):
            qaug[i, h * BLOCK:(h + 1) * BLOCK, 128:256] = jnp.broadcast_to(ones_lane, (BLOCK, 128)).astype(BF16)

    def norm_block(i):
        def chunk(j, _):
            rows = pl.ds(pl.multiple_of((j % 2) * INNER, INNER), INNER)
            ent = agf[0, i, j // 4, (j // 2) % 2, rows, :].astype(F32) + lead_row
            xhat = stats(ent)[0]
            put = pl.ds(pl.multiple_of(j * INNER, INNER), INNER)
            normed[i, put, :] = (xhat * gain1 + shift1).astype(BF16)
            return 0

        lax.fori_loop(0, BLOCK // INNER, chunk, 0)

    share(0, 0).wait_recv()
    norm_block(0)
    share(0, 1).wait_recv()
    arrive(0, 2)
    norm_block(1)
    weight_pass(*w_out_z)
    weight_pass(*w_qkv_z)
    share(0, 2).wait_recv()
    norm_block(2)
    weight_finish(*w_out_z)
    rows_start()
    arrive(0, 3)
    share(0, 3).wait_recv()
    norm_block(3)

    landed(su.at[pl.ds(0, 7)], aq_r.at[1])
    weight_finish(*w_qkv_z)
    weight_start(*w_up_z)

    def project_block(q, _):
        rows = pl.ds(pl.multiple_of(q * BLOCK, BLOCK), BLOCK)
        pj = mm(normed[q], wq[...].reshape(width, 384))
        qv = (pj[:, 0:128] + mine[3:4, :]).astype(BF16).astype(F32) * 0.125
        for h in range(2):
            qaug[q, h * BLOCK:(h + 1) * BLOCK, 0:128] = (qv * head_lane[h]).astype(BF16)
        kv = pj[:, 128:256].astype(BF16)
        kaug[rows, 0:128] = kv
        kt[:, rows] = kv.T
        vb = (pj[:, 256:384] + mine[4:5, :]).astype(BF16)
        vv[rows, :] = vb
        vt2[:, rows] = vb.T
        return 0

    lax.fori_loop(0, 4, project_block, 0)

    def mate_copy(op, i):
        return rc(part.at[op, i, :, 1 - c], pr.at[op, i], p_s.at[op], p_r.at[op, i], mate, s)

    def far_copy(op, h):
        return rc(cs.at[op, 3, h], au.at[op, 1 - h], n_s.at[op], f_r.at[op], near(h + 1), s)

    def near_copy(op, i, a):
        h = a if i == 2 else 1 - a
        return rc(cs.at[op, i, a], rr.at[op, a, h], n_s.at[op], n_r.at[op], near(a + 1), s)

    def put_part(op, i, blk):
        part[op, i] = blk.astype(BF16).reshape(2, 2, HALF, width)
        mate_copy(op, i).start()

    def fold(op, i):
        mate_copy(op, i).wait_recv()

        def chunk(j, _):
            a = j // 2
            rows = pl.ds(pl.multiple_of((j % 2) * INNER, INNER), INNER)
            cs[op, i, a, rows, :] = (
                part[op, i, a, c, rows, :].astype(F32) + pr[op, i, a, rows, :].astype(F32)
            ).astype(BF16)
            return 0

        lax.fori_loop(0, ROWS // INNER, chunk, 0)

    def fold_before(op, i, near_too=True):
        @pl.when(i < 3)
        def _():
            fold(op, i + 1)

        @pl.when(i == 2)
        def _():
            send_far(op)

        if near_too:
            @pl.when(i == 1)
            def _():
                send_near(op, 2)

    def send_far(op):
        for h in (0, 1):
            far_copy(op, h).start()

    def send_near(op, i):
        for a in (0, 1):
            near_copy(op, i, a).start()

    def send_last(op):
        landed(au.at[op], f_r.at[op])
        for a in (0, 1):
            def chunk(j, _):
                rows = pl.ds(pl.multiple_of(j * INNER, INNER), INNER)
                cs[op, 1, a, rows, :] = (
                    cs[op, 1, a, rows, :].astype(F32) + au[op, a, rows, :].astype(F32)
                ).astype(BF16)
                return 0

            lax.fori_loop(0, HALF // INNER, chunk, 0)
            near_copy(op, 1, a).start()

    def wait_sums(op):
        landed(rr.at[op], n_r.at[op])

    def place(j):
        return j // 2, pl.ds(pl.multiple_of((j % 2) * INNER, INNER), INNER)

    def plane_total(op, j):
        h, rows = place(j)
        total = cs[op, 0, h, rows, :].astype(F32)
        return total + rr[op, 0, h, rows, :].astype(F32) + rr[op, 1, h, rows, :].astype(F32)

    def own_rows(op, j):
        h, rows = place(j)
        return agf[op, 0, h, c, rows, :].astype(F32)

    def set_rows(op, j, v):
        h, rows = place(j)
        agf[op, 0, h, c, rows, :] = v

    def end_sums(op):
        left(part.at[op, :, :, 0], p_s.at[op])
        left(cs.at[op, pl.ds(0, 3)], n_s.at[op])

    def attend_block(n, _):
        i = 3 - n

        @pl.when(n == 3)
        def _():
            landed(wo.at[0], wg_r.at[1])
            for r in (1, 2):
                rows_share(r).start()

        st = mm(kaug[...], qaug[i], NT)
        p = jnp.exp(st - jnp.max(st, axis=0, keepdims=True))
        inverse = 1.0 / jnp.sum(p, axis=0, keepdims=True)
        pb = p.astype(BF16)
        pst[i] = pb
        out = mm(vt2[...], pb) * inverse
        ot[i, 0:64, :] = out[0:64, 0:BLOCK]
        ot[i, 64:128, :] = out[64:128, BLOCK:]
        invl[i] = jnp.broadcast_to(inverse, (8, 2 * BLOCK))
        att[i] = ot[i].T.astype(BF16)
        for blk in range(4):
            @pl.when(i == blk)
            def _():
                for a in (0, 1):
                    for k in cores(blk):
                        heads_copy(blk, a, k).start()

        return 0

    landed(wo.at[0], wg_r.at[0])
    for r in (1, 2):
        rows_across(r).start()
    lax.fori_loop(0, 4, attend_block, 0)
    landed(wo.at[0], wg_r.at[2])
    rows_share(3).start()
    arrive(1, 1)
    for r in (1, 2):
        gather(1, r, 1).start()
    for h in (0, 1):
        top = pl.multiple_of((h * 2 + c) * HALF, HALF)
        aown[b, h * HALF:(h + 1) * HALF] = att[0, pl.ds(top, HALF), :]
    weight_pass(*w_up_z)
    fetches[5].wait()

    @pl.when(inner)
    def _():
        weight_start(*w_down_z)

    landed(wo.at[pl.ds(0, 4)], wg_r.at[3])
    landed(aown.at[pl.ds(0, 7)], h_r.at[0])
    heads = jnp.concatenate([aown[d] for d in range(PLANE)], axis=1)
    mid[...] = mm(heads, wo[...].reshape(1024, width))

    def middle_chunk(j, _):
        rows = pl.ds(pl.multiple_of(j * INNER, INNER), INNER)
        m = own_rows(0, j) + lead_row + mid[rows, :] + shift_out
        mid[rows, :] = m
        set_rows(2, j, (stats(m)[0] * gain2 + shift2).astype(BF16))
        return 0

    lax.fori_loop(0, ROWS // INNER, middle_chunk, 0)
    start_gather(2)
    arrive(1, 2)
    arrive(1, 3)

    weight_finish(*w_up_z)

    @pl.when(ends)
    def _():
        weight_start(*w_down_z)

    bias = jnp.concatenate([mine[11 + j:12 + j, :] for j in range(4)], axis=1)

    def arrivals(op, i):
        for blk in range(4):
            @pl.when(i == blk)
            def _():
                arrive(op, blk)
                share(op, blk).wait_recv()

    def down_grad_first(f, _):
        cols = pl.ds(pl.multiple_of(f * BLOCK, BLOCK), BLOCK)
        gdf[pl.ds(pl.multiple_of(f * BLOCK, BLOCK), BLOCK), :] = mm(
            hid[:3 * BLOCK, cols], agf[1, 0:3].reshape(3 * BLOCK, width), TN
        )
        return 0

    def up_block(i, _):
        @pl.when(i == 3)
        def _():
            for blk in range(3):
                share(1, blk).wait_recv()
            lax.fori_loop(0, 2, down_grad_first, 0)

        arrivals(2, i)


        hp = mm(block(2, i), wu[...].reshape(width, 512)) + bias
        phi = 0.5 + 0.5 * lax.erf(hp * 0.7071067811865476)
        hid[pl.ds(pl.multiple_of(i * BLOCK, BLOCK), BLOCK), :] = (hp * phi).astype(BF16)
        gder[i] = phi + hp * jnp.exp(hp * hp * -0.5) * 0.3989422804014327
        return 0

    lax.fori_loop(0, 4, up_block, 0)
    weight_pass(*w_down_z)
    share(1, 3).wait_recv()

    def down_grad(f, _):
        cols = pl.ds(pl.multiple_of(f * BLOCK, BLOCK), BLOCK)
        g = gdf[pl.ds(pl.multiple_of(f * BLOCK, BLOCK), BLOCK), :] + mm(hid[3 * BLOCK:, cols], block(1, 3), TN)
        gds[pl.ds(2 * f, 2)] = g.astype(BF16).reshape(2, 128, width)
        return 0

    lax.fori_loop(0, 2, down_grad, 0)
    grad_start_some(*g_down_z, 3)
    grad_start_some(*g_down_z, 2)
    down_half(0)
    for i in range(4):
        for j in range(i + 1):
            upper = normed[j, :, i * BLOCK:(i + 1) * BLOCK].T
            if i != j:
                normed[j, :, i * BLOCK:(i + 1) * BLOCK] = normed[i, :, j * BLOCK:(j + 1) * BLOCK].T
            normed[i, :, j * BLOCK:(j + 1) * BLOCK] = upper
    weight_finish(*w_down_z)
    gub[...] = jnp.zeros_like(gub)

    def back_block(n, _):
        i = 3 - n
        rows = pl.ds(pl.multiple_of(i * BLOCK, BLOCK), BLOCK)
        gh = mm(block(1, i), wd[...].reshape(512, width), NT)
        gp = (gder[i] * gh).astype(BF16)
        gpre[rows, :] = gp
        gub[...] += jnp.sum(gp.astype(F32).reshape(BLOCK // 8, 8, 512), axis=0)
        put_part(0, i, mm(gp, wu[...].reshape(width, 512), NT))
        fold_before(0, i)
        return 0

    lax.fori_loop(0, 4, back_block, 0)
    fold(0, 0)

    def up_grad(f, _):
        cols = pl.ds(pl.multiple_of(f * BLOCK, BLOCK), BLOCK)
        g = mm(agf[2, :, :, :, :, cols].reshape(1024, BLOCK), gpre[...], TN)
        gus[pl.ds(2 * f, 2)] = g.astype(BF16).reshape(2, 4, 32, 512)
        return 0

    grad_pass(*g_down_z)
    lax.fori_loop(0, 4, up_grad, 0)
    grad_start(*g_up_z)

    def out_block(n, _):
        i = 3 - n
        rows = pl.ds(pl.multiple_of(i * BLOCK, BLOCK), BLOCK)
        put_part(1, i, mm(hid[rows, :], wd[...].reshape(512, width)))
        fold_before(1, i, near_too=False)
        return 0

    send_last(0)
    lax.fori_loop(0, 4, out_block, 0)
    fold(1, 0)

    wait_sums(0)
    acc[...] = jnp.zeros_like(acc)

    def add_row(n, v):
        acc[n] += jnp.sum(v.reshape(INNER // 8, 8, width), axis=0)

    def norm_back(v, grad, gain):
        xhat, rstd = stats(v)
        d = grad * gain
        mean_d = jnp.mean(d, axis=-1, keepdims=True)
        mean_dx = jnp.mean(d * xhat, axis=-1, keepdims=True)
        return rstd * (d - mean_d - xhat * mean_dx), xhat

    def second_chunk(j, _):
        rows = pl.ds(pl.multiple_of(j * INNER, INNER), INNER)
        gs = plane_total(0, j)
        g, xhat = norm_back(mid[rows, :], gs, gain2)
        ct = own_rows(1, j)
        gm = ct + g
        gmid[rows, :] = gm
        gb = gm.astype(BF16)
        set_rows(3, j, gb)
        add_row(1, gs * xhat)
        add_row(6, gs)
        add_row(5, gb.astype(F32))
        add_row(7, ct)
        return 0

    grad_pass_on(*g_down_z)
    lax.fori_loop(0, ROWS // INNER, second_chunk, 0)
    gbo = agf[3, 0, :, c].reshape(ROWS, width)
    gha = mm(gbo, wo[...].reshape(1024, width), NT).astype(BF16)
    for d in range(PLANE):
        dsend[d] = gha[:, d * 128:(d + 1) * 128]
    for i, a in GRANULES:
        for k in cores(i):
            back_copy(i, a, k).start()
    for h in (0, 1):
        dob[0, h, c] = dsend[b, h * HALF:(h + 1) * HALF, :]
    start_gather(3)

    grad_pass(*g_up_z)
    dk[...] = jnp.zeros_like(dk)
    dv[...] = jnp.zeros_like(dv)
    goa[...] = jnp.zeros_like(goa)

    def attend_back(i, _):
        for blk in range(4):
            @pl.when(i == blk)
            def _():
                landed(dob.at[blk] if blk else dob.at[0, :, 0], g_r.at[blk])

        dot_t = dob[i].reshape(BLOCK, 128).astype(F32).T
        inv = jnp.concatenate(
            [jnp.broadcast_to(invl[i, 0:1, h * BLOCK:(h + 1) * BLOCK], (64, BLOCK)) for h in range(2)], axis=0
        )
        dos = dot_t * inv
        prod = dos * ot[i]
        deltas = [jnp.sum(prod[h * 64:(h + 1) * 64], axis=0, keepdims=True) for h in range(2)]
        do_rows = dos.T
        zero = jnp.zeros((64, BLOCK), F32)
        dq_parts = []
        for h in range(2):
            halves = [dos[0:64], zero] if h == 0 else [zero, dos[64:128]]
            dp = mm(vv[...], jnp.concatenate(halves, axis=0).astype(BF16))
            pb = pst[i, :, h * BLOCK:(h + 1) * BLOCK]
            ds = (pb.astype(F32) * (dp - deltas[h])).astype(BF16)
            dv[...] += mm(pb, (do_rows * head_lane[h]).astype(BF16))
            dk[...] += mm(ds, qaug[i, h * BLOCK:(h + 1) * BLOCK, 0:128])
            dq_parts.append(mm(kt[h * 64:(h + 1) * 64, :], ds))
        dq = jnp.concatenate(dq_parts, axis=0).T * 0.125
        gproj[pl.ds(pl.multiple_of(i * BLOCK, BLOCK), BLOCK), 0:128] = dq.astype(BF16)
        return 0

    lax.fori_loop(0, 4, attend_back, 0)
    send_near(1, 2)
    gproj[:, 128:256] = dk[...].astype(BF16)
    gproj[:, 256:384] = dv[...].astype(BF16)

    gqs[...] = mm(normed[...].reshape(1024, 1024), gproj[...]).astype(BF16).reshape(8, 4, 32, 384)
    grad_start_some(*g_qkv_z, 3)
    grad_start_some(*g_qkv_z, 2)
    grad_pass_on(*g_up_z)
    arrive(3, 1)

    def project_back(n, _):
        i = 3 - n
        rows = pl.ds(pl.multiple_of(i * BLOCK, BLOCK), BLOCK)
        put_part(2, i, mm(gproj[rows, :], wq[...].reshape(width, 384), NT))
        fold_before(2, i)
        return 0

    lax.fori_loop(0, 4, project_back, 0)
    fold(2, 0)
    arrive(3, 2)
    share(3, 0).wait_recv()
    arrive(3, 3)
    grad_pass(*g_qkv_z)
    def out_grad(i, _):
        for blk in (1, 2, 3):
            @pl.when(i == blk)
            def _():
                share(3, blk).wait_recv()

        goa[...] += mm(att[i], block(3, i), TN)
        return 0

    lax.fori_loop(0, 4, out_grad, 0)
    gos[...] = goa[...].astype(BF16).reshape(4, 32, width)
    grad_start_some(*g_out_z, 3)
    grad_start_some(*g_qkv_z, 1)
    grad_start_some(*g_out_z, 2)
    grad_start_some(*g_out_z, 1)
    down_half(1)
    send_last(2)
    send_last(1)

    def others(kind, stage, got, via, pieces):
        return [got(s), via]

    grad_pass(*g_out_z)
    grad_pass_on(*g_qkv_z)
    wait_sums(2)

    def first_chunk(j, _):
        rows = pl.ds(pl.multiple_of(j * INNER, INNER), INNER)
        gn = plane_total(2, j)
        g, xhat = norm_back(own_rows(0, j) + lead_row, gn, gain1)
        ge = gmid[rows, :] + g
        ig_o[rows, :] = ge.astype(BF16)
        add_row(0, gn * xhat)
        add_row(2, gn)
        add_row(9, ge)
        return 0

    lax.fori_loop(0, ROWS // INNER, first_chunk, 0)
    deliver(1).start()
    acc[8] = acc[9] * lead_days

    sums = [jnp.sum(acc[n], axis=0, keepdims=True) for n in range(10)]
    packed = jnp.concatenate(sums + [jnp.zeros((6, width), F32)], axis=0)
    for d in range(PLANE):
        vs[d] = packed[:, d * 128:(d + 1) * 128]

    def vec_swap(k):
        return rc(vs.at[peer(k)], vsr.at[k - 1], v_s.at[1], v_r.at[1], peer(k), s)

    for k in range(1, PLANE):
        vec_swap(k).start()
    gq_cols = jnp.sum(gproj[:, 0:128].astype(F32), axis=0, keepdims=True)
    gv_cols = jnp.sum(gproj[:, 256:384].astype(F32), axis=0, keepdims=True)
    gub_row = jnp.sum(gub[...], axis=0, keepdims=True)
    extra = jnp.concatenate(
        [jnp.zeros((3, 128), F32), gq_cols, gv_cols, jnp.zeros((6, 128), F32)]
        + [gub_row[:, j * 128:(j + 1) * 128] for j in range(4)]
        + [jnp.zeros((1, 128), F32)],
        axis=0,
    )
    grad_finish(*g_up_z)
    for d in range(PLANE):
        gu2[d] = sum(
            [t[d].astype(F32) for t in others(*g_up_z)], gus[d, s].astype(F32)
        ).astype(BF16)
    for k in range(1, PLANE):
        swap(2, k, gu2.at[peer(k)], gua.at[b]).start()
    gua[b] = gu2[b]
    grad_pass_on(*g_out_z)
    wait_sums(1)

    def output_chunk(j, _):
        rows = pl.ds(pl.multiple_of(j * INNER, INNER), INNER)
        out_o[rows, :] = (mid[rows, :] + plane_total(1, j) + shift_down).astype(BF16)
        return 0

    lax.fori_loop(0, ROWS // INNER, output_chunk, 0)
    deliver(0).start()

    landed(vs.at[pl.ds(0, 7)], v_r.at[1])
    total = vs[b] + extra
    for k in range(PLANE - 1):
        total = total + vsr[k]
    vz[...] = total
    for k in range(1, DEPTH):
        yc(1, k, vz, vzr.at[k - 1]).start()

    grad_finish(*g_qkv_z)
    for d in range(PLANE):
        gq2[d] = sum(
            [t[d].astype(F32) for t in others(*g_qkv_z)], gqs[d, s].astype(F32)
        ).astype(BF16)
    for k in range(1, PLANE):
        swap(3, k, gq2.at[peer(k)], gqa.at[b]).start()
    gqa[b] = gq2[b]
    grad_finish(*g_out_z)
    gout_o[...] = sum([t[...].astype(F32) for t in others(*g_out_z)], gos[s].astype(F32))
    deliver(3).start()
    grad_finish(*g_down_z)
    gdown_o[...] = sum([t[...].astype(F32) for t in others(*g_down_z)], gds[s].astype(F32))
    deliver(5).start()
    landed(gu2.at[pl.ds(0, 7)], aq_r.at[2])
    for d in range(PLANE):
        gup_o[:, d * 512:(d + 1) * 512] = gua[d].astype(F32)
    deliver(4).start()
    landed(vzr, y_r.at[1])
    vz_sum = vz[...] + vzr[0] + vzr[1] + vzr[2]
    columns = pltpu.roll(vz_sum, (128 - 32 * s) % 128, 1)
    gain_o[...] = columns[0:2, 0:32]
    shift_o[...] = columns[2:8, 0:32]
    lead_o[...] = columns[8:10, 0:32]
    bias_o[...] = jnp.sum(jnp.where(line == 11 + s, vz_sum, 0.0), axis=0, keepdims=True)
    for n in range(6, 10):
        deliver(n).start()
    landed(gq2.at[pl.ds(0, 7)], aq_r.at[3])
    for d in range(PLANE):
        for j in range(3):
            gqkv_o[:, j * width + d * 128:j * width + (d + 1) * 128] = (
                gqa[d, :, j * 128:(j + 1) * 128].astype(F32)
            )

    deliver(2).start()
    for op in range(4):
        left(agf.at[op, pl.ds(0, 3), :, 0], ag_s.at[op])
        left(agf.at[op, :, :, 0], fw_s.at[op])
    for op in range(3):
        end_sums(op)
    left(wo.at[pl.ds(0, 3)], wg_s.at[0])
    left(wo.at[pl.ds(0, 4)], wg_s.at[1])
    left(aown.at[pl.ds(0, 7)], h_s.at[0])
    left(dsend.at[pl.ds(0, 7)], g_s.at[0])
    for kind, sent in enumerate((sq, su, gu2, gq2)):
        left(sent.at[pl.ds(0, 7)], aq_s.at[kind])
    left(vecf.at[pl.ds(0, 7)], v_s.at[0])
    left(vs.at[pl.ds(0, 7)], v_s.at[1])
    left(ztr, y_s.at[0])
    left(vzr, y_s.at[1])
    for moved in (w_out_z, w_qkv_z, w_up_z, w_down_z):
        weight_sent(*moved)
    for moved in (g_down_z, g_up_z, g_qkv_z, g_out_z):
        grad_sent(*moved)
    for n in range(10):
        deliver(n).wait()


def hand_over(*refs):
    count = len(refs) // 3
    given, taken, held, sems = refs[:count], refs[count:2 * count], refs[2 * count:3 * count], refs[-1]
    into = [pltpu.make_async_copy(given[n], held[n], sems.at[0, n]) for n in range(count)]
    out = [pltpu.make_async_copy(held[n], taken[n], sems.at[1, n]) for n in range(count)]
    for copy in into:
        copy.start()
    for n in range(count):
        into[n].wait()
        out[n].start()
    for copy in out:
        copy.wait()


def plane_body(
    tokens, cotangent, w_qkv, w_out, w_up, w_down,
    up_bias, norm_gains, shift_rows, lead_weight, lead_steps, valid_cells,
):
    width = tokens.shape[2]
    vmem = pl.BlockSpec(memory_space=pltpu.VMEM)
    anywhere = pl.BlockSpec(memory_space=pl.ANY)
    dma = pltpu.SemaphoreType.DMA
    V = pltpu.VMEM
    out_shape = (
        jax.ShapeDtypeStruct((ROWS, width), BF16),
        jax.ShapeDtypeStruct((ROWS, width), BF16),
        jax.ShapeDtypeStruct((32, 3 * width), F32),
        jax.ShapeDtypeStruct((32, width), F32),
        jax.ShapeDtypeStruct((32, 4 * width), F32),
        jax.ShapeDtypeStruct((128, width), F32),
        jax.ShapeDtypeStruct((2, 32), F32),
        jax.ShapeDtypeStruct((6, 32), F32),
        jax.ShapeDtypeStruct((2, 32), F32),
        jax.ShapeDtypeStruct((1, 128), F32),
    )
    scratch = [
        V((ROWS, width), BF16), V((ROWS, width), BF16),
        V((32, 3 * width), F32), V((32, width), F32),
        V((32, 4 * width), F32), V((128, width), F32),
        V((2, 32), F32), V((6, 32), F32), V((2, 32), F32), V((1, 128), F32),
        V((32, 3 * width), BF16), V((32, 4 * width), BF16),
        V((16, 128), F32), V((2, 16, 128), BF16),
        V((4, 4, 2, 2, HALF, width), BF16),
        V((PLANE, DEPTH, 32, 384), BF16),
        V((PLANE, 128, width), BF16),
        V((PLANE, DEPTH, 32, 512), BF16),
        V((DEPTH, 128, width), BF16),
        V((PLANE, 32, 384), BF16),
        V((PLANE, 32, 512), BF16),
        V((3, 16, 128), BF16),
        V((16, 128), BF16),
        V((PLANE, 16, 128), BF16),
        V((16, width), F32),
        V((4, BLOCK, width), BF16),
        V((4, 2 * BLOCK, 256), BF16),
        V((1024, 256), BF16),
        V((128, 1024), BF16),
        V((1024, 128), BF16),
        V((128, 1024), BF16),
        V((4, 1024, 2 * BLOCK), BF16),
        V((4, 128, BLOCK), F32),
        V((4, 8, 2 * BLOCK), F32),
        V((4, BLOCK, 128), BF16),
        V((PLANE, ROWS, 128), BF16),
        V((PLANE, ROWS, 128), BF16),
        V((4, 2, 2, HALF, 128), BF16),
        V((1024, 384), BF16),
        V((1024, 128), F32),
        V((1024, 128), F32),
        V((1024, 512), BF16),
        V((4, BLOCK, 512), F32),
        V((1024, 512), BF16),
        V((ROWS, width), F32),
        V((ROWS, width), F32),
        V((512, width), F32),
        V((3, 4, 2, 2, HALF, width), BF16),
        V((3, 4, 2, HALF, width), BF16),
        V((3, 4, 2, HALF, width), BF16),
        V((3, 2, HALF, width), BF16),
        V((3, 2, 2, HALF, width), BF16),
        V((DEPTH, 128, width), BF16),
        V((PLANE, DEPTH, 32, 512), BF16),
        V((PLANE, DEPTH, 32, 384), BF16),
        V((DEPTH, 32, width), BF16),
        V((DEPTH, 128, width), BF16),
        V((DEPTH, PLANE, 32, 512), BF16),
        V((DEPTH, PLANE, 32, 384), BF16),
        V((DEPTH, 32, width), BF16),
        V((128, width), BF16),
        V((PLANE, 32, 512), BF16),
        V((PLANE, 32, 384), BF16),
        V((32, width), BF16),
        V((PLANE, 32, 512), BF16),
        V((PLANE, 32, 384), BF16),
        V((PLANE, 32, 512), BF16),
        V((PLANE, 32, 384), BF16),
        V((128, width), F32),
        V((10, 8, width), F32),
        V((8, 512), F32),
        V((PLANE, 16, 128), F32),
        V((PLANE - 1, 16, 128), F32),
        V((16, 128), F32),
        V((3, 16, 128), F32),
        dma((8,)), dma((10,)),
        dma((4,)), dma((4, 2)), dma((4,)), dma((4,)), dma((4, 4)),
        dma((4,)), dma((4,)), dma((2,)), dma((2,)), dma((2,)), dma((2,)),
        dma((4,)), dma((4, 2)), dma((4,)), dma((4, 5)),
        dma((3,)), dma((3, 4)), dma((3,)), dma((3,)), dma((3,)),
        dma((2,)), dma((4,)), dma((1,)), dma((1,)), dma((1,)), dma((4,)),
    ]
    results = pl.pallas_call(
        plane_kernel,
        out_shape=out_shape,
        in_specs=[pl.BlockSpec(memory_space=pltpu.SMEM)] + [vmem] * 5 + [anywhere] * 6,
        out_specs=tuple([anywhere] * 10),
        scratch_shapes=scratch,
        compiler_params=pltpu.CompilerParams(
            collective_id=0, has_side_effects=True, vmem_limit_bytes=63 * 2**20
        ),
    )(
        lead_steps, norm_gains, shift_rows, lead_weight, up_bias[None], valid_cells,
        tokens[0], cotangent[0], w_qkv, w_out, w_up, w_down,
    )
    results = pl.pallas_call(
        hand_over,
        out_shape=out_shape,
        in_specs=[anywhere] * len(out_shape),
        out_specs=tuple([anywhere] * len(out_shape)),
        scratch_shapes=[V(o.shape, o.dtype) for o in out_shape] + [dma((2, len(out_shape)))],
    )(*results)
    output, input_grad, g_qkv, g_out, g_up, g_down, g_gains, g_shifts, g_lead, g_bias = results
    return (
        output[None], input_grad[None], g_qkv, g_out, g_up, g_down, g_bias[0],
        g_gains, g_shifts, g_lead,
    )


def plane_fits(mesh):
    return mesh.shape["band"] == PLANE and mesh.shape["samp"] == DEPTH


def solution(mesh):
    return jax.shard_map(
        plane_body if plane_fits(mesh) else body,
        mesh=mesh,
        in_specs=(
            P("samp", "band", None),
            P("samp", "band", None),
            P(("band", "samp"), None),
            P(("band", "samp"), None),
            P(("band", "samp"), None),
            P(("band", "samp"), None),
            P(("band", "samp")),
            P(None, ("band", "samp")),
            P(None, ("band", "samp")),
            P(None, ("band", "samp")),
            P("samp"),
            P("samp", "band"),
        ),
        out_specs=(
            P("samp", "band", None),
            P("samp", "band", None),
            P(("band", "samp"), None),
            P(("band", "samp"), None),
            P(("band", "samp"), None),
            P(("band", "samp"), None),
            P(("band", "samp")),
            P(None, ("band", "samp")),
            P(None, ("band", "samp")),
            P(None, ("band", "samp")),
        ),
        check_vma=False,
    )
```

```python
import jax
import jax.numpy as jnp
from jax import lax
from jax.experimental import pallas as pl
from jax.experimental.pallas import tpu as pltpu
from jax.sharding import PartitionSpec as P

HEADS = 16


eps = 1e-05
masked = 10000.0


def layer_norm(values, gain_row, shift_row):
    centered = values - jnp.mean(values, axis=-1, keepdims=True)
    variance = jnp.mean(centered * centered, axis=-1, keepdims=True)
    return centered * lax.rsqrt(variance + eps) * gain_row + shift_row


def gelu_exact(values):
    return jax.nn.gelu(values, approximate=False)


def body(
    tokens,
    cotangent,
    w_qkv,
    w_out,
    w_up,
    w_down,
    up_bias,
    norm_gains,
    shift_rows,
    lead_weight,
    lead_steps,
    valid_cells,
):
    whole = (
        lax.all_gather(w_qkv, ("band", "samp"), axis=0, tiled=True),
        lax.all_gather(w_out, ("band", "samp"), axis=0, tiled=True),
        lax.all_gather(w_up, ("band", "samp"), axis=0, tiled=True),
        lax.all_gather(w_down, ("band", "samp"), axis=0, tiled=True),
        lax.all_gather(up_bias, ("band", "samp"), axis=0, tiled=True),
        lax.all_gather(norm_gains, ("band", "samp"), axis=1, tiled=True),
        lax.all_gather(shift_rows, ("band", "samp"), axis=1, tiled=True),
        lax.all_gather(lead_weight, ("band", "samp"), axis=1, tiled=True),
    )
    qkv_full = whole[0]
    out_full = whole[1]
    up_full = whole[2]
    down_full = whole[3]
    up_shift = whole[4].astype(jnp.float32)
    gain_all = whole[5].astype(jnp.float32)
    shift_all = whole[6].astype(jnp.float32)
    lead_all = whole[7].astype(jnp.float32)
    row_count = tokens.shape[1]
    width = tokens.shape[2]
    head_count = HEADS
    head_size = width // head_count
    score_scale = head_size ** (-0.5)
    lead_days = lead_steps[0].astype(jnp.float32) * 0.25
    entering = tokens[0].astype(jnp.float32) + lead_days * lead_all[0] + lead_all[1]
    normed, norm_first_back = jax.vjp(layer_norm, entering, gain_all[0], shift_all[0])
    normed_low = normed.astype(jnp.bfloat16)
    project = jnp.dot(normed_low, qkv_full, preferred_element_type=jnp.float32)
    queries = (project[:, :width] + shift_all[1]).astype(jnp.bfloat16)
    key_rows = project[:, width : 2 * width].astype(jnp.bfloat16)
    value_rows = (project[:, 2 * width :] + shift_all[2]).astype(jnp.bfloat16)
    key_open = (valid_cells[0] > 0).astype(jnp.bfloat16)
    keys_all, values_all, open_all = (
        lax.all_gather(key_rows, "band", axis=0, tiled=True),
        lax.all_gather(value_rows, "band", axis=0, tiled=True),
        lax.all_gather(key_open, "band", axis=0, tiled=True),
    )
    seq_total = keys_all.shape[0]
    block_rows = min(512, seq_total)
    block_count = seq_total // block_rows
    block_ids = jnp.arange(block_count)
    bias_all = (open_all.astype(jnp.float32) - 1.0) * masked
    query_heads = queries.reshape(row_count, head_count, head_size)

    def block_keys(step_index):
        first_row = step_index * block_rows
        key_block = lax.dynamic_slice_in_dim(keys_all, first_row, block_rows, 0).reshape(
            block_rows, head_count, head_size
        )
        value_block = lax.dynamic_slice_in_dim(values_all, first_row, block_rows, 0).reshape(
            block_rows, head_count, head_size
        )
        bias_block = lax.dynamic_slice_in_dim(bias_all, first_row, block_rows, 0)
        scores = (
            jnp.einsum("qhe,khe->hqk", query_heads, key_block, preferred_element_type=jnp.float32)
            * score_scale
            + bias_block
        )
        return (scores, key_block, value_block)

    def max_step(running, step_index):
        row_max, exp_total = running
        scores = block_keys(step_index)[0]
        new_max = jnp.maximum(row_max, jnp.max(scores, axis=-1))
        exp_total = exp_total * jnp.exp(row_max - new_max) + jnp.sum(
            jnp.exp(scores - new_max[..., None]), axis=-1
        )
        return ((new_max, exp_total), None)

    start_max = jnp.full((head_count, row_count), -jnp.inf, jnp.float32)
    start_total = jnp.zeros((head_count, row_count), jnp.float32)
    row_max, exp_total = lax.scan(max_step, (start_max, start_total), block_ids)[0]
    log_total = row_max + jnp.log(exp_total)

    def out_step(running, step_index):
        scores, key_block, value_block = block_keys(step_index)
        weights_low = jnp.exp(scores - log_total[..., None]).astype(jnp.bfloat16)
        return (
            running
            + jnp.einsum(
                "hqk,khe->qhe", weights_low, value_block, preferred_element_type=jnp.float32
            ),
            None,
        )

    attended_heads = lax.scan(
        out_step, jnp.zeros((row_count, head_count, head_size), jnp.float32), block_ids
    )[0]
    attended_low = attended_heads.reshape(row_count, width).astype(jnp.bfloat16)
    middle = (
        entering
        + jnp.dot(attended_low, out_full, preferred_element_type=jnp.float32)
        + shift_all[3]
    )
    second, norm_second_back = jax.vjp(layer_norm, middle, gain_all[1], shift_all[4])
    second_low = second.astype(jnp.bfloat16)
    hidden_pre = jnp.dot(second_low, up_full, preferred_element_type=jnp.float32) + up_shift
    hidden, gelu_back = jax.vjp(gelu_exact, hidden_pre)
    hidden_low = hidden.astype(jnp.bfloat16)
    result = (
        middle + jnp.dot(hidden_low, down_full, preferred_element_type=jnp.float32) + shift_all[5]
    )
    output = result.astype(jnp.bfloat16)
    grad_result = cotangent[0]
    grad_result_f = grad_result.astype(jnp.float32)
    grad_down_w = jnp.einsum(
        "tf,td->fd", hidden_low, grad_result, preferred_element_type=jnp.float32
    )
    grad_shift_down = jnp.sum(grad_result_f, axis=0)
    grad_hidden = jnp.einsum(
        "td,fd->tf", grad_result, down_full, preferred_element_type=jnp.float32
    )
    grad_pre_low = gelu_back(grad_hidden)[0].astype(jnp.bfloat16)
    grad_up_w = jnp.einsum(
        "td,tf->df", second_low, grad_pre_low, preferred_element_type=jnp.float32
    )
    grad_up_shift = jnp.sum(grad_pre_low.astype(jnp.float32), axis=0)
    grad_second = jnp.einsum("tf,df->td", grad_pre_low, up_full, preferred_element_type=jnp.float32)
    grad_middle_norm, grad_gain_second, grad_shift_second = norm_second_back(grad_second)
    grad_middle = grad_result_f + grad_middle_norm
    ffn_sums = (
        lax.psum_scatter(grad_up_w, ("band", "samp"), scatter_dimension=0, tiled=True),
        lax.psum_scatter(grad_down_w, ("band", "samp"), scatter_dimension=0, tiled=True),
        lax.psum_scatter(grad_up_shift, ("band", "samp"), scatter_dimension=0, tiled=True),
    )
    grad_branch = grad_middle.astype(jnp.bfloat16)
    grad_shift_out = jnp.sum(grad_branch.astype(jnp.float32), axis=0)
    grad_out_w = jnp.einsum(
        "td,te->de", attended_low, grad_branch, preferred_element_type=jnp.float32
    )
    grad_attended = jnp.einsum(
        "te,de->td", grad_branch, out_full, preferred_element_type=jnp.float32
    ).astype(jnp.bfloat16)
    grad_heads = grad_attended.reshape(row_count, head_count, head_size)
    delta = jnp.einsum("qhe,qhe->hq", grad_heads.astype(jnp.float32), attended_heads)
    zero_heads = jnp.zeros((row_count, head_count, head_size), jnp.float32)

    def key_grad_step(g_queries, step_index):
        scores, key_block, value_block = block_keys(step_index)
        weights_full = jnp.exp(scores - log_total[..., None])
        g_weights = jnp.einsum(
            "qhe,khe->hqk", grad_heads, value_block, preferred_element_type=jnp.float32
        )
        g_scores = (weights_full * (g_weights - delta[..., None])).astype(jnp.bfloat16)
        g_queries = (
            g_queries
            + jnp.einsum("hqk,khe->qhe", g_scores, key_block, preferred_element_type=jnp.float32)
            * score_scale
        )
        key_term = (
            jnp.einsum("hqk,qhe->khe", g_scores, query_heads, preferred_element_type=jnp.float32)
            * score_scale
        )
        value_term = jnp.einsum(
            "hqk,qhe->khe",
            weights_full.astype(jnp.bfloat16),
            grad_heads,
            preferred_element_type=jnp.float32,
        )
        return (
            g_queries,
            (key_term.reshape(block_rows, width), value_term.reshape(block_rows, width)),
        )

    grad_query_heads, block_terms = lax.scan(key_grad_step, zero_heads, block_ids)
    grad_query_f = grad_query_heads.reshape(row_count, width)
    key_sum, value_sum = (
        lax.psum_scatter(
            block_terms[0].reshape(seq_total, width), "band", scatter_dimension=0, tiled=True
        ),
        lax.psum_scatter(
            block_terms[1].reshape(seq_total, width), "band", scatter_dimension=0, tiled=True
        ),
    )
    grad_query_low = grad_query_f.astype(jnp.bfloat16)
    grad_key_low = key_sum.astype(jnp.bfloat16)
    grad_value_low = value_sum.astype(jnp.bfloat16)
    grad_project = jnp.concatenate([grad_query_low, grad_key_low, grad_value_low], axis=-1)
    grad_qkv_w = jnp.einsum(
        "td,te->de", normed_low, grad_project, preferred_element_type=jnp.float32
    )
    grad_shift_query = jnp.sum(grad_query_low.astype(jnp.float32), axis=0)
    grad_shift_value = jnp.sum(grad_value_low.astype(jnp.float32), axis=0)
    grad_normed = jnp.einsum(
        "te,de->td", grad_project, qkv_full, preferred_element_type=jnp.float32
    )
    grad_entering_norm, grad_gain_first, grad_shift_first = norm_first_back(grad_normed)
    grad_entering = grad_middle + grad_entering_norm
    input_grad = grad_entering.astype(jnp.bfloat16)
    entering_sum = jnp.sum(grad_entering, axis=0)
    grad_lead_rows = jnp.stack([lead_days * entering_sum, entering_sum])
    grad_gain_rows = jnp.stack([grad_gain_first, grad_gain_second])
    grad_shift_stack = jnp.stack(
        [
            grad_shift_first,
            grad_shift_query,
            grad_shift_value,
            grad_shift_out,
            grad_shift_second,
            grad_shift_down,
        ]
    )
    attention_sums = (
        lax.psum_scatter(grad_qkv_w, ("band", "samp"), scatter_dimension=0, tiled=True),
        lax.psum_scatter(grad_out_w, ("band", "samp"), scatter_dimension=0, tiled=True),
        lax.psum_scatter(grad_gain_rows, ("band", "samp"), scatter_dimension=1, tiled=True),
        lax.psum_scatter(grad_shift_stack, ("band", "samp"), scatter_dimension=1, tiled=True),
        lax.psum_scatter(grad_lead_rows, ("band", "samp"), scatter_dimension=1, tiled=True),
    )
    return (
        output[None],
        input_grad[None],
        attention_sums[0],
        attention_sums[1],
        ffn_sums[0],
        ffn_sums[1],
        ffn_sums[2],
        attention_sums[2],
        attention_sums[3],
        attention_sums[4],
    )


MESH = pl.DeviceIdType.MESH
F32 = jnp.float32
BF16 = jnp.bfloat16
PLANE = 8
DEPTH = 4
ROWS = 128
HALF = 64
BLOCK = 256
NN = (((1,), (0,)), ((), ()))
NT = (((1,), (1,)), ((), ()))
TN = (((0,), (0,)), ((), ()))
INNER = 32


def mm(left, right, dims=NN):
    return lax.dot_general(left, right, dims, preferred_element_type=F32)


def plane_kernel(
    lead_ref, gain_in, shift_in, leadw_in, bias_in, valid_in,
    tok_in, cot_in, wqkv_in, wout_in, wup_in, wdown_in,
    out_h, ig_h, gqkv_h, gout_h, gup_h, gdown_h, gain_h, shift_h, lead_h, bias_h,
    out_o, ig_o, gqkv_o, gout_o, gup_o, gdown_o, gain_o, shift_o, lead_o, bias_o,
    wqkv, wup, vcol, vec_in,
    agf, wq, wo, wu, wd, sq, su, ztr, vt, vecf, vrow,
    normed, qaug, kaug, kt, vv, vt2, pst, ot, invl, att, aown, dsend, dob, gproj, dk, dv,
    hid, gder, gpre, mid, gmid, gdf, sct,
    part, pr, cs, au, rr,
    gds, gus, gqs, gos, gdr, gur, gqr, gor_, gda, guc, gqc, goc, gu2, gq2, gua, gqa, goa,
    acc, gub, vs, vsr, vz, vzr,
    in_s, out_s, ag_s, ag_r, ac_r, fw_s, fw_r, aq_s, aq_r, v_s, v_r, y_s, y_r, w_s, w_r, z_s, z_r,
    p_s, p_r, f_r, n_s, n_r, wg_s, wg_r, h_s, h_r, g_s, g_r,
):
    b = lax.axis_index("band")
    s = lax.axis_index("samp")
    c = b % 2
    x = (b // 2) % 2
    y = b // 4
    mate = b + 1 - 2 * c

    def chip(r):
        xx = x + (r % 2) * (1 - 2 * x)
        yy = y + (r // 2) * (1 - 2 * y)
        return yy * 2 + xx

    def near(r):
        return chip(r) * 2 + c

    def peer(k):
        return (b + k) % PLANE

    def level(k):
        return (s + k) % DEPTH

    barrier = pltpu.get_barrier_semaphore()
    for k in range(1, PLANE):
        pl.semaphore_signal(barrier, inc=1, device_id=(peer(k), s), device_id_type=MESH)
    for k in range(1, DEPTH):
        pl.semaphore_signal(barrier, inc=1, device_id=(b, level(k)), device_id_type=MESH)

    width = tok_in.shape[1]
    fetches = [
        pltpu.make_async_copy(src, dst, in_s.at[n])
        for n, (src, dst) in enumerate((
            (wqkv_in, wqkv), (wout_in, wo.at[b, pl.ds(pl.multiple_of(s * 32, 32), 32)]),
            (tok_in.at[pl.ds(0, HALF)], agf.at[0, 0, 0, c]),
            (tok_in.at[pl.ds(HALF, HALF)], agf.at[0, 0, 1, c]),
            (wup_in, wup), (wdown_in, wd.at[s]),
            (cot_in.at[pl.ds(0, HALF)], agf.at[1, 0, 0, c]),
            (cot_in.at[pl.ds(HALF, HALF)], agf.at[1, 0, 1, c]),
        ))
    ]
    for fetch in fetches:
        fetch.start()
    vcol[...] = jnp.zeros_like(vcol)
    vcol[0:2, 0:32] = gain_in[...].astype(F32)
    vcol[2:8, 0:32] = shift_in[...].astype(F32)
    vcol[8:10, 0:32] = leadw_in[...].astype(F32)
    line = lax.broadcasted_iota(jnp.int32, (16, 128), 0)
    tile = pltpu.roll(vcol[...], s * 32, 1)
    tile = jnp.where(line == 11 + s, bias_in[...].astype(F32), tile)
    vec_in[0] = tile.astype(BF16)
    opened = jnp.where(valid_in[...] > 0, 1.0, 0.0)
    vec_in[1] = jnp.where(line == 10, opened, 0.0).astype(BF16)
    far = (s + 2) % DEPTH
    ends = (s == 0) | (s == DEPTH - 1)
    inner = (s > 0) & (s < DEPTH - 1)

    @pl.when(s == 0)
    def _():
        for kept in (gdr, gur, gqr, gor_):
            kept[0] = jnp.zeros(kept.shape[1:], BF16)

    @pl.when(s == DEPTH - 1)
    def _():
        for kept in (gda, guc, gqc, goc):
            kept[...] = jnp.zeros(kept.shape, BF16)

    fetches[0].wait()
    for d in range(PLANE):
        for j in range(3):
            sq[d, :, j * 128:(j + 1) * 128] = wqkv[:, j * width + d * 128:j * width + (d + 1) * 128]
    fetches[1].wait()
    pl.semaphore_wait(barrier, PLANE - 1 + DEPTH - 1)

    def rc(src, dst, ss, rs, band, samp):
        return pltpu.make_async_remote_copy(
            src_ref=src, dst_ref=dst, send_sem=ss, recv_sem=rs,
            device_id=(band, samp), device_id_type=MESH,
        )

    def landed(ref, sem):
        rc(ref, ref, aq_s.at[0], sem, mate, s).wait_recv()

    def left(ref, sem):
        rc(ref, ref, sem, aq_r.at[0], mate, s).wait_send()

    def yc(kind, k, src, dst):
        return rc(src, dst, y_s.at[kind], y_r.at[kind], b, level(k))

    def weight_copy(kind, region, pieces, role, to):
        return rc(region(s), region(s), w_s.at[kind], w_r.at[kind, role], b, to)

    def weight_hand(kind, region, pieces):
        return rc(region(far), region(far), w_s.at[kind], w_r.at[kind, 2], b, 3 * (s - 1))

    def weight_start(*moved):
        @pl.when(s == 1)
        def _():
            weight_copy(*moved, 1, s - 1).start()

        weight_copy(*moved, 0, far).start()

        @pl.when(ends)
        def _():
            weight_copy(*moved, 1, 1 + s // 3).start()

        @pl.when(s == 2)
        def _():
            weight_copy(*moved, 1, s + 1).start()

        @pl.when(inner)
        def _():
            weight_copy(*moved, 2, DEPTH - 1 - s).start()

    def weight_pass(kind, region, pieces):
        @pl.when(inner)
        def _():
            landed(region(far), w_r.at[kind, 0])
            weight_hand(kind, region, pieces).start()

    def weight_most(kind, region, pieces):
        landed(region(DEPTH - 1 - far), w_r.at[kind, 1])

        @pl.when(ends)
        def _():
            landed(region(far), w_r.at[kind, 0])

    def weight_last(kind, region, pieces):
        landed(region(DEPTH - 1 - s), w_r.at[kind, 2])

    def weight_finish(*moved):
        weight_most(*moved)
        weight_last(*moved)

    def weight_sent(kind, region, pieces):
        @pl.when(ends)
        def _():
            left(pieces(2), w_s.at[kind])

        @pl.when(inner)
        def _():
            left(pieces(4), w_s.at[kind])

    def grad_up(kind, stage, got, via, pieces, t):
        return rc(stage(t), got(t), z_s.at[kind], z_r.at[kind, t], b, s + 1)

    def grad_down_to(kind, stage, got, via, pieces, t):
        return rc(stage(t), got(t), z_s.at[kind], z_r.at[kind, t], b, s - 1)

    def grad_down_last(kind, stage, got, via, pieces):
        return rc(stage(s - 1), via, z_s.at[kind], z_r.at[kind, DEPTH], b, s - 1)

    def grad_start(*moved):
        for hops in (3, 2, 1):
            grad_start_some(*moved, hops)

    def grad_start_some(kind, stage, got, via, pieces, hops):
        @pl.when(s == 0)
        def _():
            grad_up(kind, stage, got, via, pieces, hops).start()

        @pl.when(s == DEPTH - 1)
        def _():
            if hops == 1:
                grad_down_last(kind, stage, got, via, pieces).start()
            else:
                grad_down_to(kind, stage, got, via, pieces, DEPTH - 1 - hops).start()

    def down_half(half):
        rows = pl.ds(half * HALF, HALF)

        @pl.when(s == 0)
        def _():
            rc(gds.at[1, rows], gdr.at[1, rows], z_s.at[0], z_r.at[0, 1], b, 1).start()

        @pl.when(s == DEPTH - 1)
        def _():
            rc(gds.at[2, rows], gda.at[rows], z_s.at[0], z_r.at[0, DEPTH], b, DEPTH - 2).start()

    def add_in(kind, stage, got, via, pieces, t):
        landed(got(t), z_r.at[kind, t])
        term, more = stage(t), got(t)
        if len(via.shape) == 3:
            def add(j, _):
                term[j] = (term[j].astype(F32) + more[j].astype(F32)).astype(BF16)
                return 0

            lax.fori_loop(0, via.shape[0], add, 0)
        else:
            def add_rows(j, _):
                rows = pl.ds(pl.multiple_of(j * INNER, INNER), INNER)
                term[rows, :] = (term[rows, :].astype(F32) + more[rows, :].astype(F32)).astype(BF16)
                return 0

            lax.fori_loop(0, via.shape[0] // INNER, add_rows, 0)

    def grad_pass(*moved):
        @pl.when(s == 1)
        def _():
            add_in(*moved, 3)
            grad_up(*moved, 3).start()

        @pl.when(s == 2)
        def _():
            add_in(*moved, 0)
            grad_down_to(*moved, 0).start()

    def grad_pass_on(*moved):
        @pl.when(s == 1)
        def _():
            add_in(*moved, 2)
            grad_up(*moved, 2).start()
            add_in(*moved, 0)
            grad_down_last(*moved).start()

        @pl.when(s == 2)
        def _():
            add_in(*moved, 1)
            grad_down_last(*moved).start()
            add_in(*moved, 3)
            grad_up(*moved, 3).start()

    def grad_finish(kind, stage, got, via, pieces):
        @pl.when(s > 0)
        def _():
            landed(got(s), z_r.at[kind, s])

        @pl.when(s < DEPTH - 1)
        def _():
            landed(via, z_r.at[kind, DEPTH])

    def grad_sent(kind, stage, got, via, pieces):
        left(pieces(3), z_s.at[kind])

    results = ((out_o, out_h), (ig_o, ig_h), (gqkv_o, gqkv_h), (gout_o, gout_h), (gup_o, gup_h), (gdown_o, gdown_h),
               (gain_o, gain_h), (shift_o, shift_h), (lead_o, lead_h), (bias_o, bias_h))

    def deliver(n):
        return pltpu.make_async_copy(results[n][0], results[n][1], out_s.at[n])

    w_out_z = (
        0, lambda t: wo.at[b, pl.ds(pl.multiple_of(t * 32, 32), 32)],
        lambda n: wo.at[b, pl.ds(0, n * 32)],
    )
    w_qkv_z = (1, lambda t: wq.at[:, t], lambda n: wq.at[:, pl.ds(0, n)])
    w_up_z = (2, lambda t: wu.at[:, t], lambda n: wu.at[:, pl.ds(0, n)])
    w_down_z = (3, lambda t: wd.at[t], lambda n: wd.at[pl.ds(0, n)])
    g_down_z = (0, lambda t: gds.at[t], lambda t: gdr.at[t], gda, lambda n: gds.at[pl.ds(0, n)])
    g_up_z = (1, lambda t: gus.at[:, t], lambda t: gur.at[t], guc, lambda n: gus.at[:, pl.ds(0, n)])
    g_qkv_z = (2, lambda t: gqs.at[:, t], lambda t: gqr.at[t], gqc, lambda n: gqs.at[:, pl.ds(0, n)])
    g_out_z = (3, lambda t: gos.at[t], lambda t: gor_.at[t], goc, lambda n: gos.at[pl.ds(0, n)])

    def gather(op, r, turn):
        return rc(
            agf.at[op, 0, (turn + r) % 2, c], agf.at[op, 1 + turn, r - 1, c],
            ag_s.at[op], ag_r.at[op, turn], near(r), s,
        )

    def across(op, r):
        return rc(
            agf.at[op, 1, r - 1, c], agf.at[op, 3, r % 2, c],
            ag_s.at[op], ac_r.at[op], near(3 - r), s,
        )

    def share(op, blk):
        return rc(
            agf.at[op, blk, :, c], agf.at[op, blk, :, c],
            fw_s.at[op], fw_r.at[op, blk], mate, s,
        )

    def start_gather(op):
        for turn in (0, 1):
            for r in (1, 2):
                gather(op, r, turn).start()
        share(op, 0).start()

    def arrive(op, blk):
        if blk in (1, 2):
            landed(agf.at[op, blk, :, c], ag_r.at[op, blk - 1])
        if blk == 1:
            for r in (1, 2):
                across(op, r).start()
        if blk == 3:
            landed(agf.at[op, 3, :, c], ac_r.at[op])
        if blk:
            share(op, blk).start()

    def block(op, i):
        return agf[op, i].reshape(BLOCK, -1)

    def rows_half(dev, h):
        return wo.at[dev, pl.ds(h * HALF, HALF)]

    def rows_copy(r, turn):
        part_ = rows_half(b, (turn + r) % 2)
        return rc(part_, part_, wg_s.at[0], wg_r.at[turn], near(r), s)

    def rows_across(r):
        part_ = rows_half(near(r), r % 2)
        return rc(part_, part_, wg_s.at[0], wg_r.at[2], near(3 - r), s)

    def rows_share(r):
        dev = near(r) if r else b
        return rc(wo.at[dev], wo.at[dev], wg_s.at[1], wg_r.at[3], mate, s)

    def rows_start():
        for turn in (0, 1):
            for r in (1, 2):
                rows_copy(r, turn).start()
        rows_share(0).start()

    def granule(i, a):
        return (i, a) if i in (0, 3) else (a + 1, 1 - a if i == 1 else a)

    GRANULES = [(i, a) for i in (1, 0, 2, 3) for a in (0, 1)]

    def heads_copy(i, a, k):
        r, h = granule(i, a)
        rows = pl.ds(pl.multiple_of((a * 2 + k) * HALF, HALF), HALF)
        return rc(
            att.at[i, rows], aown.at[b, pl.ds(h * HALF, HALF)],
            h_s.at[0], h_r.at[0], chip(r) * 2 + k, s,
        )

    def cores(i):
        return (1 - c,) if i == 0 else (0, 1)

    def back_copy(i, a, k):
        r, h = granule(i, a)
        dev = chip(r) * 2 + k
        return rc(
            dsend.at[dev, pl.ds(h * HALF, HALF)], dob.at[i, a, c],
            g_s.at[0], g_r.at[i], dev, s,
        )

    def swap(kind, k, src, dst):
        return rc(src, dst, aq_s.at[kind], aq_r.at[kind], peer(k), s)

    for k in range(1, DEPTH):
        yc(0, k, vec_in.at[0], ztr.at[k - 1]).start()
    for k in range(1, PLANE):
        swap(0, k, sq.at[peer(k)], wq.at[b, s]).start()
    weight_start(*w_out_z)
    fetches[2].wait()
    fetches[3].wait()
    for r in (1, 2):
        gather(0, r, 0).start()
    wq[b, s] = sq[b]
    fetches[4].wait()
    for d in range(PLANE):
        su[d] = wup[:, d * 512:(d + 1) * 512]
    wu[b, s] = su[b]

    landed(ztr, y_r.at[0])
    vt[...] = (
        vec_in[0].astype(F32) + vec_in[1].astype(F32)
        + ztr[0].astype(F32) + ztr[1].astype(F32) + ztr[2].astype(F32)
    ).astype(BF16)

    def spread(k):
        return rc(vt, vecf.at[b], v_s.at[0], v_r.at[0], peer(k), s)

    for k in range(1, PLANE):
        spread(k).start()
    for r in (1, 2):
        gather(0, r, 1).start()
    share(0, 0).start()
    vecf[b] = vt[...]
    landed(sq.at[pl.ds(0, 7)], aq_r.at[0])
    weight_start(*w_qkv_z)
    for k in range(1, PLANE):
        swap(1, k, su.at[peer(k)], wu.at[b, s]).start()
    arrive(0, 1)
    fetches[6].wait()
    fetches[7].wait()
    for r in (1, 2):
        gather(1, r, 0).start()
    share(1, 0).start()
    landed(vecf.at[pl.ds(0, 7)], v_r.at[0])
    for d in range(PLANE):
        vrow[:, d * 128:(d + 1) * 128] = vecf[d].astype(F32)
    lead_days = lead_ref[0].astype(F32) * 0.25
    lane = lax.broadcasted_iota(jnp.int32, (1, 128), 1)
    head_lane = [(lane < 64).astype(F32), (lane >= 64).astype(F32)]
    ones_lane = jnp.where(lane < 2, 1.0, 0.0).astype(F32)
    ends_lane = jnp.where(lane == 0, 9984.0, jnp.where(lane == 1, 16.0, 0.0)).astype(F32)
    gain1, gain2 = vrow[0:1, :], vrow[1:2, :]
    shift1, shift_out, shift2, shift_down = vrow[2:3, :], vrow[5:6, :], vrow[6:7, :], vrow[7:8, :]
    lead_row = lead_days * vrow[8:9, :] + vrow[9:10, :]
    mine = vecf[b].astype(F32)

    def stats(v):
        mean = jnp.mean(v, axis=-1, keepdims=True)
        centered = v - mean
        variance = jnp.mean(centered * centered, axis=-1, keepdims=True)
        rstd = lax.rsqrt(variance + eps)
        return centered * rstd, rstd

    for r in range(4):
        for k in range(2):
            row = jnp.broadcast_to(vecf[chip(r) * 2 + k].astype(F32)[10:11, :], (128, 128))
            column = ((row.T - 1.0) * ends_lane).astype(BF16)
            for h in range(2):
                if r in (0, 3):
                    blk, a = r, h
                else:
                    blk, a = (1 if h == r % 2 else 2), r - 1
                top = blk * BLOCK + (a * 2 + k) * HALF
                kaug[top:top + HALF, 128:256] = column[h * HALF:(h + 1) * HALF]
    for h in range(2):
        for i in range(4):
            qaug[i, h * BLOCK:(h + 1) * BLOCK, 128:256] = jnp.broadcast_to(ones_lane, (BLOCK, 128)).astype(BF16)

    def norm_block(i):
        def chunk(j, _):
            rows = pl.ds(pl.multiple_of((j % 2) * INNER, INNER), INNER)
            ent = agf[0, i, j // 4, (j // 2) % 2, rows, :].astype(F32) + lead_row
            xhat = stats(ent)[0]
            put = pl.ds(pl.multiple_of(j * INNER, INNER), INNER)
            normed[i, put, :] = (xhat * gain1 + shift1).astype(BF16)
            return 0

        lax.fori_loop(0, BLOCK // INNER, chunk, 0)

    share(0, 0).wait_recv()
    norm_block(0)
    share(0, 1).wait_recv()
    arrive(0, 2)
    norm_block(1)
    weight_pass(*w_out_z)
    weight_pass(*w_qkv_z)
    share(0, 2).wait_recv()
    norm_block(2)
    weight_finish(*w_out_z)
    rows_start()
    landed(su.at[pl.ds(0, 7)], aq_r.at[1])

    @pl.when(inner)
    def _():
        weight_copy(*w_up_z, 1, 3 * (s - 1)).start()

    arrive(0, 3)
    share(0, 3).wait_recv()
    @pl.when(ends)
    def _():
        weight_start(*w_up_z)

    norm_block(3)

    weight_finish(*w_qkv_z)
    @pl.when(inner)
    def _():
        weight_copy(*w_up_z, 0, far).start()
        weight_copy(*w_up_z, 2, DEPTH - 1 - s).start()


    def project_block(q, _):
        rows = pl.ds(pl.multiple_of(q * BLOCK, BLOCK), BLOCK)
        pj = mm(normed[q], wq[...].reshape(width, 384))
        qv = (pj[:, 0:128] + mine[3:4, :]).astype(BF16).astype(F32) * 0.125
        for h in range(2):
            qaug[q, h * BLOCK:(h + 1) * BLOCK, 0:128] = (qv * head_lane[h]).astype(BF16)
        kv = pj[:, 128:256].astype(BF16)
        kaug[rows, 0:128] = kv
        kt[:, rows] = kv.T
        vb = (pj[:, 256:384] + mine[4:5, :]).astype(BF16)
        vv[rows, :] = vb
        vt2[:, rows] = vb.T
        return 0

    lax.fori_loop(0, 4, project_block, 0)

    def mate_copy(op, i):
        return rc(part.at[op, i, :, 1 - c], pr.at[op, i], p_s.at[op], p_r.at[op, i], mate, s)

    def far_copy(op, h):
        return rc(cs.at[op, 3, h], au.at[op, 1 - h], n_s.at[op], f_r.at[op], near(h + 1), s)

    def near_copy(op, i, a):
        h = a if i == 2 else 1 - a
        return rc(cs.at[op, i, a], rr.at[op, a, h], n_s.at[op], n_r.at[op], near(a + 1), s)

    def put_part(op, i, blk):
        part[op, i] = blk.astype(BF16).reshape(2, 2, HALF, width)
        mate_copy(op, i).start()

    def fold(op, i):
        mate_copy(op, i).wait_recv()

        def chunk(j, _):
            a = j // 2
            rows = pl.ds(pl.multiple_of((j % 2) * INNER, INNER), INNER)
            cs[op, i, a, rows, :] = (
                part[op, i, a, c, rows, :].astype(F32) + pr[op, i, a, rows, :].astype(F32)
            ).astype(BF16)
            return 0

        lax.fori_loop(0, ROWS // INNER, chunk, 0)

    def fold_before(op, i, near_too=True):
        @pl.when(i < 3)
        def _():
            fold(op, i + 1)

        @pl.when(i == 2)
        def _():
            send_far(op)

        if near_too:
            @pl.when(i == 1)
            def _():
                send_near(op, 2)

    def send_far(op):
        for h in (0, 1):
            far_copy(op, h).start()

    def send_near(op, i):
        for a in (0, 1):
            near_copy(op, i, a).start()

    def send_last(op):
        landed(au.at[op], f_r.at[op])
        for a in (0, 1):
            def chunk(j, _):
                rows = pl.ds(pl.multiple_of(j * INNER, INNER), INNER)
                cs[op, 1, a, rows, :] = (
                    cs[op, 1, a, rows, :].astype(F32) + au[op, a, rows, :].astype(F32)
                ).astype(BF16)
                return 0

            lax.fori_loop(0, HALF // INNER, chunk, 0)
            near_copy(op, 1, a).start()

    def wait_sums(op):
        landed(rr.at[op], n_r.at[op])

    def place(j):
        return j // 2, pl.ds(pl.multiple_of((j % 2) * INNER, INNER), INNER)

    def plane_total(op, j):
        h, rows = place(j)
        total = cs[op, 0, h, rows, :].astype(F32)
        return total + rr[op, 0, h, rows, :].astype(F32) + rr[op, 1, h, rows, :].astype(F32)

    def own_rows(op, j):
        h, rows = place(j)
        return agf[op, 0, h, c, rows, :].astype(F32)

    def set_rows(op, j, v):
        h, rows = place(j)
        agf[op, 0, h, c, rows, :] = v

    def end_sums(op):
        left(part.at[op, :, :, 0], p_s.at[op])
        left(cs.at[op, pl.ds(0, 3)], n_s.at[op])

    def attend_block(n, _):
        i = 3 - n

        @pl.when(n == 3)
        def _():
            landed(wo.at[0], wg_r.at[1])
            for r in (1, 2):
                rows_share(r).start()

        st = mm(kaug[...], qaug[i], NT)
        p = jnp.exp(st - jnp.max(st, axis=0, keepdims=True))
        inverse = 1.0 / jnp.sum(p, axis=0, keepdims=True)
        pb = p.astype(BF16)
        pst[i] = pb
        out = mm(vt2[...], pb) * inverse
        ot[i, 0:64, :] = out[0:64, 0:BLOCK]
        ot[i, 64:128, :] = out[64:128, BLOCK:]
        invl[i] = jnp.broadcast_to(inverse, (8, 2 * BLOCK))
        att[i] = ot[i].T.astype(BF16)
        for blk in range(4):
            @pl.when(i == blk)
            def _():
                for a in (0, 1):
                    for k in cores(blk):
                        heads_copy(blk, a, k).start()

        return 0

    landed(wo.at[0], wg_r.at[0])
    for r in (1, 2):
        rows_across(r).start()
    lax.fori_loop(0, 4, attend_block, 0)
    landed(wo.at[0], wg_r.at[2])
    rows_share(3).start()
    arrive(1, 1)
    for h in (0, 1):
        top = pl.multiple_of((h * 2 + c) * HALF, HALF)
        aown[b, h * HALF:(h + 1) * HALF] = att[0, pl.ds(top, HALF), :]
    weight_pass(*w_up_z)
    fetches[5].wait()

    @pl.when(inner)
    def _():
        weight_start(*w_down_z)

    landed(wo.at[pl.ds(0, 4)], wg_r.at[3])
    landed(aown.at[pl.ds(0, 7)], h_r.at[0])
    heads = jnp.concatenate([aown[d] for d in range(PLANE)], axis=1)
    mid[...] = mm(heads, wo[...].reshape(1024, width))

    def middle_chunk(j, _):
        rows = pl.ds(pl.multiple_of(j * INNER, INNER), INNER)
        m = own_rows(0, j) + lead_row + mid[rows, :] + shift_out
        mid[rows, :] = m
        set_rows(2, j, (stats(m)[0] * gain2 + shift2).astype(BF16))
        return 0

    lax.fori_loop(0, ROWS // INNER, middle_chunk, 0)
    start_gather(2)
    arrive(1, 3)
    arrive(2, 1)
    for r in (1, 2):
        gather(1, r, 1).start()

    @pl.when(ends)
    def _():
        weight_start(*w_down_z)

    weight_finish(*w_up_z)

    bias = jnp.concatenate([mine[11 + j:12 + j, :] for j in range(4)], axis=1)

    def arrivals(op, i):
        for blk in range(4):
            @pl.when(i == blk)
            def _():
                if blk != 1:
                    arrive(op, blk)
                share(op, blk).wait_recv()

    def down_grad_first(f, _):
        cols = pl.ds(pl.multiple_of(f * BLOCK, BLOCK), BLOCK)
        gdf[pl.ds(pl.multiple_of(f * BLOCK, BLOCK), BLOCK), :] = mm(
            hid[:2 * BLOCK, cols], agf[1, 0:2].reshape(2 * BLOCK, width), TN
        )
        return 0

    def up_block(i, _):
        @pl.when(i == 3)
        def _():
            for blk in range(2):
                share(1, blk).wait_recv()
            lax.fori_loop(0, 2, down_grad_first, 0)

        arrivals(2, i)


        hp = mm(block(2, i), wu[...].reshape(width, 512)) + bias
        phi = 0.5 + 0.5 * lax.erf(hp * 0.7071067811865476)
        hid[pl.ds(pl.multiple_of(i * BLOCK, BLOCK), BLOCK), :] = (hp * phi).astype(BF16)
        gder[i] = phi + hp * jnp.exp(hp * hp * -0.5) * 0.3989422804014327
        return 0

    lax.fori_loop(0, 4, up_block, 0)
    weight_pass(*w_down_z)
    arrive(1, 2)
    share(1, 2).wait_recv()
    share(1, 3).wait_recv()

    def down_grad(f, _):
        cols = pl.ds(pl.multiple_of(f * BLOCK, BLOCK), BLOCK)
        g = gdf[pl.ds(pl.multiple_of(f * BLOCK, BLOCK), BLOCK), :] + mm(
            hid[2 * BLOCK:, cols], agf[1, 2:4].reshape(2 * BLOCK, width), TN
        )
        gds[pl.ds(2 * f, 2)] = g.astype(BF16).reshape(2, 128, width)
        return 0

    lax.fori_loop(0, 2, down_grad, 0)
    grad_start_some(*g_down_z, 3)
    grad_start_some(*g_down_z, 2)
    down_half(0)
    for i in range(4):
        for j in range(i + 1):
            upper = normed[j, :, i * BLOCK:(i + 1) * BLOCK].T
            if i != j:
                normed[j, :, i * BLOCK:(i + 1) * BLOCK] = normed[i, :, j * BLOCK:(j + 1) * BLOCK].T
            normed[i, :, j * BLOCK:(j + 1) * BLOCK] = upper
    def turn_second(i, _):
        cols = pl.ds(pl.multiple_of(i * BLOCK, BLOCK), BLOCK)
        blk = block(2, i)
        for f in range(4):
            sct[f, :, cols] = blk[:, f * BLOCK:(f + 1) * BLOCK].T
        return 0

    lax.fori_loop(0, 4, turn_second, 0)

    def even_out(n, _):
        i = n // 4
        rows = pl.ds(pl.multiple_of((n % 4) * BLOCK, BLOCK), BLOCK)
        pst[i, rows, :] = (pst[i, rows, :].astype(F32) * invl[i, 0:1, :]).astype(BF16)
        return 0

    lax.fori_loop(0, 16, even_out, 0)

    left(wo.at[pl.ds(0, 3)], wg_s.at[0])
    left(wo.at[pl.ds(0, 4)], wg_s.at[1])
    weight_sent(*w_out_z)

    def wo_block(i, j):
        return wo[2 * i:2 * i + 2, :, j * BLOCK:(j + 1) * BLOCK].reshape(BLOCK, BLOCK)

    for i in range(4):
        for j in range(i + 1):
            upper = wo_block(j, i).T.reshape(2, ROWS, BLOCK)
            if i != j:
                wo[2 * j:2 * j + 2, :, i * BLOCK:(i + 1) * BLOCK] = wo_block(i, j).T.reshape(2, ROWS, BLOCK)
            wo[2 * i:2 * i + 2, :, j * BLOCK:(j + 1) * BLOCK] = upper
    weight_finish(*w_down_z)
    gub[...] = jnp.zeros_like(gub)

    def back_block(n, _):
        i = 3 - n
        rows = pl.ds(pl.multiple_of(i * BLOCK, BLOCK), BLOCK)
        gp = (gder[i] * mm(block(1, i), wd[...].reshape(512, width), NT)).astype(BF16)
        put_part(0, i, mm(gp, wu[...].reshape(width, 512), NT))
        gpre[rows, :] = gp
        gub[...] += jnp.sum(gp.astype(F32).reshape(BLOCK // 8, 8, 512), axis=0)
        fold_before(0, i)
        return 0

    lax.fori_loop(0, 4, back_block, 0)
    fold(0, 0)

    def up_grad(f, _):
        g = mm(sct[pl.ds(2 * f, 2)].reshape(2 * BLOCK, 1024), gpre[...])
        gus[pl.ds(4 * f, 4)] = g.astype(BF16).reshape(4, 4, 32, 512)
        return 0

    grad_pass(*g_down_z)
    lax.fori_loop(0, 2, up_grad, 0)
    grad_start(*g_up_z)

    def out_block(n, _):
        i = 3 - n
        rows = pl.ds(pl.multiple_of(i * BLOCK, BLOCK), BLOCK)
        put_part(1, i, mm(hid[rows, :], wd[...].reshape(512, width)))
        fold_before(1, i)
        return 0

    send_last(0)
    lax.fori_loop(0, 4, out_block, 0)
    fold(1, 0)

    wait_sums(0)
    acc[...] = jnp.zeros_like(acc)

    def add_row(n, v):
        acc[n] += jnp.sum(v.reshape(INNER // 8, 8, width), axis=0)

    def norm_back(v, grad, gain):
        xhat, rstd = stats(v)
        d = grad * gain
        mean_d = jnp.mean(d, axis=-1, keepdims=True)
        mean_dx = jnp.mean(d * xhat, axis=-1, keepdims=True)
        return rstd * (d - mean_d - xhat * mean_dx), xhat

    def second_chunk(j, _):
        rows = pl.ds(pl.multiple_of(j * INNER, INNER), INNER)
        gs = plane_total(0, j)
        g, xhat = norm_back(mid[rows, :], gs, gain2)
        ct = own_rows(1, j)
        gm = ct + g
        gmid[rows, :] = gm
        gb = gm.astype(BF16)
        set_rows(3, j, gb)
        add_row(1, gs * xhat)
        add_row(6, gs)
        return 0

    grad_pass_on(*g_down_z)
    lax.fori_loop(0, ROWS // INNER, second_chunk, 0)
    gbo = agf[3, 0, :, c].reshape(ROWS, width)
    gha = mm(gbo, wo[...].reshape(width, 1024)).astype(BF16)
    for d in range(PLANE):
        dsend[d] = gha[:, d * 128:(d + 1) * 128]
    for i, a in GRANULES:
        for k in cores(i):
            back_copy(i, a, k).start()
    for h in (0, 1):
        dob[0, h, c] = dsend[b, h * HALF:(h + 1) * HALF, :]
    start_gather(3)

    grad_pass(*g_up_z)
    dk[...] = jnp.zeros_like(dk)
    dv[...] = jnp.zeros_like(dv)
    goa[...] = jnp.zeros_like(goa)

    def attend_back(i, _):
        for blk in range(4):
            @pl.when(i == blk)
            def _():
                landed(dob.at[blk] if blk else dob.at[0, :, 0], g_r.at[blk])

        do_rows = dob[i].reshape(BLOCK, 128)
        do_cols = do_rows.T.astype(F32)
        prod = do_cols * ot[i]
        delta = jnp.concatenate(
            [jnp.sum(prod[h * 64:(h + 1) * 64], axis=0, keepdims=True) for h in range(2)], axis=1
        )
        zero = jnp.zeros((64, BLOCK), F32)
        spread_cols = jnp.concatenate([
            jnp.concatenate([do_cols[0:64], zero], axis=0),
            jnp.concatenate([zero, do_cols[64:128]], axis=0),
        ], axis=1).astype(BF16)
        spread_rows = jnp.concatenate(
            [(do_rows.astype(F32) * head_lane[h]).astype(BF16) for h in range(2)], axis=0
        )
        pb = pst[i]
        ds = (pb.astype(F32) * (mm(vv[...], spread_cols) - delta)).astype(BF16)
        dv[...] += mm(pb, spread_rows)
        dk[...] += mm(ds, qaug[i, :, 0:128])
        dq = mm(kt[...], ds)
        dq = jnp.concatenate([dq[0:64, 0:BLOCK], dq[64:128, BLOCK:]], axis=0).T * 0.125
        gproj[pl.ds(pl.multiple_of(i * BLOCK, BLOCK), BLOCK), 0:128] = dq.astype(BF16)
        return 0

    lax.fori_loop(0, 4, attend_back, 0)
    gproj[:, 128:256] = dk[...].astype(BF16)
    gproj[:, 256:384] = dv[...].astype(BF16)

    gqs[...] = mm(normed[...].reshape(1024, 1024), gproj[...]).astype(BF16).reshape(8, 4, 32, 384)
    grad_start_some(*g_qkv_z, 3)
    grad_start_some(*g_qkv_z, 2)
    grad_pass_on(*g_up_z)
    arrive(3, 1)

    def project_back(n, _):
        i = 3 - n
        rows = pl.ds(pl.multiple_of(i * BLOCK, BLOCK), BLOCK)
        put_part(2, i, mm(gproj[rows, :], wq[...].reshape(width, 384), NT))

        @pl.when(n == 2)
        def _():
            fold(2, 3)
            send_far(2)

        @pl.when(n == 3)
        def _():
            fold(2, 2)
            send_near(2, 2)

        return 0

    lax.fori_loop(0, 4, project_back, 0)
    fold(2, 1)
    fold(2, 0)
    arrive(3, 2)
    share(3, 0).wait_recv()
    arrive(3, 3)
    grad_pass(*g_qkv_z)
    def out_grad(i, _):
        for blk in (1, 2, 3):
            @pl.when(i == blk)
            def _():
                share(3, blk).wait_recv()

        goa[...] += mm(att[i], block(3, i), TN)
        return 0

    lax.fori_loop(0, 4, out_grad, 0)
    gos[...] = goa[...].astype(BF16).reshape(4, 32, width)
    grad_start_some(*g_out_z, 3)
    grad_start_some(*g_out_z, 2)
    grad_start_some(*g_qkv_z, 1)
    grad_start_some(*g_out_z, 1)
    down_half(1)
    send_last(2)
    send_last(1)

    def others(kind, stage, got, via, pieces):
        return [got(s), via]

    grad_pass(*g_out_z)
    grad_pass_on(*g_qkv_z)
    def own_sums(j, _):
        add_row(5, own_rows(3, j))
        add_row(7, own_rows(1, j))
        return 0

    lax.fori_loop(0, ROWS // INNER, own_sums, 0)
    wait_sums(2)

    def first_chunk(j, _):
        rows = pl.ds(pl.multiple_of(j * INNER, INNER), INNER)
        gn = plane_total(2, j)
        g, xhat = norm_back(own_rows(0, j) + lead_row, gn, gain1)
        ge = gmid[rows, :] + g
        ig_o[rows, :] = ge.astype(BF16)
        add_row(0, gn * xhat)
        add_row(2, gn)
        add_row(9, ge)
        return 0

    lax.fori_loop(0, ROWS // INNER, first_chunk, 0)
    deliver(1).start()
    acc[8] = acc[9] * lead_days

    sums = [jnp.sum(acc[n], axis=0, keepdims=True) for n in range(10)]
    packed = jnp.concatenate(sums + [jnp.zeros((6, width), F32)], axis=0)
    for d in range(PLANE):
        vs[d] = packed[:, d * 128:(d + 1) * 128]

    def vec_swap(k):
        return rc(vs.at[peer(k)], vsr.at[k - 1], v_s.at[1], v_r.at[1], peer(k), s)

    for k in range(1, PLANE):
        vec_swap(k).start()
    gq_cols = jnp.sum(gproj[:, 0:128].astype(F32), axis=0, keepdims=True)
    gv_cols = jnp.sum(gproj[:, 256:384].astype(F32), axis=0, keepdims=True)
    gub_row = jnp.sum(gub[...], axis=0, keepdims=True)
    extra = jnp.concatenate(
        [jnp.zeros((3, 128), F32), gq_cols, gv_cols, jnp.zeros((6, 128), F32)]
        + [gub_row[:, j * 128:(j + 1) * 128] for j in range(4)]
        + [jnp.zeros((1, 128), F32)],
        axis=0,
    )
    grad_finish(*g_up_z)
    for d in range(PLANE):
        gu2[d] = sum(
            [t[d].astype(F32) for t in others(*g_up_z)], gus[d, s].astype(F32)
        ).astype(BF16)
    for k in range(1, PLANE):
        swap(2, k, gu2.at[peer(k)], gua.at[b]).start()
    gua[b] = gu2[b]
    grad_pass_on(*g_out_z)
    landed(vs.at[pl.ds(0, 7)], v_r.at[1])
    total = vs[b] + extra
    for k in range(PLANE - 1):
        total = total + vsr[k]
    vz[...] = total
    for k in range(1, DEPTH):
        yc(1, k, vz, vzr.at[k - 1]).start()

    wait_sums(1)

    def output_chunk(j, _):
        rows = pl.ds(pl.multiple_of(j * INNER, INNER), INNER)
        out_o[rows, :] = (mid[rows, :] + plane_total(1, j) + shift_down).astype(BF16)
        return 0

    lax.fori_loop(0, ROWS // INNER, output_chunk, 0)
    deliver(0).start()

    grad_finish(*g_qkv_z)
    for d in range(PLANE):
        gq2[d] = sum(
            [t[d].astype(F32) for t in others(*g_qkv_z)], gqs[d, s].astype(F32)
        ).astype(BF16)
    for k in range(1, PLANE):
        swap(3, k, gq2.at[peer(k)], gqa.at[b]).start()
    gqa[b] = gq2[b]
    grad_finish(*g_out_z)
    gout_o[...] = sum([t[...].astype(F32) for t in others(*g_out_z)], gos[s].astype(F32))
    deliver(3).start()
    grad_finish(*g_down_z)
    gdown_o[...] = sum([t[...].astype(F32) for t in others(*g_down_z)], gds[s].astype(F32))
    deliver(5).start()
    landed(gu2.at[pl.ds(0, 7)], aq_r.at[2])
    for d in range(PLANE):
        gup_o[:, d * 512:(d + 1) * 512] = gua[d].astype(F32)
    deliver(4).start()
    landed(vzr, y_r.at[1])
    vz_sum = vz[...] + vzr[0] + vzr[1] + vzr[2]
    columns = pltpu.roll(vz_sum, (128 - 32 * s) % 128, 1)
    gain_o[...] = columns[0:2, 0:32]
    shift_o[...] = columns[2:8, 0:32]
    lead_o[...] = columns[8:10, 0:32]
    bias_o[...] = jnp.sum(jnp.where(line == 11 + s, vz_sum, 0.0), axis=0, keepdims=True)
    for n in range(6, 10):
        deliver(n).start()
    landed(gq2.at[pl.ds(0, 7)], aq_r.at[3])
    for d in range(PLANE):
        for j in range(3):
            gqkv_o[:, j * width + d * 128:j * width + (d + 1) * 128] = (
                gqa[d, :, j * 128:(j + 1) * 128].astype(F32)
            )

    deliver(2).start()
    for op in range(4):
        left(agf.at[op, pl.ds(0, 3), :, 0], ag_s.at[op])
        left(agf.at[op, :, :, 0], fw_s.at[op])
    for op in range(3):
        end_sums(op)
    left(aown.at[pl.ds(0, 7)], h_s.at[0])
    left(dsend.at[pl.ds(0, 7)], g_s.at[0])
    for kind, sent in enumerate((sq, su, gu2, gq2)):
        left(sent.at[pl.ds(0, 7)], aq_s.at[kind])
    left(vecf.at[pl.ds(0, 7)], v_s.at[0])
    left(vs.at[pl.ds(0, 7)], v_s.at[1])
    left(ztr, y_s.at[0])
    left(vzr, y_s.at[1])
    for moved in (w_qkv_z, w_up_z, w_down_z):
        weight_sent(*moved)
    for moved in (g_down_z, g_up_z, g_qkv_z, g_out_z):
        grad_sent(*moved)
    for n in range(10):
        deliver(n).wait()


def hand_over(*refs):
    count = len(refs) // 3
    given, taken, held, sems = refs[:count], refs[count:2 * count], refs[2 * count:3 * count], refs[-1]
    into = [pltpu.make_async_copy(given[n], held[n], sems.at[0, n]) for n in range(count)]
    out = [pltpu.make_async_copy(held[n], taken[n], sems.at[1, n]) for n in range(count)]
    for copy in into:
        copy.start()
    for n in range(count):
        into[n].wait()
        out[n].start()
    for copy in out:
        copy.wait()


def plane_body(
    tokens, cotangent, w_qkv, w_out, w_up, w_down,
    up_bias, norm_gains, shift_rows, lead_weight, lead_steps, valid_cells,
):
    width = tokens.shape[2]
    vmem = pl.BlockSpec(memory_space=pltpu.VMEM)
    anywhere = pl.BlockSpec(memory_space=pl.ANY)
    dma = pltpu.SemaphoreType.DMA
    V = pltpu.VMEM
    out_shape = (
        jax.ShapeDtypeStruct((ROWS, width), BF16),
        jax.ShapeDtypeStruct((ROWS, width), BF16),
        jax.ShapeDtypeStruct((32, 3 * width), F32),
        jax.ShapeDtypeStruct((32, width), F32),
        jax.ShapeDtypeStruct((32, 4 * width), F32),
        jax.ShapeDtypeStruct((128, width), F32),
        jax.ShapeDtypeStruct((2, 32), F32),
        jax.ShapeDtypeStruct((6, 32), F32),
        jax.ShapeDtypeStruct((2, 32), F32),
        jax.ShapeDtypeStruct((1, 128), F32),
    )
    scratch = [
        V((ROWS, width), BF16), V((ROWS, width), BF16),
        V((32, 3 * width), F32), V((32, width), F32),
        V((32, 4 * width), F32), V((128, width), F32),
        V((2, 32), F32), V((6, 32), F32), V((2, 32), F32), V((1, 128), F32),
        V((32, 3 * width), BF16), V((32, 4 * width), BF16),
        V((16, 128), F32), V((2, 16, 128), BF16),
        V((4, 4, 2, 2, HALF, width), BF16),
        V((PLANE, DEPTH, 32, 384), BF16),
        V((PLANE, 128, width), BF16),
        V((PLANE, DEPTH, 32, 512), BF16),
        V((DEPTH, 128, width), BF16),
        V((PLANE, 32, 384), BF16),
        V((PLANE, 32, 512), BF16),
        V((3, 16, 128), BF16),
        V((16, 128), BF16),
        V((PLANE, 16, 128), BF16),
        V((16, width), F32),
        V((4, BLOCK, width), BF16),
        V((4, 2 * BLOCK, 256), BF16),
        V((1024, 256), BF16),
        V((128, 1024), BF16),
        V((1024, 128), BF16),
        V((128, 1024), BF16),
        V((4, 1024, 2 * BLOCK), BF16),
        V((4, 128, BLOCK), F32),
        V((4, 8, 2 * BLOCK), F32),
        V((4, BLOCK, 128), BF16),
        V((PLANE, ROWS, 128), BF16),
        V((PLANE, ROWS, 128), BF16),
        V((4, 2, 2, HALF, 128), BF16),
        V((1024, 384), BF16),
        V((1024, 128), F32),
        V((1024, 128), F32),
        V((1024, 512), BF16),
        V((4, BLOCK, 512), F32),
        V((1024, 512), BF16),
        V((ROWS, width), F32),
        V((ROWS, width), F32),
        V((512, width), F32),
        V((4, BLOCK, 1024), BF16),
        V((3, 4, 2, 2, HALF, width), BF16),
        V((3, 4, 2, HALF, width), BF16),
        V((3, 4, 2, HALF, width), BF16),
        V((3, 2, HALF, width), BF16),
        V((3, 2, 2, HALF, width), BF16),
        V((DEPTH, 128, width), BF16),
        V((PLANE, DEPTH, 32, 512), BF16),
        V((PLANE, DEPTH, 32, 384), BF16),
        V((DEPTH, 32, width), BF16),
        V((DEPTH, 128, width), BF16),
        V((DEPTH, PLANE, 32, 512), BF16),
        V((DEPTH, PLANE, 32, 384), BF16),
        V((DEPTH, 32, width), BF16),
        V((128, width), BF16),
        V((PLANE, 32, 512), BF16),
        V((PLANE, 32, 384), BF16),
        V((32, width), BF16),
        V((PLANE, 32, 512), BF16),
        V((PLANE, 32, 384), BF16),
        V((PLANE, 32, 512), BF16),
        V((PLANE, 32, 384), BF16),
        V((128, width), F32),
        V((10, 8, width), F32),
        V((8, 512), F32),
        V((PLANE, 16, 128), F32),
        V((PLANE - 1, 16, 128), F32),
        V((16, 128), F32),
        V((3, 16, 128), F32),
        dma((8,)), dma((10,)),
        dma((4,)), dma((4, 2)), dma((4,)), dma((4,)), dma((4, 4)),
        dma((4,)), dma((4,)), dma((2,)), dma((2,)), dma((2,)), dma((2,)),
        dma((4,)), dma((4, 3)), dma((4,)), dma((4, 5)),
        dma((3,)), dma((3, 4)), dma((3,)), dma((3,)), dma((3,)),
        dma((2,)), dma((4,)), dma((1,)), dma((1,)), dma((1,)), dma((4,)),
    ]
    results = pl.pallas_call(
        plane_kernel,
        out_shape=out_shape,
        in_specs=[pl.BlockSpec(memory_space=pltpu.SMEM)] + [vmem] * 5 + [anywhere] * 6,
        out_specs=tuple([anywhere] * 10),
        scratch_shapes=scratch,
        compiler_params=pltpu.CompilerParams(
            collective_id=0, has_side_effects=True, vmem_limit_bytes=63 * 2**20
        ),
    )(
        lead_steps, norm_gains, shift_rows, lead_weight, up_bias[None], valid_cells,
        tokens[0], cotangent[0], w_qkv, w_out, w_up, w_down,
    )
    results = pl.pallas_call(
        hand_over,
        out_shape=out_shape,
        in_specs=[anywhere] * len(out_shape),
        out_specs=tuple([anywhere] * len(out_shape)),
        scratch_shapes=[V(o.shape, o.dtype) for o in out_shape] + [dma((2, len(out_shape)))],
    )(*results)
    output, input_grad, g_qkv, g_out, g_up, g_down, g_gains, g_shifts, g_lead, g_bias = results
    return (
        output[None], input_grad[None], g_qkv, g_out, g_up, g_down, g_bias[0],
        g_gains, g_shifts, g_lead,
    )


def plane_fits(mesh):
    return mesh.shape["band"] == PLANE and mesh.shape["samp"] == DEPTH


def solution(mesh):
    return jax.shard_map(
        plane_body if plane_fits(mesh) else body,
        mesh=mesh,
        in_specs=(
            P("samp", "band", None),
            P("samp", "band", None),
            P(("band", "samp"), None),
            P(("band", "samp"), None),
            P(("band", "samp"), None),
            P(("band", "samp"), None),
            P(("band", "samp")),
            P(None, ("band", "samp")),
            P(None, ("band", "samp")),
            P(None, ("band", "samp")),
            P("samp"),
            P("samp", "band"),
        ),
        out_specs=(
            P("samp", "band", None),
            P("samp", "band", None),
            P(("band", "samp"), None),
            P(("band", "samp"), None),
            P(("band", "samp"), None),
            P(("band", "samp"), None),
            P(("band", "samp")),
            P(None, ("band", "samp")),
            P(None, ("band", "samp")),
            P(None, ("band", "samp")),
        ),
        check_vma=False,
    )
```

```python
import jax
import jax.numpy as jnp
from jax import lax
from jax.experimental import pallas as pl
from jax.experimental.pallas import tpu as pltpu
from jax.sharding import PartitionSpec as P

HEADS = 16


eps = 1e-05
masked = 10000.0


def layer_norm(values, gain_row, shift_row):
    centered = values - jnp.mean(values, axis=-1, keepdims=True)
    variance = jnp.mean(centered * centered, axis=-1, keepdims=True)
    return centered * lax.rsqrt(variance + eps) * gain_row + shift_row


def gelu_exact(values):
    return jax.nn.gelu(values, approximate=False)


def body(
    tokens,
    cotangent,
    w_qkv,
    w_out,
    w_up,
    w_down,
    up_bias,
    norm_gains,
    shift_rows,
    lead_weight,
    lead_steps,
    valid_cells,
):
    whole = (
        lax.all_gather(w_qkv, ("band", "samp"), axis=0, tiled=True),
        lax.all_gather(w_out, ("band", "samp"), axis=0, tiled=True),
        lax.all_gather(w_up, ("band", "samp"), axis=0, tiled=True),
        lax.all_gather(w_down, ("band", "samp"), axis=0, tiled=True),
        lax.all_gather(up_bias, ("band", "samp"), axis=0, tiled=True),
        lax.all_gather(norm_gains, ("band", "samp"), axis=1, tiled=True),
        lax.all_gather(shift_rows, ("band", "samp"), axis=1, tiled=True),
        lax.all_gather(lead_weight, ("band", "samp"), axis=1, tiled=True),
    )
    qkv_full = whole[0]
    out_full = whole[1]
    up_full = whole[2]
    down_full = whole[3]
    up_shift = whole[4].astype(jnp.float32)
    gain_all = whole[5].astype(jnp.float32)
    shift_all = whole[6].astype(jnp.float32)
    lead_all = whole[7].astype(jnp.float32)
    row_count = tokens.shape[1]
    width = tokens.shape[2]
    head_count = HEADS
    head_size = width // head_count
    score_scale = head_size ** (-0.5)
    lead_days = lead_steps[0].astype(jnp.float32) * 0.25
    entering = tokens[0].astype(jnp.float32) + lead_days * lead_all[0] + lead_all[1]
    normed, norm_first_back = jax.vjp(layer_norm, entering, gain_all[0], shift_all[0])
    normed_low = normed.astype(jnp.bfloat16)
    project = jnp.dot(normed_low, qkv_full, preferred_element_type=jnp.float32)
    queries = (project[:, :width] + shift_all[1]).astype(jnp.bfloat16)
    key_rows = project[:, width : 2 * width].astype(jnp.bfloat16)
    value_rows = (project[:, 2 * width :] + shift_all[2]).astype(jnp.bfloat16)
    key_open = (valid_cells[0] > 0).astype(jnp.bfloat16)
    keys_all, values_all, open_all = (
        lax.all_gather(key_rows, "band", axis=0, tiled=True),
        lax.all_gather(value_rows, "band", axis=0, tiled=True),
        lax.all_gather(key_open, "band", axis=0, tiled=True),
    )
    seq_total = keys_all.shape[0]
    block_rows = min(512, seq_total)
    block_count = seq_total // block_rows
    block_ids = jnp.arange(block_count)
    bias_all = (open_all.astype(jnp.float32) - 1.0) * masked
    query_heads = queries.reshape(row_count, head_count, head_size)

    def block_keys(step_index):
        first_row = step_index * block_rows
        key_block = lax.dynamic_slice_in_dim(keys_all, first_row, block_rows, 0).reshape(
            block_rows, head_count, head_size
        )
        value_block = lax.dynamic_slice_in_dim(values_all, first_row, block_rows, 0).reshape(
            block_rows, head_count, head_size
        )
        bias_block = lax.dynamic_slice_in_dim(bias_all, first_row, block_rows, 0)
        scores = (
            jnp.einsum("qhe,khe->hqk", query_heads, key_block, preferred_element_type=jnp.float32)
            * score_scale
            + bias_block
        )
        return (scores, key_block, value_block)

    def max_step(running, step_index):
        row_max, exp_total = running
        scores = block_keys(step_index)[0]
        new_max = jnp.maximum(row_max, jnp.max(scores, axis=-1))
        exp_total = exp_total * jnp.exp(row_max - new_max) + jnp.sum(
            jnp.exp(scores - new_max[..., None]), axis=-1
        )
        return ((new_max, exp_total), None)

    start_max = jnp.full((head_count, row_count), -jnp.inf, jnp.float32)
    start_total = jnp.zeros((head_count, row_count), jnp.float32)
    row_max, exp_total = lax.scan(max_step, (start_max, start_total), block_ids)[0]
    log_total = row_max + jnp.log(exp_total)

    def out_step(running, step_index):
        scores, key_block, value_block = block_keys(step_index)
        weights_low = jnp.exp(scores - log_total[..., None]).astype(jnp.bfloat16)
        return (
            running
            + jnp.einsum(
                "hqk,khe->qhe", weights_low, value_block, preferred_element_type=jnp.float32
            ),
            None,
        )

    attended_heads = lax.scan(
        out_step, jnp.zeros((row_count, head_count, head_size), jnp.float32), block_ids
    )[0]
    attended_low = attended_heads.reshape(row_count, width).astype(jnp.bfloat16)
    middle = (
        entering
        + jnp.dot(attended_low, out_full, preferred_element_type=jnp.float32)
        + shift_all[3]
    )
    second, norm_second_back = jax.vjp(layer_norm, middle, gain_all[1], shift_all[4])
    second_low = second.astype(jnp.bfloat16)
    hidden_pre = jnp.dot(second_low, up_full, preferred_element_type=jnp.float32) + up_shift
    hidden, gelu_back = jax.vjp(gelu_exact, hidden_pre)
    hidden_low = hidden.astype(jnp.bfloat16)
    result = (
        middle + jnp.dot(hidden_low, down_full, preferred_element_type=jnp.float32) + shift_all[5]
    )
    output = result.astype(jnp.bfloat16)
    grad_result = cotangent[0]
    grad_result_f = grad_result.astype(jnp.float32)
    grad_down_w = jnp.einsum(
        "tf,td->fd", hidden_low, grad_result, preferred_element_type=jnp.float32
    )
    grad_shift_down = jnp.sum(grad_result_f, axis=0)
    grad_hidden = jnp.einsum(
        "td,fd->tf", grad_result, down_full, preferred_element_type=jnp.float32
    )
    grad_pre_low = gelu_back(grad_hidden)[0].astype(jnp.bfloat16)
    grad_up_w = jnp.einsum(
        "td,tf->df", second_low, grad_pre_low, preferred_element_type=jnp.float32
    )
    grad_up_shift = jnp.sum(grad_pre_low.astype(jnp.float32), axis=0)
    grad_second = jnp.einsum("tf,df->td", grad_pre_low, up_full, preferred_element_type=jnp.float32)
    grad_middle_norm, grad_gain_second, grad_shift_second = norm_second_back(grad_second)
    grad_middle = grad_result_f + grad_middle_norm
    ffn_sums = (
        lax.psum_scatter(grad_up_w, ("band", "samp"), scatter_dimension=0, tiled=True),
        lax.psum_scatter(grad_down_w, ("band", "samp"), scatter_dimension=0, tiled=True),
        lax.psum_scatter(grad_up_shift, ("band", "samp"), scatter_dimension=0, tiled=True),
    )
    grad_branch = grad_middle.astype(jnp.bfloat16)
    grad_shift_out = jnp.sum(grad_branch.astype(jnp.float32), axis=0)
    grad_out_w = jnp.einsum(
        "td,te->de", attended_low, grad_branch, preferred_element_type=jnp.float32
    )
    grad_attended = jnp.einsum(
        "te,de->td", grad_branch, out_full, preferred_element_type=jnp.float32
    ).astype(jnp.bfloat16)
    grad_heads = grad_attended.reshape(row_count, head_count, head_size)
    delta = jnp.einsum("qhe,qhe->hq", grad_heads.astype(jnp.float32), attended_heads)
    zero_heads = jnp.zeros((row_count, head_count, head_size), jnp.float32)

    def key_grad_step(g_queries, step_index):
        scores, key_block, value_block = block_keys(step_index)
        weights_full = jnp.exp(scores - log_total[..., None])
        g_weights = jnp.einsum(
            "qhe,khe->hqk", grad_heads, value_block, preferred_element_type=jnp.float32
        )
        g_scores = (weights_full * (g_weights - delta[..., None])).astype(jnp.bfloat16)
        g_queries = (
            g_queries
            + jnp.einsum("hqk,khe->qhe", g_scores, key_block, preferred_element_type=jnp.float32)
            * score_scale
        )
        key_term = (
            jnp.einsum("hqk,qhe->khe", g_scores, query_heads, preferred_element_type=jnp.float32)
            * score_scale
        )
        value_term = jnp.einsum(
            "hqk,qhe->khe",
            weights_full.astype(jnp.bfloat16),
            grad_heads,
            preferred_element_type=jnp.float32,
        )
        return (
            g_queries,
            (key_term.reshape(block_rows, width), value_term.reshape(block_rows, width)),
        )

    grad_query_heads, block_terms = lax.scan(key_grad_step, zero_heads, block_ids)
    grad_query_f = grad_query_heads.reshape(row_count, width)
    key_sum, value_sum = (
        lax.psum_scatter(
            block_terms[0].reshape(seq_total, width), "band", scatter_dimension=0, tiled=True
        ),
        lax.psum_scatter(
            block_terms[1].reshape(seq_total, width), "band", scatter_dimension=0, tiled=True
        ),
    )
    grad_query_low = grad_query_f.astype(jnp.bfloat16)
    grad_key_low = key_sum.astype(jnp.bfloat16)
    grad_value_low = value_sum.astype(jnp.bfloat16)
    grad_project = jnp.concatenate([grad_query_low, grad_key_low, grad_value_low], axis=-1)
    grad_qkv_w = jnp.einsum(
        "td,te->de", normed_low, grad_project, preferred_element_type=jnp.float32
    )
    grad_shift_query = jnp.sum(grad_query_low.astype(jnp.float32), axis=0)
    grad_shift_value = jnp.sum(grad_value_low.astype(jnp.float32), axis=0)
    grad_normed = jnp.einsum(
        "te,de->td", grad_project, qkv_full, preferred_element_type=jnp.float32
    )
    grad_entering_norm, grad_gain_first, grad_shift_first = norm_first_back(grad_normed)
    grad_entering = grad_middle + grad_entering_norm
    input_grad = grad_entering.astype(jnp.bfloat16)
    entering_sum = jnp.sum(grad_entering, axis=0)
    grad_lead_rows = jnp.stack([lead_days * entering_sum, entering_sum])
    grad_gain_rows = jnp.stack([grad_gain_first, grad_gain_second])
    grad_shift_stack = jnp.stack(
        [
            grad_shift_first,
            grad_shift_query,
            grad_shift_value,
            grad_shift_out,
            grad_shift_second,
            grad_shift_down,
        ]
    )
    attention_sums = (
        lax.psum_scatter(grad_qkv_w, ("band", "samp"), scatter_dimension=0, tiled=True),
        lax.psum_scatter(grad_out_w, ("band", "samp"), scatter_dimension=0, tiled=True),
        lax.psum_scatter(grad_gain_rows, ("band", "samp"), scatter_dimension=1, tiled=True),
        lax.psum_scatter(grad_shift_stack, ("band", "samp"), scatter_dimension=1, tiled=True),
        lax.psum_scatter(grad_lead_rows, ("band", "samp"), scatter_dimension=1, tiled=True),
    )
    return (
        output[None],
        input_grad[None],
        attention_sums[0],
        attention_sums[1],
        ffn_sums[0],
        ffn_sums[1],
        ffn_sums[2],
        attention_sums[2],
        attention_sums[3],
        attention_sums[4],
    )


MESH = pl.DeviceIdType.MESH
F32 = jnp.float32
BF16 = jnp.bfloat16
PLANE = 8
DEPTH = 4
ROWS = 128
HALF = 64
BLOCK = 256
NN = (((1,), (0,)), ((), ()))
NT = (((1,), (1,)), ((), ()))
TN = (((0,), (0,)), ((), ()))
INNER = 32


def mm(left, right, dims=NN):
    return lax.dot_general(left, right, dims, preferred_element_type=F32)


def plane_kernel(
    lead_ref, gain_in, shift_in, leadw_in, bias_in, valid_in,
    tok_in, cot_in, wqkv_in, wout_in, wup_in, wdown_in,
    out_h, ig_h, gqkv_h, gout_h, gup_h, gdown_h, gain_h, shift_h, lead_h, bias_h,
    out_o, ig_o, gqkv_o, gout_o, gup_o, gdown_o, gain_o, shift_o, lead_o, bias_o,
    wqkv, wup, vcol, vec_in,
    agf, tokown, gbown, wq, wo, wu, wd, sq, su, ztr, vt, vecf, vrow,
    normed, qaug, kaug, kt, vv, vt2, pst, ot, invl, att, aown, dsend, dob, gsend, gcol, gproj, dk, dv,
    hid, gder, gpre, mid, gmid, gdf, sct,
    part, pr, cs, au, rr,
    gds, gus, gqs, gos, gdr, gur, gqr, gor_, gda, guc, gqc, goc, go2, go3, gu2, gq2, gua, gqa,
    acc, gub, vs, vsr, vz, vzr,
    in_s, out_s, ag_s, ag_r, ac_r, fw_s, fw_r, aq_s, aq_r, v_s, v_r, y_s, y_r, w_s, w_r, z_s, z_r,
    p_s, p_r, f_r, n_s, n_r, wg_s, wg_r, h_s, h_r, g_s, g_r, gc_s, gc_r,
):
    b = lax.axis_index("band")
    s = lax.axis_index("samp")
    c = b % 2
    x = (b // 2) % 2
    y = b // 4
    mate = b + 1 - 2 * c

    def chip(r):
        xx = x + (r % 2) * (1 - 2 * x)
        yy = y + (r // 2) * (1 - 2 * y)
        return yy * 2 + xx

    def near(r):
        return chip(r) * 2 + c

    def peer(k):
        return (b + k) % PLANE

    def level(k):
        return (s + k) % DEPTH

    barrier = pltpu.get_barrier_semaphore()
    for k in range(1, PLANE):
        pl.semaphore_signal(barrier, inc=1, device_id=(peer(k), s), device_id_type=MESH)
    for k in range(1, DEPTH):
        pl.semaphore_signal(barrier, inc=1, device_id=(b, level(k)), device_id_type=MESH)

    width = tok_in.shape[1]
    fetches = [
        pltpu.make_async_copy(src, dst, in_s.at[n])
        for n, (src, dst) in enumerate((
            (wqkv_in, wqkv), (wout_in, wo.at[b, pl.ds(pl.multiple_of(s * 32, 32), 32)]),
            (tok_in.at[pl.ds(0, HALF)], agf.at[0, 0, 0, c]),
            (tok_in.at[pl.ds(HALF, HALF)], agf.at[0, 0, 1, c]),
            (wup_in, wup), (wdown_in, wd.at[s]),
            (cot_in.at[pl.ds(0, HALF)], agf.at[1, 0, 0, c]),
            (cot_in.at[pl.ds(HALF, HALF)], agf.at[1, 0, 1, c]),
        ))
    ]
    for fetch in fetches:
        fetch.start()
    vcol[...] = jnp.zeros_like(vcol)
    vcol[0:2, 0:32] = gain_in[...].astype(F32)
    vcol[2:8, 0:32] = shift_in[...].astype(F32)
    vcol[8:10, 0:32] = leadw_in[...].astype(F32)
    line = lax.broadcasted_iota(jnp.int32, (16, 128), 0)
    tile = pltpu.roll(vcol[...], s * 32, 1)
    tile = jnp.where(line == 11 + s, bias_in[...].astype(F32), tile)
    vec_in[0] = tile.astype(BF16)
    opened = jnp.where(valid_in[...] > 0, 1.0, 0.0)
    vec_in[1] = jnp.where(line == 10, opened, 0.0).astype(BF16)
    far = (s + 2) % DEPTH
    ends = (s == 0) | (s == DEPTH - 1)
    inner = (s > 0) & (s < DEPTH - 1)

    @pl.when(s == 0)
    def _():
        for kept in (gdr, gur, gqr, gor_):
            kept[0] = jnp.zeros(kept.shape[1:], BF16)

    @pl.when(s == DEPTH - 1)
    def _():
        for kept in (gda, guc, gqc, goc):
            kept[...] = jnp.zeros(kept.shape, BF16)

    fetches[0].wait()
    for d in range(PLANE):
        for j in range(3):
            sq[d, :, j * 128:(j + 1) * 128] = wqkv[:, j * width + d * 128:j * width + (d + 1) * 128]
    fetches[1].wait()
    pl.semaphore_wait(barrier, PLANE - 1 + DEPTH - 1)

    def rc(src, dst, ss, rs, band, samp):
        return pltpu.make_async_remote_copy(
            src_ref=src, dst_ref=dst, send_sem=ss, recv_sem=rs,
            device_id=(band, samp), device_id_type=MESH,
        )

    def landed(ref, sem):
        rc(ref, ref, aq_s.at[0], sem, mate, s).wait_recv()

    def left(ref, sem):
        rc(ref, ref, sem, aq_r.at[0], mate, s).wait_send()

    def yc(kind, k, src, dst):
        return rc(src, dst, y_s.at[kind], y_r.at[kind], b, level(k))

    def weight_copy(kind, region, pieces, role, to):
        return rc(region(s), region(s), w_s.at[kind], w_r.at[kind, role], b, to)

    def weight_hand(kind, region, pieces):
        return rc(region(far), region(far), w_s.at[kind], w_r.at[kind, 2], b, 3 * (s - 1))

    def weight_start(*moved):
        @pl.when(s == 1)
        def _():
            weight_copy(*moved, 1, s - 1).start()

        weight_copy(*moved, 0, far).start()

        @pl.when(ends)
        def _():
            weight_copy(*moved, 1, 1 + s // 3).start()

        @pl.when(s == 2)
        def _():
            weight_copy(*moved, 1, s + 1).start()

        @pl.when(inner)
        def _():
            weight_copy(*moved, 2, DEPTH - 1 - s).start()

    def weight_pass(kind, region, pieces):
        @pl.when(inner)
        def _():
            landed(region(far), w_r.at[kind, 0])
            weight_hand(kind, region, pieces).start()

    def weight_most(kind, region, pieces):
        landed(region(DEPTH - 1 - far), w_r.at[kind, 1])

        @pl.when(ends)
        def _():
            landed(region(far), w_r.at[kind, 0])

    def weight_last(kind, region, pieces):
        landed(region(DEPTH - 1 - s), w_r.at[kind, 2])

    def weight_finish(*moved):
        weight_most(*moved)
        weight_last(*moved)

    def weight_sent(kind, region, pieces):
        @pl.when(ends)
        def _():
            left(pieces(2), w_s.at[kind])

        @pl.when(inner)
        def _():
            left(pieces(4), w_s.at[kind])

    def grad_up(kind, stage, got, via, pieces, t):
        return rc(stage(t), got(t), z_s.at[kind], z_r.at[kind, t], b, s + 1)

    def grad_down_to(kind, stage, got, via, pieces, t):
        return rc(stage(t), got(t), z_s.at[kind], z_r.at[kind, t], b, s - 1)

    def grad_down_last(kind, stage, got, via, pieces):
        return rc(stage(s - 1), via, z_s.at[kind], z_r.at[kind, DEPTH], b, s - 1)

    def grad_start(*moved):
        for hops in (3, 2, 1):
            grad_start_some(*moved, hops)

    def grad_start_some(kind, stage, got, via, pieces, hops):
        @pl.when(s == 0)
        def _():
            grad_up(kind, stage, got, via, pieces, hops).start()

        @pl.when(s == DEPTH - 1)
        def _():
            if hops == 1:
                grad_down_last(kind, stage, got, via, pieces).start()
            else:
                grad_down_to(kind, stage, got, via, pieces, DEPTH - 1 - hops).start()

    def down_half(half):
        rows = pl.ds(half * HALF, HALF)

        @pl.when(s == 0)
        def _():
            rc(gds.at[1, rows], gdr.at[1, rows], z_s.at[0], z_r.at[0, 1], b, 1).start()

        @pl.when(s == DEPTH - 1)
        def _():
            rc(gds.at[2, rows], gda.at[rows], z_s.at[0], z_r.at[0, DEPTH], b, DEPTH - 2).start()

    def add_in(kind, stage, got, via, pieces, t):
        landed(got(t), z_r.at[kind, t])
        term, more = stage(t), got(t)
        if len(via.shape) == 3:
            def add(j, _):
                term[j] = (term[j].astype(F32) + more[j].astype(F32)).astype(BF16)
                return 0

            lax.fori_loop(0, via.shape[0], add, 0)
        else:
            def add_rows(j, _):
                rows = pl.ds(pl.multiple_of(j * INNER, INNER), INNER)
                term[rows, :] = (term[rows, :].astype(F32) + more[rows, :].astype(F32)).astype(BF16)
                return 0

            lax.fori_loop(0, via.shape[0] // INNER, add_rows, 0)

    def grad_pass(*moved):
        @pl.when(s == 1)
        def _():
            add_in(*moved, 3)
            grad_up(*moved, 3).start()

        @pl.when(s == 2)
        def _():
            add_in(*moved, 0)
            grad_down_to(*moved, 0).start()

    def grad_pass_on(*moved):
        @pl.when(s == 1)
        def _():
            add_in(*moved, 2)
            grad_up(*moved, 2).start()
            add_in(*moved, 0)
            grad_down_last(*moved).start()

        @pl.when(s == 2)
        def _():
            add_in(*moved, 1)
            grad_down_last(*moved).start()
            add_in(*moved, 3)
            grad_up(*moved, 3).start()

    def grad_finish(kind, stage, got, via, pieces):
        @pl.when(s > 0)
        def _():
            landed(got(s), z_r.at[kind, s])

        @pl.when(s < DEPTH - 1)
        def _():
            landed(via, z_r.at[kind, DEPTH])

    def grad_sent(kind, stage, got, via, pieces):
        left(pieces(3), z_s.at[kind])

    results = ((out_o, out_h), (ig_o, ig_h), (gqkv_o, gqkv_h), (gout_o, gout_h), (gup_o, gup_h), (gdown_o, gdown_h),
               (gain_o, gain_h), (shift_o, shift_h), (lead_o, lead_h), (bias_o, bias_h))

    def deliver(n):
        return pltpu.make_async_copy(results[n][0], results[n][1], out_s.at[n])

    w_out_z = (
        0, lambda t: wo.at[b, pl.ds(pl.multiple_of(t * 32, 32), 32)],
        lambda n: wo.at[b, pl.ds(0, n * 32)],
    )
    w_qkv_z = (1, lambda t: wq.at[:, t], lambda n: wq.at[:, pl.ds(0, n)])
    w_up_z = (2, lambda t: wu.at[:, t], lambda n: wu.at[:, pl.ds(0, n)])
    w_down_z = (3, lambda t: wd.at[t], lambda n: wd.at[pl.ds(0, n)])
    g_down_z = (0, lambda t: gds.at[t], lambda t: gdr.at[t], gda, lambda n: gds.at[pl.ds(0, n)])
    g_up_z = (1, lambda t: gus.at[:, t], lambda t: gur.at[t], guc, lambda n: gus.at[:, pl.ds(0, n)])
    g_qkv_z = (2, lambda t: gqs.at[:, t], lambda t: gqr.at[t], gqc, lambda n: gqs.at[:, pl.ds(0, n)])
    g_out_z = (3, lambda t: gos.at[:, t], lambda t: gor_.at[t], goc, lambda n: gos.at[:, pl.ds(0, n)])

    def gather(op, r, turn):
        return rc(
            agf.at[op % 3, 0, (turn + r) % 2, c], agf.at[op % 3, 1 + turn, r - 1, c],
            ag_s.at[op], ag_r.at[op, turn], near(r), s,
        )

    def across(op, r):
        return rc(
            agf.at[op % 3, 1, r - 1, c], agf.at[op % 3, 3, r % 2, c],
            ag_s.at[op], ac_r.at[op], near(3 - r), s,
        )

    def share(op, blk):
        return rc(
            agf.at[op % 3, blk, :, c], agf.at[op % 3, blk, :, c],
            fw_s.at[op], fw_r.at[op, blk], mate, s,
        )

    def start_gather(op):
        for turn in (0, 1):
            for r in (1, 2):
                gather(op, r, turn).start()
        share(op, 0).start()

    def arrive(op, blk):
        if blk in (1, 2):
            landed(agf.at[op % 3, blk, :, c], ag_r.at[op, blk - 1])
        if blk == 1:
            for r in (1, 2):
                across(op, r).start()
        if blk == 3:
            landed(agf.at[op % 3, 3, :, c], ac_r.at[op])
        if blk:
            share(op, blk).start()

    def gathered(op):
        left(agf.at[op % 3, pl.ds(0, 3), :, 0], ag_s.at[op])
        left(agf.at[op % 3, :, :, 0], fw_s.at[op])

    def block(op, i):
        return agf[op, i].reshape(BLOCK, -1)

    def rows_half(dev, h):
        return wo.at[dev, pl.ds(h * HALF, HALF)]

    def rows_copy(r, turn):
        part_ = rows_half(b, (turn + r) % 2)
        return rc(part_, part_, wg_s.at[0], wg_r.at[turn], near(r), s)

    def rows_across(r):
        part_ = rows_half(near(r), r % 2)
        return rc(part_, part_, wg_s.at[0], wg_r.at[2], near(3 - r), s)

    def rows_share(r):
        dev = near(r) if r else b
        return rc(wo.at[dev], wo.at[dev], wg_s.at[1], wg_r.at[3], mate, s)

    def rows_start():
        for turn in (0, 1):
            for r in (1, 2):
                rows_copy(r, turn).start()
        rows_share(0).start()

    def granule(i, a):
        return (i, a) if i in (0, 3) else (a + 1, 1 - a if i == 1 else a)

    GRANULES = [(i, a) for i in (1, 0, 2, 3) for a in (0, 1)]

    def heads_copy(i, a, k):
        r, h = granule(i, a)
        rows = pl.ds(pl.multiple_of((a * 2 + k) * HALF, HALF), HALF)
        return rc(
            att.at[i, rows], aown.at[b, pl.ds(h * HALF, HALF)],
            h_s.at[0], h_r.at[0], chip(r) * 2 + k, s,
        )

    def cores(i):
        return (1 - c,) if i == 0 else (0, 1)

    def back_copy(i, a, k):
        r, h = granule(i, a)
        dev = chip(r) * 2 + k
        return rc(
            dsend.at[dev, pl.ds(h * HALF, HALF)], dob.at[i, a, c],
            g_s.at[0], g_r.at[i], dev, s,
        )

    def branch_copy(i, a, k):
        r, h = granule(i, a)
        dev = chip(r) * 2 + k
        return rc(
            gsend.at[dev, pl.ds(h * HALF, HALF)], gcol.at[i, a, c],
            gc_s.at[0], gc_r.at[0], dev, s,
        )

    def swap(kind, k, src, dst):
        return rc(src, dst, aq_s.at[kind], aq_r.at[kind], peer(k), s)

    for k in range(1, DEPTH):
        yc(0, k, vec_in.at[0], ztr.at[k - 1]).start()
    for k in range(1, PLANE):
        swap(0, k, sq.at[peer(k)], wq.at[b, s]).start()
    weight_start(*w_out_z)
    fetches[2].wait()
    fetches[3].wait()
    for r in (1, 2):
        gather(0, r, 0).start()
    wq[b, s] = sq[b]
    fetches[4].wait()
    for d in range(PLANE):
        su[d] = wup[:, d * 512:(d + 1) * 512]
    wu[b, s] = su[b]

    landed(ztr, y_r.at[0])
    vt[...] = (
        vec_in[0].astype(F32) + vec_in[1].astype(F32)
        + ztr[0].astype(F32) + ztr[1].astype(F32) + ztr[2].astype(F32)
    ).astype(BF16)

    def spread(k):
        return rc(vt, vecf.at[b], v_s.at[0], v_r.at[0], peer(k), s)

    for k in range(1, PLANE):
        spread(k).start()
    for r in (1, 2):
        gather(0, r, 1).start()
    share(0, 0).start()
    vecf[b] = vt[...]
    landed(sq.at[pl.ds(0, 7)], aq_r.at[0])
    weight_start(*w_qkv_z)
    for k in range(1, PLANE):
        swap(1, k, su.at[peer(k)], wu.at[b, s]).start()
    arrive(0, 1)
    fetches[6].wait()
    fetches[7].wait()
    for r in (1, 2):
        gather(1, r, 0).start()
    share(1, 0).start()
    landed(vecf.at[pl.ds(0, 7)], v_r.at[0])
    for d in range(PLANE):
        vrow[:, d * 128:(d + 1) * 128] = vecf[d].astype(F32)
    lead_days = lead_ref[0].astype(F32) * 0.25
    lane = lax.broadcasted_iota(jnp.int32, (1, 128), 1)
    head_lane = [(lane < 64).astype(F32), (lane >= 64).astype(F32)]
    ones_lane = jnp.where(lane < 2, 1.0, 0.0).astype(F32)
    ends_lane = jnp.where(lane == 0, 9984.0, jnp.where(lane == 1, 16.0, 0.0)).astype(F32)
    gain1, gain2 = vrow[0:1, :], vrow[1:2, :]
    shift1, shift_out, shift2, shift_down = vrow[2:3, :], vrow[5:6, :], vrow[6:7, :], vrow[7:8, :]
    lead_row = lead_days * vrow[8:9, :] + vrow[9:10, :]
    mine = vecf[b].astype(F32)

    def stats(v):
        mean = jnp.mean(v, axis=-1, keepdims=True)
        centered = v - mean
        variance = jnp.mean(centered * centered, axis=-1, keepdims=True)
        rstd = lax.rsqrt(variance + eps)
        return centered * rstd, rstd

    for r in range(4):
        for k in range(2):
            row = jnp.broadcast_to(vecf[chip(r) * 2 + k].astype(F32)[10:11, :], (128, 128))
            column = ((row.T - 1.0) * ends_lane).astype(BF16)
            for h in range(2):
                if r in (0, 3):
                    blk, a = r, h
                else:
                    blk, a = (1 if h == r % 2 else 2), r - 1
                top = blk * BLOCK + (a * 2 + k) * HALF
                kaug[top:top + HALF, 128:256] = column[h * HALF:(h + 1) * HALF]
    for h in range(2):
        for i in range(4):
            qaug[i, h * BLOCK:(h + 1) * BLOCK, 128:256] = jnp.broadcast_to(ones_lane, (BLOCK, 128)).astype(BF16)

    def norm_block(i):
        def chunk(j, _):
            rows = pl.ds(pl.multiple_of((j % 2) * INNER, INNER), INNER)
            ent = agf[0, i, j // 4, (j // 2) % 2, rows, :].astype(F32) + lead_row
            xhat = stats(ent)[0]
            put = pl.ds(pl.multiple_of(j * INNER, INNER), INNER)
            normed[i, put, :] = (xhat * gain1 + shift1).astype(BF16)
            return 0

        lax.fori_loop(0, BLOCK // INNER, chunk, 0)

    share(0, 0).wait_recv()
    norm_block(0)
    share(0, 1).wait_recv()
    arrive(0, 2)
    norm_block(1)
    weight_pass(*w_out_z)
    weight_pass(*w_qkv_z)
    share(0, 2).wait_recv()
    norm_block(2)
    weight_finish(*w_out_z)
    rows_start()
    landed(su.at[pl.ds(0, 7)], aq_r.at[1])

    @pl.when(inner)
    def _():
        weight_copy(*w_up_z, 1, 3 * (s - 1)).start()

    arrive(0, 3)
    share(0, 3).wait_recv()
    @pl.when(ends)
    def _():
        weight_start(*w_up_z)

    norm_block(3)

    weight_finish(*w_qkv_z)
    @pl.when(inner)
    def _():
        weight_copy(*w_up_z, 0, far).start()
        weight_copy(*w_up_z, 2, DEPTH - 1 - s).start()


    def project_block(q, _):
        rows = pl.ds(pl.multiple_of(q * BLOCK, BLOCK), BLOCK)
        pj = mm(normed[q], wq[...].reshape(width, 384))
        qv = (pj[:, 0:128] + mine[3:4, :]).astype(BF16).astype(F32) * 0.125
        for h in range(2):
            qaug[q, h * BLOCK:(h + 1) * BLOCK, 0:128] = (qv * head_lane[h]).astype(BF16)
        kv = pj[:, 128:256].astype(BF16)
        kaug[rows, 0:128] = kv
        kt[:, rows] = kv.T
        vb = (pj[:, 256:384] + mine[4:5, :]).astype(BF16)
        vv[rows, :] = vb
        vt2[:, rows] = vb.T
        return 0

    lax.fori_loop(0, 4, project_block, 0)

    def mate_copy(op, i):
        return rc(part.at[op, i, :, 1 - c], pr.at[op, i], p_s.at[op], p_r.at[op, i], mate, s)

    def far_copy(op, h):
        return rc(cs.at[op, 3, h], au.at[op, 1 - h], n_s.at[op], f_r.at[op], near(h + 1), s)

    def near_copy(op, i, a):
        h = a if i == 2 else 1 - a
        return rc(cs.at[op, i, a], rr.at[op, a, h], n_s.at[op], n_r.at[op], near(a + 1), s)

    def put_part(op, i, blk):
        part[op, i] = blk.astype(BF16).reshape(2, 2, HALF, width)
        mate_copy(op, i).start()

    def fold(op, i):
        mate_copy(op, i).wait_recv()

        def chunk(j, _):
            a = j // 2
            rows = pl.ds(pl.multiple_of((j % 2) * INNER, INNER), INNER)
            cs[op, i, a, rows, :] = (
                part[op, i, a, c, rows, :].astype(F32) + pr[op, i, a, rows, :].astype(F32)
            ).astype(BF16)
            return 0

        lax.fori_loop(0, ROWS // INNER, chunk, 0)

    def fold_before(op, i, near_too=True):
        @pl.when(i < 3)
        def _():
            fold(op, i + 1)

        @pl.when(i == 2)
        def _():
            send_far(op)

        if near_too:
            @pl.when(i == 1)
            def _():
                send_near(op, 2)

    def send_far(op):
        for h in (0, 1):
            far_copy(op, h).start()

    def send_near(op, i):
        for a in (0, 1):
            near_copy(op, i, a).start()

    def send_last(op):
        landed(au.at[op], f_r.at[op])
        for a in (0, 1):
            def chunk(j, _):
                rows = pl.ds(pl.multiple_of(j * INNER, INNER), INNER)
                cs[op, 1, a, rows, :] = (
                    cs[op, 1, a, rows, :].astype(F32) + au[op, a, rows, :].astype(F32)
                ).astype(BF16)
                return 0

            lax.fori_loop(0, HALF // INNER, chunk, 0)
            near_copy(op, 1, a).start()

    def wait_sums(op):
        landed(rr.at[op], n_r.at[op])

    def place(j):
        return j // 2, pl.ds(pl.multiple_of((j % 2) * INNER, INNER), INNER)

    def plane_total(op, j):
        h, rows = place(j)
        total = cs[op, 0, h, rows, :].astype(F32)
        return total + rr[op, 0, h, rows, :].astype(F32) + rr[op, 1, h, rows, :].astype(F32)

    def own_rows(op, j):
        h, rows = place(j)
        kept = {0: tokown, 3: gbown}.get(op)
        v = agf[op, 0, h, c, rows, :] if kept is None else kept[h, rows, :]
        return v.astype(F32)

    def set_rows(op, j, v):
        h, rows = place(j)
        if op == 3:
            gbown[h, rows, :] = v
        else:
            agf[op, 0, h, c, rows, :] = v

    def end_sums(op):
        left(part.at[op, :, :, 0], p_s.at[op])
        left(cs.at[op, pl.ds(0, 3)], n_s.at[op])

    def attend_block(n, _):
        i = 3 - n

        @pl.when(n == 3)
        def _():
            landed(wo.at[0], wg_r.at[1])
            for r in (1, 2):
                rows_share(r).start()

        st = mm(kaug[...], qaug[i], NT)
        p = jnp.exp(st - jnp.max(st, axis=0, keepdims=True))
        inverse = 1.0 / jnp.sum(p, axis=0, keepdims=True)
        pb = p.astype(BF16)
        pst[i] = pb
        out = mm(vt2[...], pb) * inverse
        ot[i, 0:64, :] = out[0:64, 0:BLOCK]
        ot[i, 64:128, :] = out[64:128, BLOCK:]
        invl[i] = jnp.broadcast_to(inverse, (8, 2 * BLOCK))
        att[i] = ot[i].T.astype(BF16)
        for blk in range(4):
            @pl.when(i == blk)
            def _():
                for a in (0, 1):
                    for k in cores(blk):
                        heads_copy(blk, a, k).start()

        return 0

    tokown[...] = agf[0, 0, :, c]
    gathered(0)
    landed(wo.at[0], wg_r.at[0])
    for r in (1, 2):
        rows_across(r).start()
    lax.fori_loop(0, 4, attend_block, 0)
    landed(wo.at[0], wg_r.at[2])
    rows_share(3).start()
    arrive(1, 1)
    for h in (0, 1):
        top = pl.multiple_of((h * 2 + c) * HALF, HALF)
        aown[b, h * HALF:(h + 1) * HALF] = att[0, pl.ds(top, HALF), :]
    weight_pass(*w_up_z)
    fetches[5].wait()

    @pl.when(inner)
    def _():
        weight_start(*w_down_z)

    landed(wo.at[pl.ds(0, 4)], wg_r.at[3])
    landed(aown.at[pl.ds(0, 7)], h_r.at[0])
    heads = jnp.concatenate([aown[d] for d in range(PLANE)], axis=1)
    mid[...] = mm(heads, wo[...].reshape(1024, width))
    agf[0, 0, :, c] = heads.reshape(2, HALF, width)

    def middle_chunk(j, _):
        rows = pl.ds(pl.multiple_of(j * INNER, INNER), INNER)
        m = own_rows(0, j) + lead_row + mid[rows, :] + shift_out
        mid[rows, :] = m
        set_rows(2, j, (stats(m)[0] * gain2 + shift2).astype(BF16))
        return 0

    lax.fori_loop(0, ROWS // INNER, middle_chunk, 0)
    start_gather(2)
    arrive(1, 3)
    arrive(2, 1)
    for r in (1, 2):
        gather(1, r, 1).start()
    start_gather(3)

    @pl.when(ends)
    def _():
        weight_start(*w_down_z)

    weight_finish(*w_up_z)

    bias = jnp.concatenate([mine[11 + j:12 + j, :] for j in range(4)], axis=1)

    def arrivals(op, i):
        for blk in range(4):
            @pl.when(i == blk)
            def _():
                if blk != 1:
                    arrive(op, blk)
                share(op, blk).wait_recv()

    def down_grad_first(f, _):
        cols = pl.ds(pl.multiple_of(f * BLOCK, BLOCK), BLOCK)
        gdf[pl.ds(pl.multiple_of(f * BLOCK, BLOCK), BLOCK), :] = mm(
            hid[:2 * BLOCK, cols], agf[1, 0:2].reshape(2 * BLOCK, width), TN
        )
        return 0

    def up_block(i, _):
        @pl.when(i == 3)
        def _():
            for blk in range(2):
                share(1, blk).wait_recv()
            lax.fori_loop(0, 2, down_grad_first, 0)

        arrivals(2, i)


        hp = mm(block(2, i), wu[...].reshape(width, 512)) + bias
        phi = 0.5 + 0.5 * lax.erf(hp * 0.7071067811865476)
        hid[pl.ds(pl.multiple_of(i * BLOCK, BLOCK), BLOCK), :] = (hp * phi).astype(BF16)
        gder[i] = phi + hp * jnp.exp(hp * hp * -0.5) * 0.3989422804014327
        return 0

    lax.fori_loop(0, 4, up_block, 0)
    weight_pass(*w_down_z)
    arrive(1, 2)
    share(1, 2).wait_recv()
    share(1, 3).wait_recv()

    def down_grad(f, _):
        cols = pl.ds(pl.multiple_of(f * BLOCK, BLOCK), BLOCK)
        g = gdf[pl.ds(pl.multiple_of(f * BLOCK, BLOCK), BLOCK), :] + mm(
            hid[2 * BLOCK:, cols], agf[1, 2:4].reshape(2 * BLOCK, width), TN
        )
        gds[pl.ds(2 * f, 2)] = g.astype(BF16).reshape(2, 128, width)
        return 0

    lax.fori_loop(0, 2, down_grad, 0)
    grad_start_some(*g_down_z, 3)
    grad_start_some(*g_down_z, 2)
    down_half(0)
    for i in range(4):
        for j in range(i + 1):
            upper = normed[j, :, i * BLOCK:(i + 1) * BLOCK].T
            if i != j:
                normed[j, :, i * BLOCK:(i + 1) * BLOCK] = normed[i, :, j * BLOCK:(j + 1) * BLOCK].T
            normed[i, :, j * BLOCK:(j + 1) * BLOCK] = upper
    def turn_second(i, _):
        cols = pl.ds(pl.multiple_of(i * BLOCK, BLOCK), BLOCK)
        blk = block(2, i)
        for f in range(4):
            sct[f, :, cols] = blk[:, f * BLOCK:(f + 1) * BLOCK].T
        return 0

    lax.fori_loop(0, 4, turn_second, 0)

    def even_out(n, _):
        i = n // 4
        rows = pl.ds(pl.multiple_of((n % 4) * BLOCK, BLOCK), BLOCK)
        pst[i, rows, :] = (pst[i, rows, :].astype(F32) * invl[i, 0:1, :]).astype(BF16)
        return 0

    lax.fori_loop(0, 16, even_out, 0)

    left(wo.at[pl.ds(0, 3)], wg_s.at[0])
    left(wo.at[pl.ds(0, 4)], wg_s.at[1])
    weight_sent(*w_out_z)

    def wo_block(i, j):
        return wo[2 * i:2 * i + 2, :, j * BLOCK:(j + 1) * BLOCK].reshape(BLOCK, BLOCK)

    for i in range(4):
        for j in range(i + 1):
            upper = wo_block(j, i).T.reshape(2, ROWS, BLOCK)
            if i != j:
                wo[2 * j:2 * j + 2, :, i * BLOCK:(i + 1) * BLOCK] = wo_block(i, j).T.reshape(2, ROWS, BLOCK)
            wo[2 * i:2 * i + 2, :, j * BLOCK:(j + 1) * BLOCK] = upper
    arrive(3, 1)
    arrive(3, 2)
    weight_finish(*w_down_z)
    gub[...] = jnp.zeros_like(gub)
    arrive(3, 3)

    def back_block(n, _):
        i = 3 - n
        rows = pl.ds(pl.multiple_of(i * BLOCK, BLOCK), BLOCK)
        gp = (gder[i] * mm(block(1, i), wd[...].reshape(512, width), NT)).astype(BF16)
        put_part(0, i, mm(gp, wu[...].reshape(width, 512), NT))
        gpre[rows, :] = gp
        gub[...] += jnp.sum(gp.astype(F32).reshape(BLOCK // 8, 8, 512), axis=0)
        fold_before(0, i)
        return 0

    grad_pass(*g_down_z)
    lax.fori_loop(0, 4, back_block, 0)
    fold(0, 0)

    def up_grad(f, _):
        g = mm(sct[pl.ds(2 * f, 2)].reshape(2 * BLOCK, 1024), gpre[...])
        gus[pl.ds(4 * f, 4)] = g.astype(BF16).reshape(4, 4, 32, 512)
        return 0

    lax.fori_loop(0, 2, up_grad, 0)
    grad_start(*g_up_z)

    def out_block(n, _):
        i = 3 - n
        rows = pl.ds(pl.multiple_of(i * BLOCK, BLOCK), BLOCK)
        put_part(1, i, mm(hid[rows, :], wd[...].reshape(512, width)))
        fold_before(1, i, near_too=False)
        return 0

    send_last(0)
    grad_pass_on(*g_down_z)
    lax.fori_loop(0, 4, out_block, 0)
    fold(1, 0)

    wait_sums(0)
    acc[...] = jnp.zeros_like(acc)

    def add_row(n, v):
        acc[n] += jnp.sum(v.reshape(INNER // 8, 8, width), axis=0)

    def norm_back(v, grad, gain):
        xhat, rstd = stats(v)
        d = grad * gain
        mean_d = jnp.mean(d, axis=-1, keepdims=True)
        mean_dx = jnp.mean(d * xhat, axis=-1, keepdims=True)
        return rstd * (d - mean_d - xhat * mean_dx), xhat

    def second_chunk(j, _):
        rows = pl.ds(pl.multiple_of(j * INNER, INNER), INNER)
        gs = plane_total(0, j)
        g, xhat = norm_back(mid[rows, :], gs, gain2)
        ct = own_rows(1, j)
        gm = ct + g
        gmid[rows, :] = gm
        gb = gm.astype(BF16)
        set_rows(3, j, gb)
        add_row(1, gs * xhat)
        add_row(6, gs)
        return 0

    lax.fori_loop(0, ROWS // INNER, second_chunk, 0)
    gbo = gbown[...].reshape(ROWS, width)
    gha = mm(gbo, wo[...].reshape(width, 1024)).astype(BF16)
    for d in range(PLANE):
        dsend[d] = gha[:, d * 128:(d + 1) * 128]
    for i, a in GRANULES:
        for k in cores(i):
            back_copy(i, a, k).start()
    for h in (0, 1):
        dob[0, h, c] = dsend[b, h * HALF:(h + 1) * HALF, :]
    for d in range(PLANE):
        gsend[d] = gbo[:, d * 128:(d + 1) * 128]
    for i, a in GRANULES:
        for k in cores(i):
            branch_copy(i, a, k).start()
    for h in (0, 1):
        gcol[0, h, c] = gsend[b, h * HALF:(h + 1) * HALF, :]

    grad_pass(*g_up_z)
    dk[...] = jnp.zeros_like(dk)
    dv[...] = jnp.zeros_like(dv)

    def attend_back(i, _):
        for blk in range(4):
            @pl.when(i == blk)
            def _():
                landed(dob.at[blk] if blk else dob.at[0, :, 0], g_r.at[blk])

        do_rows = dob[i].reshape(BLOCK, 128)
        do_cols = do_rows.T.astype(F32)
        prod = do_cols * ot[i]
        delta = jnp.concatenate(
            [jnp.sum(prod[h * 64:(h + 1) * 64], axis=0, keepdims=True) for h in range(2)], axis=1
        )
        zero = jnp.zeros((64, BLOCK), F32)
        spread_cols = jnp.concatenate([
            jnp.concatenate([do_cols[0:64], zero], axis=0),
            jnp.concatenate([zero, do_cols[64:128]], axis=0),
        ], axis=1).astype(BF16)
        spread_rows = jnp.concatenate(
            [(do_rows.astype(F32) * head_lane[h]).astype(BF16) for h in range(2)], axis=0
        )
        pb = pst[i]
        ds = (pb.astype(F32) * (mm(vv[...], spread_cols) - delta)).astype(BF16)
        dv[...] += mm(pb, spread_rows)
        dk[...] += mm(ds, qaug[i, :, 0:128])
        dq = mm(kt[...], ds)
        dq = jnp.concatenate([dq[0:64, 0:BLOCK], dq[64:128, BLOCK:]], axis=0).T * 0.125
        gproj[pl.ds(pl.multiple_of(i * BLOCK, BLOCK), BLOCK), 0:128] = dq.astype(BF16)
        return 0

    lax.fori_loop(0, 4, attend_back, 0)
    gproj[:, 128:256] = dk[...].astype(BF16)
    gproj[:, 256:384] = dv[...].astype(BF16)

    put_part(2, 3, mm(gproj[3 * BLOCK:, :], wq[...].reshape(width, 384), NT))
    gqs[...] = mm(normed[...].reshape(1024, 1024), gproj[...]).astype(BF16).reshape(8, 4, 32, 384)
    grad_start_some(*g_qkv_z, 3)
    grad_start_some(*g_qkv_z, 2)
    fold(2, 3)
    send_far(2)
    grad_pass_on(*g_up_z)

    def project_back(n, _):
        i = 2 - n
        rows = pl.ds(pl.multiple_of(i * BLOCK, BLOCK), BLOCK)
        put_part(2, i, mm(gproj[rows, :], wq[...].reshape(width, 384), NT))

        @pl.when(n == 1)
        def _():
            fold(2, 2)
            send_near(2, 2)

        return 0

    lax.fori_loop(0, 3, project_back, 0)
    fold(2, 1)
    fold(2, 0)
    grad_pass(*g_qkv_z)
    for i in range(4):
        share(3, i).wait_recv()
    landed(aown.at[pl.ds(0, 7)], gc_r.at[0])
    gos[...] = mm(gcol[...].reshape(1024, 128), agf[0].reshape(1024, width), TN).T.astype(BF16).reshape(
        PLANE, DEPTH, 32, 128
    )
    grad_start_some(*g_out_z, 3)
    grad_start_some(*g_out_z, 2)
    grad_start_some(*g_qkv_z, 1)
    grad_start_some(*g_out_z, 1)
    send_last(2)
    send_near(1, 2)
    send_last(1)

    def others(kind, stage, got, via, pieces):
        return [got(s), via]

    grad_pass(*g_out_z)
    grad_pass_on(*g_qkv_z)
    def own_sums(j, _):
        add_row(5, own_rows(3, j))
        add_row(7, own_rows(1, j))
        return 0

    lax.fori_loop(0, ROWS // INNER, own_sums, 0)
    wait_sums(2)

    def first_chunk(j, _):
        rows = pl.ds(pl.multiple_of(j * INNER, INNER), INNER)
        gn = plane_total(2, j)
        g, xhat = norm_back(own_rows(0, j) + lead_row, gn, gain1)
        ge = gmid[rows, :] + g
        ig_o[rows, :] = ge.astype(BF16)
        add_row(0, gn * xhat)
        add_row(2, gn)
        add_row(9, ge)
        return 0

    lax.fori_loop(0, ROWS // INNER, first_chunk, 0)
    deliver(1).start()
    acc[8] = acc[9] * lead_days

    sums = [jnp.sum(acc[n], axis=0, keepdims=True) for n in range(10)]
    packed = jnp.concatenate(sums + [jnp.zeros((6, width), F32)], axis=0)
    for d in range(PLANE):
        vs[d] = packed[:, d * 128:(d + 1) * 128]

    def vec_swap(k):
        return rc(vs.at[peer(k)], vsr.at[k - 1], v_s.at[1], v_r.at[1], peer(k), s)

    for k in range(1, PLANE):
        vec_swap(k).start()
    gq_cols = jnp.sum(gproj[:, 0:128].astype(F32), axis=0, keepdims=True)
    gv_cols = jnp.sum(gproj[:, 256:384].astype(F32), axis=0, keepdims=True)
    gub_row = jnp.sum(gub[...], axis=0, keepdims=True)
    extra = jnp.concatenate(
        [jnp.zeros((3, 128), F32), gq_cols, gv_cols, jnp.zeros((6, 128), F32)]
        + [gub_row[:, j * 128:(j + 1) * 128] for j in range(4)]
        + [jnp.zeros((1, 128), F32)],
        axis=0,
    )
    grad_finish(*g_up_z)
    for d in range(PLANE):
        gu2[d] = sum(
            [t[d].astype(F32) for t in others(*g_up_z)], gus[d, s].astype(F32)
        ).astype(BF16)
    for k in range(1, PLANE):
        swap(2, k, gu2.at[peer(k)], gua.at[b]).start()
    gua[b] = gu2[b]
    grad_pass_on(*g_out_z)
    landed(vs.at[pl.ds(0, 7)], v_r.at[1])
    total = vs[b] + extra
    for k in range(PLANE - 1):
        total = total + vsr[k]
    vz[...] = total
    for k in range(1, DEPTH):
        yc(1, k, vz, vzr.at[k - 1]).start()
    down_half(1)

    grad_finish(*g_qkv_z)
    for d in range(PLANE):
        gq2[d] = sum(
            [t[d].astype(F32) for t in others(*g_qkv_z)], gqs[d, s].astype(F32)
        ).astype(BF16)
    for k in range(1, PLANE):
        swap(3, k, gq2.at[peer(k)], gqa.at[b]).start()
    gqa[b] = gq2[b]
    grad_finish(*g_out_z)
    for d in range(PLANE):
        go2[d] = sum(
            [t[d].astype(F32) for t in others(*g_out_z)], gos[d, s].astype(F32)
        ).astype(BF16)
    for k in range(1, PLANE):
        swap(4, k, go2.at[peer(k)], go3.at[b]).start()
    go3[b] = go2[b]
    wait_sums(1)

    def output_chunk(j, _):
        rows = pl.ds(pl.multiple_of(j * INNER, INNER), INNER)
        out_o[rows, :] = (mid[rows, :] + plane_total(1, j) + shift_down).astype(BF16)
        return 0

    lax.fori_loop(0, ROWS // INNER, output_chunk, 0)
    deliver(0).start()

    grad_finish(*g_down_z)
    gdown_o[...] = sum([t[...].astype(F32) for t in others(*g_down_z)], gds[s].astype(F32))
    deliver(5).start()
    landed(gu2.at[pl.ds(0, 7)], aq_r.at[2])
    for d in range(PLANE):
        gup_o[:, d * 512:(d + 1) * 512] = gua[d].astype(F32)
    deliver(4).start()
    landed(vzr, y_r.at[1])
    vz_sum = vz[...] + vzr[0] + vzr[1] + vzr[2]
    columns = pltpu.roll(vz_sum, (128 - 32 * s) % 128, 1)
    gain_o[...] = columns[0:2, 0:32]
    shift_o[...] = columns[2:8, 0:32]
    lead_o[...] = columns[8:10, 0:32]
    bias_o[...] = jnp.sum(jnp.where(line == 11 + s, vz_sum, 0.0), axis=0, keepdims=True)
    for n in range(6, 10):
        deliver(n).start()
    landed(go2.at[pl.ds(0, 7)], aq_r.at[4])
    for d in range(PLANE):
        gout_o[:, d * 128:(d + 1) * 128] = go3[d].astype(F32)
    deliver(3).start()
    landed(gq2.at[pl.ds(0, 7)], aq_r.at[3])
    for d in range(PLANE):
        for j in range(3):
            gqkv_o[:, j * width + d * 128:j * width + (d + 1) * 128] = (
                gqa[d, :, j * 128:(j + 1) * 128].astype(F32)
            )

    deliver(2).start()
    for op in (1, 2, 3):
        gathered(op)
    for op in range(3):
        end_sums(op)
    left(aown.at[pl.ds(0, 7)], h_s.at[0])
    left(dsend.at[pl.ds(0, 7)], g_s.at[0])
    left(gsend.at[pl.ds(0, 7)], gc_s.at[0])
    for kind, sent in enumerate((sq, su, gu2, gq2, go2)):
        left(sent.at[pl.ds(0, 7)], aq_s.at[kind])
    left(vecf.at[pl.ds(0, 7)], v_s.at[0])
    left(vs.at[pl.ds(0, 7)], v_s.at[1])
    left(ztr, y_s.at[0])
    left(vzr, y_s.at[1])
    for moved in (w_qkv_z, w_up_z, w_down_z):
        weight_sent(*moved)
    for moved in (g_down_z, g_up_z, g_qkv_z, g_out_z):
        grad_sent(*moved)
    for n in range(10):
        deliver(n).wait()


def hand_over(*refs):
    count = len(refs) // 3
    given, taken, held, sems = refs[:count], refs[count:2 * count], refs[2 * count:3 * count], refs[-1]
    into = [pltpu.make_async_copy(given[n], held[n], sems.at[0, n]) for n in range(count)]
    out = [pltpu.make_async_copy(held[n], taken[n], sems.at[1, n]) for n in range(count)]
    for copy in into:
        copy.start()
    for n in range(count):
        into[n].wait()
        out[n].start()
    for copy in out:
        copy.wait()


def plane_body(
    tokens, cotangent, w_qkv, w_out, w_up, w_down,
    up_bias, norm_gains, shift_rows, lead_weight, lead_steps, valid_cells,
):
    width = tokens.shape[2]
    vmem = pl.BlockSpec(memory_space=pltpu.VMEM)
    anywhere = pl.BlockSpec(memory_space=pl.ANY)
    dma = pltpu.SemaphoreType.DMA
    V = pltpu.VMEM
    out_shape = (
        jax.ShapeDtypeStruct((ROWS, width), BF16),
        jax.ShapeDtypeStruct((ROWS, width), BF16),
        jax.ShapeDtypeStruct((32, 3 * width), F32),
        jax.ShapeDtypeStruct((32, width), F32),
        jax.ShapeDtypeStruct((32, 4 * width), F32),
        jax.ShapeDtypeStruct((128, width), F32),
        jax.ShapeDtypeStruct((2, 32), F32),
        jax.ShapeDtypeStruct((6, 32), F32),
        jax.ShapeDtypeStruct((2, 32), F32),
        jax.ShapeDtypeStruct((1, 128), F32),
    )
    scratch = [
        V((ROWS, width), BF16), V((ROWS, width), BF16),
        V((32, 3 * width), F32), V((32, width), F32),
        V((32, 4 * width), F32), V((128, width), F32),
        V((2, 32), F32), V((6, 32), F32), V((2, 32), F32), V((1, 128), F32),
        V((32, 3 * width), BF16), V((32, 4 * width), BF16),
        V((16, 128), F32), V((2, 16, 128), BF16),
        V((3, 4, 2, 2, HALF, width), BF16),
        V((2, HALF, width), BF16), V((2, HALF, width), BF16),
        V((PLANE, DEPTH, 32, 384), BF16),
        V((PLANE, 128, width), BF16),
        V((PLANE, DEPTH, 32, 512), BF16),
        V((DEPTH, 128, width), BF16),
        V((PLANE, 32, 384), BF16),
        V((PLANE, 32, 512), BF16),
        V((3, 16, 128), BF16),
        V((16, 128), BF16),
        V((PLANE, 16, 128), BF16),
        V((16, width), F32),
        V((4, BLOCK, width), BF16),
        V((4, 2 * BLOCK, 256), BF16),
        V((1024, 256), BF16),
        V((128, 1024), BF16),
        V((1024, 128), BF16),
        V((128, 1024), BF16),
        V((4, 1024, 2 * BLOCK), BF16),
        V((4, 128, BLOCK), F32),
        V((4, 8, 2 * BLOCK), F32),
        V((4, BLOCK, 128), BF16),
        V((PLANE, ROWS, 128), BF16),
        V((PLANE, ROWS, 128), BF16),
        V((4, 2, 2, HALF, 128), BF16),
        V((PLANE, ROWS, 128), BF16),
        V((4, 2, 2, HALF, 128), BF16),
        V((1024, 384), BF16),
        V((1024, 128), F32),
        V((1024, 128), F32),
        V((1024, 512), BF16),
        V((4, BLOCK, 512), F32),
        V((1024, 512), BF16),
        V((ROWS, width), F32),
        V((ROWS, width), F32),
        V((512, width), F32),
        V((4, BLOCK, 1024), BF16),
        V((3, 4, 2, 2, HALF, width), BF16),
        V((3, 4, 2, HALF, width), BF16),
        V((3, 4, 2, HALF, width), BF16),
        V((3, 2, HALF, width), BF16),
        V((3, 2, 2, HALF, width), BF16),
        V((DEPTH, 128, width), BF16),
        V((PLANE, DEPTH, 32, 512), BF16),
        V((PLANE, DEPTH, 32, 384), BF16),
        V((PLANE, DEPTH, 32, 128), BF16),
        V((DEPTH, 128, width), BF16),
        V((DEPTH, PLANE, 32, 512), BF16),
        V((DEPTH, PLANE, 32, 384), BF16),
        V((DEPTH, PLANE, 32, 128), BF16),
        V((128, width), BF16),
        V((PLANE, 32, 512), BF16),
        V((PLANE, 32, 384), BF16),
        V((PLANE, 32, 128), BF16),
        V((PLANE, 32, 128), BF16), V((PLANE, 32, 128), BF16),
        V((PLANE, 32, 512), BF16),
        V((PLANE, 32, 384), BF16),
        V((PLANE, 32, 512), BF16),
        V((PLANE, 32, 384), BF16),
        V((10, 8, width), F32),
        V((8, 512), F32),
        V((PLANE, 16, 128), F32),
        V((PLANE - 1, 16, 128), F32),
        V((16, 128), F32),
        V((3, 16, 128), F32),
        dma((8,)), dma((10,)),
        dma((4,)), dma((4, 2)), dma((4,)), dma((4,)), dma((4, 4)),
        dma((5,)), dma((5,)), dma((2,)), dma((2,)), dma((2,)), dma((2,)),
        dma((4,)), dma((4, 3)), dma((4,)), dma((4, 5)),
        dma((3,)), dma((3, 4)), dma((3,)), dma((3,)), dma((3,)),
        dma((2,)), dma((4,)), dma((1,)), dma((1,)), dma((1,)), dma((4,)), dma((1,)), dma((1,)),
    ]
    results = pl.pallas_call(
        plane_kernel,
        out_shape=out_shape,
        in_specs=[pl.BlockSpec(memory_space=pltpu.SMEM)] + [vmem] * 5 + [anywhere] * 6,
        out_specs=tuple([anywhere] * 10),
        scratch_shapes=scratch,
        compiler_params=pltpu.CompilerParams(
            collective_id=0, has_side_effects=True, vmem_limit_bytes=63 * 2**20
        ),
    )(
        lead_steps, norm_gains, shift_rows, lead_weight, up_bias[None], valid_cells,
        tokens[0], cotangent[0], w_qkv, w_out, w_up, w_down,
    )
    results = pl.pallas_call(
        hand_over,
        out_shape=out_shape,
        in_specs=[anywhere] * len(out_shape),
        out_specs=tuple([anywhere] * len(out_shape)),
        scratch_shapes=[V(o.shape, o.dtype) for o in out_shape] + [dma((2, len(out_shape)))],
    )(*results)
    output, input_grad, g_qkv, g_out, g_up, g_down, g_gains, g_shifts, g_lead, g_bias = results
    return (
        output[None], input_grad[None], g_qkv, g_out, g_up, g_down, g_bias[0],
        g_gains, g_shifts, g_lead,
    )


def plane_fits(mesh):
    return mesh.shape["band"] == PLANE and mesh.shape["samp"] == DEPTH


def solution(mesh):
    return jax.shard_map(
        plane_body if plane_fits(mesh) else body,
        mesh=mesh,
        in_specs=(
            P("samp", "band", None),
            P("samp", "band", None),
            P(("band", "samp"), None),
            P(("band", "samp"), None),
            P(("band", "samp"), None),
            P(("band", "samp"), None),
            P(("band", "samp")),
            P(None, ("band", "samp")),
            P(None, ("band", "samp")),
            P(None, ("band", "samp")),
            P("samp"),
            P("samp", "band"),
        ),
        out_specs=(
            P("samp", "band", None),
            P("samp", "band", None),
            P(("band", "samp"), None),
            P(("band", "samp"), None),
            P(("band", "samp"), None),
            P(("band", "samp"), None),
            P(("band", "samp")),
            P(None, ("band", "samp")),
            P(None, ("band", "samp")),
            P(None, ("band", "samp")),
        ),
        check_vma=False,
    )
```

```python
import jax
import jax.numpy as jnp
from jax import lax
from jax.experimental import pallas as pl
from jax.experimental.pallas import tpu as pltpu
from jax.sharding import PartitionSpec as P

HEADS = 16


eps = 1e-05
masked = 10000.0


def layer_norm(values, gain_row, shift_row):
    centered = values - jnp.mean(values, axis=-1, keepdims=True)
    variance = jnp.mean(centered * centered, axis=-1, keepdims=True)
    return centered * lax.rsqrt(variance + eps) * gain_row + shift_row


def gelu_exact(values):
    return jax.nn.gelu(values, approximate=False)


def body(
    tokens,
    cotangent,
    w_qkv,
    w_out,
    w_up,
    w_down,
    up_bias,
    norm_gains,
    shift_rows,
    lead_weight,
    lead_steps,
    valid_cells,
):
    whole = (
        lax.all_gather(w_qkv, ("band", "samp"), axis=0, tiled=True),
        lax.all_gather(w_out, ("band", "samp"), axis=0, tiled=True),
        lax.all_gather(w_up, ("band", "samp"), axis=0, tiled=True),
        lax.all_gather(w_down, ("band", "samp"), axis=0, tiled=True),
        lax.all_gather(up_bias, ("band", "samp"), axis=0, tiled=True),
        lax.all_gather(norm_gains, ("band", "samp"), axis=1, tiled=True),
        lax.all_gather(shift_rows, ("band", "samp"), axis=1, tiled=True),
        lax.all_gather(lead_weight, ("band", "samp"), axis=1, tiled=True),
    )
    qkv_full = whole[0]
    out_full = whole[1]
    up_full = whole[2]
    down_full = whole[3]
    up_shift = whole[4].astype(jnp.float32)
    gain_all = whole[5].astype(jnp.float32)
    shift_all = whole[6].astype(jnp.float32)
    lead_all = whole[7].astype(jnp.float32)
    row_count = tokens.shape[1]
    width = tokens.shape[2]
    head_count = HEADS
    head_size = width // head_count
    score_scale = head_size ** (-0.5)
    lead_days = lead_steps[0].astype(jnp.float32) * 0.25
    entering = tokens[0].astype(jnp.float32) + lead_days * lead_all[0] + lead_all[1]
    normed, norm_first_back = jax.vjp(layer_norm, entering, gain_all[0], shift_all[0])
    normed_low = normed.astype(jnp.bfloat16)
    project = jnp.dot(normed_low, qkv_full, preferred_element_type=jnp.float32)
    queries = (project[:, :width] + shift_all[1]).astype(jnp.bfloat16)
    key_rows = project[:, width : 2 * width].astype(jnp.bfloat16)
    value_rows = (project[:, 2 * width :] + shift_all[2]).astype(jnp.bfloat16)
    key_open = (valid_cells[0] > 0).astype(jnp.bfloat16)
    keys_all, values_all, open_all = (
        lax.all_gather(key_rows, "band", axis=0, tiled=True),
        lax.all_gather(value_rows, "band", axis=0, tiled=True),
        lax.all_gather(key_open, "band", axis=0, tiled=True),
    )
    seq_total = keys_all.shape[0]
    block_rows = min(512, seq_total)
    block_count = seq_total // block_rows
    block_ids = jnp.arange(block_count)
    bias_all = (open_all.astype(jnp.float32) - 1.0) * masked
    query_heads = queries.reshape(row_count, head_count, head_size)

    def block_keys(step_index):
        first_row = step_index * block_rows
        key_block = lax.dynamic_slice_in_dim(keys_all, first_row, block_rows, 0).reshape(
            block_rows, head_count, head_size
        )
        value_block = lax.dynamic_slice_in_dim(values_all, first_row, block_rows, 0).reshape(
            block_rows, head_count, head_size
        )
        bias_block = lax.dynamic_slice_in_dim(bias_all, first_row, block_rows, 0)
        scores = (
            jnp.einsum("qhe,khe->hqk", query_heads, key_block, preferred_element_type=jnp.float32)
            * score_scale
            + bias_block
        )
        return (scores, key_block, value_block)

    def max_step(running, step_index):
        row_max, exp_total = running
        scores = block_keys(step_index)[0]
        new_max = jnp.maximum(row_max, jnp.max(scores, axis=-1))
        exp_total = exp_total * jnp.exp(row_max - new_max) + jnp.sum(
            jnp.exp(scores - new_max[..., None]), axis=-1
        )
        return ((new_max, exp_total), None)

    start_max = jnp.full((head_count, row_count), -jnp.inf, jnp.float32)
    start_total = jnp.zeros((head_count, row_count), jnp.float32)
    row_max, exp_total = lax.scan(max_step, (start_max, start_total), block_ids)[0]
    log_total = row_max + jnp.log(exp_total)

    def out_step(running, step_index):
        scores, key_block, value_block = block_keys(step_index)
        weights_low = jnp.exp(scores - log_total[..., None]).astype(jnp.bfloat16)
        return (
            running
            + jnp.einsum(
                "hqk,khe->qhe", weights_low, value_block, preferred_element_type=jnp.float32
            ),
            None,
        )

    attended_heads = lax.scan(
        out_step, jnp.zeros((row_count, head_count, head_size), jnp.float32), block_ids
    )[0]
    attended_low = attended_heads.reshape(row_count, width).astype(jnp.bfloat16)
    middle = (
        entering
        + jnp.dot(attended_low, out_full, preferred_element_type=jnp.float32)
        + shift_all[3]
    )
    second, norm_second_back = jax.vjp(layer_norm, middle, gain_all[1], shift_all[4])
    second_low = second.astype(jnp.bfloat16)
    hidden_pre = jnp.dot(second_low, up_full, preferred_element_type=jnp.float32) + up_shift
    hidden, gelu_back = jax.vjp(gelu_exact, hidden_pre)
    hidden_low = hidden.astype(jnp.bfloat16)
    result = (
        middle + jnp.dot(hidden_low, down_full, preferred_element_type=jnp.float32) + shift_all[5]
    )
    output = result.astype(jnp.bfloat16)
    grad_result = cotangent[0]
    grad_result_f = grad_result.astype(jnp.float32)
    grad_down_w = jnp.einsum(
        "tf,td->fd", hidden_low, grad_result, preferred_element_type=jnp.float32
    )
    grad_shift_down = jnp.sum(grad_result_f, axis=0)
    grad_hidden = jnp.einsum(
        "td,fd->tf", grad_result, down_full, preferred_element_type=jnp.float32
    )
    grad_pre_low = gelu_back(grad_hidden)[0].astype(jnp.bfloat16)
    grad_up_w = jnp.einsum(
        "td,tf->df", second_low, grad_pre_low, preferred_element_type=jnp.float32
    )
    grad_up_shift = jnp.sum(grad_pre_low.astype(jnp.float32), axis=0)
    grad_second = jnp.einsum("tf,df->td", grad_pre_low, up_full, preferred_element_type=jnp.float32)
    grad_middle_norm, grad_gain_second, grad_shift_second = norm_second_back(grad_second)
    grad_middle = grad_result_f + grad_middle_norm
    ffn_sums = (
        lax.psum_scatter(grad_up_w, ("band", "samp"), scatter_dimension=0, tiled=True),
        lax.psum_scatter(grad_down_w, ("band", "samp"), scatter_dimension=0, tiled=True),
        lax.psum_scatter(grad_up_shift, ("band", "samp"), scatter_dimension=0, tiled=True),
    )
    grad_branch = grad_middle.astype(jnp.bfloat16)
    grad_shift_out = jnp.sum(grad_branch.astype(jnp.float32), axis=0)
    grad_out_w = jnp.einsum(
        "td,te->de", attended_low, grad_branch, preferred_element_type=jnp.float32
    )
    grad_attended = jnp.einsum(
        "te,de->td", grad_branch, out_full, preferred_element_type=jnp.float32
    ).astype(jnp.bfloat16)
    grad_heads = grad_attended.reshape(row_count, head_count, head_size)
    delta = jnp.einsum("qhe,qhe->hq", grad_heads.astype(jnp.float32), attended_heads)
    zero_heads = jnp.zeros((row_count, head_count, head_size), jnp.float32)

    def key_grad_step(g_queries, step_index):
        scores, key_block, value_block = block_keys(step_index)
        weights_full = jnp.exp(scores - log_total[..., None])
        g_weights = jnp.einsum(
            "qhe,khe->hqk", grad_heads, value_block, preferred_element_type=jnp.float32
        )
        g_scores = (weights_full * (g_weights - delta[..., None])).astype(jnp.bfloat16)
        g_queries = (
            g_queries
            + jnp.einsum("hqk,khe->qhe", g_scores, key_block, preferred_element_type=jnp.float32)
            * score_scale
        )
        key_term = (
            jnp.einsum("hqk,qhe->khe", g_scores, query_heads, preferred_element_type=jnp.float32)
            * score_scale
        )
        value_term = jnp.einsum(
            "hqk,qhe->khe",
            weights_full.astype(jnp.bfloat16),
            grad_heads,
            preferred_element_type=jnp.float32,
        )
        return (
            g_queries,
            (key_term.reshape(block_rows, width), value_term.reshape(block_rows, width)),
        )

    grad_query_heads, block_terms = lax.scan(key_grad_step, zero_heads, block_ids)
    grad_query_f = grad_query_heads.reshape(row_count, width)
    key_sum, value_sum = (
        lax.psum_scatter(
            block_terms[0].reshape(seq_total, width), "band", scatter_dimension=0, tiled=True
        ),
        lax.psum_scatter(
            block_terms[1].reshape(seq_total, width), "band", scatter_dimension=0, tiled=True
        ),
    )
    grad_query_low = grad_query_f.astype(jnp.bfloat16)
    grad_key_low = key_sum.astype(jnp.bfloat16)
    grad_value_low = value_sum.astype(jnp.bfloat16)
    grad_project = jnp.concatenate([grad_query_low, grad_key_low, grad_value_low], axis=-1)
    grad_qkv_w = jnp.einsum(
        "td,te->de", normed_low, grad_project, preferred_element_type=jnp.float32
    )
    grad_shift_query = jnp.sum(grad_query_low.astype(jnp.float32), axis=0)
    grad_shift_value = jnp.sum(grad_value_low.astype(jnp.float32), axis=0)
    grad_normed = jnp.einsum(
        "te,de->td", grad_project, qkv_full, preferred_element_type=jnp.float32
    )
    grad_entering_norm, grad_gain_first, grad_shift_first = norm_first_back(grad_normed)
    grad_entering = grad_middle + grad_entering_norm
    input_grad = grad_entering.astype(jnp.bfloat16)
    entering_sum = jnp.sum(grad_entering, axis=0)
    grad_lead_rows = jnp.stack([lead_days * entering_sum, entering_sum])
    grad_gain_rows = jnp.stack([grad_gain_first, grad_gain_second])
    grad_shift_stack = jnp.stack(
        [
            grad_shift_first,
            grad_shift_query,
            grad_shift_value,
            grad_shift_out,
            grad_shift_second,
            grad_shift_down,
        ]
    )
    attention_sums = (
        lax.psum_scatter(grad_qkv_w, ("band", "samp"), scatter_dimension=0, tiled=True),
        lax.psum_scatter(grad_out_w, ("band", "samp"), scatter_dimension=0, tiled=True),
        lax.psum_scatter(grad_gain_rows, ("band", "samp"), scatter_dimension=1, tiled=True),
        lax.psum_scatter(grad_shift_stack, ("band", "samp"), scatter_dimension=1, tiled=True),
        lax.psum_scatter(grad_lead_rows, ("band", "samp"), scatter_dimension=1, tiled=True),
    )
    return (
        output[None],
        input_grad[None],
        attention_sums[0],
        attention_sums[1],
        ffn_sums[0],
        ffn_sums[1],
        ffn_sums[2],
        attention_sums[2],
        attention_sums[3],
        attention_sums[4],
    )


MESH = pl.DeviceIdType.MESH
F32 = jnp.float32
BF16 = jnp.bfloat16
PLANE = 8
DEPTH = 4
ROWS = 128
HALF = 64
BLOCK = 256
NN = (((1,), (0,)), ((), ()))
NT = (((1,), (1,)), ((), ()))
TN = (((0,), (0,)), ((), ()))
INNER = 32


def mm(left, right, dims=NN):
    return lax.dot_general(left, right, dims, preferred_element_type=F32)


def plane_kernel(
    lead_ref, gain_in, shift_in, leadw_in, bias_in, valid_in,
    tok_in, cot_in, wqkv_in, wout_in, wup_in, wdown_in,
    out_h, ig_h, gqkv_h, gout_h, gup_h, gdown_h, gain_h, shift_h, lead_h, bias_h,
    out_o, ig_o, gqkv_o, gout_o, gup_o, gdown_o, gain_o, shift_o, lead_o, bias_o,
    wqkv, wup, vcol, vec_in,
    agf, tokown, gbown, wq, wo, wu, wd, sq, su, ztr, vt, vecf, vrow,
    normed, qaug, kaug, kt, vv, vt2, pst, ot, invl, att, aown, dsend, dob, gsend, gcol, gproj, dk, dv,
    hid, gder, gpre, mid, gmid, gdf, sct,
    part, pr, cs, au, rr,
    gds, gus, gqs, gos, gdr, gur, gqr, gor_, gda, guc, gqc, goc, go2, go3, gu2, gq2, gua, gqa,
    acc, gub, vs, vsr, vz, vzr,
    in_s, out_s, ag_s, ag_r, ac_r, fw_s, fw_r, aq_s, aq_r, v_s, v_r, y_s, y_r, w_s, w_r, z_s, z_r,
    p_s, p_r, f_r, n_s, n_r, wg_s, wg_r, h_s, h_r, g_s, g_r, gc_s, gc_r,
):
    b = lax.axis_index("band")
    s = lax.axis_index("samp")
    c = b % 2
    x = (b // 2) % 2
    y = b // 4
    mate = b + 1 - 2 * c

    def chip(r):
        xx = x + (r % 2) * (1 - 2 * x)
        yy = y + (r // 2) * (1 - 2 * y)
        return yy * 2 + xx

    def near(r):
        return chip(r) * 2 + c

    def peer(k):
        return (b + k) % PLANE

    def level(k):
        return (s + k) % DEPTH

    barrier = pltpu.get_barrier_semaphore()
    for k in range(1, PLANE):
        pl.semaphore_signal(barrier, inc=1, device_id=(peer(k), s), device_id_type=MESH)
    for k in range(1, DEPTH):
        pl.semaphore_signal(barrier, inc=1, device_id=(b, level(k)), device_id_type=MESH)

    width = tok_in.shape[1]
    fetches = [
        pltpu.make_async_copy(src, dst, in_s.at[n])
        for n, (src, dst) in enumerate((
            (wqkv_in, wqkv), (wout_in, wo.at[b, pl.ds(pl.multiple_of(s * 32, 32), 32)]),
            (tok_in.at[pl.ds(0, HALF)], agf.at[0, 0, 0, c]),
            (tok_in.at[pl.ds(HALF, HALF)], agf.at[0, 0, 1, c]),
            (wup_in, wup), (wdown_in, wd.at[s]),
            (cot_in.at[pl.ds(0, HALF)], agf.at[1, 0, 0, c]),
            (cot_in.at[pl.ds(HALF, HALF)], agf.at[1, 0, 1, c]),
        ))
    ]
    for fetch in fetches:
        fetch.start()
    vcol[...] = jnp.zeros_like(vcol)
    vcol[0:2, 0:32] = gain_in[...].astype(F32)
    vcol[2:8, 0:32] = shift_in[...].astype(F32)
    vcol[8:10, 0:32] = leadw_in[...].astype(F32)
    line = lax.broadcasted_iota(jnp.int32, (16, 128), 0)
    tile = pltpu.roll(vcol[...], s * 32, 1)
    tile = jnp.where(line == 11 + s, bias_in[...].astype(F32), tile)
    vec_in[0] = tile.astype(BF16)
    opened = jnp.where(valid_in[...] > 0, 1.0, 0.0)
    vec_in[1] = jnp.where(line == 10, opened, 0.0).astype(BF16)
    far = (s + 2) % DEPTH
    ends = (s == 0) | (s == DEPTH - 1)
    inner = (s > 0) & (s < DEPTH - 1)

    @pl.when(s == 0)
    def _():
        for kept in (gdr, gur, gqr, gor_):
            kept[0] = jnp.zeros(kept.shape[1:], BF16)

    @pl.when(s == DEPTH - 1)
    def _():
        for kept in (gda, guc, gqc, goc):
            kept[...] = jnp.zeros(kept.shape, BF16)

    fetches[0].wait()
    for d in range(PLANE):
        for j in range(3):
            sq[d, :, j * 128:(j + 1) * 128] = wqkv[:, j * width + d * 128:j * width + (d + 1) * 128]
    fetches[1].wait()
    pl.semaphore_wait(barrier, PLANE - 1 + DEPTH - 1)

    def rc(src, dst, ss, rs, band, samp):
        return pltpu.make_async_remote_copy(
            src_ref=src, dst_ref=dst, send_sem=ss, recv_sem=rs,
            device_id=(band, samp), device_id_type=MESH,
        )

    def landed(ref, sem):
        rc(ref, ref, aq_s.at[0], sem, mate, s).wait_recv()

    def left(ref, sem):
        rc(ref, ref, sem, aq_r.at[0], mate, s).wait_send()

    def yc(kind, k, src, dst):
        return rc(src, dst, y_s.at[kind], y_r.at[kind], b, level(k))

    def weight_copy(kind, region, pieces, role, to):
        return rc(region(s), region(s), w_s.at[kind], w_r.at[kind, role], b, to)

    def weight_hand(kind, region, pieces):
        return rc(region(far), region(far), w_s.at[kind], w_r.at[kind, 2], b, 3 * (s - 1))

    def weight_start(*moved):
        @pl.when(s == 1)
        def _():
            weight_copy(*moved, 1, s - 1).start()

        weight_copy(*moved, 0, far).start()

        @pl.when(ends)
        def _():
            weight_copy(*moved, 1, 1 + s // 3).start()

        @pl.when(s == 2)
        def _():
            weight_copy(*moved, 1, s + 1).start()

        @pl.when(inner)
        def _():
            weight_copy(*moved, 2, DEPTH - 1 - s).start()

    def weight_pass(kind, region, pieces):
        @pl.when(inner)
        def _():
            landed(region(far), w_r.at[kind, 0])
            weight_hand(kind, region, pieces).start()

    def weight_most(kind, region, pieces):
        landed(region(DEPTH - 1 - far), w_r.at[kind, 1])

        @pl.when(ends)
        def _():
            landed(region(far), w_r.at[kind, 0])

    def weight_last(kind, region, pieces):
        landed(region(DEPTH - 1 - s), w_r.at[kind, 2])

    def weight_finish(*moved):
        weight_most(*moved)
        weight_last(*moved)

    def weight_sent(kind, region, pieces):
        @pl.when(ends)
        def _():
            left(pieces(2), w_s.at[kind])

        @pl.when(inner)
        def _():
            left(pieces(4), w_s.at[kind])

    def grad_up(kind, stage, got, via, pieces, t):
        return rc(stage(t), got(t), z_s.at[kind], z_r.at[kind, t], b, s + 1)

    def grad_down_to(kind, stage, got, via, pieces, t):
        return rc(stage(t), got(t), z_s.at[kind], z_r.at[kind, t], b, s - 1)

    def grad_down_last(kind, stage, got, via, pieces):
        return rc(stage(s - 1), via, z_s.at[kind], z_r.at[kind, DEPTH], b, s - 1)

    def grad_start(*moved):
        for hops in (3, 2, 1):
            grad_start_some(*moved, hops)

    def grad_start_some(kind, stage, got, via, pieces, hops):
        @pl.when(s == 0)
        def _():
            grad_up(kind, stage, got, via, pieces, hops).start()

        @pl.when(s == DEPTH - 1)
        def _():
            if hops == 1:
                grad_down_last(kind, stage, got, via, pieces).start()
            else:
                grad_down_to(kind, stage, got, via, pieces, DEPTH - 1 - hops).start()

    def down_half(half):
        rows = pl.ds(half * HALF, HALF)

        @pl.when(s == 0)
        def _():
            rc(gds.at[1, rows], gdr.at[1, rows], z_s.at[0], z_r.at[0, 1], b, 1).start()

        @pl.when(s == DEPTH - 1)
        def _():
            rc(gds.at[2, rows], gda.at[rows], z_s.at[0], z_r.at[0, DEPTH], b, DEPTH - 2).start()

    def add_in(kind, stage, got, via, pieces, t):
        landed(got(t), z_r.at[kind, t])
        term, more = stage(t), got(t)
        if len(via.shape) == 3:
            def add(j, _):
                term[j] = (term[j].astype(F32) + more[j].astype(F32)).astype(BF16)
                return 0

            lax.fori_loop(0, via.shape[0], add, 0)
        else:
            def add_rows(j, _):
                rows = pl.ds(pl.multiple_of(j * INNER, INNER), INNER)
                term[rows, :] = (term[rows, :].astype(F32) + more[rows, :].astype(F32)).astype(BF16)
                return 0

            lax.fori_loop(0, via.shape[0] // INNER, add_rows, 0)

    def grad_pass(*moved):
        @pl.when(s == 1)
        def _():
            add_in(*moved, 3)
            grad_up(*moved, 3).start()

        @pl.when(s == 2)
        def _():
            add_in(*moved, 0)
            grad_down_to(*moved, 0).start()

    def grad_pass_on(*moved):
        @pl.when(s == 1)
        def _():
            add_in(*moved, 2)
            grad_up(*moved, 2).start()
            add_in(*moved, 0)
            grad_down_last(*moved).start()

        @pl.when(s == 2)
        def _():
            add_in(*moved, 1)
            grad_down_last(*moved).start()
            add_in(*moved, 3)
            grad_up(*moved, 3).start()

    def grad_finish(kind, stage, got, via, pieces):
        @pl.when(s > 0)
        def _():
            landed(got(s), z_r.at[kind, s])

        @pl.when(s < DEPTH - 1)
        def _():
            landed(via, z_r.at[kind, DEPTH])

    def grad_sent(kind, stage, got, via, pieces):
        left(pieces(3), z_s.at[kind])

    results = ((out_o, out_h), (ig_o, ig_h), (gqkv_o, gqkv_h), (gout_o, gout_h), (gup_o, gup_h), (gdown_o, gdown_h),
               (gain_o, gain_h), (shift_o, shift_h), (lead_o, lead_h), (bias_o, bias_h))

    def deliver(n):
        return pltpu.make_async_copy(results[n][0], results[n][1], out_s.at[n])

    w_out_z = (
        0, lambda t: wo.at[b, pl.ds(pl.multiple_of(t * 32, 32), 32)],
        lambda n: wo.at[b, pl.ds(0, n * 32)],
    )
    w_qkv_z = (1, lambda t: wq.at[:, t], lambda n: wq.at[:, pl.ds(0, n)])
    w_up_z = (2, lambda t: wu.at[:, t], lambda n: wu.at[:, pl.ds(0, n)])
    w_down_z = (3, lambda t: wd.at[t], lambda n: wd.at[pl.ds(0, n)])
    g_down_z = (0, lambda t: gds.at[t], lambda t: gdr.at[t], gda, lambda n: gds.at[pl.ds(0, n)])
    g_up_z = (1, lambda t: gus.at[:, t], lambda t: gur.at[t], guc, lambda n: gus.at[:, pl.ds(0, n)])
    g_qkv_z = (2, lambda t: gqs.at[:, t], lambda t: gqr.at[t], gqc, lambda n: gqs.at[:, pl.ds(0, n)])
    g_out_z = (3, lambda t: gos.at[:, t], lambda t: gor_.at[t], goc, lambda n: gos.at[:, pl.ds(0, n)])

    def gather(op, r, turn):
        return rc(
            agf.at[op % 3, 0, (turn + r) % 2, c], agf.at[op % 3, 1 + turn, r - 1, c],
            ag_s.at[op], ag_r.at[op, turn], near(r), s,
        )

    def across(op, r):
        return rc(
            agf.at[op % 3, 1, r - 1, c], agf.at[op % 3, 3, r % 2, c],
            ag_s.at[op], ac_r.at[op], near(3 - r), s,
        )

    def share(op, blk):
        return rc(
            agf.at[op % 3, blk, :, c], agf.at[op % 3, blk, :, c],
            fw_s.at[op], fw_r.at[op, blk], mate, s,
        )

    def start_gather(op):
        for turn in (0, 1):
            for r in (1, 2):
                gather(op, r, turn).start()
        share(op, 0).start()

    def arrive(op, blk):
        if blk in (1, 2):
            landed(agf.at[op % 3, blk, :, c], ag_r.at[op, blk - 1])
        if blk == 1:
            for r in (1, 2):
                across(op, r).start()
        if blk == 3:
            landed(agf.at[op % 3, 3, :, c], ac_r.at[op])
        if blk:
            share(op, blk).start()

    def gathered(op):
        left(agf.at[op % 3, pl.ds(0, 3), :, 0], ag_s.at[op])
        left(agf.at[op % 3, :, :, 0], fw_s.at[op])

    def block(op, i):
        return agf[op, i].reshape(BLOCK, -1)

    def rows_half(dev, h):
        return wo.at[dev, pl.ds(h * HALF, HALF)]

    def rows_copy(r, turn):
        part_ = rows_half(b, (turn + r) % 2)
        return rc(part_, part_, wg_s.at[0], wg_r.at[turn], near(r), s)

    def rows_across(r):
        part_ = rows_half(near(r), r % 2)
        return rc(part_, part_, wg_s.at[0], wg_r.at[2], near(3 - r), s)

    def rows_share(r):
        dev = near(r) if r else b
        return rc(wo.at[dev], wo.at[dev], wg_s.at[1], wg_r.at[3], mate, s)

    def rows_start():
        for turn in (0, 1):
            for r in (1, 2):
                rows_copy(r, turn).start()
        rows_share(0).start()

    def granule(i, a):
        return (i, a) if i in (0, 3) else (a + 1, 1 - a if i == 1 else a)

    GRANULES = [(i, a) for i in (1, 0, 2, 3) for a in (0, 1)]

    def heads_copy(i, a, k):
        r, h = granule(i, a)
        rows = pl.ds(pl.multiple_of((a * 2 + k) * HALF, HALF), HALF)
        return rc(
            att.at[i, rows], aown.at[b, pl.ds(h * HALF, HALF)],
            h_s.at[0], h_r.at[0], chip(r) * 2 + k, s,
        )

    def cores(i):
        return (1 - c,) if i == 0 else (0, 1)

    def back_copy(i, a, k):
        r, h = granule(i, a)
        dev = chip(r) * 2 + k
        return rc(
            dsend.at[dev, pl.ds(h * HALF, HALF)], dob.at[i, a, c],
            g_s.at[0], g_r.at[i], dev, s,
        )

    def branch_copy(i, a, k):
        r, h = granule(i, a)
        dev = chip(r) * 2 + k
        return rc(
            gsend.at[dev, pl.ds(h * HALF, HALF)], gcol.at[i, a, c],
            gc_s.at[0], gc_r.at[0], dev, s,
        )

    def swap(kind, k, src, dst):
        return rc(src, dst, aq_s.at[kind], aq_r.at[kind], peer(k), s)

    for k in range(1, DEPTH):
        yc(0, k, vec_in.at[0], ztr.at[k - 1]).start()
    for k in range(1, PLANE):
        swap(0, k, sq.at[peer(k)], wq.at[b, s]).start()
    weight_start(*w_out_z)
    fetches[2].wait()
    fetches[3].wait()
    for r in (1, 2):
        gather(0, r, 0).start()
    wq[b, s] = sq[b]
    fetches[4].wait()
    for d in range(PLANE):
        su[d] = wup[:, d * 512:(d + 1) * 512]
    wu[b, s] = su[b]

    landed(sq.at[pl.ds(0, 7)], aq_r.at[0])
    weight_start(*w_qkv_z)
    landed(ztr, y_r.at[0])
    vt[...] = (
        vec_in[0].astype(F32) + vec_in[1].astype(F32)
        + ztr[0].astype(F32) + ztr[1].astype(F32) + ztr[2].astype(F32)
    ).astype(BF16)

    def spread(k):
        return rc(vt, vecf.at[b], v_s.at[0], v_r.at[0], peer(k), s)

    for k in range(1, PLANE):
        spread(k).start()
    for r in (1, 2):
        gather(0, r, 1).start()
    share(0, 0).start()
    vecf[b] = vt[...]
    for k in range(1, PLANE):
        swap(1, k, su.at[peer(k)], wu.at[b, s]).start()
    arrive(0, 1)
    fetches[6].wait()
    fetches[7].wait()
    for r in (1, 2):
        gather(1, r, 0).start()
    share(1, 0).start()
    landed(vecf.at[pl.ds(0, 7)], v_r.at[0])
    for d in range(PLANE):
        vrow[:, d * 128:(d + 1) * 128] = vecf[d].astype(F32)
    lead_days = lead_ref[0].astype(F32) * 0.25
    lane = lax.broadcasted_iota(jnp.int32, (1, 128), 1)
    head_lane = [(lane < 64).astype(F32), (lane >= 64).astype(F32)]
    ones_lane = jnp.where(lane < 2, 1.0, 0.0).astype(F32)
    ends_lane = jnp.where(lane == 0, 9984.0, jnp.where(lane == 1, 16.0, 0.0)).astype(F32)
    gain1, gain2 = vrow[0:1, :], vrow[1:2, :]
    shift1, shift_out, shift2, shift_down = vrow[2:3, :], vrow[5:6, :], vrow[6:7, :], vrow[7:8, :]
    lead_row = lead_days * vrow[8:9, :] + vrow[9:10, :]
    mine = vecf[b].astype(F32)

    def stats(v):
        mean = jnp.mean(v, axis=-1, keepdims=True)
        centered = v - mean
        variance = jnp.mean(centered * centered, axis=-1, keepdims=True)
        rstd = lax.rsqrt(variance + eps)
        return centered * rstd, rstd

    for r in range(4):
        for k in range(2):
            row = jnp.broadcast_to(vecf[chip(r) * 2 + k].astype(F32)[10:11, :], (128, 128))
            column = ((row.T - 1.0) * ends_lane).astype(BF16)
            for h in range(2):
                if r in (0, 3):
                    blk, a = r, h
                else:
                    blk, a = (1 if h == r % 2 else 2), r - 1
                top = blk * BLOCK + (a * 2 + k) * HALF
                kaug[top:top + HALF, 128:256] = column[h * HALF:(h + 1) * HALF]
    for h in range(2):
        for i in range(4):
            qaug[i, h * BLOCK:(h + 1) * BLOCK, 128:256] = jnp.broadcast_to(ones_lane, (BLOCK, 128)).astype(BF16)

    def norm_block(i):
        def chunk(j, _):
            rows = pl.ds(pl.multiple_of((j % 2) * INNER, INNER), INNER)
            ent = agf[0, i, j // 4, (j // 2) % 2, rows, :].astype(F32) + lead_row
            xhat = stats(ent)[0]
            put = pl.ds(pl.multiple_of(j * INNER, INNER), INNER)
            normed[i, put, :] = (xhat * gain1 + shift1).astype(BF16)
            return 0

        lax.fori_loop(0, BLOCK // INNER, chunk, 0)

    share(0, 0).wait_recv()
    norm_block(0)
    share(0, 1).wait_recv()
    arrive(0, 2)
    norm_block(1)
    weight_pass(*w_out_z)
    weight_pass(*w_qkv_z)
    share(0, 2).wait_recv()
    norm_block(2)
    weight_finish(*w_out_z)
    rows_start()
    landed(su.at[pl.ds(0, 7)], aq_r.at[1])

    @pl.when(inner)
    def _():
        weight_copy(*w_up_z, 1, 3 * (s - 1)).start()

    arrive(0, 3)
    share(0, 3).wait_recv()
    @pl.when(ends)
    def _():
        weight_start(*w_up_z)

    norm_block(3)

    weight_finish(*w_qkv_z)
    @pl.when(inner)
    def _():
        weight_copy(*w_up_z, 0, far).start()
        weight_copy(*w_up_z, 2, DEPTH - 1 - s).start()


    def project_block(q, _):
        rows = pl.ds(pl.multiple_of(q * BLOCK, BLOCK), BLOCK)
        pj = mm(normed[q], wq[...].reshape(width, 384))
        qv = (pj[:, 0:128] + mine[3:4, :]).astype(BF16).astype(F32) * 0.125
        for h in range(2):
            qaug[q, h * BLOCK:(h + 1) * BLOCK, 0:128] = (qv * head_lane[h]).astype(BF16)
        kv = pj[:, 128:256].astype(BF16)
        kaug[rows, 0:128] = kv
        kt[:, rows] = kv.T
        vb = (pj[:, 256:384] + mine[4:5, :]).astype(BF16)
        vv[rows, :] = vb
        vt2[:, rows] = vb.T
        return 0

    lax.fori_loop(0, 4, project_block, 0)

    def mate_copy(op, i):
        return rc(part.at[op, i, :, 1 - c], pr.at[op, i], p_s.at[op], p_r.at[op, i], mate, s)

    def far_copy(op, h):
        return rc(cs.at[op, 3, h], au.at[op, 1 - h], n_s.at[op], f_r.at[op], near(h + 1), s)

    def near_copy(op, i, a):
        h = a if i == 2 else 1 - a
        return rc(cs.at[op, i, a], rr.at[op, a, h], n_s.at[op], n_r.at[op], near(a + 1), s)

    def put_part(op, i, blk):
        part[op, i] = blk.astype(BF16).reshape(2, 2, HALF, width)
        mate_copy(op, i).start()

    def fold(op, i):
        mate_copy(op, i).wait_recv()

        def chunk(j, _):
            a = j // 2
            rows = pl.ds(pl.multiple_of((j % 2) * INNER, INNER), INNER)
            cs[op, i, a, rows, :] = (
                part[op, i, a, c, rows, :].astype(F32) + pr[op, i, a, rows, :].astype(F32)
            ).astype(BF16)
            return 0

        lax.fori_loop(0, ROWS // INNER, chunk, 0)

    def fold_before(op, i, near_too=True):
        @pl.when(i < 3)
        def _():
            fold(op, i + 1)

        @pl.when(i == 2)
        def _():
            send_far(op)

        if near_too:
            @pl.when(i == 1)
            def _():
                send_near(op, 2)

    def send_far(op):
        for h in (0, 1):
            far_copy(op, h).start()

    def send_near(op, i):
        for a in (0, 1):
            near_copy(op, i, a).start()

    def send_last(op):
        landed(au.at[op], f_r.at[op])
        for a in (0, 1):
            def chunk(j, _):
                rows = pl.ds(pl.multiple_of(j * INNER, INNER), INNER)
                cs[op, 1, a, rows, :] = (
                    cs[op, 1, a, rows, :].astype(F32) + au[op, a, rows, :].astype(F32)
                ).astype(BF16)
                return 0

            lax.fori_loop(0, HALF // INNER, chunk, 0)
            near_copy(op, 1, a).start()

    def wait_sums(op):
        landed(rr.at[op], n_r.at[op])

    def place(j):
        return j // 2, pl.ds(pl.multiple_of((j % 2) * INNER, INNER), INNER)

    def plane_total(op, j):
        h, rows = place(j)
        total = cs[op, 0, h, rows, :].astype(F32)
        return total + rr[op, 0, h, rows, :].astype(F32) + rr[op, 1, h, rows, :].astype(F32)

    def own_rows(op, j):
        h, rows = place(j)
        kept = {0: tokown, 3: gbown}.get(op)
        v = agf[op, 0, h, c, rows, :] if kept is None else kept[h, rows, :]
        return v.astype(F32)

    def set_rows(op, j, v):
        h, rows = place(j)
        if op == 3:
            gbown[h, rows, :] = v
        else:
            agf[op, 0, h, c, rows, :] = v

    def end_sums(op):
        left(part.at[op, :, :, 0], p_s.at[op])
        left(cs.at[op, pl.ds(0, 3)], n_s.at[op])

    def attend_block(n, _):
        i = 3 - n

        @pl.when(n == 3)
        def _():
            landed(wo.at[0], wg_r.at[1])
            for r in (1, 2):
                rows_share(r).start()

        st = mm(kaug[...], qaug[i], NT)
        p = jnp.exp(st - jnp.max(st, axis=0, keepdims=True))
        inverse = 1.0 / jnp.sum(p, axis=0, keepdims=True)
        pb = p.astype(BF16)
        pst[i] = pb
        out = mm(vt2[...], pb) * inverse
        ot[i, 0:64, :] = out[0:64, 0:BLOCK]
        ot[i, 64:128, :] = out[64:128, BLOCK:]
        invl[i] = jnp.broadcast_to(inverse, (8, 2 * BLOCK))
        att[i] = ot[i].T.astype(BF16)
        for blk in range(4):
            @pl.when(i == blk)
            def _():
                for a in (0, 1):
                    for k in cores(blk):
                        heads_copy(blk, a, k).start()

        return 0

    tokown[...] = agf[0, 0, :, c]
    gathered(0)
    landed(wo.at[0], wg_r.at[0])
    for r in (1, 2):
        rows_across(r).start()
    lax.fori_loop(0, 4, attend_block, 0)
    landed(wo.at[0], wg_r.at[2])
    rows_share(3).start()
    arrive(1, 1)
    for h in (0, 1):
        top = pl.multiple_of((h * 2 + c) * HALF, HALF)
        aown[b, h * HALF:(h + 1) * HALF] = att[0, pl.ds(top, HALF), :]
    weight_pass(*w_up_z)
    fetches[5].wait()

    @pl.when(inner)
    def _():
        weight_start(*w_down_z)

    landed(wo.at[pl.ds(0, 4)], wg_r.at[3])
    landed(aown.at[pl.ds(0, 7)], h_r.at[0])
    heads = jnp.concatenate([aown[d] for d in range(PLANE)], axis=1)
    mid[...] = mm(heads, wo[...].reshape(1024, width))
    agf[0, 0, :, c] = heads.reshape(2, HALF, width)

    def middle_chunk(j, _):
        rows = pl.ds(pl.multiple_of(j * INNER, INNER), INNER)
        m = own_rows(0, j) + lead_row + mid[rows, :] + shift_out
        mid[rows, :] = m
        set_rows(2, j, (stats(m)[0] * gain2 + shift2).astype(BF16))
        return 0

    lax.fori_loop(0, ROWS // INNER, middle_chunk, 0)
    start_gather(2)
    arrive(1, 3)
    arrive(2, 1)
    for r in (1, 2):
        gather(1, r, 1).start()
    start_gather(3)

    @pl.when(ends)
    def _():
        weight_start(*w_down_z)

    weight_finish(*w_up_z)

    bias = jnp.concatenate([mine[11 + j:12 + j, :] for j in range(4)], axis=1)

    def arrivals(op, i):
        for blk in range(4):
            @pl.when(i == blk)
            def _():
                if blk != 1:
                    arrive(op, blk)
                share(op, blk).wait_recv()

    def down_grad_first(f, _):
        cols = pl.ds(pl.multiple_of(f * BLOCK, BLOCK), BLOCK)
        gdf[pl.ds(pl.multiple_of(f * BLOCK, BLOCK), BLOCK), :] = mm(
            hid[:2 * BLOCK, cols], agf[1, 0:2].reshape(2 * BLOCK, width), TN
        )
        return 0

    def up_block(i, _):
        @pl.when(i == 3)
        def _():
            for blk in range(2):
                share(1, blk).wait_recv()
            lax.fori_loop(0, 2, down_grad_first, 0)

        arrivals(2, i)


        hp = mm(block(2, i), wu[...].reshape(width, 512)) + bias
        phi = 0.5 + 0.5 * lax.erf(hp * 0.7071067811865476)
        hid[pl.ds(pl.multiple_of(i * BLOCK, BLOCK), BLOCK), :] = (hp * phi).astype(BF16)
        gder[i] = phi + hp * jnp.exp(hp * hp * -0.5) * 0.3989422804014327
        return 0

    lax.fori_loop(0, 4, up_block, 0)
    weight_pass(*w_down_z)
    arrive(1, 2)
    share(1, 2).wait_recv()
    share(1, 3).wait_recv()

    def down_grad(f, _):
        cols = pl.ds(pl.multiple_of(f * BLOCK, BLOCK), BLOCK)
        g = gdf[pl.ds(pl.multiple_of(f * BLOCK, BLOCK), BLOCK), :] + mm(
            hid[2 * BLOCK:, cols], agf[1, 2:4].reshape(2 * BLOCK, width), TN
        )
        gds[pl.ds(2 * f, 2)] = g.astype(BF16).reshape(2, 128, width)
        return 0

    lax.fori_loop(0, 2, down_grad, 0)
    grad_start_some(*g_down_z, 3)
    grad_start_some(*g_down_z, 2)
    down_half(0)
    for i in range(4):
        for j in range(i + 1):
            upper = normed[j, :, i * BLOCK:(i + 1) * BLOCK].T
            if i != j:
                normed[j, :, i * BLOCK:(i + 1) * BLOCK] = normed[i, :, j * BLOCK:(j + 1) * BLOCK].T
            normed[i, :, j * BLOCK:(j + 1) * BLOCK] = upper
    def turn_second(i, _):
        cols = pl.ds(pl.multiple_of(i * BLOCK, BLOCK), BLOCK)
        blk = block(2, i)
        for f in range(4):
            sct[f, :, cols] = blk[:, f * BLOCK:(f + 1) * BLOCK].T
        return 0

    lax.fori_loop(0, 4, turn_second, 0)

    def even_out(n, _):
        i = n // 4
        rows = pl.ds(pl.multiple_of((n % 4) * BLOCK, BLOCK), BLOCK)
        pst[i, rows, :] = (pst[i, rows, :].astype(F32) * invl[i, 0:1, :]).astype(BF16)
        return 0

    lax.fori_loop(0, 16, even_out, 0)

    left(wo.at[pl.ds(0, 3)], wg_s.at[0])
    left(wo.at[pl.ds(0, 4)], wg_s.at[1])
    weight_sent(*w_out_z)

    def wo_block(i, j):
        return wo[2 * i:2 * i + 2, :, j * BLOCK:(j + 1) * BLOCK].reshape(BLOCK, BLOCK)

    for i in range(4):
        for j in range(i + 1):
            upper = wo_block(j, i).T.reshape(2, ROWS, BLOCK)
            if i != j:
                wo[2 * j:2 * j + 2, :, i * BLOCK:(i + 1) * BLOCK] = wo_block(i, j).T.reshape(2, ROWS, BLOCK)
            wo[2 * i:2 * i + 2, :, j * BLOCK:(j + 1) * BLOCK] = upper
    arrive(3, 1)
    arrive(3, 2)
    weight_finish(*w_down_z)
    gub[...] = jnp.zeros_like(gub)
    arrive(3, 3)

    def back_block(n, _):
        i = 3 - n
        rows = pl.ds(pl.multiple_of(i * BLOCK, BLOCK), BLOCK)
        gp = (gder[i] * mm(block(1, i), wd[...].reshape(512, width), NT)).astype(BF16)
        put_part(0, i, mm(gp, wu[...].reshape(width, 512), NT))
        gpre[rows, :] = gp
        gub[...] += jnp.sum(gp.astype(F32).reshape(BLOCK // 8, 8, 512), axis=0)
        fold_before(0, i)
        return 0

    grad_pass(*g_down_z)
    lax.fori_loop(0, 4, back_block, 0)
    fold(0, 0)

    def up_grad(f, _):
        g = mm(sct[pl.ds(2 * f, 2)].reshape(2 * BLOCK, 1024), gpre[...])
        gus[pl.ds(4 * f, 4)] = g.astype(BF16).reshape(4, 4, 32, 512)
        return 0

    lax.fori_loop(0, 2, up_grad, 0)
    grad_start(*g_up_z)

    def out_block(n, _):
        i = 3 - n
        rows = pl.ds(pl.multiple_of(i * BLOCK, BLOCK), BLOCK)
        put_part(1, i, mm(hid[rows, :], wd[...].reshape(512, width)))
        fold_before(1, i, near_too=False)
        return 0

    send_last(0)
    grad_pass_on(*g_down_z)
    lax.fori_loop(0, 4, out_block, 0)
    fold(1, 0)

    wait_sums(0)
    acc[...] = jnp.zeros_like(acc)

    def add_row(n, v):
        acc[n] += jnp.sum(v.reshape(INNER // 8, 8, width), axis=0)

    def norm_back(v, grad, gain):
        xhat, rstd = stats(v)
        d = grad * gain
        mean_d = jnp.mean(d, axis=-1, keepdims=True)
        mean_dx = jnp.mean(d * xhat, axis=-1, keepdims=True)
        return rstd * (d - mean_d - xhat * mean_dx), xhat

    def second_chunk(j, _):
        rows = pl.ds(pl.multiple_of(j * INNER, INNER), INNER)
        gs = plane_total(0, j)
        g, xhat = norm_back(mid[rows, :], gs, gain2)
        ct = own_rows(1, j)
        gm = ct + g
        gmid[rows, :] = gm
        gb = gm.astype(BF16)
        set_rows(3, j, gb)
        add_row(1, gs * xhat)
        add_row(6, gs)
        return 0

    lax.fori_loop(0, ROWS // INNER, second_chunk, 0)
    gbo = gbown[...].reshape(ROWS, width)
    gha = mm(gbo, wo[...].reshape(width, 1024)).astype(BF16)
    for d in range(PLANE):
        dsend[d] = gha[:, d * 128:(d + 1) * 128]
    for i, a in GRANULES:
        for k in cores(i):
            back_copy(i, a, k).start()
    for h in (0, 1):
        dob[0, h, c] = dsend[b, h * HALF:(h + 1) * HALF, :]
    for d in range(PLANE):
        gsend[d] = gbo[:, d * 128:(d + 1) * 128]
    for i, a in GRANULES:
        for k in cores(i):
            branch_copy(i, a, k).start()
    for h in (0, 1):
        gcol[0, h, c] = gsend[b, h * HALF:(h + 1) * HALF, :]

    grad_pass(*g_up_z)
    dk[...] = jnp.zeros_like(dk)
    dv[...] = jnp.zeros_like(dv)

    def attend_back(i, _):
        for blk in range(4):
            @pl.when(i == blk)
            def _():
                landed(dob.at[blk] if blk else dob.at[0, :, 0], g_r.at[blk])

        do_rows = dob[i].reshape(BLOCK, 128)
        do_cols = do_rows.T.astype(F32)
        prod = do_cols * ot[i]
        delta = jnp.concatenate(
            [jnp.sum(prod[h * 64:(h + 1) * 64], axis=0, keepdims=True) for h in range(2)], axis=1
        )
        zero = jnp.zeros((64, BLOCK), F32)
        spread_cols = jnp.concatenate([
            jnp.concatenate([do_cols[0:64], zero], axis=0),
            jnp.concatenate([zero, do_cols[64:128]], axis=0),
        ], axis=1).astype(BF16)
        spread_rows = jnp.concatenate(
            [(do_rows.astype(F32) * head_lane[h]).astype(BF16) for h in range(2)], axis=0
        )
        pb = pst[i]
        ds = (pb.astype(F32) * (mm(vv[...], spread_cols) - delta)).astype(BF16)
        dv[...] += mm(pb, spread_rows)
        dk[...] += mm(ds, qaug[i, :, 0:128])
        dq = mm(kt[...], ds)
        dq = jnp.concatenate([dq[0:64, 0:BLOCK], dq[64:128, BLOCK:]], axis=0).T * 0.125
        gproj[pl.ds(pl.multiple_of(i * BLOCK, BLOCK), BLOCK), 0:128] = dq.astype(BF16)
        return 0

    lax.fori_loop(0, 4, attend_back, 0)
    gproj[:, 128:256] = dk[...].astype(BF16)
    gproj[:, 256:384] = dv[...].astype(BF16)

    put_part(2, 3, mm(gproj[3 * BLOCK:, :], wq[...].reshape(width, 384), NT))
    gqs[...] = mm(normed[...].reshape(1024, 1024), gproj[...]).astype(BF16).reshape(8, 4, 32, 384)
    grad_start_some(*g_qkv_z, 3)
    grad_start_some(*g_qkv_z, 2)
    fold(2, 3)
    send_far(2)
    grad_pass_on(*g_up_z)

    def project_back(n, _):
        i = 2 - n
        rows = pl.ds(pl.multiple_of(i * BLOCK, BLOCK), BLOCK)
        put_part(2, i, mm(gproj[rows, :], wq[...].reshape(width, 384), NT))

        @pl.when(n == 1)
        def _():
            fold(2, 2)
            send_near(2, 2)

        return 0

    lax.fori_loop(0, 3, project_back, 0)
    fold(2, 1)
    fold(2, 0)
    grad_pass(*g_qkv_z)
    for i in range(4):
        share(3, i).wait_recv()
    landed(aown.at[pl.ds(0, 7)], gc_r.at[0])
    gos[...] = mm(gcol[...].reshape(1024, 128), agf[0].reshape(1024, width), TN).T.astype(BF16).reshape(
        PLANE, DEPTH, 32, 128
    )
    grad_start_some(*g_out_z, 3)
    grad_start_some(*g_out_z, 2)
    grad_start_some(*g_qkv_z, 1)
    grad_start_some(*g_out_z, 1)
    send_last(2)
    send_near(1, 2)
    send_last(1)

    def others(kind, stage, got, via, pieces):
        return [got(s), via]

    grad_pass(*g_out_z)
    grad_pass_on(*g_qkv_z)
    def own_sums(j, _):
        add_row(5, own_rows(3, j))
        add_row(7, own_rows(1, j))
        return 0

    lax.fori_loop(0, ROWS // INNER, own_sums, 0)
    wait_sums(2)

    def first_chunk(j, _):
        rows = pl.ds(pl.multiple_of(j * INNER, INNER), INNER)
        gn = plane_total(2, j)
        g, xhat = norm_back(own_rows(0, j) + lead_row, gn, gain1)
        ge = gmid[rows, :] + g
        ig_o[rows, :] = ge.astype(BF16)
        add_row(0, gn * xhat)
        add_row(2, gn)
        add_row(9, ge)
        return 0

    lax.fori_loop(0, ROWS // INNER, first_chunk, 0)
    deliver(1).start()
    acc[8] = acc[9] * lead_days

    sums = [jnp.sum(acc[n], axis=0, keepdims=True) for n in range(10)]
    packed = jnp.concatenate(sums + [jnp.zeros((6, width), F32)], axis=0)
    for d in range(PLANE):
        vs[d] = packed[:, d * 128:(d + 1) * 128]

    def vec_swap(k):
        return rc(vs.at[peer(k)], vsr.at[k - 1], v_s.at[1], v_r.at[1], peer(k), s)

    for k in range(1, PLANE):
        vec_swap(k).start()
    gq_cols = jnp.sum(gproj[:, 0:128].astype(F32), axis=0, keepdims=True)
    gv_cols = jnp.sum(gproj[:, 256:384].astype(F32), axis=0, keepdims=True)
    gub_row = jnp.sum(gub[...], axis=0, keepdims=True)
    extra = jnp.concatenate(
        [jnp.zeros((3, 128), F32), gq_cols, gv_cols, jnp.zeros((6, 128), F32)]
        + [gub_row[:, j * 128:(j + 1) * 128] for j in range(4)]
        + [jnp.zeros((1, 128), F32)],
        axis=0,
    )
    grad_finish(*g_up_z)
    for d in range(PLANE):
        gu2[d] = sum(
            [t[d].astype(F32) for t in others(*g_up_z)], gus[d, s].astype(F32)
        ).astype(BF16)
    for k in range(1, PLANE):
        swap(2, k, gu2.at[peer(k)], gua.at[b]).start()
    gua[b] = gu2[b]
    grad_pass_on(*g_out_z)
    landed(vs.at[pl.ds(0, 7)], v_r.at[1])
    total = vs[b] + extra
    for k in range(PLANE - 1):
        total = total + vsr[k]
    vz[...] = total
    for k in range(1, DEPTH):
        yc(1, k, vz, vzr.at[k - 1]).start()
    down_half(1)

    grad_finish(*g_qkv_z)
    for d in range(PLANE):
        gq2[d] = sum(
            [t[d].astype(F32) for t in others(*g_qkv_z)], gqs[d, s].astype(F32)
        ).astype(BF16)
    for k in range(1, PLANE):
        swap(3, k, gq2.at[peer(k)], gqa.at[b]).start()
    gqa[b] = gq2[b]
    grad_finish(*g_out_z)
    for d in range(PLANE):
        go2[d] = sum(
            [t[d].astype(F32) for t in others(*g_out_z)], gos[d, s].astype(F32)
        ).astype(BF16)
    for k in range(1, PLANE):
        swap(4, k, go2.at[peer(k)], go3.at[b]).start()
    go3[b] = go2[b]
    wait_sums(1)

    def output_chunk(j, _):
        rows = pl.ds(pl.multiple_of(j * INNER, INNER), INNER)
        out_o[rows, :] = (mid[rows, :] + plane_total(1, j) + shift_down).astype(BF16)
        return 0

    lax.fori_loop(0, ROWS // INNER, output_chunk, 0)
    deliver(0).start()

    grad_finish(*g_down_z)
    gdown_o[...] = sum([t[...].astype(F32) for t in others(*g_down_z)], gds[s].astype(F32))
    deliver(5).start()
    landed(gu2.at[pl.ds(0, 7)], aq_r.at[2])
    for d in range(PLANE):
        gup_o[:, d * 512:(d + 1) * 512] = gua[d].astype(F32)
    deliver(4).start()
    landed(vzr, y_r.at[1])
    vz_sum = vz[...] + vzr[0] + vzr[1] + vzr[2]
    columns = pltpu.roll(vz_sum, (128 - 32 * s) % 128, 1)
    gain_o[...] = columns[0:2, 0:32]
    shift_o[...] = columns[2:8, 0:32]
    lead_o[...] = columns[8:10, 0:32]
    bias_o[...] = jnp.sum(jnp.where(line == 11 + s, vz_sum, 0.0), axis=0, keepdims=True)
    for n in range(6, 10):
        deliver(n).start()
    landed(go2.at[pl.ds(0, 7)], aq_r.at[4])
    for d in range(PLANE):
        gout_o[:, d * 128:(d + 1) * 128] = go3[d].astype(F32)
    deliver(3).start()
    landed(gq2.at[pl.ds(0, 7)], aq_r.at[3])
    for d in range(PLANE):
        for j in range(3):
            gqkv_o[:, j * width + d * 128:j * width + (d + 1) * 128] = (
                gqa[d, :, j * 128:(j + 1) * 128].astype(F32)
            )

    deliver(2).start()
    for op in (1, 2, 3):
        gathered(op)
    for op in range(3):
        end_sums(op)
    left(aown.at[pl.ds(0, 7)], h_s.at[0])
    left(dsend.at[pl.ds(0, 7)], g_s.at[0])
    left(gsend.at[pl.ds(0, 7)], gc_s.at[0])
    for kind, sent in enumerate((sq, su, gu2, gq2, go2)):
        left(sent.at[pl.ds(0, 7)], aq_s.at[kind])
    left(vecf.at[pl.ds(0, 7)], v_s.at[0])
    left(vs.at[pl.ds(0, 7)], v_s.at[1])
    left(ztr, y_s.at[0])
    left(vzr, y_s.at[1])
    for moved in (w_qkv_z, w_up_z, w_down_z):
        weight_sent(*moved)
    for moved in (g_down_z, g_up_z, g_qkv_z, g_out_z):
        grad_sent(*moved)
    for n in range(10):
        deliver(n).wait()


def hand_over(*refs):
    count = len(refs) // 3
    given, taken, held, sems = refs[:count], refs[count:2 * count], refs[2 * count:3 * count], refs[-1]
    into = [pltpu.make_async_copy(given[n], held[n], sems.at[0, n]) for n in range(count)]
    out = [pltpu.make_async_copy(held[n], taken[n], sems.at[1, n]) for n in range(count)]
    for copy in into:
        copy.start()
    for n in range(count):
        into[n].wait()
        out[n].start()
    for copy in out:
        copy.wait()


def plane_body(
    tokens, cotangent, w_qkv, w_out, w_up, w_down,
    up_bias, norm_gains, shift_rows, lead_weight, lead_steps, valid_cells,
):
    width = tokens.shape[2]
    vmem = pl.BlockSpec(memory_space=pltpu.VMEM)
    anywhere = pl.BlockSpec(memory_space=pl.ANY)
    dma = pltpu.SemaphoreType.DMA
    V = pltpu.VMEM
    out_shape = (
        jax.ShapeDtypeStruct((ROWS, width), BF16),
        jax.ShapeDtypeStruct((ROWS, width), BF16),
        jax.ShapeDtypeStruct((32, 3 * width), F32),
        jax.ShapeDtypeStruct((32, width), F32),
        jax.ShapeDtypeStruct((32, 4 * width), F32),
        jax.ShapeDtypeStruct((128, width), F32),
        jax.ShapeDtypeStruct((2, 32), F32),
        jax.ShapeDtypeStruct((6, 32), F32),
        jax.ShapeDtypeStruct((2, 32), F32),
        jax.ShapeDtypeStruct((1, 128), F32),
    )
    scratch = [
        V((ROWS, width), BF16), V((ROWS, width), BF16),
        V((32, 3 * width), F32), V((32, width), F32),
        V((32, 4 * width), F32), V((128, width), F32),
        V((2, 32), F32), V((6, 32), F32), V((2, 32), F32), V((1, 128), F32),
        V((32, 3 * width), BF16), V((32, 4 * width), BF16),
        V((16, 128), F32), V((2, 16, 128), BF16),
        V((3, 4, 2, 2, HALF, width), BF16),
        V((2, HALF, width), BF16), V((2, HALF, width), BF16),
        V((PLANE, DEPTH, 32, 384), BF16),
        V((PLANE, 128, width), BF16),
        V((PLANE, DEPTH, 32, 512), BF16),
        V((DEPTH, 128, width), BF16),
        V((PLANE, 32, 384), BF16),
        V((PLANE, 32, 512), BF16),
        V((3, 16, 128), BF16),
        V((16, 128), BF16),
        V((PLANE, 16, 128), BF16),
        V((16, width), F32),
        V((4, BLOCK, width), BF16),
        V((4, 2 * BLOCK, 256), BF16),
        V((1024, 256), BF16),
        V((128, 1024), BF16),
        V((1024, 128), BF16),
        V((128, 1024), BF16),
        V((4, 1024, 2 * BLOCK), BF16),
        V((4, 128, BLOCK), F32),
        V((4, 8, 2 * BLOCK), F32),
        V((4, BLOCK, 128), BF16),
        V((PLANE, ROWS, 128), BF16),
        V((PLANE, ROWS, 128), BF16),
        V((4, 2, 2, HALF, 128), BF16),
        V((PLANE, ROWS, 128), BF16),
        V((4, 2, 2, HALF, 128), BF16),
        V((1024, 384), BF16),
        V((1024, 128), F32),
        V((1024, 128), F32),
        V((1024, 512), BF16),
        V((4, BLOCK, 512), F32),
        V((1024, 512), BF16),
        V((ROWS, width), F32),
        V((ROWS, width), F32),
        V((512, width), F32),
        V((4, BLOCK, 1024), BF16),
        V((3, 4, 2, 2, HALF, width), BF16),
        V((3, 4, 2, HALF, width), BF16),
        V((3, 4, 2, HALF, width), BF16),
        V((3, 2, HALF, width), BF16),
        V((3, 2, 2, HALF, width), BF16),
        V((DEPTH, 128, width), BF16),
        V((PLANE, DEPTH, 32, 512), BF16),
        V((PLANE, DEPTH, 32, 384), BF16),
        V((PLANE, DEPTH, 32, 128), BF16),
        V((DEPTH, 128, width), BF16),
        V((DEPTH, PLANE, 32, 512), BF16),
        V((DEPTH, PLANE, 32, 384), BF16),
        V((DEPTH, PLANE, 32, 128), BF16),
        V((128, width), BF16),
        V((PLANE, 32, 512), BF16),
        V((PLANE, 32, 384), BF16),
        V((PLANE, 32, 128), BF16),
        V((PLANE, 32, 128), BF16), V((PLANE, 32, 128), BF16),
        V((PLANE, 32, 512), BF16),
        V((PLANE, 32, 384), BF16),
        V((PLANE, 32, 512), BF16),
        V((PLANE, 32, 384), BF16),
        V((10, 8, width), F32),
        V((8, 512), F32),
        V((PLANE, 16, 128), F32),
        V((PLANE - 1, 16, 128), F32),
        V((16, 128), F32),
        V((3, 16, 128), F32),
        dma((8,)), dma((10,)),
        dma((4,)), dma((4, 2)), dma((4,)), dma((4,)), dma((4, 4)),
        dma((5,)), dma((5,)), dma((2,)), dma((2,)), dma((2,)), dma((2,)),
        dma((4,)), dma((4, 3)), dma((4,)), dma((4, 5)),
        dma((3,)), dma((3, 4)), dma((3,)), dma((3,)), dma((3,)),
        dma((2,)), dma((4,)), dma((1,)), dma((1,)), dma((1,)), dma((4,)), dma((1,)), dma((1,)),
    ]
    results = pl.pallas_call(
        plane_kernel,
        out_shape=out_shape,
        in_specs=[pl.BlockSpec(memory_space=pltpu.SMEM)] + [vmem] * 5 + [anywhere] * 6,
        out_specs=tuple([anywhere] * 10),
        scratch_shapes=scratch,
        compiler_params=pltpu.CompilerParams(
            collective_id=0, has_side_effects=True, vmem_limit_bytes=63 * 2**20
        ),
    )(
        lead_steps, norm_gains, shift_rows, lead_weight, up_bias[None], valid_cells,
        tokens[0], cotangent[0], w_qkv, w_out, w_up, w_down,
    )
    results = pl.pallas_call(
        hand_over,
        out_shape=out_shape,
        in_specs=[anywhere] * len(out_shape),
        out_specs=tuple([anywhere] * len(out_shape)),
        scratch_shapes=[V(o.shape, o.dtype) for o in out_shape] + [dma((2, len(out_shape)))],
    )(*results)
    output, input_grad, g_qkv, g_out, g_up, g_down, g_gains, g_shifts, g_lead, g_bias = results
    return (
        output[None], input_grad[None], g_qkv, g_out, g_up, g_down, g_bias[0],
        g_gains, g_shifts, g_lead,
    )


def plane_fits(mesh):
    return mesh.shape["band"] == PLANE and mesh.shape["samp"] == DEPTH


def solution(mesh):
    return jax.shard_map(
        plane_body if plane_fits(mesh) else body,
        mesh=mesh,
        in_specs=(
            P("samp", "band", None),
            P("samp", "band", None),
            P(("band", "samp"), None),
            P(("band", "samp"), None),
            P(("band", "samp"), None),
            P(("band", "samp"), None),
            P(("band", "samp")),
            P(None, ("band", "samp")),
            P(None, ("band", "samp")),
            P(None, ("band", "samp")),
            P("samp"),
            P("samp", "band"),
        ),
        out_specs=(
            P("samp", "band", None),
            P("samp", "band", None),
            P(("band", "samp"), None),
            P(("band", "samp"), None),
            P(("band", "samp"), None),
            P(("band", "samp"), None),
            P(("band", "samp")),
            P(None, ("band", "samp")),
            P(None, ("band", "samp")),
            P(None, ("band", "samp")),
        ),
        check_vma=False,
    )
```

```python
import jax
import jax.numpy as jnp
from jax import lax
from jax.experimental import pallas as pl
from jax.experimental.pallas import tpu as pltpu
from jax.sharding import PartitionSpec as P

HEADS = 16


eps = 1e-05
masked = 10000.0


def layer_norm(values, gain_row, shift_row):
    centered = values - jnp.mean(values, axis=-1, keepdims=True)
    variance = jnp.mean(centered * centered, axis=-1, keepdims=True)
    return centered * lax.rsqrt(variance + eps) * gain_row + shift_row


def gelu_exact(values):
    return jax.nn.gelu(values, approximate=False)


def body(
    tokens,
    cotangent,
    w_qkv,
    w_out,
    w_up,
    w_down,
    up_bias,
    norm_gains,
    shift_rows,
    lead_weight,
    lead_steps,
    valid_cells,
):
    whole = (
        lax.all_gather(w_qkv, ("band", "samp"), axis=0, tiled=True),
        lax.all_gather(w_out, ("band", "samp"), axis=0, tiled=True),
        lax.all_gather(w_up, ("band", "samp"), axis=0, tiled=True),
        lax.all_gather(w_down, ("band", "samp"), axis=0, tiled=True),
        lax.all_gather(up_bias, ("band", "samp"), axis=0, tiled=True),
        lax.all_gather(norm_gains, ("band", "samp"), axis=1, tiled=True),
        lax.all_gather(shift_rows, ("band", "samp"), axis=1, tiled=True),
        lax.all_gather(lead_weight, ("band", "samp"), axis=1, tiled=True),
    )
    qkv_full = whole[0]
    out_full = whole[1]
    up_full = whole[2]
    down_full = whole[3]
    up_shift = whole[4].astype(jnp.float32)
    gain_all = whole[5].astype(jnp.float32)
    shift_all = whole[6].astype(jnp.float32)
    lead_all = whole[7].astype(jnp.float32)
    row_count = tokens.shape[1]
    width = tokens.shape[2]
    head_count = HEADS
    head_size = width // head_count
    score_scale = head_size ** (-0.5)
    lead_days = lead_steps[0].astype(jnp.float32) * 0.25
    entering = tokens[0].astype(jnp.float32) + lead_days * lead_all[0] + lead_all[1]
    normed, norm_first_back = jax.vjp(layer_norm, entering, gain_all[0], shift_all[0])
    normed_low = normed.astype(jnp.bfloat16)
    project = jnp.dot(normed_low, qkv_full, preferred_element_type=jnp.float32)
    queries = (project[:, :width] + shift_all[1]).astype(jnp.bfloat16)
    key_rows = project[:, width : 2 * width].astype(jnp.bfloat16)
    value_rows = (project[:, 2 * width :] + shift_all[2]).astype(jnp.bfloat16)
    key_open = (valid_cells[0] > 0).astype(jnp.bfloat16)
    keys_all, values_all, open_all = (
        lax.all_gather(key_rows, "band", axis=0, tiled=True),
        lax.all_gather(value_rows, "band", axis=0, tiled=True),
        lax.all_gather(key_open, "band", axis=0, tiled=True),
    )
    seq_total = keys_all.shape[0]
    block_rows = min(512, seq_total)
    block_count = seq_total // block_rows
    block_ids = jnp.arange(block_count)
    bias_all = (open_all.astype(jnp.float32) - 1.0) * masked
    query_heads = queries.reshape(row_count, head_count, head_size)

    def block_keys(step_index):
        first_row = step_index * block_rows
        key_block = lax.dynamic_slice_in_dim(keys_all, first_row, block_rows, 0).reshape(
            block_rows, head_count, head_size
        )
        value_block = lax.dynamic_slice_in_dim(values_all, first_row, block_rows, 0).reshape(
            block_rows, head_count, head_size
        )
        bias_block = lax.dynamic_slice_in_dim(bias_all, first_row, block_rows, 0)
        scores = (
            jnp.einsum("qhe,khe->hqk", query_heads, key_block, preferred_element_type=jnp.float32)
            * score_scale
            + bias_block
        )
        return (scores, key_block, value_block)

    def max_step(running, step_index):
        row_max, exp_total = running
        scores = block_keys(step_index)[0]
        new_max = jnp.maximum(row_max, jnp.max(scores, axis=-1))
        exp_total = exp_total * jnp.exp(row_max - new_max) + jnp.sum(
            jnp.exp(scores - new_max[..., None]), axis=-1
        )
        return ((new_max, exp_total), None)

    start_max = jnp.full((head_count, row_count), -jnp.inf, jnp.float32)
    start_total = jnp.zeros((head_count, row_count), jnp.float32)
    row_max, exp_total = lax.scan(max_step, (start_max, start_total), block_ids)[0]
    log_total = row_max + jnp.log(exp_total)

    def out_step(running, step_index):
        scores, key_block, value_block = block_keys(step_index)
        weights_low = jnp.exp(scores - log_total[..., None]).astype(jnp.bfloat16)
        return (
            running
            + jnp.einsum(
                "hqk,khe->qhe", weights_low, value_block, preferred_element_type=jnp.float32
            ),
            None,
        )

    attended_heads = lax.scan(
        out_step, jnp.zeros((row_count, head_count, head_size), jnp.float32), block_ids
    )[0]
    attended_low = attended_heads.reshape(row_count, width).astype(jnp.bfloat16)
    middle = (
        entering
        + jnp.dot(attended_low, out_full, preferred_element_type=jnp.float32)
        + shift_all[3]
    )
    second, norm_second_back = jax.vjp(layer_norm, middle, gain_all[1], shift_all[4])
    second_low = second.astype(jnp.bfloat16)
    hidden_pre = jnp.dot(second_low, up_full, preferred_element_type=jnp.float32) + up_shift
    hidden, gelu_back = jax.vjp(gelu_exact, hidden_pre)
    hidden_low = hidden.astype(jnp.bfloat16)
    result = (
        middle + jnp.dot(hidden_low, down_full, preferred_element_type=jnp.float32) + shift_all[5]
    )
    output = result.astype(jnp.bfloat16)
    grad_result = cotangent[0]
    grad_result_f = grad_result.astype(jnp.float32)
    grad_down_w = jnp.einsum(
        "tf,td->fd", hidden_low, grad_result, preferred_element_type=jnp.float32
    )
    grad_shift_down = jnp.sum(grad_result_f, axis=0)
    grad_hidden = jnp.einsum(
        "td,fd->tf", grad_result, down_full, preferred_element_type=jnp.float32
    )
    grad_pre_low = gelu_back(grad_hidden)[0].astype(jnp.bfloat16)
    grad_up_w = jnp.einsum(
        "td,tf->df", second_low, grad_pre_low, preferred_element_type=jnp.float32
    )
    grad_up_shift = jnp.sum(grad_pre_low.astype(jnp.float32), axis=0)
    grad_second = jnp.einsum("tf,df->td", grad_pre_low, up_full, preferred_element_type=jnp.float32)
    grad_middle_norm, grad_gain_second, grad_shift_second = norm_second_back(grad_second)
    grad_middle = grad_result_f + grad_middle_norm
    ffn_sums = (
        lax.psum_scatter(grad_up_w, ("band", "samp"), scatter_dimension=0, tiled=True),
        lax.psum_scatter(grad_down_w, ("band", "samp"), scatter_dimension=0, tiled=True),
        lax.psum_scatter(grad_up_shift, ("band", "samp"), scatter_dimension=0, tiled=True),
    )
    grad_branch = grad_middle.astype(jnp.bfloat16)
    grad_shift_out = jnp.sum(grad_branch.astype(jnp.float32), axis=0)
    grad_out_w = jnp.einsum(
        "td,te->de", attended_low, grad_branch, preferred_element_type=jnp.float32
    )
    grad_attended = jnp.einsum(
        "te,de->td", grad_branch, out_full, preferred_element_type=jnp.float32
    ).astype(jnp.bfloat16)
    grad_heads = grad_attended.reshape(row_count, head_count, head_size)
    delta = jnp.einsum("qhe,qhe->hq", grad_heads.astype(jnp.float32), attended_heads)
    zero_heads = jnp.zeros((row_count, head_count, head_size), jnp.float32)

    def key_grad_step(g_queries, step_index):
        scores, key_block, value_block = block_keys(step_index)
        weights_full = jnp.exp(scores - log_total[..., None])
        g_weights = jnp.einsum(
            "qhe,khe->hqk", grad_heads, value_block, preferred_element_type=jnp.float32
        )
        g_scores = (weights_full * (g_weights - delta[..., None])).astype(jnp.bfloat16)
        g_queries = (
            g_queries
            + jnp.einsum("hqk,khe->qhe", g_scores, key_block, preferred_element_type=jnp.float32)
            * score_scale
        )
        key_term = (
            jnp.einsum("hqk,qhe->khe", g_scores, query_heads, preferred_element_type=jnp.float32)
            * score_scale
        )
        value_term = jnp.einsum(
            "hqk,qhe->khe",
            weights_full.astype(jnp.bfloat16),
            grad_heads,
            preferred_element_type=jnp.float32,
        )
        return (
            g_queries,
            (key_term.reshape(block_rows, width), value_term.reshape(block_rows, width)),
        )

    grad_query_heads, block_terms = lax.scan(key_grad_step, zero_heads, block_ids)
    grad_query_f = grad_query_heads.reshape(row_count, width)
    key_sum, value_sum = (
        lax.psum_scatter(
            block_terms[0].reshape(seq_total, width), "band", scatter_dimension=0, tiled=True
        ),
        lax.psum_scatter(
            block_terms[1].reshape(seq_total, width), "band", scatter_dimension=0, tiled=True
        ),
    )
    grad_query_low = grad_query_f.astype(jnp.bfloat16)
    grad_key_low = key_sum.astype(jnp.bfloat16)
    grad_value_low = value_sum.astype(jnp.bfloat16)
    grad_project = jnp.concatenate([grad_query_low, grad_key_low, grad_value_low], axis=-1)
    grad_qkv_w = jnp.einsum(
        "td,te->de", normed_low, grad_project, preferred_element_type=jnp.float32
    )
    grad_shift_query = jnp.sum(grad_query_low.astype(jnp.float32), axis=0)
    grad_shift_value = jnp.sum(grad_value_low.astype(jnp.float32), axis=0)
    grad_normed = jnp.einsum(
        "te,de->td", grad_project, qkv_full, preferred_element_type=jnp.float32
    )
    grad_entering_norm, grad_gain_first, grad_shift_first = norm_first_back(grad_normed)
    grad_entering = grad_middle + grad_entering_norm
    input_grad = grad_entering.astype(jnp.bfloat16)
    entering_sum = jnp.sum(grad_entering, axis=0)
    grad_lead_rows = jnp.stack([lead_days * entering_sum, entering_sum])
    grad_gain_rows = jnp.stack([grad_gain_first, grad_gain_second])
    grad_shift_stack = jnp.stack(
        [
            grad_shift_first,
            grad_shift_query,
            grad_shift_value,
            grad_shift_out,
            grad_shift_second,
            grad_shift_down,
        ]
    )
    attention_sums = (
        lax.psum_scatter(grad_qkv_w, ("band", "samp"), scatter_dimension=0, tiled=True),
        lax.psum_scatter(grad_out_w, ("band", "samp"), scatter_dimension=0, tiled=True),
        lax.psum_scatter(grad_gain_rows, ("band", "samp"), scatter_dimension=1, tiled=True),
        lax.psum_scatter(grad_shift_stack, ("band", "samp"), scatter_dimension=1, tiled=True),
        lax.psum_scatter(grad_lead_rows, ("band", "samp"), scatter_dimension=1, tiled=True),
    )
    return (
        output[None],
        input_grad[None],
        attention_sums[0],
        attention_sums[1],
        ffn_sums[0],
        ffn_sums[1],
        ffn_sums[2],
        attention_sums[2],
        attention_sums[3],
        attention_sums[4],
    )


MESH = pl.DeviceIdType.MESH
F32 = jnp.float32
BF16 = jnp.bfloat16
PLANE = 8
DEPTH = 4
ROWS = 128
HALF = 64
BLOCK = 256
NN = (((1,), (0,)), ((), ()))
NT = (((1,), (1,)), ((), ()))
TN = (((0,), (0,)), ((), ()))
INNER = 32


def mm(left, right, dims=NN):
    return lax.dot_general(left, right, dims, preferred_element_type=F32)


def plane_kernel(
    lead_ref, gain_in, shift_in, leadw_in, bias_in, valid_in,
    tok_in, cot_in, wqkv_in, wout_in, wup_in, wdown_in,
    out_h, ig_h, gqkv_h, gout_h, gup_h, gdown_h, gain_h, shift_h, lead_h, bias_h,
    out_o, ig_o, gqkv_o, gout_o, gup_o, gdown_o, gain_o, shift_o, lead_o, bias_o,
    wqkv, wup, vcol, vec_in,
    agf, tokown, gbown, wq, wo, wu, wd, sq, su, ztr, vt, vecf, vrow,
    normed, qaug, kaug, kt, vv, vt2, pst, ot, invl, att, aown, dsend, dob, gsend, gcol, gproj, dk, dv,
    hid, gder, gpre, mid, gmid, gdf, sct,
    part, pr, cs, au, rr,
    gds, gus, gqs, gos, gdr, gur, gqr, gor_, gda, guc, gqc, goc, go2, go3, gu2, gq2, gua, gqa,
    acc, gub, vs, vsr, vz, vzr,
    in_s, out_s, ag_s, ag_r, ac_r, fw_s, fw_r, aq_s, aq_r, v_s, v_r, y_s, y_r, w_s, w_r, z_s, z_r,
    p_s, p_r, f_r, n_s, n_r, wg_s, wg_r, h_s, h_r, g_s, g_r, gc_s, gc_r,
):
    b = lax.axis_index("band")
    s = lax.axis_index("samp")
    c = b % 2
    x = (b // 2) % 2
    y = b // 4
    mate = b + 1 - 2 * c

    def chip(r):
        xx = x + (r % 2) * (1 - 2 * x)
        yy = y + (r // 2) * (1 - 2 * y)
        return yy * 2 + xx

    def near(r):
        return chip(r) * 2 + c

    def peer(k):
        return (b + k) % PLANE

    def level(k):
        return (s + k) % DEPTH

    barrier = pltpu.get_barrier_semaphore()
    for k in range(1, PLANE):
        pl.semaphore_signal(barrier, inc=1, device_id=(peer(k), s), device_id_type=MESH)
    for k in range(1, DEPTH):
        pl.semaphore_signal(barrier, inc=1, device_id=(b, level(k)), device_id_type=MESH)

    width = tok_in.shape[1]
    fetches = [
        pltpu.make_async_copy(src, dst, in_s.at[n])
        for n, (src, dst) in enumerate((
            (wqkv_in, wqkv), (wout_in, wo.at[b, pl.ds(pl.multiple_of(s * 32, 32), 32)]),
            (tok_in.at[pl.ds(0, HALF)], agf.at[0, 0, 0, c]),
            (tok_in.at[pl.ds(HALF, HALF)], agf.at[0, 0, 1, c]),
            (wup_in, wup), (wdown_in, wd.at[s]),
            (cot_in.at[pl.ds(0, HALF)], agf.at[1, 0, 0, c]),
            (cot_in.at[pl.ds(HALF, HALF)], agf.at[1, 0, 1, c]),
        ))
    ]
    for fetch in fetches:
        fetch.start()
    vcol[...] = jnp.zeros_like(vcol)
    vcol[0:2, 0:32] = gain_in[...].astype(F32)
    vcol[2:8, 0:32] = shift_in[...].astype(F32)
    vcol[8:10, 0:32] = leadw_in[...].astype(F32)
    line = lax.broadcasted_iota(jnp.int32, (16, 128), 0)
    tile = pltpu.roll(vcol[...], s * 32, 1)
    tile = jnp.where(line == 11 + s, bias_in[...].astype(F32), tile)
    vec_in[0] = tile.astype(BF16)
    opened = jnp.where(valid_in[...] > 0, 1.0, 0.0)
    vec_in[1] = jnp.where(line == 10, opened, 0.0).astype(BF16)
    far = (s + 2) % DEPTH
    ends = (s == 0) | (s == DEPTH - 1)
    inner = (s > 0) & (s < DEPTH - 1)

    @pl.when(s == 0)
    def _():
        for kept in (gdr, gur, gqr, gor_):
            kept[0] = jnp.zeros(kept.shape[1:], BF16)

    @pl.when(s == DEPTH - 1)
    def _():
        for kept in (gda, guc, gqc, goc):
            kept[...] = jnp.zeros(kept.shape, BF16)

    fetches[0].wait()
    for d in range(PLANE):
        for j in range(3):
            sq[d, :, j * 128:(j + 1) * 128] = wqkv[:, j * width + d * 128:j * width + (d + 1) * 128]
    fetches[1].wait()
    pl.semaphore_wait(barrier, PLANE - 1 + DEPTH - 1)

    def rc(src, dst, ss, rs, band, samp):
        return pltpu.make_async_remote_copy(
            src_ref=src, dst_ref=dst, send_sem=ss, recv_sem=rs,
            device_id=(band, samp), device_id_type=MESH,
        )

    def landed(ref, sem):
        rc(ref, ref, aq_s.at[0], sem, mate, s).wait_recv()

    def left(ref, sem):
        rc(ref, ref, sem, aq_r.at[0], mate, s).wait_send()

    def yc(kind, k, src, dst):
        return rc(src, dst, y_s.at[kind], y_r.at[kind], b, level(k))

    def weight_copy(kind, region, pieces, role, to):
        return rc(region(s), region(s), w_s.at[kind], w_r.at[kind, role], b, to)

    def weight_hand(kind, region, pieces):
        return rc(region(far), region(far), w_s.at[kind], w_r.at[kind, 2], b, 3 * (s - 1))

    def weight_start(*moved):
        @pl.when(s == 1)
        def _():
            weight_copy(*moved, 1, s - 1).start()

        weight_copy(*moved, 0, far).start()

        @pl.when(ends)
        def _():
            weight_copy(*moved, 1, 1 + s // 3).start()

        @pl.when(s == 2)
        def _():
            weight_copy(*moved, 1, s + 1).start()

        @pl.when(inner)
        def _():
            weight_copy(*moved, 2, DEPTH - 1 - s).start()

    def weight_pass(kind, region, pieces):
        @pl.when(inner)
        def _():
            landed(region(far), w_r.at[kind, 0])
            weight_hand(kind, region, pieces).start()

    def weight_most(kind, region, pieces):
        landed(region(DEPTH - 1 - far), w_r.at[kind, 1])

        @pl.when(ends)
        def _():
            landed(region(far), w_r.at[kind, 0])

    def weight_last(kind, region, pieces):
        landed(region(DEPTH - 1 - s), w_r.at[kind, 2])

    def weight_finish(*moved):
        weight_most(*moved)
        weight_last(*moved)

    def weight_sent(kind, region, pieces):
        @pl.when(ends)
        def _():
            left(pieces(2), w_s.at[kind])

        @pl.when(inner)
        def _():
            left(pieces(4), w_s.at[kind])

    def grad_up(kind, stage, got, via, pieces, t):
        return rc(stage(t), got(t), z_s.at[kind], z_r.at[kind, t], b, s + 1)

    def grad_down_to(kind, stage, got, via, pieces, t):
        return rc(stage(t), got(t), z_s.at[kind], z_r.at[kind, t], b, s - 1)

    def grad_down_last(kind, stage, got, via, pieces):
        return rc(stage(s - 1), via, z_s.at[kind], z_r.at[kind, DEPTH], b, s - 1)

    def grad_start(*moved):
        for hops in (3, 2, 1):
            grad_start_some(*moved, hops)

    def grad_start_some(kind, stage, got, via, pieces, hops):
        @pl.when(s == 0)
        def _():
            grad_up(kind, stage, got, via, pieces, hops).start()

        @pl.when(s == DEPTH - 1)
        def _():
            if hops == 1:
                grad_down_last(kind, stage, got, via, pieces).start()
            else:
                grad_down_to(kind, stage, got, via, pieces, DEPTH - 1 - hops).start()

    def down_half(half):
        rows = pl.ds(half * HALF, HALF)

        @pl.when(s == 0)
        def _():
            rc(gds.at[1, rows], gdr.at[1, rows], z_s.at[0], z_r.at[0, 1], b, 1).start()

        @pl.when(s == DEPTH - 1)
        def _():
            rc(gds.at[2, rows], gda.at[rows], z_s.at[0], z_r.at[0, DEPTH], b, DEPTH - 2).start()

    def add_in(kind, stage, got, via, pieces, t):
        landed(got(t), z_r.at[kind, t])
        term, more = stage(t), got(t)
        if len(via.shape) == 3:
            def add(j, _):
                term[j] = (term[j].astype(F32) + more[j].astype(F32)).astype(BF16)
                return 0

            lax.fori_loop(0, via.shape[0], add, 0)
        else:
            def add_rows(j, _):
                rows = pl.ds(pl.multiple_of(j * INNER, INNER), INNER)
                term[rows, :] = (term[rows, :].astype(F32) + more[rows, :].astype(F32)).astype(BF16)
                return 0

            lax.fori_loop(0, via.shape[0] // INNER, add_rows, 0)

    def grad_pass(*moved):
        @pl.when(s == 1)
        def _():
            add_in(*moved, 3)
            grad_up(*moved, 3).start()

        @pl.when(s == 2)
        def _():
            add_in(*moved, 0)
            grad_down_to(*moved, 0).start()

    def grad_pass_on(*moved):
        @pl.when(s == 1)
        def _():
            add_in(*moved, 2)
            grad_up(*moved, 2).start()
            add_in(*moved, 0)
            grad_down_last(*moved).start()

        @pl.when(s == 2)
        def _():
            add_in(*moved, 1)
            grad_down_last(*moved).start()
            add_in(*moved, 3)
            grad_up(*moved, 3).start()

    def grad_finish(kind, stage, got, via, pieces):
        @pl.when(s > 0)
        def _():
            landed(got(s), z_r.at[kind, s])

        @pl.when(s < DEPTH - 1)
        def _():
            landed(via, z_r.at[kind, DEPTH])

    def grad_sent(kind, stage, got, via, pieces):
        left(pieces(3), z_s.at[kind])

    results = ((out_o, out_h), (ig_o, ig_h), (gqkv_o, gqkv_h), (gout_o, gout_h), (gup_o, gup_h), (gdown_o, gdown_h),
               (gain_o, gain_h), (shift_o, shift_h), (lead_o, lead_h), (bias_o, bias_h))

    def deliver(n):
        return pltpu.make_async_copy(results[n][0], results[n][1], (in_s.at[n] if n < 8 else out_s.at[n - 8]))

    w_out_z = (
        0, lambda t: wo.at[b, pl.ds(pl.multiple_of(t * 32, 32), 32)],
        lambda n: wo.at[b, pl.ds(0, n * 32)],
    )
    w_qkv_z = (1, lambda t: wq.at[:, t], lambda n: wq.at[:, pl.ds(0, n)])
    w_up_z = (2, lambda t: wu.at[:, t], lambda n: wu.at[:, pl.ds(0, n)])
    w_down_z = (3, lambda t: wd.at[t], lambda n: wd.at[pl.ds(0, n)])
    g_down_z = (0, lambda t: gds.at[t], lambda t: gdr.at[t], gda, lambda n: gds.at[pl.ds(0, n)])
    g_up_z = (1, lambda t: gus.at[:, t], lambda t: gur.at[t], guc, lambda n: gus.at[:, pl.ds(0, n)])
    g_qkv_z = (2, lambda t: gqs.at[:, t], lambda t: gqr.at[t], gqc, lambda n: gqs.at[:, pl.ds(0, n)])
    g_out_z = (3, lambda t: gos.at[:, t], lambda t: gor_.at[t], goc, lambda n: gos.at[:, pl.ds(0, n)])

    def gather(op, r, turn):
        return rc(
            agf.at[op % 3, 0, (turn + r) % 2, c], agf.at[op % 3, 1 + turn, r - 1, c],
            ag_s.at[op], ag_r.at[op, turn], near(r), s,
        )

    def across(op, r):
        return rc(
            agf.at[op % 3, 1, r - 1, c], agf.at[op % 3, 3, r % 2, c],
            ag_s.at[op], ac_r.at[op], near(3 - r), s,
        )

    def share(op, blk):
        return rc(
            agf.at[op % 3, blk, :, c], agf.at[op % 3, blk, :, c],
            fw_s.at[op], fw_r.at[op, blk], mate, s,
        )

    def start_gather(op):
        for turn in (0, 1):
            for r in (1, 2):
                gather(op, r, turn).start()
        share(op, 0).start()

    def arrive(op, blk):
        if blk in (1, 2):
            landed(agf.at[op % 3, blk, :, c], ag_r.at[op, blk - 1])
        if blk == 1:
            for r in (1, 2):
                across(op, r).start()
        if blk == 3:
            landed(agf.at[op % 3, 3, :, c], ac_r.at[op])
        if blk:
            share(op, blk).start()

    def gathered(op):
        left(agf.at[op % 3, pl.ds(0, 3), :, 0], ag_s.at[op])
        left(agf.at[op % 3, :, :, 0], fw_s.at[op])

    def block(op, i):
        return agf[op, i].reshape(BLOCK, -1)

    def rows_half(dev, h):
        return wo.at[dev, pl.ds(h * HALF, HALF)]

    def rows_copy(r, turn):
        part_ = rows_half(b, (turn + r) % 2)
        return rc(part_, part_, wg_s.at[0], wg_r.at[turn], near(r), s)

    def rows_across(r):
        part_ = rows_half(near(r), r % 2)
        return rc(part_, part_, wg_s.at[0], wg_r.at[2], near(3 - r), s)

    def rows_share(r):
        dev = near(r) if r else b
        return rc(wo.at[dev], wo.at[dev], wg_s.at[1], wg_r.at[3], mate, s)

    def rows_start():
        for turn in (0, 1):
            for r in (1, 2):
                rows_copy(r, turn).start()
        rows_share(0).start()

    def granule(i, a):
        return (i, a) if i in (0, 3) else (a + 1, 1 - a if i == 1 else a)

    GRANULES = [(i, a) for i in (1, 0, 2, 3) for a in (0, 1)]

    def heads_copy(i, a, k):
        r, h = granule(i, a)
        rows = pl.ds(pl.multiple_of((a * 2 + k) * HALF, HALF), HALF)
        return rc(
            att.at[i, rows], aown.at[b, pl.ds(h * HALF, HALF)],
            h_s.at[0], h_r.at[0], chip(r) * 2 + k, s,
        )

    def cores(i):
        return (1 - c,) if i == 0 else (0, 1)

    def back_copy(i, a, k):
        r, h = granule(i, a)
        dev = chip(r) * 2 + k
        return rc(
            dsend.at[dev, pl.ds(h * HALF, HALF)], dob.at[i, a, c],
            g_s.at[0], g_r.at[i], dev, s,
        )

    def branch_copy(i, a, k):
        r, h = granule(i, a)
        dev = chip(r) * 2 + k
        return rc(
            gsend.at[dev, pl.ds(h * HALF, HALF)], gcol.at[i, a, c],
            gc_s.at[0], gc_r.at[0], dev, s,
        )

    def swap(kind, k, src, dst):
        return rc(src, dst, aq_s.at[kind], aq_r.at[kind], peer(k), s)

    for k in range(1, DEPTH):
        yc(0, k, vec_in.at[0], ztr.at[k - 1]).start()
    for k in range(1, PLANE):
        swap(0, k, sq.at[peer(k)], wq.at[b, s]).start()
    weight_start(*w_out_z)
    fetches[2].wait()
    fetches[3].wait()
    for r in (1, 2):
        gather(0, r, 0).start()
    wq[b, s] = sq[b]
    fetches[4].wait()
    for d in range(PLANE):
        su[d] = wup[:, d * 512:(d + 1) * 512]
    wu[b, s] = su[b]

    landed(sq.at[pl.ds(0, 7)], aq_r.at[0])
    weight_start(*w_qkv_z)
    landed(ztr, y_r.at[0])
    vt[...] = (
        vec_in[0].astype(F32) + vec_in[1].astype(F32)
        + ztr[0].astype(F32) + ztr[1].astype(F32) + ztr[2].astype(F32)
    ).astype(BF16)

    def spread(k):
        return rc(vt, vecf.at[b], v_s.at[0], v_r.at[0], peer(k), s)

    for k in range(1, PLANE):
        spread(k).start()
    for r in (1, 2):
        gather(0, r, 1).start()
    share(0, 0).start()
    vecf[b] = vt[...]
    for k in range(1, PLANE):
        swap(1, k, su.at[peer(k)], wu.at[b, s]).start()
    arrive(0, 1)
    fetches[6].wait()
    fetches[7].wait()
    for r in (1, 2):
        gather(1, r, 0).start()
    share(1, 0).start()
    landed(vecf.at[pl.ds(0, 7)], v_r.at[0])
    for d in range(PLANE):
        vrow[:, d * 128:(d + 1) * 128] = vecf[d].astype(F32)
    lead_days = lead_ref[0].astype(F32) * 0.25
    lane = lax.broadcasted_iota(jnp.int32, (1, 128), 1)
    head_lane = [(lane < 64).astype(F32), (lane >= 64).astype(F32)]
    ones_lane = jnp.where(lane < 2, 1.0, 0.0).astype(F32)
    ends_lane = jnp.where(lane == 0, 9984.0, jnp.where(lane == 1, 16.0, 0.0)).astype(F32)
    gain1, gain2 = vrow[0:1, :], vrow[1:2, :]
    shift1, shift_out, shift2, shift_down = vrow[2:3, :], vrow[5:6, :], vrow[6:7, :], vrow[7:8, :]
    lead_row = lead_days * vrow[8:9, :] + vrow[9:10, :]
    mine = vecf[b].astype(F32)

    def stats(v):
        mean = jnp.mean(v, axis=-1, keepdims=True)
        centered = v - mean
        variance = jnp.mean(centered * centered, axis=-1, keepdims=True)
        rstd = lax.rsqrt(variance + eps)
        return centered * rstd, rstd

    for r in range(4):
        for k in range(2):
            row = jnp.broadcast_to(vecf[chip(r) * 2 + k].astype(F32)[10:11, :], (128, 128))
            column = ((row.T - 1.0) * ends_lane).astype(BF16)
            for h in range(2):
                if r in (0, 3):
                    blk, a = r, h
                else:
                    blk, a = (1 if h == r % 2 else 2), r - 1
                top = blk * BLOCK + (a * 2 + k) * HALF
                kaug[top:top + HALF, 128:256] = column[h * HALF:(h + 1) * HALF]
    for h in range(2):
        for i in range(4):
            qaug[i, h * BLOCK:(h + 1) * BLOCK, 128:256] = jnp.broadcast_to(ones_lane, (BLOCK, 128)).astype(BF16)

    def norm_block(i):
        def chunk(j, _):
            rows = pl.ds(pl.multiple_of((j % 2) * INNER, INNER), INNER)
            ent = agf[0, i, j // 4, (j // 2) % 2, rows, :].astype(F32) + lead_row
            xhat = stats(ent)[0]
            put = pl.ds(pl.multiple_of(j * INNER, INNER), INNER)
            normed[i, put, :] = (xhat * gain1 + shift1).astype(BF16)
            return 0

        lax.fori_loop(0, BLOCK // INNER, chunk, 0)

    share(0, 0).wait_recv()
    norm_block(0)
    share(0, 1).wait_recv()
    arrive(0, 2)
    norm_block(1)
    weight_pass(*w_out_z)
    weight_pass(*w_qkv_z)
    share(0, 2).wait_recv()
    norm_block(2)
    weight_finish(*w_out_z)
    rows_start()
    landed(su.at[pl.ds(0, 7)], aq_r.at[1])

    @pl.when(inner)
    def _():
        weight_copy(*w_up_z, 1, 3 * (s - 1)).start()

    arrive(0, 3)
    share(0, 3).wait_recv()
    @pl.when(ends)
    def _():
        weight_start(*w_up_z)

    norm_block(3)

    weight_finish(*w_qkv_z)
    @pl.when(inner)
    def _():
        weight_copy(*w_up_z, 0, far).start()
        weight_copy(*w_up_z, 2, DEPTH - 1 - s).start()


    def project_block(q, _):
        rows = pl.ds(pl.multiple_of(q * BLOCK, BLOCK), BLOCK)
        pj = mm(normed[q], wq[...].reshape(width, 384))
        qv = (pj[:, 0:128] + mine[3:4, :]).astype(BF16).astype(F32) * 0.125
        for h in range(2):
            qaug[q, h * BLOCK:(h + 1) * BLOCK, 0:128] = (qv * head_lane[h]).astype(BF16)
        kv = pj[:, 128:256].astype(BF16)
        kaug[rows, 0:128] = kv
        kt[:, rows] = kv.T
        vb = (pj[:, 256:384] + mine[4:5, :]).astype(BF16)
        vv[rows, :] = vb
        vt2[:, rows] = vb.T
        return 0

    lax.fori_loop(0, 4, project_block, 0)

    def mate_copy(op, i):
        return rc(part.at[op, i, :, 1 - c], pr.at[op, i], p_s.at[op], p_r.at[op, i], mate, s)

    def far_copy(op, h):
        return rc(cs.at[op, 3, h], au.at[op, 1 - h], n_s.at[op], f_r.at[op], near(h + 1), s)

    def near_copy(op, i, a):
        h = a if i == 2 else 1 - a
        return rc(cs.at[op, i, a], rr.at[op, a, h], n_s.at[op], n_r.at[op], near(a + 1), s)

    def put_part(op, i, blk):
        part[op, i] = blk.astype(BF16).reshape(2, 2, HALF, width)
        mate_copy(op, i).start()

    def fold(op, i):
        mate_copy(op, i).wait_recv()

        def chunk(j, _):
            a = j // 2
            rows = pl.ds(pl.multiple_of((j % 2) * INNER, INNER), INNER)
            cs[op, i, a, rows, :] = (
                part[op, i, a, c, rows, :].astype(F32) + pr[op, i, a, rows, :].astype(F32)
            ).astype(BF16)
            return 0

        lax.fori_loop(0, ROWS // INNER, chunk, 0)

    def fold_before(op, i, near_too=True):
        @pl.when(i < 3)
        def _():
            fold(op, i + 1)

        @pl.when(i == 2)
        def _():
            send_far(op)

        if near_too:
            @pl.when(i == 1)
            def _():
                send_near(op, 2)

    def send_far(op):
        for h in (0, 1):
            far_copy(op, h).start()

    def send_near(op, i):
        for a in (0, 1):
            near_copy(op, i, a).start()

    def send_last(op):
        landed(au.at[op], f_r.at[op])
        for a in (0, 1):
            def chunk(j, _):
                rows = pl.ds(pl.multiple_of(j * INNER, INNER), INNER)
                cs[op, 1, a, rows, :] = (
                    cs[op, 1, a, rows, :].astype(F32) + au[op, a, rows, :].astype(F32)
                ).astype(BF16)
                return 0

            lax.fori_loop(0, HALF // INNER, chunk, 0)
            near_copy(op, 1, a).start()

    def wait_sums(op):
        landed(rr.at[op], n_r.at[op])

    def place(j):
        return j // 2, pl.ds(pl.multiple_of((j % 2) * INNER, INNER), INNER)

    def plane_total(op, j):
        h, rows = place(j)
        total = cs[op, 0, h, rows, :].astype(F32)
        return total + rr[op, 0, h, rows, :].astype(F32) + rr[op, 1, h, rows, :].astype(F32)

    def own_rows(op, j):
        h, rows = place(j)
        kept = {0: tokown, 3: gbown}.get(op)
        v = agf[op, 0, h, c, rows, :] if kept is None else kept[h, rows, :]
        return v.astype(F32)

    def set_rows(op, j, v):
        h, rows = place(j)
        if op == 3:
            gbown[h, rows, :] = v
        else:
            agf[op, 0, h, c, rows, :] = v

    def end_sums(op):
        left(part.at[op, :, :, 0], p_s.at[op])
        left(cs.at[op, pl.ds(0, 3)], n_s.at[op])

    def attend_block(n, _):
        i = 3 - n

        @pl.when(n == 3)
        def _():
            landed(wo.at[0], wg_r.at[1])
            for r in (1, 2):
                rows_share(r).start()

        st = mm(kaug[...], qaug[i], NT)
        p = jnp.exp(st - jnp.max(st, axis=0, keepdims=True))
        inverse = 1.0 / jnp.sum(p, axis=0, keepdims=True)
        pb = p.astype(BF16)
        pst[i] = pb
        out = mm(vt2[...], pb) * inverse
        ot[i, 0:64, :] = out[0:64, 0:BLOCK]
        ot[i, 64:128, :] = out[64:128, BLOCK:]
        invl[i] = jnp.broadcast_to(inverse, (8, 2 * BLOCK))
        att[i] = ot[i].T.astype(BF16)
        for blk in range(4):
            @pl.when(i == blk)
            def _():
                for a in (0, 1):
                    for k in cores(blk):
                        heads_copy(blk, a, k).start()

        return 0

    tokown[...] = agf[0, 0, :, c]
    gathered(0)
    landed(wo.at[0], wg_r.at[0])
    for r in (1, 2):
        rows_across(r).start()
    lax.fori_loop(0, 4, attend_block, 0)
    landed(wo.at[0], wg_r.at[2])
    rows_share(3).start()
    arrive(1, 1)
    for h in (0, 1):
        top = pl.multiple_of((h * 2 + c) * HALF, HALF)
        aown[b, h * HALF:(h + 1) * HALF] = att[0, pl.ds(top, HALF), :]
    weight_pass(*w_up_z)
    fetches[5].wait()

    @pl.when(inner)
    def _():
        weight_start(*w_down_z)

    landed(wo.at[pl.ds(0, 4)], wg_r.at[3])
    landed(aown.at[pl.ds(0, 7)], h_r.at[0])
    heads = jnp.concatenate([aown[d] for d in range(PLANE)], axis=1)
    mid[...] = mm(heads, wo[...].reshape(1024, width))
    agf[0, 0, :, c] = heads.reshape(2, HALF, width)

    def middle_chunk(j, _):
        rows = pl.ds(pl.multiple_of(j * INNER, INNER), INNER)
        m = own_rows(0, j) + lead_row + mid[rows, :] + shift_out
        mid[rows, :] = m
        set_rows(2, j, (stats(m)[0] * gain2 + shift2).astype(BF16))
        return 0

    lax.fori_loop(0, ROWS // INNER, middle_chunk, 0)
    start_gather(2)
    arrive(1, 3)
    arrive(2, 1)
    for r in (1, 2):
        gather(1, r, 1).start()
    start_gather(3)

    @pl.when(ends)
    def _():
        weight_start(*w_down_z)

    weight_finish(*w_up_z)

    bias = jnp.concatenate([mine[11 + j:12 + j, :] for j in range(4)], axis=1)

    def arrivals(op, i):
        for blk in range(4):
            @pl.when(i == blk)
            def _():
                if blk != 1:
                    arrive(op, blk)
                share(op, blk).wait_recv()

    def down_grad_first(f, _):
        cols = pl.ds(pl.multiple_of(f * BLOCK, BLOCK), BLOCK)
        gdf[pl.ds(pl.multiple_of(f * BLOCK, BLOCK), BLOCK), :] = mm(
            hid[:2 * BLOCK, cols], agf[1, 0:2].reshape(2 * BLOCK, width), TN
        )
        return 0

    def up_block(i, _):
        @pl.when(i == 3)
        def _():
            for blk in range(2):
                share(1, blk).wait_recv()
            lax.fori_loop(0, 2, down_grad_first, 0)

        arrivals(2, i)


        hp = mm(block(2, i), wu[...].reshape(width, 512)) + bias
        phi = 0.5 + 0.5 * lax.erf(hp * 0.7071067811865476)
        hid[pl.ds(pl.multiple_of(i * BLOCK, BLOCK), BLOCK), :] = (hp * phi).astype(BF16)
        gder[i] = phi + hp * jnp.exp(hp * hp * -0.5) * 0.3989422804014327
        return 0

    lax.fori_loop(0, 4, up_block, 0)
    weight_pass(*w_down_z)
    arrive(1, 2)
    share(1, 2).wait_recv()
    share(1, 3).wait_recv()

    def down_grad(f, _):
        cols = pl.ds(pl.multiple_of(f * BLOCK, BLOCK), BLOCK)
        g = gdf[pl.ds(pl.multiple_of(f * BLOCK, BLOCK), BLOCK), :] + mm(
            hid[2 * BLOCK:, cols], agf[1, 2:4].reshape(2 * BLOCK, width), TN
        )
        gds[pl.ds(2 * f, 2)] = g.astype(BF16).reshape(2, 128, width)
        return 0

    lax.fori_loop(0, 2, down_grad, 0)
    grad_start_some(*g_down_z, 3)
    grad_start_some(*g_down_z, 2)
    down_half(0)
    for i in range(4):
        for j in range(i + 1):
            upper = normed[j, :, i * BLOCK:(i + 1) * BLOCK].T
            if i != j:
                normed[j, :, i * BLOCK:(i + 1) * BLOCK] = normed[i, :, j * BLOCK:(j + 1) * BLOCK].T
            normed[i, :, j * BLOCK:(j + 1) * BLOCK] = upper
    def turn_second(i, _):
        cols = pl.ds(pl.multiple_of(i * BLOCK, BLOCK), BLOCK)
        blk = block(2, i)
        for f in range(4):
            sct[f, :, cols] = blk[:, f * BLOCK:(f + 1) * BLOCK].T
        return 0

    lax.fori_loop(0, 4, turn_second, 0)

    def even_out(n, _):
        i = n // 4
        rows = pl.ds(pl.multiple_of((n % 4) * BLOCK, BLOCK), BLOCK)
        pst[i, rows, :] = (pst[i, rows, :].astype(F32) * invl[i, 0:1, :]).astype(BF16)
        return 0

    lax.fori_loop(0, 16, even_out, 0)

    left(wo.at[pl.ds(0, 3)], wg_s.at[0])
    left(wo.at[pl.ds(0, 4)], wg_s.at[1])
    weight_sent(*w_out_z)

    def wo_block(i, j):
        return wo[2 * i:2 * i + 2, :, j * BLOCK:(j + 1) * BLOCK].reshape(BLOCK, BLOCK)

    for i in range(4):
        for j in range(i + 1):
            upper = wo_block(j, i).T.reshape(2, ROWS, BLOCK)
            if i != j:
                wo[2 * j:2 * j + 2, :, i * BLOCK:(i + 1) * BLOCK] = wo_block(i, j).T.reshape(2, ROWS, BLOCK)
            wo[2 * i:2 * i + 2, :, j * BLOCK:(j + 1) * BLOCK] = upper
    arrive(3, 1)
    arrive(3, 2)
    weight_finish(*w_down_z)
    gub[...] = jnp.zeros_like(gub)
    arrive(3, 3)

    def back_block(n, _):
        i = 3 - n
        rows = pl.ds(pl.multiple_of(i * BLOCK, BLOCK), BLOCK)
        gp = (gder[i] * mm(block(1, i), wd[...].reshape(512, width), NT)).astype(BF16)
        put_part(0, i, mm(gp, wu[...].reshape(width, 512), NT))
        gpre[rows, :] = gp
        gub[...] += jnp.sum(gp.astype(F32).reshape(BLOCK // 8, 8, 512), axis=0)
        fold_before(0, i)
        return 0

    grad_pass(*g_down_z)
    lax.fori_loop(0, 4, back_block, 0)
    fold(0, 0)

    def up_grad(f, _):
        g = mm(sct[pl.ds(2 * f, 2)].reshape(2 * BLOCK, 1024), gpre[...])
        gus[pl.ds(4 * f, 4)] = g.astype(BF16).reshape(4, 4, 32, 512)
        return 0

    lax.fori_loop(0, 2, up_grad, 0)
    grad_start(*g_up_z)

    def out_block(n, _):
        i = 3 - n
        rows = pl.ds(pl.multiple_of(i * BLOCK, BLOCK), BLOCK)
        put_part(1, i, mm(hid[rows, :], wd[...].reshape(512, width)))
        fold_before(1, i, near_too=False)
        return 0

    send_last(0)
    grad_pass_on(*g_down_z)
    lax.fori_loop(0, 4, out_block, 0)
    fold(1, 0)

    wait_sums(0)
    acc[...] = jnp.zeros_like(acc)

    def add_row(n, v):
        acc[n] += jnp.sum(v.reshape(INNER // 8, 8, width), axis=0)

    def norm_back(v, grad, gain):
        xhat, rstd = stats(v)
        d = grad * gain
        mean_d = jnp.mean(d, axis=-1, keepdims=True)
        mean_dx = jnp.mean(d * xhat, axis=-1, keepdims=True)
        return rstd * (d - mean_d - xhat * mean_dx), xhat

    def second_chunk(j, _):
        rows = pl.ds(pl.multiple_of(j * INNER, INNER), INNER)
        gs = plane_total(0, j)
        g, xhat = norm_back(mid[rows, :], gs, gain2)
        ct = own_rows(1, j)
        gm = ct + g
        gmid[rows, :] = gm
        gb = gm.astype(BF16)
        set_rows(3, j, gb)
        add_row(1, gs * xhat)
        add_row(6, gs)
        return 0

    lax.fori_loop(0, ROWS // INNER, second_chunk, 0)
    gbo = gbown[...].reshape(ROWS, width)
    gha = mm(gbo, wo[...].reshape(width, 1024)).astype(BF16)
    for d in range(PLANE):
        dsend[d] = gha[:, d * 128:(d + 1) * 128]
    for i, a in GRANULES:
        for k in cores(i):
            back_copy(i, a, k).start()
    for h in (0, 1):
        dob[0, h, c] = dsend[b, h * HALF:(h + 1) * HALF, :]
    for d in range(PLANE):
        gsend[d] = gbo[:, d * 128:(d + 1) * 128]
    for i, a in GRANULES:
        for k in cores(i):
            branch_copy(i, a, k).start()
    for h in (0, 1):
        gcol[0, h, c] = gsend[b, h * HALF:(h + 1) * HALF, :]

    grad_pass(*g_up_z)
    dk[...] = jnp.zeros_like(dk)
    dv[...] = jnp.zeros_like(dv)

    def attend_back(i, _):
        for blk in range(4):
            @pl.when(i == blk)
            def _():
                landed(dob.at[blk] if blk else dob.at[0, :, 0], g_r.at[blk])

        do_rows = dob[i].reshape(BLOCK, 128)
        do_cols = do_rows.T.astype(F32)
        prod = do_cols * ot[i]
        delta = jnp.concatenate(
            [jnp.sum(prod[h * 64:(h + 1) * 64], axis=0, keepdims=True) for h in range(2)], axis=1
        )
        zero = jnp.zeros((64, BLOCK), F32)
        spread_cols = jnp.concatenate([
            jnp.concatenate([do_cols[0:64], zero], axis=0),
            jnp.concatenate([zero, do_cols[64:128]], axis=0),
        ], axis=1).astype(BF16)
        spread_rows = jnp.concatenate(
            [(do_rows.astype(F32) * head_lane[h]).astype(BF16) for h in range(2)], axis=0
        )
        pb = pst[i]
        ds = (pb.astype(F32) * (mm(vv[...], spread_cols) - delta)).astype(BF16)
        dv[...] += mm(pb, spread_rows)
        dk[...] += mm(ds, qaug[i, :, 0:128])
        dq = mm(kt[...], ds)
        dq = jnp.concatenate([dq[0:64, 0:BLOCK], dq[64:128, BLOCK:]], axis=0).T * 0.125
        gproj[pl.ds(pl.multiple_of(i * BLOCK, BLOCK), BLOCK), 0:128] = dq.astype(BF16)
        return 0

    lax.fori_loop(0, 4, attend_back, 0)
    gproj[:, 128:256] = dk[...].astype(BF16)
    gproj[:, 256:384] = dv[...].astype(BF16)

    put_part(2, 3, mm(gproj[3 * BLOCK:, :], wq[...].reshape(width, 384), NT))
    gqs[...] = mm(normed[...].reshape(1024, 1024), gproj[...]).astype(BF16).reshape(8, 4, 32, 384)
    grad_start_some(*g_qkv_z, 3)
    grad_start_some(*g_qkv_z, 2)
    fold(2, 3)
    send_far(2)
    grad_pass_on(*g_up_z)

    def project_back(n, _):
        i = 2 - n
        rows = pl.ds(pl.multiple_of(i * BLOCK, BLOCK), BLOCK)
        put_part(2, i, mm(gproj[rows, :], wq[...].reshape(width, 384), NT))

        @pl.when(n == 1)
        def _():
            fold(2, 2)
            send_near(2, 2)

        return 0

    lax.fori_loop(0, 3, project_back, 0)
    fold(2, 1)
    fold(2, 0)
    grad_pass(*g_qkv_z)
    for i in range(4):
        share(3, i).wait_recv()
    landed(aown.at[pl.ds(0, 7)], gc_r.at[0])
    gos[...] = mm(gcol[...].reshape(1024, 128), agf[0].reshape(1024, width), TN).T.astype(BF16).reshape(
        PLANE, DEPTH, 32, 128
    )
    grad_start_some(*g_out_z, 3)
    grad_start_some(*g_out_z, 2)
    grad_start_some(*g_qkv_z, 1)
    grad_start_some(*g_out_z, 1)
    send_last(2)
    send_near(1, 2)
    send_last(1)

    def others(kind, stage, got, via, pieces):
        return [got(s), via]

    grad_pass(*g_out_z)
    grad_pass_on(*g_qkv_z)
    def own_sums(j, _):
        add_row(5, own_rows(3, j))
        add_row(7, own_rows(1, j))
        return 0

    lax.fori_loop(0, ROWS // INNER, own_sums, 0)
    wait_sums(2)

    def first_chunk(j, _):
        rows = pl.ds(pl.multiple_of(j * INNER, INNER), INNER)
        gn = plane_total(2, j)
        g, xhat = norm_back(own_rows(0, j) + lead_row, gn, gain1)
        ge = gmid[rows, :] + g
        ig_o[rows, :] = ge.astype(BF16)
        add_row(0, gn * xhat)
        add_row(2, gn)
        add_row(9, ge)
        return 0

    lax.fori_loop(0, ROWS // INNER, first_chunk, 0)
    deliver(1).start()
    acc[8] = acc[9] * lead_days

    sums = [jnp.sum(acc[n], axis=0, keepdims=True) for n in range(10)]
    packed = jnp.concatenate(sums + [jnp.zeros((6, width), F32)], axis=0)
    for d in range(PLANE):
        vs[d] = packed[:, d * 128:(d + 1) * 128]

    def vec_swap(k):
        return rc(vs.at[peer(k)], vsr.at[k - 1], v_s.at[1], v_r.at[1], peer(k), s)

    for k in range(1, PLANE):
        vec_swap(k).start()
    gq_cols = jnp.sum(gproj[:, 0:128].astype(F32), axis=0, keepdims=True)
    gv_cols = jnp.sum(gproj[:, 256:384].astype(F32), axis=0, keepdims=True)
    gub_row = jnp.sum(gub[...], axis=0, keepdims=True)
    extra = jnp.concatenate(
        [jnp.zeros((3, 128), F32), gq_cols, gv_cols, jnp.zeros((6, 128), F32)]
        + [gub_row[:, j * 128:(j + 1) * 128] for j in range(4)]
        + [jnp.zeros((1, 128), F32)],
        axis=0,
    )
    grad_finish(*g_up_z)
    for d in range(PLANE):
        gu2[d] = sum(
            [t[d].astype(F32) for t in others(*g_up_z)], gus[d, s].astype(F32)
        ).astype(BF16)
    for k in range(1, PLANE):
        swap(2, k, gu2.at[peer(k)], gua.at[b]).start()
    gua[b] = gu2[b]
    grad_pass_on(*g_out_z)
    landed(vs.at[pl.ds(0, 7)], v_r.at[1])
    total = vs[b] + extra
    for k in range(PLANE - 1):
        total = total + vsr[k]
    vz[...] = total
    for k in range(1, DEPTH):
        yc(1, k, vz, vzr.at[k - 1]).start()
    down_half(1)

    grad_finish(*g_qkv_z)
    for d in range(PLANE):
        gq2[d] = sum(
            [t[d].astype(F32) for t in others(*g_qkv_z)], gqs[d, s].astype(F32)
        ).astype(BF16)
    for k in range(1, PLANE):
        swap(3, k, gq2.at[peer(k)], gqa.at[b]).start()
    gqa[b] = gq2[b]
    grad_finish(*g_out_z)
    for d in range(PLANE):
        go2[d] = sum(
            [t[d].astype(F32) for t in others(*g_out_z)], gos[d, s].astype(F32)
        ).astype(BF16)
    for k in range(1, PLANE):
        swap(4, k, go2.at[peer(k)], go3.at[b]).start()
    go3[b] = go2[b]
    wait_sums(1)

    def output_chunk(j, _):
        rows = pl.ds(pl.multiple_of(j * INNER, INNER), INNER)
        out_o[rows, :] = (mid[rows, :] + plane_total(1, j) + shift_down).astype(BF16)
        return 0

    lax.fori_loop(0, ROWS // INNER, output_chunk, 0)
    deliver(0).start()

    grad_finish(*g_down_z)
    gdown_o[...] = sum([t[...].astype(F32) for t in others(*g_down_z)], gds[s].astype(F32))
    deliver(5).start()
    landed(gu2.at[pl.ds(0, 7)], aq_r.at[2])
    for d in range(PLANE):
        gup_o[:, d * 512:(d + 1) * 512] = gua[d].astype(F32)
    deliver(4).start()
    landed(vzr, y_r.at[1])
    vz_sum = vz[...] + vzr[0] + vzr[1] + vzr[2]
    columns = pltpu.roll(vz_sum, (128 - 32 * s) % 128, 1)
    gain_o[...] = columns[0:2, 0:32]
    shift_o[...] = columns[2:8, 0:32]
    lead_o[...] = columns[8:10, 0:32]
    bias_o[...] = jnp.sum(jnp.where(line == 11 + s, vz_sum, 0.0), axis=0, keepdims=True)
    for n in range(6, 10):
        deliver(n).start()
    landed(go2.at[pl.ds(0, 7)], aq_r.at[4])
    for d in range(PLANE):
        gout_o[:, d * 128:(d + 1) * 128] = go3[d].astype(F32)
    deliver(3).start()
    landed(gq2.at[pl.ds(0, 7)], aq_r.at[3])
    for d in range(PLANE):
        for j in range(3):
            gqkv_o[:, j * width + d * 128:j * width + (d + 1) * 128] = (
                gqa[d, :, j * 128:(j + 1) * 128].astype(F32)
            )

    deliver(2).start()
    for op in (1, 2, 3):
        gathered(op)
    for op in range(3):
        end_sums(op)
    left(aown.at[pl.ds(0, 7)], h_s.at[0])
    left(dsend.at[pl.ds(0, 7)], g_s.at[0])
    left(gsend.at[pl.ds(0, 7)], gc_s.at[0])
    for kind, sent in enumerate((sq, su, gu2, gq2, go2)):
        left(sent.at[pl.ds(0, 7)], aq_s.at[kind])
    left(vecf.at[pl.ds(0, 7)], v_s.at[0])
    left(vs.at[pl.ds(0, 7)], v_s.at[1])
    left(ztr, y_s.at[0])
    left(vzr, y_s.at[1])
    for moved in (w_qkv_z, w_up_z, w_down_z):
        weight_sent(*moved)
    for moved in (g_down_z, g_up_z, g_qkv_z, g_out_z):
        grad_sent(*moved)
    for n in range(10):
        deliver(n).wait()


def hand_over(*refs):
    count = len(refs) // 3
    given, taken, held, sems = refs[:count], refs[count:2 * count], refs[2 * count:3 * count], refs[-1]
    into = [pltpu.make_async_copy(given[n], held[n], sems.at[0, n]) for n in range(count)]
    out = [pltpu.make_async_copy(held[n], taken[n], sems.at[1, n]) for n in range(count)]
    for copy in into:
        copy.start()
    for n in range(count):
        into[n].wait()
        out[n].start()
    for copy in out:
        copy.wait()


def plane_body(
    tokens, cotangent, w_qkv, w_out, w_up, w_down,
    up_bias, norm_gains, shift_rows, lead_weight, lead_steps, valid_cells,
):
    width = tokens.shape[2]
    vmem = pl.BlockSpec(memory_space=pltpu.VMEM)
    anywhere = pl.BlockSpec(memory_space=pl.ANY)
    dma = pltpu.SemaphoreType.DMA
    V = pltpu.VMEM
    out_shape = (
        jax.ShapeDtypeStruct((ROWS, width), BF16),
        jax.ShapeDtypeStruct((ROWS, width), BF16),
        jax.ShapeDtypeStruct((32, 3 * width), F32),
        jax.ShapeDtypeStruct((32, width), F32),
        jax.ShapeDtypeStruct((32, 4 * width), F32),
        jax.ShapeDtypeStruct((128, width), F32),
        jax.ShapeDtypeStruct((2, 32), F32),
        jax.ShapeDtypeStruct((6, 32), F32),
        jax.ShapeDtypeStruct((2, 32), F32),
        jax.ShapeDtypeStruct((1, 128), F32),
    )
    scratch = [
        V((ROWS, width), BF16), V((ROWS, width), BF16),
        V((32, 3 * width), F32), V((32, width), F32),
        V((32, 4 * width), F32), V((128, width), F32),
        V((2, 32), F32), V((6, 32), F32), V((2, 32), F32), V((1, 128), F32),
        V((32, 3 * width), BF16), V((32, 4 * width), BF16),
        V((16, 128), F32), V((2, 16, 128), BF16),
        V((3, 4, 2, 2, HALF, width), BF16),
        V((2, HALF, width), BF16), V((2, HALF, width), BF16),
        V((PLANE, DEPTH, 32, 384), BF16),
        V((PLANE, 128, width), BF16),
        V((PLANE, DEPTH, 32, 512), BF16),
        V((DEPTH, 128, width), BF16),
        V((PLANE, 32, 384), BF16),
        V((PLANE, 32, 512), BF16),
        V((3, 16, 128), BF16),
        V((16, 128), BF16),
        V((PLANE, 16, 128), BF16),
        V((16, width), F32),
        V((4, BLOCK, width), BF16),
        V((4, 2 * BLOCK, 256), BF16),
        V((1024, 256), BF16),
        V((128, 1024), BF16),
        V((1024, 128), BF16),
        V((128, 1024), BF16),
        V((4, 1024, 2 * BLOCK), BF16),
        V((4, 128, BLOCK), F32),
        V((4, 8, 2 * BLOCK), F32),
        V((4, BLOCK, 128), BF16),
        V((PLANE, ROWS, 128), BF16),
        V((PLANE, ROWS, 128), BF16),
        V((4, 2, 2, HALF, 128), BF16),
        V((PLANE, ROWS, 128), BF16),
        V((4, 2, 2, HALF, 128), BF16),
        V((1024, 384), BF16),
        V((1024, 128), F32),
        V((1024, 128), F32),
        V((1024, 512), BF16),
        V((4, BLOCK, 512), F32),
        V((1024, 512), BF16),
        V((ROWS, width), F32),
        V((ROWS, width), F32),
        V((512, width), F32),
        V((4, BLOCK, 1024), BF16),
        V((3, 4, 2, 2, HALF, width), BF16),
        V((3, 4, 2, HALF, width), BF16),
        V((3, 4, 2, HALF, width), BF16),
        V((3, 2, HALF, width), BF16),
        V((3, 2, 2, HALF, width), BF16),
        V((DEPTH, 128, width), BF16),
        V((PLANE, DEPTH, 32, 512), BF16),
        V((PLANE, DEPTH, 32, 384), BF16),
        V((PLANE, DEPTH, 32, 128), BF16),
        V((DEPTH, 128, width), BF16),
        V((DEPTH, PLANE, 32, 512), BF16),
        V((DEPTH, PLANE, 32, 384), BF16),
        V((DEPTH, PLANE, 32, 128), BF16),
        V((128, width), BF16),
        V((PLANE, 32, 512), BF16),
        V((PLANE, 32, 384), BF16),
        V((PLANE, 32, 128), BF16),
        V((PLANE, 32, 128), BF16), V((PLANE, 32, 128), BF16),
        V((PLANE, 32, 512), BF16),
        V((PLANE, 32, 384), BF16),
        V((PLANE, 32, 512), BF16),
        V((PLANE, 32, 384), BF16),
        V((10, 8, width), F32),
        V((8, 512), F32),
        V((PLANE, 16, 128), F32),
        V((PLANE - 1, 16, 128), F32),
        V((16, 128), F32),
        V((3, 16, 128), F32),
        dma((8,)), dma((2,)),
        dma((4,)), dma((4, 2)), dma((4,)), dma((4,)), dma((4, 4)),
        dma((5,)), dma((5,)), dma((2,)), dma((2,)), dma((2,)), dma((2,)),
        dma((4,)), dma((4, 3)), dma((4,)), dma((4, 5)),
        dma((3,)), dma((3, 4)), dma((3,)), dma((3,)), dma((3,)),
        dma((2,)), dma((4,)), dma((1,)), dma((1,)), dma((1,)), dma((4,)), dma((1,)), dma((1,)),
    ]
    results = pl.pallas_call(
        plane_kernel,
        out_shape=out_shape,
        in_specs=[pl.BlockSpec(memory_space=pltpu.SMEM)] + [vmem] * 5 + [anywhere] * 6,
        out_specs=tuple([anywhere] * 10),
        scratch_shapes=scratch,
        compiler_params=pltpu.CompilerParams(
            collective_id=0, has_side_effects=True, vmem_limit_bytes=63 * 2**20
        ),
    )(
        lead_steps, norm_gains, shift_rows, lead_weight, up_bias[None], valid_cells,
        tokens[0], cotangent[0], w_qkv, w_out, w_up, w_down,
    )
    results = pl.pallas_call(
        hand_over,
        out_shape=out_shape,
        in_specs=[anywhere] * len(out_shape),
        out_specs=tuple([anywhere] * len(out_shape)),
        scratch_shapes=[V(o.shape, o.dtype) for o in out_shape] + [dma((2, len(out_shape)))],
    )(*results)
    output, input_grad, g_qkv, g_out, g_up, g_down, g_gains, g_shifts, g_lead, g_bias = results
    return (
        output[None], input_grad[None], g_qkv, g_out, g_up, g_down, g_bias[0],
        g_gains, g_shifts, g_lead,
    )


def plane_fits(mesh):
    return mesh.shape["band"] == PLANE and mesh.shape["samp"] == DEPTH


def solution(mesh):
    return jax.shard_map(
        plane_body if plane_fits(mesh) else body,
        mesh=mesh,
        in_specs=(
            P("samp", "band", None),
            P("samp", "band", None),
            P(("band", "samp"), None),
            P(("band", "samp"), None),
            P(("band", "samp"), None),
            P(("band", "samp"), None),
            P(("band", "samp")),
            P(None, ("band", "samp")),
            P(None, ("band", "samp")),
            P(None, ("band", "samp")),
            P("samp"),
            P("samp", "band"),
        ),
        out_specs=(
            P("samp", "band", None),
            P("samp", "band", None),
            P(("band", "samp"), None),
            P(("band", "samp"), None),
            P(("band", "samp"), None),
            P(("band", "samp"), None),
            P(("band", "samp")),
            P(None, ("band", "samp")),
            P(None, ("band", "samp")),
            P(None, ("band", "samp")),
        ),
        check_vma=False,
    )
```
